32 devices in a mesh: fsdp: 8 (over z, y), ctx: 4 (over x, core).
Axes of the slice: x: 2, y: 2, z: 4, core: 2. Of those that a mesh axis runs over, the one named last changes fastest.
Arguments:
- tokens_in: bfloat16 [32768, 1536], P(('fsdp', 'ctx')), may hold values from -6 to 6
- cotangent: bfloat16 [32768, 1536], P(('fsdp', 'ctx')), may hold values from -6 to 6
- doc_lengths: int32 [8, 4], P('fsdp'), may hold values from 1 to 4093, as said below
- in_proj: float32 [1536, 6448], P('fsdp'), may hold values from -0.15625 to 0.15625
- out_proj: float32 [3072, 1536], P('fsdp'), may hold values from -0.109375 to 0.109375
- norm_gain: float32 [1536], replicated, may hold values from 0.5 to 1.5
- gate_gain: float32 [3072], replicated, may hold values from 0.5 to 1.5
- conv_weight: float32 [3328, 4], replicated, may hold values from -3 to 3
- conv_bias: float32 [3328], replicated, may hold values from -0.5 to 0.5
- delta_bias: float32 [48], replicated, may hold values from -12 to -4
- decay_log: float32 [48], replicated, may hold values from 0 to 2.77
- skip_scale: float32 [48], replicated, may hold values from 0.05 to 0.3
- in_first: float32 [1536, 6448], P('fsdp'), may hold values from -32 to 32
- in_second: float32 [1536, 6448], P('fsdp'), may hold values from 155.12372 to 620.4949
- out_first: float32 [3072, 1536], P('fsdp'), may hold values from -128 to 128
- out_second: float32 [3072, 1536], P('fsdp'), may hold values from 1723.5968 to 6894.387
- small_first: float32 [21392], replicated, may hold values from -64 to 64
- small_second: float32 [21392], replicated, may hold values from 430.8992 to 1723.5968
Outputs:
- block_out: bfloat16 [32768, 1536], P(('fsdp', 'ctx'))
- input_grad: float32 [32768, 1536], P(('fsdp', 'ctx'))
- in_proj_new: float32 [1536, 6448], P('fsdp')
- in_first_new: float32 [1536, 6448], P('fsdp')
- in_second_new: float32 [1536, 6448], P('fsdp')
- out_proj_new: float32 [3072, 1536], P('fsdp')
- out_first_new: float32 [3072, 1536], P('fsdp')
- out_second_new: float32 [3072, 1536], P('fsdp')
- small_new: float32 [21392], replicated
- small_first_new: float32 [21392], replicated
- small_second_new: float32 [21392], replicated
The draws below stay inside these ranges and needn't reach their ends.
Inputs may be any that keep to these rules, and one draw needn't show every extreme that they name: `doc_lengths`: each row's lengths sum to 4096; all but one of them are at most 256, so one document of every group covers positions of every index of ctx; where the long one stands is drawn. In some group all other documents have length 1, so that its long one has 4093 positions.
All inputs are finite; a program needn't handle non-finite values.
Results may differ from the reference program's by a relative error of at most 0.002.
The reference program's roundings to bfloat16 on the way count: a program that leaves them out, or rounds other values in their place, can miss the bound.
Values may be sent and summed in bfloat16 or wider, within the bound.
A program may use at most 448 MiB of HBM per device.

```python
import math
import jax
import jax.numpy as jnp
from jax import lax

D = 1536
DI = 3072
NH = 48
HD = 64
DS = 128
CONV = 4
SPAN = 256
DOCS = 4
STEP = 5
TOK_DEV = 1024
ZW = 6448
CONVD = 3328
VEC = 21392
GROUPS = 8
STREAM = 4096
TOKENS = 32768


def draw_doc_lengths(key, part):
    key = jax.random.fold_in(key, 11)
    short_key, order_key, pick_key = jax.random.split(key, 3)
    shorts = jax.random.randint(short_key, (GROUPS, DOCS - 1), 1, TOK_DEV // 4 + 1)
    chosen = jax.random.randint(pick_key, (), 0, GROUPS)
    rows = jnp.arange(GROUPS, dtype=jnp.int32)[:, None]
    shorts = jnp.where(rows == chosen, 1, shorts).astype(jnp.int32)
    longest = STREAM - jnp.sum(shorts, axis=1, keepdims=True)
    lengths = jnp.concatenate([longest, shorts], axis=1).astype(jnp.int32)
    scores = jax.random.randint(order_key, (GROUPS, DOCS), 0, 1 << 20) * DOCS + jnp.arange(DOCS, dtype=jnp.int32)[None, :]
    order = jnp.argsort(scores, axis=1)
    return jnp.take_along_axis(lengths, order, axis=1).astype(jnp.int32)


def level_of(rng, dims, cuts, least, largest):
    loudness = 1.0
    for position, blocks in cuts:
        steps = jax.random.uniform(jax.random.fold_in(jax.random.fold_in(rng, 6), position), (blocks,), jnp.float32, least / len(cuts), largest / len(cuts))
        loudness = loudness * jnp.repeat(jnp.exp(steps), dims[position] // blocks).reshape((-1,) + (1,) * (len(dims) - 1 - position))
    return loudness


def centred(stream_key, dims, spread, most, cuts=(), kind=jnp.bfloat16):
    values = jax.random.normal(stream_key, dims, jnp.float32) * spread
    if len(cuts) > 0:
        values = level_of(stream_key, dims, cuts, -0.22, 0.18) * values
    return jnp.clip(values, min=-most, max=most).astype(kind)


def setup_inputs(seed: int = 0) -> dict:
    key_list = jax.random.split(jax.random.key(seed), 19)
    tokens_in = centred(key_list[0], (TOKENS, D), 1.0, 6.0, ((0, 32),))
    cotangent = centred(key_list[1], (TOKENS, D), 1.0, 6.0, ((0, 32),))
    doc_lengths = draw_doc_lengths(jax.random.fold_in(key_list[18], 71), 0)
    in_proj = centred(key_list[3], (D, ZW), D ** -0.5, 0.15625, ((0, 8),), jnp.float32)
    out_proj = centred(key_list[4], (DI, D), DI ** -0.5, 0.109375, ((0, 8),), jnp.float32)
    norm_gain = jnp.clip(1.0 + 0.1 * jax.random.normal(key_list[5], (D,), jnp.float32), 0.5, 1.5)
    gate_gain = jnp.clip(1.0 + 0.1 * jax.random.normal(key_list[6], (DI,), jnp.float32), 0.5, 1.5)
    conv_weight = centred(key_list[7], (CONVD, CONV), CONV ** -0.5, 3.0, (), jnp.float32)
    conv_bias = jnp.clip(jax.random.uniform(key_list[8], (CONVD,), jnp.float32, -0.5, 0.5), -0.5, 0.5)
    delta_bias = jnp.clip(jax.random.uniform(key_list[9], (NH,), jnp.float32, -12.0, -4.0), -12.0, -4.0)
    decay_log = jnp.clip(jax.random.uniform(key_list[10], (NH,), jnp.float32, 0.0, 2.77), 0.0, 2.77)
    skip_scale = jnp.clip(jax.random.uniform(key_list[11], (NH,), jnp.float32, 0.05, 0.3), 0.05, 0.3)
    in_first = centred(key_list[12], (D, ZW), (0.111 * 0.3 * TOKENS ** 0.5), 32.0, ((0, 8),), jnp.float32)
    in_second = jnp.clip(jnp.exp(math.log(620.4949) - 1.3862944 * jax.random.uniform(key_list[13], (D, ZW), jnp.float32) ** level_of(key_list[13], (D, ZW), ((0, 8),), -0.2, 0.2)), 155.12372, 620.4949)
    out_first = centred(key_list[14], (DI, D), (0.111 * TOKENS ** 0.5), 128.0, ((0, 8),), jnp.float32)
    out_second = jnp.clip(jnp.exp(math.log(6894.387) - 1.3862944 * jax.random.uniform(key_list[15], (DI, D), jnp.float32) ** level_of(key_list[15], (DI, D), ((0, 8),), -0.2, 0.2)), 1723.5968, 6894.387)
    small_first = centred(key_list[16], (VEC,), (0.111 * 0.5 * TOKENS ** 0.5), 64.0, (), jnp.float32)
    small_second = jnp.clip(jnp.exp(jax.random.uniform(key_list[17], (VEC,), jnp.float32, math.log(430.8992), math.log(1723.5968))), 430.8992, 1723.5968)
    return dict(tokens_in=tokens_in, cotangent=cotangent, doc_lengths=doc_lengths, in_proj=in_proj, out_proj=out_proj, norm_gain=norm_gain, gate_gain=gate_gain, conv_weight=conv_weight, conv_bias=conv_bias, delta_bias=delta_bias, decay_log=decay_log, skip_scale=skip_scale, in_first=in_first, in_second=in_second, out_first=out_first, out_second=out_second, small_first=small_first, small_second=small_second)


@jax.custom_vjp
def low(v):
    return lax.optimization_barrier(v.astype(jnp.bfloat16)).astype(jnp.float32)

@jax.custom_vjp
def low_back(v):
    return v

def low_keep(v):
    return (low(v), None)

def low_pass(kept, grad):
    return (grad,)

def back_keep(v):
    return (v, None)

def back_low(kept, grad):
    return (low(grad),)
low.defvjp(low_keep, low_pass)
low_back.defvjp(back_keep, back_low)
highest = lax.Precision.HIGHEST
norm_eps = 1e-05
beta_one = 0.9
beta_two = 0.95
adam_eps = 1e-08
learn_rate = 0.05
weight_decay = 0.1

def segment_info(lengths, positions):
    ends = jnp.cumsum(lengths).astype(jnp.int32)
    starts = (ends - lengths).astype(jnp.int32)
    segment = lax.optimization_barrier(jnp.sum((positions[:, None] >= ends[None, :]).astype(jnp.int32), axis=1)).astype(jnp.int32)
    first = lax.optimization_barrier(jnp.sum((positions[:, None] == starts[None, :]).astype(jnp.int32), axis=1)).astype(jnp.int32)
    return (segment, first)

def rms_norm(inputs, gain):
    return inputs * lax.rsqrt(lax.optimization_barrier(jnp.mean(inputs * inputs, axis=-1, keepdims=True)) + norm_eps) * gain[None, :]

def prepare(mixed, edge, segment, edge_segment, conv_weight, conv_bias, delta_bias, decay_log):
    count = mixed.shape[0]
    gate_part = mixed[:, :DI]
    conv_part = mixed[:, DI:DI + CONVD]
    raw_step = mixed[:, DI + CONVD:]
    extended = jnp.concatenate([edge, conv_part], axis=0)
    ext_segment = jnp.concatenate([edge_segment, segment], axis=0)
    total = jnp.zeros_like(conv_part) + conv_bias[None, :]
    for offset in range(CONV):
        same = (ext_segment[offset:offset + count] == segment).astype(jnp.float32)
        total = total + conv_weight[:, offset][None, :] * extended[offset:offset + count] * same[:, None]
    conved = jax.nn.silu(total)
    inner = conved[:, :DI].reshape(count, NH, HD)
    keys_in = conved[:, DI:DI + DS]
    queries = conved[:, DI + DS:]
    steps = jax.nn.softplus(raw_step + delta_bias[None, :])
    log_decay = -jnp.exp(decay_log)[None, :] * steps
    return (gate_part, inner, steps, log_decay, keys_in, queries)

def split_spans(inner, steps, log_decay, keys_in, queries, segment, first):
    blocks = inner.shape[0] // SPAN
    cumul = jnp.cumsum(log_decay.reshape(blocks, SPAN, NH), axis=1)
    carry = (jnp.cumsum(first.reshape(blocks, SPAN), axis=1) == 0).astype(jnp.float32)
    return (inner.reshape(blocks, SPAN, NH, HD), steps.reshape(blocks, SPAN, NH), cumul, keys_in.reshape(blocks, SPAN, DS), queries.reshape(blocks, SPAN, DS), segment.reshape(blocks, SPAN), carry)

def span_end(inner, steps, cumul, keys_in, segment, carry):
    last = (segment == segment[-1]).astype(jnp.float32)
    weight = jnp.exp(cumul[-1][None, :] - cumul) * steps * last[:, None]
    fresh = jnp.einsum('sh,shp,sn->hpn', weight, inner, keys_in, precision=highest)
    factor = carry[-1] * jnp.exp(cumul[-1])
    return (fresh, factor)

def span_out(state, inner, steps, cumul, keys_in, queries, segment, carry):
    length = queries.shape[0]
    scores = jnp.dot(queries, keys_in.T, precision=highest)
    index = jnp.arange(length, dtype=jnp.int32)
    causal = (index[:, None] >= index[None, :]) & (segment[:, None] == segment[None, :])
    diff = cumul.T[:, :, None] - cumul.T[:, None, :]
    decay = jnp.exp(jnp.where(causal[None], diff, 0.0)) * causal.astype(jnp.float32)[None]
    weights = decay * scores[None] * steps.T[:, None, :]
    local = jnp.einsum('hts,shp->thp', weights, inner, precision=highest)
    carried = jnp.einsum('tn,hpn->thp', queries, state, precision=highest)
    return local + carried * (carry[:, None] * jnp.exp(cumul))[:, :, None]

def span_step(state, pieces):
    inner, steps, cumul, keys_in, queries, segment, carry = pieces
    fresh, factor = span_end(inner, steps, cumul, keys_in, segment, carry)
    result = span_out(state, inner, steps, cumul, keys_in, queries, segment, carry)
    return (factor[:, None, None] * state + fresh, result)

def mixer_tail(gate_part, inner, steps, log_decay, keys_in, queries, state_in, skip_scale, gate_gain, segment, first):
    pieces = split_spans(inner, steps, log_decay, keys_in, queries, segment, first)
    final, outputs = lax.scan(jax.checkpoint(span_step), state_in, pieces)
    count = inner.shape[0]
    mixer = outputs.reshape(count, NH, HD) + skip_scale[None, :, None] * inner
    gated = mixer.reshape(count, DI) * jax.nn.silu(gate_part)
    return gated * lax.rsqrt(lax.optimization_barrier(jnp.mean(gated * gated, axis=-1, keepdims=True)) + norm_eps) * gate_gain[None, :]

def adamw_update(param, grad, first, second, decay):
    first_new = beta_one * first + (1.0 - beta_one) * grad
    second_new = beta_two * second + (1.0 - beta_two) * grad * grad
    first_hat = first_new / (1.0 - beta_one ** STEP)
    second_hat = second_new / (1.0 - beta_two ** STEP)
    param_new = param - learn_rate * (first_hat / (jnp.sqrt(second_hat) + adam_eps) + decay * param)
    return (param_new, first_new, second_new)

def group_forward(inputs, lengths, in_low, out_low, norm_gain, gate_gain, conv_weight, conv_bias, delta_bias, decay_log, skip_scale):
    positions = jnp.arange(STREAM, dtype=jnp.int32)
    segment, first = segment_info(lengths, positions)
    edge_segment = segment_info(lengths, jnp.arange(CONV - 1, dtype=jnp.int32) - (CONV - 1))[0]
    normed = low(rms_norm(inputs, norm_gain))
    mixed = low_back(jnp.dot(normed, in_low, precision=highest))
    edge = jnp.zeros((CONV - 1, CONVD), jnp.float32)
    gate_part, inner, steps, log_decay, keys_in, queries = prepare(mixed, edge, segment, edge_segment, conv_weight, conv_bias, delta_bias, decay_log)
    state_in = jnp.zeros((NH, HD, DS), jnp.float32)
    mixer_out = low(mixer_tail(gate_part, inner, steps, log_decay, keys_in, queries, state_in, skip_scale, gate_gain, segment, first))
    return inputs + jnp.dot(mixer_out, out_low, precision=highest)

def reference(tokens_in, cotangent, doc_lengths, in_proj, out_proj, norm_gain, gate_gain, conv_weight, conv_bias, delta_bias, decay_log, skip_scale, in_first, in_second, out_first, out_second, small_first, small_second):
    inputs = tokens_in.astype(jnp.float32).reshape(GROUPS, STREAM, D)
    back = cotangent.astype(jnp.float32).reshape(GROUPS, STREAM, D)

    def forward(inputs, in_proj, out_proj, norm_gain, gate_gain, conv_weight, conv_bias, delta_bias, decay_log, skip_scale):
        in_low = low(in_proj)
        out_low = low(out_proj)

        def one_group(pair):
            return group_forward(pair[0], pair[1], in_low, out_low, norm_gain, gate_gain, conv_weight, conv_bias, delta_bias, decay_log, skip_scale)
        return lax.map(jax.checkpoint(one_group), (inputs, doc_lengths))
    outputs, pull = jax.vjp(forward, inputs, in_proj, out_proj, norm_gain, gate_gain, conv_weight, conv_bias, delta_bias, decay_log, skip_scale)
    grads = pull(back)
    block_out = outputs.reshape(TOKENS, D).astype(jnp.bfloat16)
    input_grad = grads[0].reshape(TOKENS, D)
    in_new, in_first_new, in_second_new = adamw_update(in_proj, grads[1], in_first, in_second, weight_decay)
    out_new, out_first_new, out_second_new = adamw_update(out_proj, grads[2], out_first, out_second, weight_decay)
    small_param = jnp.concatenate([norm_gain, gate_gain, conv_weight.reshape(-1), conv_bias, delta_bias, decay_log, skip_scale])
    small_grad = jnp.concatenate([grads[3], grads[4], grads[5].reshape(-1), grads[6], grads[7], grads[8], grads[9]])
    small_new, small_first_new, small_second_new = adamw_update(small_param, small_grad, small_first, small_second, 0.0)
    return (block_out, input_grad, in_new, in_first_new, in_second_new, out_new, out_first_new, out_second_new, small_new, small_first_new, small_second_new)
```

```python
import functools

import jax
import jax.numpy as jnp
from jax import lax
from jax.experimental import pallas as pl
from jax.experimental.pallas import tpu as pltpu
from jax.sharding import PartitionSpec as P

D = 1536
DI = 3072
NH = 48
HD = 64
DS = 128
CONV = 4
SPAN = 256
STEP = 5
CONVD = 3328
LANES = 128
PAIRS = DI // LANES
HALF = SPAN // 2
NORM_ROWS = 128
NORM_COLS = 512
MASKED = -1e30

highest = lax.Precision.HIGHEST
norm_eps = 1e-05
beta_one = 0.9
beta_two = 0.95
adam_eps = 1e-08
learn_rate = 0.05
weight_decay = 0.1
f32 = jnp.float32
bf16 = jnp.bfloat16
VMEM_LIMIT = 56 * 1024 * 1024


def split(value):
    high = value.astype(bf16)
    return high, (value - high.astype(f32)).astype(bf16)


def mm(a, b):
    return jnp.dot(a, b, preferred_element_type=f32)


def mm_nt(a, b):
    return lax.dot_general(a, b, (((1,), (1,)), ((), ())), preferred_element_type=f32)


def sigmoid(v):
    return 1.0 / (1.0 + jnp.exp(-v))


def conv_shifts(block, edge, inside, outside):
    shifted = []
    for j in range(1, CONV):
        body = inside[j - 1] * pltpu.roll(block, j, 0)
        head = body[:8] + outside[j - 1] * pltpu.roll(edge, j, 0)
        shifted.append(jnp.concatenate([head, body[8:]], axis=0))
    return shifted


def conv_pre(block, shifted, taps):
    total = taps[4:5] + taps[3:4] * block
    for j in range(1, CONV):
        total = total + taps[3 - j : 4 - j] * shifted[j - 1]
    return total


def pair_columns(packed, pair):
    turned = pltpu.roll(packed, lax.rem(LANES - 2 * pair, LANES), 1)
    lane = lax.broadcasted_iota(jnp.int32, packed.shape, 1)
    first = jnp.where(lane < HD, turned[:, 0:1], turned[:, 1:2])
    second = jnp.where(lane < HD, turned[:, 64:65], turned[:, 65:66])
    return turned, first, second


def forward_kernel(
    spans,
    block_ref,
    key_ref,
    query_ref,
    edge_ref,
    key_edge_ref,
    query_edge_ref,
    taps_ref,
    key_taps_ref,
    query_taps_ref,
    inside_ref,
    outside_ref,
    steps_ref,
    decay_ref,
    rows_ref,
    factor_ref,
    mask_ref,
    inner_out,
    local_out,
    state_out,
    key_out,
    query_out,
    scores,
    key_turned,
    query_both,
):
    pair = pl.program_id(0)

    @pl.when(pair == 0)
    def _():
        for src, edge, taps, out in (
            (key_ref, key_edge_ref, key_taps_ref, key_out),
            (query_ref, query_edge_ref, query_taps_ref, query_out),
        ):
            pre = conv_pre(
                src[...], conv_shifts(src[...], edge[...], inside_ref, outside_ref), taps[...]
            )
            out[...] = pre * sigmoid(pre)
        for k in range(spans):
            rows = pl.ds(k * SPAN, SPAN)
            keys, queries = key_out[rows, :], query_out[rows, :]
            kh, kl = split(keys)
            qh, ql = split(queries)
            query_both[rows, :] = jnp.concatenate([qh, ql], axis=1)
            scores[k] = mm_nt(
                jnp.concatenate([qh, ql], axis=1), jnp.concatenate([kh, kh], axis=1)
            ) + mm_nt(qh, kl)
            th, tl = split(keys.T)
            key_turned[k, 0] = th
            key_turned[k, 1] = tl

    block = block_ref[...]
    pre = conv_pre(
        block, conv_shifts(block, edge_ref[...], inside_ref, outside_ref), taps_ref[...]
    )
    inner = pre * sigmoid(pre)
    inner_out[...] = inner
    turned, unused, steps = pair_columns(steps_ref[...], pair)
    unused, enter, leave = pair_columns(decay_ref[...], pair)
    scaled = steps * inner
    leaving = leave * scaled
    lane = lax.broadcasted_iota(jnp.int32, (HALF, LANES), 1)
    state = None
    for k in range(spans):
        at = k * SPAN
        sh, sl = split(scaled[at : at + SPAN])
        both = jnp.concatenate([sh, sl], axis=1)
        parts = []
        for half in range(2):
            per_head = []
            width = HALF * (half + 1)
            for a in range(2):
                row = rows_ref[0, a : a + 1, pl.ds(at, width)]
                column = turned[at + half * HALF : at + (half + 1) * HALF, a : a + 1]
                decay = jnp.exp(
                    jnp.minimum(
                        column - row, mask_ref[k, pl.ds(half * HALF, HALF), pl.ds(0, width)]
                    )
                )
                weights = decay * scores[k, pl.ds(half * HALF, HALF), pl.ds(0, width)]
                wh, wl = split(weights)
                wide = mm(wh, both[:width])
                per_head.append(wide[:, :LANES] + wide[:, LANES:] + mm(wl, sh[:width]))
            parts.append(jnp.where(lane < HD, per_head[0], per_head[1]))
        local = jnp.concatenate(parts, axis=0)
        ph, pw = split(leaving[at : at + SPAN])
        fresh = mm(key_turned[k, 0], jnp.concatenate([ph, pw], axis=1))
        fresh = fresh[:, :LANES] + fresh[:, LANES:] + mm(key_turned[k, 1], ph)
        if state is None:
            state = fresh
        else:
            th, tl = split(state)
            q2 = query_both[pl.ds(at, SPAN), :]
            carried = mm(q2, jnp.concatenate([th, th], axis=0)) + mm(q2[:, :DS], tl)
            local = local + enter[at : at + SPAN] * carried
            state = factor_ref[k : k + 1] * state + fresh
        state_out[k] = state
        local_out[pl.ds(at, SPAN), :] = local


def forward_call(spans, mixed, edge, taps, inside, outside, steps, decay, rows, factor, mask):
    count = spans * SPAN
    at_pair = lambda n: pl.BlockSpec((n, LANES), lambda i: (0, i))
    at_key = lambda n: pl.BlockSpec((n, LANES), lambda i: (0, PAIRS))
    at_query = lambda n: pl.BlockSpec((n, LANES), lambda i: (0, PAIRS + 1))
    whole = lambda *s: pl.BlockSpec(s, lambda i: (0,) * len(s))
    return pl.pallas_call(
        functools.partial(forward_kernel, spans),
        grid=(PAIRS,),
        in_specs=[
            at_pair(count),
            at_key(count),
            at_query(count),
            at_pair(8),
            at_key(8),
            at_query(8),
            at_pair(8),
            at_key(8),
            at_query(8),
            whole(3, count, LANES),
            whole(3, 8, LANES),
            whole(count, LANES),
            whole(count, LANES),
            pl.BlockSpec((1, 8, count), lambda i: (i, 0, 0)),
            at_pair(8),
            whole(spans, SPAN, SPAN),
        ],
        out_specs=[
            at_pair(count),
            at_pair(count),
            pl.BlockSpec((spans, DS, LANES), lambda i: (0, 0, i)),
            whole(count, LANES),
            whole(count, LANES),
        ],
        out_shape=[
            jax.ShapeDtypeStruct((count, DI), f32),
            jax.ShapeDtypeStruct((count, DI), f32),
            jax.ShapeDtypeStruct((spans, DS, DI), f32),
            jax.ShapeDtypeStruct((count, DS), f32),
            jax.ShapeDtypeStruct((count, DS), f32),
        ],
        scratch_shapes=[
            pltpu.VMEM((spans, SPAN, SPAN), f32),
            pltpu.VMEM((spans, 2, DS, SPAN), bf16),
            pltpu.VMEM((count, 2 * DS), bf16),
        ],
        compiler_params=pltpu.CompilerParams(vmem_limit_bytes=VMEM_LIMIT),
        name="recurrence_forward",
    )(
        mixed,
        mixed,
        mixed,
        edge,
        edge,
        edge,
        taps,
        taps,
        taps,
        inside,
        outside,
        steps,
        decay,
        rows,
        factor,
        mask,
    )


def norm_kernel(
    local_ref,
    inner_ref,
    gate_ref,
    back_ref,
    query_ref,
    state_ref,
    reach_ref,
    spread_ref,
    skip_ref,
    gain_ref,
    out_ref,
    mixer_grad_ref,
    gate_grad_ref,
    gain_grad_ref,
    dots_ref,
    summary_ref,
    mixed_y,
    state_both,
    reach_wide,
):
    step = pl.program_id(0)
    chunks = [pl.ds(c * NORM_COLS, NORM_COLS) for c in range(DI // NORM_COLS)]

    @pl.when(step == 0)
    def _():
        sh, sl = split(state_ref[...])
        state_both[0] = sh
        state_both[1] = sl
        gain_grad_ref[...] = jnp.zeros_like(gain_grad_ref)
        summary_ref[...] = jnp.zeros_like(summary_ref)

    qh, ql = split(query_ref[...])
    query_both = jnp.concatenate([qh, ql], axis=1)
    rh, rl = split(reach_ref[...])
    reach_both = jnp.concatenate([rh, rl], axis=1)
    squares = jnp.zeros((NORM_ROWS, 1), f32)
    mixes = jnp.zeros((NORM_ROWS, 1), f32)
    for cols in chunks:
        sh, sl = state_both[0, :, cols], state_both[1, :, cols]
        spread = spread_ref[:, cols]
        reach = mm(reach_both, jnp.concatenate([spread, spread], axis=0))
        reach_wide[:, cols] = reach
        carried = mm(query_both, jnp.concatenate([sh, sh], axis=0)) + mm(qh, sl)
        y = local_ref[:, cols] + reach * carried
        mixed_y[:, cols] = y
        mixer = y + skip_ref[0:1, cols] * inner_ref[:, cols]
        gate = gate_ref[:, cols]
        gated = mixer * (gate * sigmoid(gate))
        squares = squares + jnp.sum(gated * gated, axis=1, keepdims=True)
        mixes = mixes + jnp.sum(
            gated * (back_ref[:, cols] * gain_ref[0:1, cols]), axis=1, keepdims=True
        )
    scale = lax.rsqrt(squares * (1.0 / DI) + norm_eps)
    pull = scale * mixes * (1.0 / DI)
    query_turned = query_ref[...].T
    th, tl = split(query_turned)
    dots = jnp.zeros((NORM_ROWS, LANES), f32)
    for cols in chunks:
        y = mixed_y[:, cols]
        mixer = y + skip_ref[0:1, cols] * inner_ref[:, cols]
        gate = gate_ref[:, cols]
        opened = sigmoid(gate)
        silu = gate * opened
        unit = mixer * silu * scale
        gain = gain_ref[0:1, cols]
        back = back_ref[:, cols]
        out_ref[:, cols] = (unit * gain).astype(bf16)
        gain_grad_ref[0:1, cols] += jnp.sum(back * unit, axis=0, keepdims=True)
        gated_grad = scale * (back * gain - unit * pull)
        mixer_grad = gated_grad * silu
        mixer_grad_ref[:, cols] = mixer_grad
        gate_grad_ref[:, cols] = (
            gated_grad * mixer * (opened * (1.0 + gate * (1.0 - opened)))
        ).astype(bf16)
        dh, dl = split(mixer_grad * y)
        spread = spread_ref[:, cols]
        dots = dots + mm_nt(dh, spread) + mm_nt(dl, spread)
        mh, ml = split(reach_wide[:, cols] * mixer_grad)
        summary_ref[:, cols] += (
            mm(jnp.concatenate([th, tl], axis=1), jnp.concatenate([mh, mh], axis=0)) + mm(th, ml)
        )
    dots_ref[...] = dots


def norm_call(local, inner, gate, back, queries, state_in, reach, spread, skip, gain):
    count = local.shape[0]
    rows = lambda n: pl.BlockSpec((NORM_ROWS, n), lambda i: (i, 0))
    whole = lambda *s: pl.BlockSpec(s, lambda i: (0,) * len(s))
    return pl.pallas_call(
        norm_kernel,
        grid=(count // NORM_ROWS,),
        in_specs=[
            rows(DI),
            rows(DI),
            rows(DI),
            rows(DI),
            rows(DS),
            whole(DS, DI),
            rows(LANES),
            whole(LANES, DI),
            whole(8, DI),
            whole(8, DI),
        ],
        out_specs=[rows(DI), rows(DI), rows(DI), whole(8, DI), rows(LANES), whole(DS, DI)],
        out_shape=[
            jax.ShapeDtypeStruct((count, DI), bf16),
            jax.ShapeDtypeStruct((count, DI), f32),
            jax.ShapeDtypeStruct((count, DI), bf16),
            jax.ShapeDtypeStruct((8, DI), f32),
            jax.ShapeDtypeStruct((count, LANES), f32),
            jax.ShapeDtypeStruct((DS, DI), f32),
        ],
        scratch_shapes=[
            pltpu.VMEM((NORM_ROWS, DI), f32),
            pltpu.VMEM((2, DS, DI), bf16),
            pltpu.VMEM((NORM_ROWS, DI), f32),
        ],
        compiler_params=pltpu.CompilerParams(vmem_limit_bytes=VMEM_LIMIT),
        name="gated_norm",
    )(local, inner, gate, back, queries, state_in, reach, spread, skip, gain)


def backward_kernel(
    spans,
    block_ref,
    edge_ref,
    taps_ref,
    inside_ref,
    outside_ref,
    keys_ref,
    queries_ref,
    back_ref,
    steps_ref,
    decay_ref,
    rows_ref,
    factor_ref,
    start_ref,
    mask_ref,
    states_ref,
    state_in_ref,
    state_back_ref,
    skip_ref,
    grad_out,
    top_out,
    tail_out,
    taps_out,
    ends_out,
    steps_out,
    scores,
    scores_grad,
    key_grad,
    query_grad,
    key_both,
    query_both,
    query_turned,
):
    pair = pl.program_id(0)
    lane = lax.broadcasted_iota(jnp.int32, (SPAN, LANES), 1)

    @pl.when(pair == 0)
    def _():
        key_grad[...] = jnp.zeros_like(key_grad)
        query_grad[...] = jnp.zeros_like(query_grad)
        scores_grad[...] = jnp.zeros_like(scores_grad)
        steps_out[...] = jnp.zeros_like(steps_out)
        for k in range(spans):
            rows = pl.ds(k * SPAN, SPAN)
            keys, queries = keys_ref[rows, :], queries_ref[rows, :]
            kh, kl = split(keys)
            qh, ql = split(queries)
            key_both[rows, :] = jnp.concatenate([kh, kl], axis=1)
            query_both[rows, :] = jnp.concatenate([qh, ql], axis=1)
            scores[k] = mm_nt(
                jnp.concatenate([kh, kl], axis=1), jnp.concatenate([qh, qh], axis=1)
            ) + mm_nt(kh, ql)
            th, tl = split(queries.T)
            query_turned[k, 0] = th
            query_turned[k, 1] = tl

    def conv_back(conved_grad, block, shifted, pre):
        opened = sigmoid(pre)
        pre_grad = conved_grad * (opened * (1.0 + pre * (1.0 - opened)))
        count = block.shape[0]
        taps = taps_ref[...]
        total = taps[3:4] * pre_grad
        sums = [None] * 8
        sums[3] = jnp.sum(pre_grad * block, axis=0, keepdims=True)
        sums[4] = jnp.sum(pre_grad, axis=0, keepdims=True)
        for j in range(1, CONV):
            total = total + taps[3 - j : 4 - j] * pltpu.roll(
                inside_ref[j - 1] * pre_grad, count - j, 0
            )
            sums[3 - j] = jnp.sum(pre_grad * shifted[j - 1], axis=0, keepdims=True)
        grad_out[...] = total.astype(bf16)
        tail_out[...] = total[count - 8 :]
        top_out[...] = pre_grad[:8]
        return sums

    block = block_ref[...]
    shifted = conv_shifts(block, edge_ref[...], inside_ref, outside_ref)
    pre = conv_pre(block, shifted, taps_ref[...])
    zero_row = jnp.zeros((1, LANES), f32)

    @pl.when(pair < PAIRS)
    def _():
        inner = pre * sigmoid(pre)
        back = back_ref[...]
        turned, unused, steps = pair_columns(steps_ref[...], pair)
        unused, enter, leave = pair_columns(decay_ref[...], pair)
        scaled = steps * inner
        leaving = leave * scaled
        entering = enter * back
        state_in = state_in_ref[...]
        state_back = state_back_ref[...]
        scaled_grads = [None] * spans
        ends = [zero_row] * 8
        for k in reversed(range(spans)):
            at = k * SPAN
            rows = pl.ds(at, SPAN)
            bh, bl = split(back[at : at + SPAN])
            both = jnp.concatenate([bh, bl], axis=1)
            sh, sl = split(scaled[at : at + SPAN])
            per_head = []
            for a in range(2):
                mine = (lane < HD) if a == 0 else (lane >= HD)
                zero = jnp.zeros((SPAN, LANES), bf16)
                left = jnp.concatenate(
                    [
                        jnp.where(mine, sh, pltpu.roll(sl.astype(f32), HD, 1).astype(bf16)),
                        jnp.where(mine, sh, zero),
                    ],
                    axis=1,
                )
                right = jnp.concatenate(
                    [
                        jnp.where(mine, bh, pltpu.roll(bh.astype(f32), HD, 1).astype(bf16)),
                        jnp.where(mine, bl, zero),
                    ],
                    axis=1,
                )
                parts = []
                for half in range(2):
                    low = half * HALF
                    width = SPAN - low
                    row = rows_ref[0, a : a + 1, pl.ds(at + low, width)]
                    column = turned[at + low : at + low + HALF, a : a + 1]
                    here = pl.ds(low, HALF)
                    there = pl.ds(low, width)
                    decay = jnp.exp(jnp.minimum(row - column, mask_ref[k, here, there]))
                    weights = decay * scores[k, here, there]
                    wh, wl = split(weights)
                    wide = mm(wh, both[low:])
                    parts.append(wide[:, :LANES] + wide[:, LANES:] + mm(wl, bh[low:]))
                    weights_grad = mm_nt(left[low : low + HALF], right[low:])
                    scores_grad[k, here, there] += decay * weights_grad
                per_head.append(jnp.concatenate(parts, axis=0))
            scaled_grad = jnp.where(lane < HD, per_head[0], per_head[1])
            gh, gl = split(state_back)
            k2 = key_both[rows, :]
            scaled_grad = scaled_grad + leave[at : at + SPAN] * (
                mm(k2, jnp.concatenate([gh, gh], axis=0)) + mm(k2[:, :DS], gl)
            )
            scaled_grads[k] = scaled_grad
            lh, ll = split(leaving[at : at + SPAN])
            key_grad[rows, :] += mm_nt(
                jnp.concatenate([lh, ll], axis=1), jnp.concatenate([gh, gh], axis=1)
            ) + mm_nt(lh, gl)
            after = states_ref[k] + start_ref[k + 1 : k + 2] * state_in
            ends[k] = jnp.sum(state_back * after, axis=0, keepdims=True)
            before = start_ref[k : k + 1] * state_in
            if k > 0:
                before = before + states_ref[k - 1]
            th, tl = split(before)
            eh, el = split(entering[at : at + SPAN])
            query_grad[rows, :] += mm_nt(
                jnp.concatenate([eh, el], axis=1), jnp.concatenate([th, th], axis=1)
            ) + mm_nt(eh, tl)
            if k > 0:
                more = mm(query_turned[k, 0], jnp.concatenate([eh, el], axis=1))
                state_back = (
                    factor_ref[k : k + 1] * state_back
                    + more[:, :LANES]
                    + more[:, LANES:]
                    + mm(query_turned[k, 1], eh)
                )
        scaled_grad = jnp.concatenate(scaled_grads, axis=0)
        target = lax.broadcasted_iota(jnp.int32, (LANES, LANES), 1)
        source = lax.broadcasted_iota(jnp.int32, (LANES, LANES), 0)
        place = (target == 2 * pair + source // HD).astype(bf16)
        dh, dl = split(inner * scaled_grad)
        steps_out[...] += mm(dh, place) + mm(dl, place)
        sums = conv_back(steps * scaled_grad + skip_ref[0:1] * back, block, shifted, pre)
        sums[5] = jnp.sum(back * inner, axis=0, keepdims=True)
        taps_out[...] = jnp.concatenate([zero_row if s is None else s for s in sums], axis=0)
        ends_out[...] = jnp.concatenate(ends, axis=0)

    def of_scores(grad_ref, ones_ref, transposed):
        for k in range(spans):
            rows = pl.ds(k * SPAN, SPAN)
            grad = scores_grad[k]
            gh, gl = split(grad.T if transposed else grad)
            ones = ones_ref[rows, :]
            wide = mm(gh, ones)
            grad_ref[rows, :] += wide[:, :DS] + wide[:, DS:] + mm(gl, ones[:, :DS])

    @pl.when(pair >= PAIRS)
    def _():
        @pl.when(pair == PAIRS)
        def _():
            of_scores(key_grad, query_both, False)

        @pl.when(pair > PAIRS)
        def _():
            of_scores(query_grad, key_both, True)

        grad = jnp.where(pair == PAIRS, key_grad[...], query_grad[...])
        sums = conv_back(grad, block, shifted, pre)
        taps_out[...] = jnp.concatenate([zero_row if s is None else s for s in sums], axis=0)
        ends_out[...] = jnp.zeros_like(ends_out)


def backward_call(
    spans,
    mixed,
    edge,
    taps,
    inside,
    outside,
    keys,
    queries,
    mixer_grad,
    steps,
    decay,
    rows,
    factor,
    start,
    mask,
    states,
    state_in,
    state_back,
    skip,
):
    count = spans * SPAN
    blocks = CONVD // LANES
    clip = lambda i: jnp.minimum(i, PAIRS - 1)
    at_block = lambda n: pl.BlockSpec((n, LANES), lambda i: (0, i))
    at_pair = lambda n: pl.BlockSpec((n, LANES), lambda i: (0, clip(i)))
    whole = lambda *s: pl.BlockSpec(s, lambda i: (0,) * len(s))
    return pl.pallas_call(
        functools.partial(backward_kernel, spans),
        grid=(blocks,),
        in_specs=[
            at_block(count),
            at_block(8),
            at_block(8),
            whole(3, count, LANES),
            whole(3, 8, LANES),
            whole(count, DS),
            whole(count, DS),
            at_pair(count),
            whole(count, LANES),
            whole(count, LANES),
            pl.BlockSpec((1, 8, count), lambda i: (clip(i), 0, 0)),
            at_pair(8),
            at_pair(8),
            whole(spans, SPAN, SPAN),
            pl.BlockSpec((spans, DS, LANES), lambda i: (0, 0, clip(i))),
            at_pair(DS),
            at_pair(DS),
            at_pair(8),
        ],
        out_specs=[
            at_block(count),
            at_block(8),
            at_block(8),
            at_block(8),
            at_block(8),
            whole(count, LANES),
        ],
        out_shape=[
            jax.ShapeDtypeStruct((count, CONVD), bf16),
            jax.ShapeDtypeStruct((8, CONVD), f32),
            jax.ShapeDtypeStruct((8, CONVD), f32),
            jax.ShapeDtypeStruct((8, CONVD), f32),
            jax.ShapeDtypeStruct((8, CONVD), f32),
            jax.ShapeDtypeStruct((count, LANES), f32),
        ],
        scratch_shapes=[
            pltpu.VMEM((spans, SPAN, SPAN), f32),
            pltpu.VMEM((spans, SPAN, SPAN), f32),
            pltpu.VMEM((count, DS), f32),
            pltpu.VMEM((count, DS), f32),
            pltpu.VMEM((count, 2 * DS), bf16),
            pltpu.VMEM((count, 2 * DS), bf16),
            pltpu.VMEM((spans, 2, DS, SPAN), bf16),
        ],
        compiler_params=pltpu.CompilerParams(vmem_limit_bytes=VMEM_LIMIT),
        name="recurrence_backward",
    )(
        mixed,
        edge,
        taps,
        inside,
        outside,
        keys,
        queries,
        mixer_grad,
        steps,
        decay,
        rows,
        factor,
        start,
        mask,
        states,
        state_in,
        state_back,
        skip,
    )


def adamw_update(param, grad, first, second, decay):
    first_new = beta_one * first + (1.0 - beta_one) * grad
    second_new = beta_two * second + (1.0 - beta_two) * grad * grad
    first_hat = first_new / (1.0 - beta_one**STEP)
    second_hat = second_new / (1.0 - beta_two**STEP)
    param_new = param - learn_rate * (first_hat / (jnp.sqrt(second_hat) + adam_eps) + decay * param)
    return (param_new, first_new, second_new)


def segment_of(lengths, positions):
    ends = jnp.cumsum(lengths)
    return jnp.sum((positions[..., None] >= ends).astype(jnp.int32), axis=-1)


def packed(low, high):
    wide = lambda v: jnp.pad(v, ((0, 0), (0, LANES // 2 - NH)))
    return jnp.concatenate([wide(low), wide(high)], axis=1)


def per_lane(values):
    rows = jnp.repeat(values, HD, axis=1)
    return jnp.pad(rows, ((0, 8 - rows.shape[0]), (0, 0)))


def spread_matrix():
    head = lax.broadcasted_iota(jnp.int32, (LANES, DI), 0)
    lane = lax.broadcasted_iota(jnp.int32, (LANES, DI), 1)
    return (head == lane // HD).astype(bf16)


def pass_on(own, factor, axis, backwards, kind):
    size, here = lax.axis_size(axis), lax.axis_index(axis)
    given = jnp.zeros_like(own)
    for turn in range(size - 1):
        source = size - 1 - turn if backwards else turn
        target = source - 1 if backwards else source + 1
        out = (factor * given + own).astype(kind)
        arrived = lax.ppermute(out, axis, [(source, target)]).astype(f32)
        given = jnp.where(here == target, arrived, given)
    return given


def gather_rows(block, axis):
    return lax.all_gather(block, axis, axis=0, tiled=True)


def owned_rows(partial):
    return lax.psum(lax.psum_scatter(partial, "fsdp", scatter_dimension=0, tiled=True), "ctx")


def on_device(
    tokens_in,
    cotangent,
    doc_lengths,
    in_proj,
    out_proj,
    norm_gain,
    gate_gain,
    conv_weight,
    conv_bias,
    delta_bias,
    decay_log,
    skip_scale,
    in_first,
    in_second,
    out_first,
    out_second,
    small_first,
    small_second,
):
    count = tokens_in.shape[0]
    spans = count // SPAN
    ctx = lax.axis_size("ctx")
    ctx_index = lax.axis_index("ctx")
    begin = ctx_index * count
    positions = begin + jnp.arange(count, dtype=jnp.int32)
    lengths = doc_lengths[0]
    segment = segment_of(lengths, positions)

    in_low = in_proj.astype(bf16)
    whole_conv = gather_rows(in_low[:, DI:], "fsdp")
    whole_gate = gather_rows(in_low[:, :DI], "fsdp")
    whole_out = gather_rows(out_proj.astype(bf16), "fsdp")

    inputs = tokens_in.astype(f32)
    scale = lax.rsqrt(jnp.mean(inputs * inputs, axis=-1, keepdims=True) + norm_eps)
    normed = (inputs * scale * norm_gain[None, :]).astype(bf16)

    mixed = mm(normed, whole_conv)
    raw_step = mixed[:, CONVD:] + delta_bias[None, :]
    edge = lax.ppermute(mixed[count - 8 :, :CONVD], "ctx", [(i, i + 1) for i in range(ctx - 1)])
    edge = jnp.where(jnp.arange(8)[:, None] >= 8 - (CONV - 1), edge, 0.0)

    back = jnp.arange(1, CONV, dtype=jnp.int32)[:, None]
    same = (segment_of(lengths, positions[None, :] - back) == segment[None, :]).astype(f32)
    row = jnp.arange(count, dtype=jnp.int32)[None, :]
    inside = jnp.broadcast_to((same * (row >= back))[:, :, None], (CONV - 1, count, LANES))
    outside = jnp.broadcast_to((same * (row < back))[:, :8, None], (CONV - 1, 8, LANES))
    span_segment = segment.reshape(spans, SPAN)
    span_begin = begin + SPAN * jnp.arange(spans, dtype=jnp.int32)
    together = span_segment[:, :, None] == span_segment[:, None, :]
    index = jnp.arange(SPAN, dtype=jnp.int32)
    causal = index[:, None] >= index[None, :]
    mask = jnp.where(together & causal[None], 0.0, MASKED).astype(f32)
    mask_turned = jnp.where(together & causal.T[None], 0.0, MASKED).astype(f32)
    enters = (span_segment == segment_of(lengths, span_begin - 1)[:, None]) & (
        span_begin[:, None] > 0
    )
    leaves = span_segment == span_segment[:, -1:]
    reaches = (segment == segment_of(lengths, begin - 1)) & (begin > 0)

    steps = jax.nn.softplus(raw_step)
    rate = -jnp.exp(decay_log)[None, :]
    log_decay = (rate * steps).reshape(spans, SPAN, NH)
    cumul = jnp.einsum("ts,bsh->bth", causal.astype(f32), log_decay, precision=highest)
    ends = cumul[:, -1]
    factor = jnp.where(enters[:, -1:], jnp.exp(ends), 0.0)
    enter = jnp.where(enters[:, :, None], jnp.exp(cumul), 0.0).reshape(count, NH)
    leave = jnp.where(leaves[:, :, None], jnp.exp(ends[:, None] - cumul), 0.0).reshape(count, NH)
    before = jnp.concatenate([jnp.zeros((1, NH), f32), jnp.cumsum(ends, axis=0)], axis=0)
    reach = jnp.where(
        reaches[:, None], jnp.exp(cumul + before[:-1, None]).reshape(count, NH), 0.0
    )
    start = jnp.concatenate([jnp.ones((1, NH), f32), jnp.cumprod(factor, axis=0)], axis=0)
    flat_cumul = cumul.reshape(count, NH)
    rows = jnp.pad(flat_cumul.T.reshape(PAIRS, 2, count), ((0, 0), (0, 6), (0, 0)))
    steps_both = packed(flat_cumul, steps)
    decay_both = packed(enter, leave)
    factor_lanes = per_lane(factor)
    start_lanes = per_lane(start)
    skip_lanes = per_lane(skip_scale[None, :])
    total_lanes = start_lanes[spans : spans + 1]
    taps = jnp.concatenate([conv_weight.T, conv_bias[None], jnp.zeros((3, CONVD), f32)], axis=0)

    inner, local, states, keys, queries = forward_call(
        spans, mixed, edge, taps, inside, outside, steps_both, decay_both, rows, factor_lanes, mask
    )
    state_in = pass_on(states[spans - 1], total_lanes, "ctx", False, f32)
    gate = mm(normed, whole_gate)
    mixer_back = jnp.einsum("td,kd->tk", cotangent, whole_out, preferred_element_type=f32)
    reach_wide = jnp.pad(reach, ((0, 0), (0, LANES - NH)))
    gain_rows = jnp.pad(gate_gain[None], ((0, 7), (0, 0)))
    mixer_low, mixer_grad, gate_grad, gate_gain_grad, dots, summary = norm_call(
        local,
        inner,
        gate,
        mixer_back,
        queries,
        state_in,
        reach_wide,
        spread_matrix(),
        skip_lanes,
        gain_rows,
    )
    state_back = pass_on(summary, total_lanes, "ctx", True, bf16)

    block_out = (inputs + mm(mixer_low, whole_out)).astype(bf16)
    out_grad = jnp.einsum("tk,td->kd", mixer_low, cotangent, preferred_element_type=f32)
    gate_rows = jnp.einsum("tk,tz->kz", normed, gate_grad, preferred_element_type=f32)
    normed_grad = jnp.einsum("tk,dk->td", gate_grad, whole_gate, preferred_element_type=f32)

    conv_grad, top, tail, taps_grad, end_dots, step_dots = backward_call(
        spans,
        mixed,
        edge,
        taps,
        inside,
        outside,
        keys,
        queries,
        mixer_grad,
        steps_both,
        decay_both,
        rows,
        factor_lanes,
        start_lanes,
        mask_turned,
        states,
        state_in,
        state_back,
        skip_lanes,
    )
    next_top = lax.ppermute(
        top[: CONV - 1], "ctx", [(i + 1, i) for i in range(ctx - 1)]
    )
    following = segment_of(lengths, begin + count + jnp.arange(CONV - 1, dtype=jnp.int32))
    more = []
    for q in range(count - (CONV - 1), count):
        row_more = jnp.zeros((CONVD,), f32)
        for j in range(count - q, CONV):
            joined = (following[q + j - count] == segment[q]).astype(f32)
            row_more = row_more + joined * taps[3 - j] * next_top[q + j - count]
        more.append(row_more)
    last_rows = tail + jnp.concatenate([jnp.zeros((5, CONVD), f32), jnp.stack(more)], axis=0)
    conv_grad = lax.dynamic_update_slice(conv_grad, last_rows.astype(bf16), (count - 8, 0))

    step_dots = step_dots[:, :NH]
    end_dots = jnp.sum(end_dots[:spans, :DI].reshape(spans, NH, HD), axis=2)
    cumul_grad = (dots[:, :NH] - steps * step_dots).reshape(spans, SPAN, NH)
    decay_grad = jnp.einsum("ts,bth->bsh", causal.astype(f32), cumul_grad, precision=highest)
    decay_grad = (decay_grad + end_dots[:, None]).reshape(count, NH)
    steps_grad = step_dots + rate * decay_grad
    decay_log_grad = jnp.sum(rate * steps * decay_grad, axis=0)
    raw_grad = steps_grad * jax.nn.sigmoid(raw_step)
    delta_grad = jnp.sum(raw_grad, axis=0)
    skip_grad = jnp.sum(taps_grad[5, :DI].reshape(NH, HD), axis=1)
    conv_grad = jnp.concatenate([conv_grad, raw_grad.astype(bf16)], axis=1)

    conv_rows = jnp.einsum("tk,tz->kz", normed, conv_grad, preferred_element_type=f32)
    normed_grad = normed_grad + jnp.einsum(
        "tk,dk->td", conv_grad, whole_conv, preferred_element_type=f32
    )
    unit = inputs * scale
    norm_gain_grad = jnp.sum(normed_grad * unit, axis=0)
    unit_grad = normed_grad * norm_gain[None, :]
    input_grad = cotangent.astype(f32) + scale * (
        unit_grad - unit * jnp.mean(unit_grad * unit, axis=-1, keepdims=True)
    )
    small_grad = lax.psum(
        jnp.concatenate(
            [
                norm_gain_grad,
                gate_gain_grad[0],
                taps_grad[:CONV].T.reshape(-1),
                taps_grad[4],
                delta_grad,
                decay_log_grad,
                skip_grad,
            ]
        ),
        ("fsdp", "ctx"),
    )
    small_param = jnp.concatenate(
        [
            norm_gain,
            gate_gain,
            conv_weight.reshape(-1),
            conv_bias,
            delta_bias,
            decay_log,
            skip_scale,
        ]
    )
    small_new, small_first_new, small_second_new = adamw_update(
        small_param, small_grad, small_first, small_second, 0.0
    )
    in_grad = jnp.concatenate([owned_rows(gate_rows), owned_rows(conv_rows)], axis=1)
    out_rows = owned_rows(out_grad)
    in_new, in_first_new, in_second_new = adamw_update(
        in_proj, in_grad, in_first, in_second, weight_decay
    )
    out_new, out_first_new, out_second_new = adamw_update(
        out_proj, out_rows, out_first, out_second, weight_decay
    )
    return (
        block_out,
        input_grad,
        in_new,
        in_first_new,
        in_second_new,
        out_new,
        out_first_new,
        out_second_new,
        small_new,
        small_first_new,
        small_second_new,
    )


def solution(mesh):
    placed = (
        P(("fsdp", "ctx"), None),
        P(("fsdp", "ctx"), None),
        P("fsdp", None),
        P("fsdp", None),
        P("fsdp", None),
        P(),
        P(),
        P(),
        P(),
        P(),
        P(),
        P(),
        P("fsdp", None),
        P("fsdp", None),
        P("fsdp", None),
        P("fsdp", None),
        P(),
        P(),
    )
    return jax.shard_map(
        on_device,
        mesh=mesh,
        in_specs=placed,
        out_specs=(
            P(("fsdp", "ctx"), None),
            P(("fsdp", "ctx"), None),
            P("fsdp", None),
            P("fsdp", None),
            P("fsdp", None),
            P("fsdp", None),
            P("fsdp", None),
            P("fsdp", None),
            P(),
            P(),
            P(),
        ),
        check_vma=False,
    )
```

```python
import functools

import jax
import jax.numpy as jnp
from jax import lax
from jax.experimental import pallas as pl
from jax.experimental.pallas import tpu as pltpu
from jax.sharding import PartitionSpec as P

D = 1536
DI = 3072
NH = 48
HD = 64
DS = 128
CONV = 4
SPAN = 256
STEP = 5
CONVD = 3328
LANES = 128
PAIRS = DI // LANES
HALF = SPAN // 2
NORM_ROWS = 128
NORM_COLS = 512
MASKED = -1e30

highest = lax.Precision.HIGHEST
norm_eps = 1e-05
beta_one = 0.9
beta_two = 0.95
adam_eps = 1e-08
learn_rate = 0.05
weight_decay = 0.1
f32 = jnp.float32
bf16 = jnp.bfloat16
VMEM_LIMIT = 56 * 1024 * 1024


def split(value):
    high = value.astype(bf16)
    return high, (value - high.astype(f32)).astype(bf16)


def mm(a, b):
    return jnp.dot(a, b, preferred_element_type=f32)


def mm_nt(a, b):
    return lax.dot_general(a, b, (((1,), (1,)), ((), ())), preferred_element_type=f32)


def sigmoid(v):
    return 1.0 / (1.0 + jnp.exp(-v))


def conv_shifts(block, edge, inside, outside):
    shifted = []
    for j in range(1, CONV):
        body = inside[j - 1] * pltpu.roll(block, j, 0)
        head = body[:8] + outside[j - 1] * pltpu.roll(edge, j, 0)
        shifted.append(jnp.concatenate([head, body[8:]], axis=0))
    return shifted


def conv_pre(block, shifted, taps):
    total = taps[4:5] + taps[3:4] * block
    for j in range(1, CONV):
        total = total + taps[3 - j : 4 - j] * shifted[j - 1]
    return total


def pair_columns(packed, pair):
    turned = pltpu.roll(packed, lax.rem(LANES - 2 * pair, LANES), 1)
    lane = lax.broadcasted_iota(jnp.int32, packed.shape, 1)
    first = jnp.where(lane < HD, turned[:, 0:1], turned[:, 1:2])
    second = jnp.where(lane < HD, turned[:, 64:65], turned[:, 65:66])
    return turned, first, second


def pair_rows(rows, pair):
    turned = pltpu.roll(rows, lax.rem(LANES - 2 * pair, LANES), 1)
    lane = lax.broadcasted_iota(jnp.int32, rows.shape, 1)
    return jnp.where(lane < HD, turned[:, 0:1], turned[:, 1:2])


def head_row(block, head):
    sublane = lax.broadcasted_iota(jnp.int32, block.shape, 0)
    return jnp.sum(jnp.where(sublane == lax.rem(head, 8), block, 0.0), axis=0, keepdims=True)


def split_three(value):
    high, low = split(value)
    return high, low, (value - high.astype(f32) - low.astype(f32)).astype(bf16)


def prepare_kernel(
    spans,
    place_ref,
    raw_ref,
    params_ref,
    steps_out,
    decay_out,
    reach_out,
    turned_out,
    factor_out,
    start_out,
    inside_out,
    outside_out,
    mask_out,
    mask_turned_out,
):
    count = spans * SPAN
    begin = place_ref[0]
    ends = []
    for d in range(place_ref.shape[0] - 1):
        ends.append(place_ref[d + 1] + (ends[-1] if ends else 0))

    def segment(position):
        total = (position >= ends[0]).astype(jnp.int32)
        for end in ends[1:]:
            total = total + (position >= end).astype(jnp.int32)
        return total

    row = lax.broadcasted_iota(jnp.int32, (count, LANES), 0)
    here = segment(row + begin)
    for j in range(1, CONV):
        same = here == segment(row + (begin - j))
        inside_out[j - 1] = jnp.where(jnp.logical_and(same, row >= j), 1.0, 0.0)
        outside_out[j - 1] = jnp.where(jnp.logical_and(same, row < j), 1.0, 0.0)[:8]
    lane = lax.broadcasted_iota(jnp.int32, (count, LANES), 1)
    raw = jnp.where(lane < NH, raw_ref[...], 0.0) + params_ref[0:1]
    steps = jnp.where(lane < NH, jnp.maximum(raw, 0.0) + jnp.log1p(jnp.exp(-jnp.abs(raw))), 0.0)
    log_decay = params_ref[1:2] * steps
    tall = lax.broadcasted_iota(jnp.int32, (SPAN, SPAN), 0)
    wide = lax.broadcasted_iota(jnp.int32, (SPAN, SPAN), 1)
    lower = (tall >= wide).astype(bf16)
    span_lane = lax.broadcasted_iota(jnp.int32, (SPAN, LANES), 1)
    before = jnp.zeros((1, LANES), f32)
    start = jnp.ones((1, LANES), f32)
    starts, factors = [start], []
    reached = here == segment(begin - 1)
    for k in range(spans):
        at = k * SPAN
        rows = pl.ds(at, SPAN)
        parts = split_three(log_decay[at : at + SPAN])
        sums = mm(lower, jnp.concatenate(parts, axis=1))
        cumul = sums[:, :LANES] + sums[:, LANES : 2 * LANES] + sums[:, 2 * LANES :]
        last = cumul[SPAN - 1 : SPAN]
        span_here = here[at : at + SPAN]
        first = begin + at
        enters = jnp.logical_and(span_here == segment(first - 1), span_here >= 0)
        enter = jnp.where(jnp.logical_and(enters, first > 0), jnp.exp(cumul), 0.0)
        leave = jnp.where(
            span_here == segment(first + SPAN - 1), jnp.exp(last - cumul), 0.0
        )
        reach = jnp.where(
            jnp.logical_and(reached[at : at + SPAN], begin > 0), jnp.exp(cumul + before), 0.0
        )
        known = span_lane < NH
        steps_out[rows, :] = jnp.where(known, cumul, 0.0) + pltpu.roll(
            steps[at : at + SPAN], LANES // 2, 1
        )
        decay_out[rows, :] = jnp.where(known, enter, 0.0) + pltpu.roll(
            jnp.where(known, leave, 0.0), LANES // 2, 1
        )
        reach_out[rows, :] = jnp.where(known, reach, 0.0)
        turned_out[:, rows] = cumul.T[:NH]
        factors.append(enter[SPAN - 1 : SPAN])
        start = start * factors[-1]
        starts.append(start)
        before = before + last
        together = segment(tall + first) == segment(wide + first)
        mask_out[k] = jnp.where(jnp.logical_and(together, tall >= wide), 0.0, MASKED)
        mask_turned_out[k] = jnp.where(jnp.logical_and(together, tall <= wide), 0.0, MASKED)
    rest = lambda rows: jnp.concatenate(
        rows + [jnp.zeros((8 - len(rows), LANES), f32)], axis=0
    )
    factor_out[...] = rest(factors)
    start_out[...] = rest(starts)


def prepare_call(spans, place, mixed, params):
    count = spans * SPAN
    whole = lambda *s: pl.BlockSpec(s, lambda i: (0,) * len(s))
    shapes = [
        (count, LANES),
        (count, LANES),
        (count, LANES),
        (NH, count),
        (8, LANES),
        (8, LANES),
        (CONV - 1, count, LANES),
        (CONV - 1, 8, LANES),
        (spans, SPAN, SPAN),
        (spans, SPAN, SPAN),
    ]
    return pl.pallas_call(
        functools.partial(prepare_kernel, spans),
        grid=(1,),
        in_specs=[
            pl.BlockSpec(memory_space=pltpu.SMEM),
            pl.BlockSpec((count, LANES), lambda i: (0, CONVD // LANES)),
            whole(8, LANES),
        ],
        out_specs=[whole(*s) for s in shapes],
        out_shape=[jax.ShapeDtypeStruct(s, f32) for s in shapes],
        compiler_params=pltpu.CompilerParams(vmem_limit_bytes=VMEM_LIMIT),
        name="steps_and_masks",
    )(place, mixed, params)


def forward_kernel(
    spans,
    block_ref,
    key_ref,
    query_ref,
    edge_ref,
    key_edge_ref,
    query_edge_ref,
    taps_ref,
    key_taps_ref,
    query_taps_ref,
    inside_ref,
    outside_ref,
    steps_ref,
    decay_ref,
    rows_ref,
    factor_ref,
    mask_ref,
    inner_out,
    local_out,
    state_out,
    key_out,
    query_out,
    scores,
    key_turned,
    query_both,
):
    pair = pl.program_id(0)

    @pl.when(pair == 0)
    def _():
        for src, edge, taps, out in (
            (key_ref, key_edge_ref, key_taps_ref, key_out),
            (query_ref, query_edge_ref, query_taps_ref, query_out),
        ):
            pre = conv_pre(
                src[...], conv_shifts(src[...], edge[...], inside_ref, outside_ref), taps[...]
            )
            out[...] = pre * sigmoid(pre)
        for k in range(spans):
            rows = pl.ds(k * SPAN, SPAN)
            keys, queries = key_out[rows, :], query_out[rows, :]
            kh, kl = split(keys)
            qh, ql = split(queries)
            query_both[rows, :] = jnp.concatenate([qh, ql], axis=1)
            scores[k] = mm_nt(
                jnp.concatenate([qh, ql], axis=1), jnp.concatenate([kh, kh], axis=1)
            ) + mm_nt(qh, kl)
            th, tl = split(keys.T)
            key_turned[k, 0] = th
            key_turned[k, 1] = tl

    block = block_ref[...]
    pre = conv_pre(
        block, conv_shifts(block, edge_ref[...], inside_ref, outside_ref), taps_ref[...]
    )
    inner = pre * sigmoid(pre)
    inner_out[...] = inner
    turned, unused, steps = pair_columns(steps_ref[...], pair)
    unused, enter, leave = pair_columns(decay_ref[...], pair)
    scaled = steps * inner
    leaving = leave * scaled
    lane = lax.broadcasted_iota(jnp.int32, (HALF, LANES), 1)
    head_rows = [head_row(rows_ref[...], 2 * pair + a) for a in range(2)]
    factor = pair_rows(factor_ref[...], pair)
    state = None
    for k in range(spans):
        at = k * SPAN
        sh, sl = split(scaled[at : at + SPAN])
        both = jnp.concatenate([sh, sl], axis=1)
        parts = []
        for half in range(2):
            per_head = []
            width = HALF * (half + 1)
            for a in range(2):
                row = head_rows[a][:, at : at + width]
                column = turned[at + half * HALF : at + (half + 1) * HALF, a : a + 1]
                decay = jnp.exp(
                    jnp.minimum(
                        column - row, mask_ref[k, pl.ds(half * HALF, HALF), pl.ds(0, width)]
                    )
                )
                weights = decay * scores[k, pl.ds(half * HALF, HALF), pl.ds(0, width)]
                wh, wl = split(weights)
                wide = mm(wh, both[:width])
                per_head.append(wide[:, :LANES] + wide[:, LANES:] + mm(wl, sh[:width]))
            parts.append(jnp.where(lane < HD, per_head[0], per_head[1]))
        local = jnp.concatenate(parts, axis=0)
        ph, pw = split(leaving[at : at + SPAN])
        fresh = mm(key_turned[k, 0], jnp.concatenate([ph, pw], axis=1))
        fresh = fresh[:, :LANES] + fresh[:, LANES:] + mm(key_turned[k, 1], ph)
        if state is None:
            state = fresh
        else:
            th, tl = split(state)
            q2 = query_both[pl.ds(at, SPAN), :]
            carried = mm(q2, jnp.concatenate([th, th], axis=0)) + mm(q2[:, :DS], tl)
            local = local + enter[at : at + SPAN] * carried
            state = factor[k : k + 1] * state + fresh
        state_out[k] = state
        local_out[pl.ds(at, SPAN), :] = local


def forward_call(spans, mixed, edge, taps, inside, outside, steps, decay, rows, factor, mask):
    count = spans * SPAN
    at_pair = lambda n: pl.BlockSpec((n, LANES), lambda i: (0, i))
    at_key = lambda n: pl.BlockSpec((n, LANES), lambda i: (0, PAIRS))
    at_query = lambda n: pl.BlockSpec((n, LANES), lambda i: (0, PAIRS + 1))
    whole = lambda *s: pl.BlockSpec(s, lambda i: (0,) * len(s))
    return pl.pallas_call(
        functools.partial(forward_kernel, spans),
        grid=(PAIRS,),
        in_specs=[
            at_pair(count),
            at_key(count),
            at_query(count),
            at_pair(8),
            at_key(8),
            at_query(8),
            at_pair(8),
            at_key(8),
            at_query(8),
            whole(3, count, LANES),
            whole(3, 8, LANES),
            whole(count, LANES),
            whole(count, LANES),
            pl.BlockSpec((8, count), lambda i: (i // 4, 0)),
            whole(8, LANES),
            whole(spans, SPAN, SPAN),
        ],
        out_specs=[
            at_pair(count),
            at_pair(count),
            pl.BlockSpec((spans, DS, LANES), lambda i: (0, 0, i)),
            whole(count, LANES),
            whole(count, LANES),
        ],
        out_shape=[
            jax.ShapeDtypeStruct((count, DI), f32),
            jax.ShapeDtypeStruct((count, DI), f32),
            jax.ShapeDtypeStruct((spans, DS, DI), f32),
            jax.ShapeDtypeStruct((count, DS), f32),
            jax.ShapeDtypeStruct((count, DS), f32),
        ],
        scratch_shapes=[
            pltpu.VMEM((spans, SPAN, SPAN), f32),
            pltpu.VMEM((spans, 2, DS, SPAN), bf16),
            pltpu.VMEM((count, 2 * DS), bf16),
        ],
        compiler_params=pltpu.CompilerParams(vmem_limit_bytes=VMEM_LIMIT),
        cost_estimate=pl.CostEstimate(flops=1, bytes_accessed=1, transcendentals=0),
        name="recurrence_forward",
    )(
        mixed,
        mixed,
        mixed,
        edge,
        edge,
        edge,
        taps,
        taps,
        taps,
        inside,
        outside,
        steps,
        decay,
        rows,
        factor,
        mask,
    )


def norm_kernel(
    local_ref,
    inner_ref,
    gate_ref,
    back_ref,
    query_ref,
    state_ref,
    reach_ref,
    spread_ref,
    skip_ref,
    gain_ref,
    out_ref,
    mixer_grad_ref,
    gate_grad_ref,
    gain_grad_ref,
    dots_ref,
    summary_ref,
    most_ref,
    mixed_y,
    state_both,
    reach_wide,
):
    step = pl.program_id(0)
    chunks = [pl.ds(c * NORM_COLS, NORM_COLS) for c in range(DI // NORM_COLS)]

    @pl.when(step == 0)
    def _():
        sh, sl = split(state_ref[...])
        state_both[0] = sh
        state_both[1] = sl
        gain_grad_ref[...] = jnp.zeros_like(gain_grad_ref)
        summary_ref[...] = jnp.zeros_like(summary_ref)
        most_ref[...] = jnp.zeros_like(most_ref)

    qh, ql = split(query_ref[...])
    query_both = jnp.concatenate([qh, ql], axis=1)
    rh, rl = split(reach_ref[...])
    reach_both = jnp.concatenate([rh, rl], axis=1)
    squares = jnp.zeros((NORM_ROWS, 1), f32)
    mixes = jnp.zeros((NORM_ROWS, 1), f32)
    for cols in chunks:
        sh, sl = state_both[0, :, cols], state_both[1, :, cols]
        spread = spread_ref[:, cols]
        reach = mm(reach_both, jnp.concatenate([spread, spread], axis=0))
        reach_wide[:, cols] = reach
        carried = mm(query_both, jnp.concatenate([sh, sh], axis=0)) + mm(qh, sl)
        y = local_ref[:, cols] + reach * carried
        mixed_y[:, cols] = y
        mixer = y + skip_ref[0:1, cols] * inner_ref[:, cols]
        gate = gate_ref[:, cols]
        gated = mixer * (gate * sigmoid(gate))
        squares = squares + jnp.sum(gated * gated, axis=1, keepdims=True)
        mixes = mixes + jnp.sum(
            gated * (back_ref[:, cols] * gain_ref[0:1, cols]), axis=1, keepdims=True
        )
    scale = lax.rsqrt(squares * (1.0 / DI) + norm_eps)
    pull = scale * mixes * (1.0 / DI)
    query_turned = query_ref[...].T
    th, tl = split(query_turned)
    dots = jnp.zeros((NORM_ROWS, LANES), f32)
    for cols in chunks:
        y = mixed_y[:, cols]
        mixer = y + skip_ref[0:1, cols] * inner_ref[:, cols]
        gate = gate_ref[:, cols]
        opened = sigmoid(gate)
        silu = gate * opened
        unit = mixer * silu * scale
        gain = gain_ref[0:1, cols]
        back = back_ref[:, cols]
        out_ref[:, cols] = (unit * gain).astype(bf16)
        gain_grad_ref[0:1, cols] += jnp.sum(back * unit, axis=0, keepdims=True)
        gated_grad = scale * (back * gain - unit * pull)
        mixer_grad = gated_grad * silu
        mixer_grad_ref[:, cols] = mixer_grad
        gate_grad = gated_grad * mixer * (opened * (1.0 + gate * (1.0 - opened)))
        gate_grad_ref[:, cols] = gate_grad.astype(bf16)
        most = jnp.max(jnp.abs(gate_grad).reshape(NORM_ROWS // 8, 8, NORM_COLS), axis=0)
        for c in range(NORM_COLS // LANES):
            most_ref[...] = jnp.maximum(most_ref[...], most[:, c * LANES : (c + 1) * LANES])
        dh, dl = split(mixer_grad * y)
        spread = spread_ref[:, cols]
        dots = dots + mm_nt(dh, spread) + mm_nt(dl, spread)
        mh, ml = split(reach_wide[:, cols] * mixer_grad)
        summary_ref[:, cols] += (
            mm(jnp.concatenate([th, tl], axis=1), jnp.concatenate([mh, mh], axis=0)) + mm(th, ml)
        )
    dots_ref[...] = dots


def norm_call(local, inner, gate, back, queries, state_in, reach, spread, skip, gain):
    count = local.shape[0]
    rows = lambda n: pl.BlockSpec((NORM_ROWS, n), lambda i: (i, 0))
    whole = lambda *s: pl.BlockSpec(s, lambda i: (0,) * len(s))
    return pl.pallas_call(
        norm_kernel,
        grid=(count // NORM_ROWS,),
        in_specs=[
            rows(DI),
            rows(DI),
            rows(DI),
            rows(DI),
            rows(DS),
            whole(DS, DI),
            rows(LANES),
            whole(LANES, DI),
            whole(8, DI),
            whole(8, DI),
        ],
        out_specs=[
            rows(DI),
            rows(DI),
            rows(DI),
            whole(8, DI),
            rows(LANES),
            whole(DS, DI),
            whole(8, LANES),
        ],
        out_shape=[
            jax.ShapeDtypeStruct((count, DI), bf16),
            jax.ShapeDtypeStruct((count, DI), f32),
            jax.ShapeDtypeStruct((count, DI), bf16),
            jax.ShapeDtypeStruct((8, DI), f32),
            jax.ShapeDtypeStruct((count, LANES), f32),
            jax.ShapeDtypeStruct((DS, DI), f32),
            jax.ShapeDtypeStruct((8, LANES), f32),
        ],
        scratch_shapes=[
            pltpu.VMEM((NORM_ROWS, DI), f32),
            pltpu.VMEM((2, DS, DI), bf16),
            pltpu.VMEM((NORM_ROWS, DI), f32),
        ],
        compiler_params=pltpu.CompilerParams(vmem_limit_bytes=VMEM_LIMIT),
        cost_estimate=pl.CostEstimate(flops=1, bytes_accessed=1, transcendentals=0),
        name="gated_norm",
    )(local, inner, gate, back, queries, state_in, reach, spread, skip, gain)


def backward_kernel(spans, first, pairs, last, *refs):
    (
        block_ref,
        edge_ref,
        taps_ref,
        inside_ref,
        outside_ref,
        keys_ref,
        queries_ref,
        back_ref,
        steps_ref,
        decay_ref,
        rows_ref,
        factor_ref,
        start_ref,
        mask_ref,
        states_ref,
        state_in_ref,
        state_back_ref,
        skip_ref,
        *refs,
    ) = refs
    if last:
        dots_ref, raw_ref, params_ref, *refs = refs
        old_scores_grad, old_key_grad, old_query_grad, old_steps, old_heads, *refs = refs
    grad_out, top_out, tail_out, taps_out, most_out, *refs = refs
    scores_grad, key_grad, query_grad, steps_out, heads_out, *refs = refs
    if last:
        sums_out, *refs = refs
    scores, key_both, query_both, query_turned = refs
    step = pl.program_id(0)
    pair = step + first
    lane = lax.broadcasted_iota(jnp.int32, (SPAN, LANES), 1)

    @pl.when(step == 0)
    def _():
        if last:
            key_grad[...] = old_key_grad[...]
            query_grad[...] = old_query_grad[...]
            scores_grad[...] = old_scores_grad[...]
            steps_out[...] = old_steps[...]
            heads_out[...] = old_heads[...]
        else:
            key_grad[...] = jnp.zeros_like(key_grad)
            query_grad[...] = jnp.zeros_like(query_grad)
            scores_grad[...] = jnp.zeros_like(scores_grad)
            steps_out[...] = jnp.zeros_like(steps_out)
            heads_out[...] = jnp.zeros_like(heads_out)
        for k in range(spans):
            rows = pl.ds(k * SPAN, SPAN)
            keys, queries = keys_ref[rows, :], queries_ref[rows, :]
            kh, kl = split(keys)
            qh, ql = split(queries)
            key_both[rows, :] = jnp.concatenate([kh, kl], axis=1)
            query_both[rows, :] = jnp.concatenate([qh, ql], axis=1)
            scores[k] = mm_nt(
                jnp.concatenate([kh, kl], axis=1), jnp.concatenate([qh, qh], axis=1)
            ) + mm_nt(kh, ql)
            th, tl = split(queries.T)
            query_turned[k, 0] = th
            query_turned[k, 1] = tl

    def conv_back(conved_grad, block, shifted, pre):
        opened = sigmoid(pre)
        pre_grad = conved_grad * (opened * (1.0 + pre * (1.0 - opened)))
        count = block.shape[0]
        taps = taps_ref[...]
        total = taps[3:4] * pre_grad
        sums = [None] * 8
        sums[3] = jnp.sum(pre_grad * block, axis=0, keepdims=True)
        sums[4] = jnp.sum(pre_grad, axis=0, keepdims=True)
        for j in range(1, CONV):
            total = total + taps[3 - j : 4 - j] * pltpu.roll(
                inside_ref[j - 1] * pre_grad, count - j, 0
            )
            sums[3 - j] = jnp.sum(pre_grad * shifted[j - 1], axis=0, keepdims=True)
        grad_out[...] = total.astype(bf16)
        tail_out[...] = total[count - 8 :]
        most_out[...] = jnp.max(jnp.abs(total).reshape(count // 8, 8, LANES), axis=0)
        top_out[...] = pre_grad[:8]
        return sums

    zero_row = jnp.zeros((1, LANES), f32)

    def of_conv():
        block = block_ref[...]
        shifted = conv_shifts(block, edge_ref[...], inside_ref, outside_ref)
        return block, shifted, conv_pre(block, shifted, taps_ref[...])

    @pl.when(step < pairs)
    def _():
        block, shifted, pre = of_conv()
        head_rows = [head_row(rows_ref[...], 2 * pair + a) for a in range(2)]
        factor = pair_rows(factor_ref[...], pair)
        start = pair_rows(start_ref[...], pair)
        skip = pair_rows(skip_ref[...], pair)
        inner = pre * sigmoid(pre)
        back = back_ref[...]
        turned, unused, steps = pair_columns(steps_ref[...], pair)
        unused, enter, leave = pair_columns(decay_ref[...], pair)
        scaled = steps * inner
        leaving = leave * scaled
        entering = enter * back
        state_in = state_in_ref[...]
        state_back = state_back_ref[...]
        scaled_grads = [None] * spans
        ends = [zero_row] * 8
        for k in reversed(range(spans)):
            at = k * SPAN
            rows = pl.ds(at, SPAN)
            bh, bl = split(back[at : at + SPAN])
            both = jnp.concatenate([bh, bl], axis=1)
            sh, sl = split(scaled[at : at + SPAN])
            per_head = []
            for a in range(2):
                mine = (lane < HD) if a == 0 else (lane >= HD)
                zero = jnp.zeros((SPAN, LANES), bf16)
                left = jnp.concatenate(
                    [
                        jnp.where(mine, sh, pltpu.roll(sl.astype(f32), HD, 1).astype(bf16)),
                        jnp.where(mine, sh, zero),
                    ],
                    axis=1,
                )
                right = jnp.concatenate(
                    [
                        jnp.where(mine, bh, pltpu.roll(bh.astype(f32), HD, 1).astype(bf16)),
                        jnp.where(mine, bl, zero),
                    ],
                    axis=1,
                )
                parts = []
                for half in range(2):
                    low = half * HALF
                    width = SPAN - low
                    row = head_rows[a][:, at + low : at + low + width]
                    column = turned[at + low : at + low + HALF, a : a + 1]
                    here = pl.ds(low, HALF)
                    there = pl.ds(low, width)
                    decay = jnp.exp(jnp.minimum(row - column, mask_ref[k, here, there]))
                    weights = decay * scores[k, here, there]
                    wh, wl = split(weights)
                    wide = mm(wh, both[low:])
                    parts.append(wide[:, :LANES] + wide[:, LANES:] + mm(wl, bh[low:]))
                    weights_grad = mm_nt(left[low : low + HALF], right[low:])
                    scores_grad[k, here, there] += decay * weights_grad
                per_head.append(jnp.concatenate(parts, axis=0))
            scaled_grad = jnp.where(lane < HD, per_head[0], per_head[1])
            gh, gl = split(state_back)
            k2 = key_both[rows, :]
            scaled_grad = scaled_grad + leave[at : at + SPAN] * (
                mm(k2, jnp.concatenate([gh, gh], axis=0)) + mm(k2[:, :DS], gl)
            )
            scaled_grads[k] = scaled_grad
            lh, ll = split(leaving[at : at + SPAN])
            key_grad[rows, :] += mm_nt(
                jnp.concatenate([lh, ll], axis=1), jnp.concatenate([gh, gh], axis=1)
            ) + mm_nt(lh, gl)
            after = states_ref[k] + start[k + 1 : k + 2] * state_in
            ends[k] = jnp.sum(state_back * after, axis=0, keepdims=True)
            before = start[k : k + 1] * state_in
            if k > 0:
                before = before + states_ref[k - 1]
            th, tl = split(before)
            eh, el = split(entering[at : at + SPAN])
            query_grad[rows, :] += mm_nt(
                jnp.concatenate([eh, el], axis=1), jnp.concatenate([th, th], axis=1)
            ) + mm_nt(eh, tl)
            if k > 0:
                more = mm(query_turned[k, 0], jnp.concatenate([eh, el], axis=1))
                state_back = (
                    factor[k : k + 1] * state_back
                    + more[:, :LANES]
                    + more[:, LANES:]
                    + mm(query_turned[k, 1], eh)
                )
        scaled_grad = jnp.concatenate(scaled_grads, axis=0)
        target = lax.broadcasted_iota(jnp.int32, (LANES, LANES), 1)
        source = lax.broadcasted_iota(jnp.int32, (LANES, LANES), 0)
        place = (target == 2 * pair + source // HD).astype(bf16)
        dh, dl = split(inner * scaled_grad)
        steps_out[...] += mm(dh, place) + mm(dl, place)
        sums = conv_back(steps * scaled_grad + skip[0:1] * back, block, shifted, pre)
        ends[4] = jnp.sum(back * inner, axis=0, keepdims=True)
        taps_out[...] = jnp.concatenate([zero_row if s is None else s for s in sums], axis=0)
        eh, el, ew = split_three(jnp.concatenate(ends, axis=0))
        heads_out[...] += mm(eh, place) + mm(el, place) + mm(ew, place)

    if not last:
        return

    def of_scores(grad_ref, ones_ref, transposed):
        for k in range(spans):
            rows = pl.ds(k * SPAN, SPAN)
            grad = scores_grad[k]
            gh, gl = split(grad.T if transposed else grad)
            ones = ones_ref[rows, :]
            wide = mm(gh, ones)
            grad_ref[rows, :] += wide[:, :DS] + wide[:, DS:] + mm(gl, ones[:, :DS])

    @pl.when(jnp.logical_and(step >= pairs, step < pairs + 2))
    def _():
        @pl.when(step == pairs)
        def _():
            of_scores(key_grad, query_both, False)

        @pl.when(step == pairs + 1)
        def _():
            of_scores(query_grad, key_both, True)

        block, shifted, pre = of_conv()
        grad = jnp.where(step == pairs, key_grad[...], query_grad[...])
        sums = conv_back(grad, block, shifted, pre)
        taps_out[...] = jnp.concatenate([zero_row if s is None else s for s in sums], axis=0)

    @pl.when(step == pairs + 2)
    def _():
        tall = lax.broadcasted_iota(jnp.int32, (SPAN, SPAN), 0)
        wide = lax.broadcasted_iota(jnp.int32, (SPAN, SPAN), 1)
        upper = (tall <= wide).astype(bf16)
        known = lane < NH
        rate = params_ref[1:2]
        delta, decay, most = zero_row, zero_row, zero_row
        for k in range(spans):
            rows = pl.ds(k * SPAN, SPAN)
            steps = jnp.where(known, pltpu.roll(steps_ref[rows, :], LANES // 2, 1), 0.0)
            step_dots = steps_out[rows, :]
            cumul_grad = dots_ref[rows, :] - steps * step_dots
            parts = mm(upper, jnp.concatenate(split_three(cumul_grad), axis=1))
            decay_grad = parts[:, :LANES] + parts[:, LANES : 2 * LANES] + parts[:, 2 * LANES :]
            decay_grad = decay_grad + heads_out[k : k + 1]
            raw = jnp.where(known, raw_ref[rows, :], 0.0) + params_ref[0:1]
            raw_grad = (step_dots + rate * decay_grad) * sigmoid(raw)
            raw_grad = jnp.where(known, raw_grad, 0.0)
            grad_out[rows, :] = raw_grad.astype(bf16)
            most = jnp.maximum(most, jnp.max(jnp.abs(raw_grad), axis=0, keepdims=True))
            delta = delta + jnp.sum(raw_grad, axis=0, keepdims=True)
            decay = decay + jnp.sum(rate * steps * decay_grad, axis=0, keepdims=True)
        sums_out[...] = jnp.concatenate(
            [delta, decay, heads_out[4:5], most, jnp.zeros((4, LANES), f32)], axis=0
        )

    @pl.when(step > pairs + 2)
    def _():
        grad_out[...] = jnp.zeros_like(grad_out)


def backward_call(spans, first, pairs, columns, shared, finish=None):
    count = spans * SPAN
    last = finish is not None
    clip_block = lambda i: jnp.minimum(i + first, CONVD // LANES - 1)
    clip = lambda i: jnp.minimum(i, pairs - 1) + first
    at_block = lambda n: pl.BlockSpec((n, LANES), lambda i: (0, clip_block(i)))
    at_pair = lambda n: pl.BlockSpec((n, LANES), lambda i: (0, clip(i)))
    out_block = lambda n: pl.BlockSpec((n, LANES), lambda i: (0, i))
    whole = lambda *s: pl.BlockSpec(s, lambda i: (0,) * len(s))
    accumulators = [
        (spans, SPAN, SPAN),
        (count, DS),
        (count, DS),
        (count, LANES),
        (8, LANES),
    ]
    wide = columns * LANES
    side = (pairs + 2 if last else pairs) * LANES
    side_block = lambda: pl.BlockSpec(
        (8, LANES), lambda i: (0, jnp.minimum(i, side // LANES - 1))
    )
    in_specs = [
        at_block(count),
        at_block(8),
        at_block(8),
        whole(CONV - 1, count, LANES),
        whole(CONV - 1, 8, LANES),
        whole(count, DS),
        whole(count, DS),
        at_pair(count),
        whole(count, LANES),
        whole(count, LANES),
        pl.BlockSpec((8, count), lambda i: (clip(i) // 4, 0)),
        whole(8, LANES),
        whole(8, LANES),
        whole(spans, SPAN, SPAN),
        pl.BlockSpec((spans, DS, LANES), lambda i: (0, 0, clip(i))),
        at_pair(DS),
        at_pair(DS),
        whole(8, LANES),
    ]
    out_specs = [out_block(count)] + [side_block()] * 4 + [whole(*s) for s in accumulators]
    out_shape = [jax.ShapeDtypeStruct((count, wide), bf16)]
    out_shape += [jax.ShapeDtypeStruct((8, side), f32)] * 4
    out_shape += [jax.ShapeDtypeStruct(s, f32) for s in accumulators]
    operands = list(shared)
    if last:
        dots, mixed, params, earlier = finish
        in_specs += [
            whole(count, LANES),
            pl.BlockSpec((count, LANES), lambda i: (0, CONVD // LANES)),
            whole(8, LANES),
        ]
        in_specs += [whole(*s) for s in accumulators]
        operands += [dots, mixed, params, *earlier]
        out_specs += [whole(8, LANES)]
        out_shape += [jax.ShapeDtypeStruct((8, LANES), f32)]
    return pl.pallas_call(
        functools.partial(backward_kernel, spans, first, pairs, last),
        grid=(columns,),
        in_specs=in_specs,
        out_specs=out_specs,
        out_shape=out_shape,
        scratch_shapes=[
            pltpu.VMEM((spans, SPAN, SPAN), f32),
            pltpu.VMEM((count, 2 * DS), bf16),
            pltpu.VMEM((count, 2 * DS), bf16),
            pltpu.VMEM((spans, 2, DS, SPAN), bf16),
        ],
        compiler_params=pltpu.CompilerParams(vmem_limit_bytes=VMEM_LIMIT),
        cost_estimate=pl.CostEstimate(flops=1, bytes_accessed=1, transcendentals=0),
        name="recurrence_backward",
    )(*operands)


MESH = pl.DeviceIdType.MESH
Z = 4
Y = 2


def gather_kernel(
    first_ref,
    second_ref,
    third_ref,
    first_out,
    second_out,
    third_out,
    own_sem,
    up_sem,
    down_sem,
    z_sem,
    y_sent,
    y_sem,
    x_sent,
    x_sem,
    core_sent,
    core_sem,
):
    f, ctx = lax.axis_index("fsdp"), lax.axis_index("ctx")
    z, y = f // Y, lax.rem(f, Y)
    x, c = ctx // 2, lax.rem(ctx, 2)
    at_z = lambda other: (other * Y + y, ctx)
    at_y = (z * Y + 1 - y, ctx)
    at_x = (f, (1 - x) * 2 + c)
    at_core = (f, x * 2 + 1 - c)
    arrays = ((first_ref, first_out), (second_ref, second_out), (third_ref, third_out))

    barrier = pltpu.get_barrier_semaphore()
    for partner in (at_y, at_x, at_core):
        pl.semaphore_signal(barrier, inc=1, device_id=partner, device_id_type=MESH)

    @pl.when(z > 0)
    def _():
        pl.semaphore_signal(barrier, inc=1, device_id=at_z(z - 1), device_id_type=MESH)

    @pl.when(z < Z - 1)
    def _():
        pl.semaphore_signal(barrier, inc=1, device_id=at_z(z + 1), device_id_type=MESH)

    middle = jnp.logical_and(z > 0, z < Z - 1).astype(jnp.int32)
    pl.semaphore_wait(barrier, 4 + middle)

    def rows_of(n):
        return arrays[n][0].shape[0]

    def move(n, block, row, size, sent, landed, partner, own=False):
        here = arrays[n][1].at[pl.ds(block * rows_of(n) + row, size)]
        source = arrays[n][0].at[pl.ds(row, size)] if own else here
        return pltpu.make_async_remote_copy(
            src_ref=source,
            dst_ref=here,
            send_sem=sent,
            recv_sem=landed,
            device_id=partner,
            device_id_type=MESH,
        )

    def third(n):
        return rows_of(n) // 6

    def gathered(n):
        return c * (rows_of(n) // 2) + x * third(n), 2 * third(n)

    def up(n, zb, own=False):
        return move(
            n, zb * Y + y, *gathered(n), up_sem.at[n, zb], z_sem.at[n, zb], at_z(z + 1), own
        )

    def down(n, zb, own=False):
        return move(
            n, zb * Y + y, *gathered(n), down_sem.at[n, zb], z_sem.at[n, zb], at_z(z - 1), own
        )

    def along_y(n, zb, yb, own=False):
        return move(n, zb * Y + yb, *gathered(n), y_sent.at[n, zb], y_sem.at[n, zb], at_y, own)

    def along_x(n, block, sender_x):
        row = c * (rows_of(n) // 2) + 2 * third(n) * sender_x
        return move(n, block, row, third(n), x_sent.at[n, block], x_sem.at[n, block], at_x)

    def core_first(n, block, core):
        row = core * (rows_of(n) // 2) + x * third(n)
        return move(
            n,
            block,
            row,
            2 * third(n),
            core_sent.at[n, block, 0],
            core_sem.at[n, block, 0],
            at_core,
        )

    def core_second(n, block, core):
        row = core * (rows_of(n) // 2) + 2 * third(n) * (1 - x)
        return move(
            n, block, row, third(n), core_sent.at[n, block, 1], core_sem.at[n, block, 1], at_core
        )

    count = len(arrays)
    own_copies = []
    for n in range(count):
        copy = pltpu.make_async_copy(
            arrays[n][0], arrays[n][1].at[pl.ds(f * rows_of(n), rows_of(n))], own_sem.at[n]
        )
        copy.start()
        own_copies.append(copy)

        @pl.when(z < Z - 1)
        def _():
            up(n, z, True).start()

        @pl.when(z > 0)
        def _():
            down(n, z, True).start()

        along_y(n, z, y, True).start()

    def spread(n, block):
        along_x(n, block, x).start()
        core_first(n, block, c).start()

    def come_along_z(distance):
        for way in (1, -1):
            zb = z - way * distance

            @pl.when(jnp.logical_and(zb >= 0, zb < Z))
            def _():
                for n in range(count):
                    up(n, zb).wait_recv()
                    if way == 1:

                        @pl.when(z < Z - 1)
                        def _():
                            up(n, zb).start()
                    else:

                        @pl.when(z > 0)
                        def _():
                            down(n, zb).start()

                    along_y(n, zb, y).start()
                    spread(n, zb * Y + y)

    def come_along_y(distance):
        for way in (1, -1) if distance else (1,):
            zb = z - way * distance

            @pl.when(jnp.logical_and(zb >= 0, zb < Z))
            def _():
                for n in range(count):
                    along_y(n, zb, 1 - y).wait_recv()
                    spread(n, zb * Y + 1 - y)

    def each_block(do):
        def at(zb, yb):
            @pl.when(jnp.logical_and(zb >= 0, zb < Z))
            def _():
                for n in range(count):
                    do(n, zb * Y + yb)

        for distance in range(Z):
            for way in (1, -1) if distance else (1,):
                if distance:
                    at(z - way * distance, y)
                at(z - way * distance, 1 - y)

    for distance in range(Z):
        if distance:
            come_along_z(distance)
            come_along_y(distance - 1)
    come_along_y(Z - 1)

    def come_along_x(n, block):
        along_x(n, block, 1 - x).wait_recv()
        core_second(n, block, c).start()

    each_block(come_along_x)

    def finish(n, block):
        core_first(n, block, 1 - c).wait_recv()
        core_second(n, block, 1 - c).wait_recv()
        along_x(n, block, x).wait_send()
        core_first(n, block, c).wait_send()
        core_second(n, block, c).wait_send()

    each_block(finish)
    for n in range(count):
        own_copies[n].wait()
        for zb in range(Z):
            along_y(n, zb, y).wait_send()

            @pl.when(jnp.logical_and(z < Z - 1, zb <= z))
            def _():
                up(n, zb).wait_send()

            @pl.when(jnp.logical_and(z > 0, zb >= z))
            def _():
                down(n, zb).wait_send()


def gather_call(blocks, size):
    count = len(blocks)
    dma = lambda *s: pltpu.SemaphoreType.DMA((count,) + s)
    return pl.pallas_call(
        gather_kernel,
        in_specs=[pl.BlockSpec(memory_space=pl.ANY)] * count,
        out_specs=[pl.BlockSpec(memory_space=pl.ANY)] * count,
        out_shape=[
            jax.ShapeDtypeStruct((b.shape[0] * size, b.shape[1]), b.dtype) for b in blocks
        ],
        scratch_shapes=[
            dma(),
            dma(Z),
            dma(Z),
            dma(Z),
            dma(Z),
            dma(Z),
            dma(size),
            dma(size),
            dma(size, 2),
            dma(size, 2),
        ],
        compiler_params=pltpu.CompilerParams(collective_id=0, has_side_effects=True),
        name="gather_rows",
    )(*blocks)


def agree_kernel(first_ref, second_ref, out_ref, own, shared, near, far, sent, landed):
    f, ctx = lax.axis_index("fsdp"), lax.axis_index("ctx")
    fsdp_size, ctx_size = lax.axis_size("fsdp"), lax.axis_size("ctx")
    partners = [(f, lax.rem(ctx + d, ctx_size)) for d in range(1, ctx_size)]
    partners += [(lax.rem(f + d, fsdp_size), ctx) for d in range(1, fsdp_size)]
    barrier = pltpu.get_barrier_semaphore()
    for partner in partners:
        pl.semaphore_signal(barrier, inc=1, device_id=partner, device_id_type=MESH)
    most = jnp.maximum(jnp.max(jnp.abs(first_ref[...])), jnp.max(jnp.abs(second_ref[...])))
    own[...] = jnp.full(own.shape, most, f32)
    pl.semaphore_wait(barrier, len(partners))

    def exchange(source, slots, first, count):
        copies = []
        for n in range(count):
            copies.append(
                pltpu.make_async_remote_copy(
                    src_ref=source,
                    dst_ref=slots.at[n],
                    send_sem=sent.at[first + n],
                    recv_sem=landed.at[first + n],
                    device_id=partners[first + n],
                    device_id_type=MESH,
                )
            )
            copies[-1].start()
        for copy in copies:
            copy.wait()

    exchange(own, near, 0, ctx_size - 1)
    shared[...] = jnp.maximum(own[...], jnp.max(near[...], axis=0))
    exchange(shared, far, ctx_size - 1, fsdp_size - 1)
    out_ref[0, 0] = jnp.max(jnp.maximum(shared[...], jnp.max(far[...], axis=0)))


def largest_anywhere(first, second, collective_id):
    partners = lax.axis_size("ctx") + lax.axis_size("fsdp") - 2
    out = pl.pallas_call(
        agree_kernel,
        in_specs=[pl.BlockSpec(memory_space=pltpu.VMEM)] * 2,
        out_specs=pl.BlockSpec(memory_space=pltpu.SMEM),
        out_shape=jax.ShapeDtypeStruct((1, 1), f32),
        scratch_shapes=[
            pltpu.VMEM((8, LANES), f32),
            pltpu.VMEM((8, LANES), f32),
            pltpu.VMEM((lax.axis_size("ctx") - 1, 8, LANES), f32),
            pltpu.VMEM((lax.axis_size("fsdp") - 1, 8, LANES), f32),
            pltpu.SemaphoreType.DMA((partners,)),
            pltpu.SemaphoreType.DMA((partners,)),
        ],
        compiler_params=pltpu.CompilerParams(collective_id=collective_id, has_side_effects=True),
        name="largest_anywhere",
    )(first, second)
    return out.reshape(()) * 1.01 + 1e-30


def adamw_update(param, grad, first, second, decay):
    first_new = beta_one * first + (1.0 - beta_one) * grad
    second_new = beta_two * second + (1.0 - beta_two) * grad * grad
    first_hat = first_new / (1.0 - beta_one**STEP)
    second_hat = second_new / (1.0 - beta_two**STEP)
    param_new = param - learn_rate * (first_hat / (jnp.sqrt(second_hat) + adam_eps) + decay * param)
    return (param_new, first_new, second_new)


def segment_of(lengths, positions):
    ends = jnp.cumsum(lengths)
    return jnp.sum((positions[..., None] >= ends).astype(jnp.int32), axis=-1)


def padded(*rows):
    out = jnp.stack([jnp.pad(r, (0, LANES - r.shape[0])) for r in rows])
    return jnp.pad(out, ((0, 8 - len(rows)), (0, 0)))


def spread_matrix():
    head = lax.broadcasted_iota(jnp.int32, (LANES, DI), 0)
    lane = lax.broadcasted_iota(jnp.int32, (LANES, DI), 1)
    return (head == lane // HD).astype(bf16)


def pass_on(own, factor, axis, backwards, kind):
    size, here = lax.axis_size(axis), lax.axis_index(axis)
    given = jnp.zeros_like(own)
    for turn in range(size - 1):
        source = size - 1 - turn if backwards else turn
        target = source - 1 if backwards else source + 1
        out = (factor * given + own).astype(kind)
        arrived = lax.ppermute(out, axis, [(source, target)]).astype(f32)
        given = jnp.where(here == target, arrived, given)
    return given


def on_small_slice():
    return lax.axis_size("fsdp") == Z * Y and lax.axis_size("ctx") == 4


def gather_rows(*blocks):
    if on_small_slice():
        return gather_call(blocks, Z * Y)
    return [lax.all_gather(b, "fsdp", axis=0, tiled=True) for b in blocks]


def swapped(value, axis, step):
    size = lax.axis_size(axis)
    return lax.ppermute(value, axis, [(i, i ^ step) for i in range(size)])


def after(value, *others):
    return lax.optimization_barrier((value,) + others)[0]


def coordinates():
    f, ctx = lax.axis_index("fsdp"), lax.axis_index("ctx")
    return ctx // 2, f % Y, f // Y, ctx % 2


CORE = ("ctx", 1)
ACROSS_X = ("ctx", 2)
ACROSS_Y = ("fsdp", 1)
ACROSS_Z = tuple(("fsdp", Y * m) for m in range(1, Z))


def row_products(columns, grads):
    return jnp.einsum("tk,tz->kz", columns, grads, preferred_element_type=f32)


def half_of(value, bit, axis):
    size = value.shape[axis] // 2
    return lax.dynamic_slice_in_dim(value, bit * size, size, axis)


class Part:
    def __init__(self, value, bound):
        self.value, self.bound = value, bound


def lowered(value, bound):
    return (value * (32768.0 / bound)).astype(jnp.float16)


def raised(value, bound):
    return value.astype(f32) * (bound * (1.0 / 32768.0))


def summed_on_chip(columns, grads, bound):
    core = coordinates()[3]
    theirs = row_products(columns, half_of(grads, 1 - core, 1))
    arrived = swapped(lowered(theirs, bound), *CORE)
    mine = row_products(columns, half_of(grads, core, 1))
    return Part(mine + raised(arrived, bound), 2.0 * bound)


def to_send(part, bit, axis):
    sent = lowered(half_of(part.value, 1 - bit, axis), part.bound)
    return Part(half_of(part.value, bit, axis), part.bound), sent


def joined_with(kept, arrived):
    return Part(kept.value + raised(arrived, kept.bound), 2.0 * kept.bound)


def by_owner(part):
    return Part(part.value.reshape(Z, Y, -1, part.value.shape[1]), part.bound)


def along_z(part):
    z = coordinates()[2]
    take = lambda at: lax.dynamic_index_in_dim(part.value[:, 0], at, 0, keepdims=False)
    sent = [lowered(take(z ^ m), part.bound) for m in range(1, Z)]
    return Part(take(z), part.bound), sent


def of_owner(kept, arrived):
    total = kept.value
    for one in arrived:
        total = total + raised(one, kept.bound)
    return Part(total, Z * kept.bound)


def both_halves(value, way, bit):
    other = swapped(value, *way)
    return jnp.where(
        bit == 0,
        jnp.concatenate([value, other], axis=1),
        jnp.concatenate([other, value], axis=1),
    )


def across_x(part):
    low = lowered(part.value, part.bound)
    total = raised(low, part.bound) + raised(swapped(low, *ACROSS_X), part.bound)
    return both_halves(total, CORE, coordinates()[3])


def owned_rows(partial):
    return lax.psum(lax.psum_scatter(partial, "fsdp", scatter_dimension=0, tiled=True), "ctx")


def sum_everywhere(value, axes):
    for axis in axes:
        step = 1
        while step < lax.axis_size(axis):
            value = value + swapped(value, axis, step)
            step *= 2
    return value


def largest(value):
    return jnp.max(jnp.abs(value)).astype(f32) + 1e-30


def on_device(
    tokens_in,
    cotangent,
    doc_lengths,
    in_proj,
    out_proj,
    norm_gain,
    gate_gain,
    conv_weight,
    conv_bias,
    delta_bias,
    decay_log,
    skip_scale,
    in_first,
    in_second,
    out_first,
    out_second,
    small_first,
    small_second,
):
    count = tokens_in.shape[0]
    spans = count // SPAN
    ctx = lax.axis_size("ctx")
    begin = lax.axis_index("ctx") * count
    lengths = doc_lengths[0]
    small_slice = on_small_slice()

    whole_conv, whole_gate, whole_out = gather_rows(
        in_proj[:, DI:].astype(bf16), in_proj[:, :DI].astype(bf16), out_proj.astype(bf16)
    )
    inputs = tokens_in.astype(f32)
    scale = lax.rsqrt(jnp.mean(inputs * inputs, axis=-1, keepdims=True) + norm_eps)
    normed = (inputs * scale * norm_gain[None, :]).astype(bf16)

    mixed = mm(normed, whole_conv)
    edge = lax.ppermute(mixed[count - 8 :, :CONVD], "ctx", [(i, i + 1) for i in range(ctx - 1)])
    edge = jnp.where(jnp.arange(8)[:, None] >= 8 - (CONV - 1), edge, 0.0)

    place = jnp.concatenate([begin[None].astype(jnp.int32), lengths.astype(jnp.int32)])
    params = padded(delta_bias, -jnp.exp(decay_log))
    (
        steps,
        decay,
        reach,
        rows,
        factor,
        start,
        inside,
        outside,
        mask,
        mask_turned,
    ) = prepare_call(spans, place, mixed, params)
    taps = jnp.concatenate([conv_weight.T, conv_bias[None], jnp.zeros((3, CONVD), f32)], axis=0)

    inner, local, states, keys, queries = forward_call(
        spans, mixed, edge, taps, inside, outside, steps, decay, rows, factor, mask
    )
    total_lanes = jnp.repeat(start[spans, :NH], HD)[None]
    state_in = pass_on(states[spans - 1], total_lanes, "ctx", False, f32)
    gate = mm(normed, whole_gate)
    mixer_back = jnp.einsum("td,kd->tk", cotangent, whole_out, preferred_element_type=f32)
    mixer_low, mixer_grad, gate_grad, gate_gain_grad, dots, summary, gate_most_rows = norm_call(
        local,
        inner,
        gate,
        mixer_back,
        queries,
        state_in,
        reach,
        spread_matrix(),
        jnp.repeat(skip_scale, HD)[None] + jnp.zeros((8, 1), f32),
        gate_gain[None] + jnp.zeros((8, 1), f32),
    )
    state_back = pass_on(summary, total_lanes, "ctx", True, bf16)

    out_bound = count * 6.0 * (DI**0.5 * 1.01) * largest(gate_gain)
    product_bound = count * (D**0.5 * 1.01) * largest(norm_gain)
    x, y, z, core = coordinates()
    if small_slice:
        out_part = summed_on_chip(mixer_low, cotangent, out_bound)
        out_kept, out_sent = to_send(out_part, x, 1)
        gate_most = largest_anywhere(gate_most_rows, gate_most_rows, 1)
        gate_part = summed_on_chip(normed, gate_grad, product_bound * gate_most)
        gate_kept, gate_sent = to_send(by_owner(gate_part), y, 1)
        mixer_grad, out_sent, gate_sent = lax.optimization_barrier(
            (mixer_grad, out_sent, gate_sent)
        )
        out_got = swapped(out_sent, *ACROSS_X)
        gate_got = swapped(gate_sent, *ACROSS_Y)
    else:
        out_rows = owned_rows(row_products(mixer_low, cotangent))
        gate_rows = owned_rows(row_products(normed, gate_grad))

    first_pairs = PAIRS // 2
    skip = padded(skip_scale)
    shared = lambda back: (
        mixed,
        edge,
        taps,
        inside,
        outside,
        keys,
        queries,
        back,
        steps,
        decay,
        rows,
        factor,
        start,
        mask_turned,
        states,
        state_in,
        state_back,
        skip,
    )
    following = segment_of(lengths, begin + count + jnp.arange(CONV, dtype=jnp.int32))
    own_last = segment_of(lengths, begin + count - CONV + jnp.arange(CONV, dtype=jnp.int32))

    def with_edge(grad, top, tail, at):
        next_top = lax.ppermute(top, "ctx", [(i + 1, i) for i in range(ctx - 1)])
        width = tail.shape[1]
        for j in range(1, CONV):
            joined = (following[:j] == own_last[CONV - j :]).astype(f32)
            more = joined[:, None] * next_top[:j] * taps[3 - j : 4 - j, at : at + width]
            tail = tail + jnp.pad(more, ((8 - j, 0), (0, 0)))
        return lax.dynamic_update_slice(grad, tail.astype(bf16), (count - 8, 0)), tail

    first_grad, top, tail, first_taps_grad, most, *sums = backward_call(
        spans, 0, first_pairs, first_pairs, shared(mixer_grad)
    )
    if small_slice:
        top, tail, most, first_grad, out_got, gate_got = lax.optimization_barrier(
            (top, tail, most, first_grad, out_got, gate_got)
        )
    first_grad, tail = with_edge(first_grad, top, tail, 0)
    if small_slice:
        out_kept, out_sent = to_send(by_owner(joined_with(out_kept, out_got)), y, 1)
        gate_kept, gate_sent = along_z(joined_with(gate_kept, gate_got))
        first_most = largest_anywhere(most, tail, 2)
        first_part = summed_on_chip(normed, first_grad, product_bound * first_most)
        first_kept, first_sent = to_send(by_owner(first_part), y, 1)
        mixer_grad, out_sent, gate_sent, first_sent = lax.optimization_barrier(
            (mixer_grad, out_sent, gate_sent, first_sent)
        )
        out_got = swapped(out_sent, *ACROSS_Y)
        gate_got = [swapped(s, *way) for s, way in zip(gate_sent, ACROSS_Z)]
        first_got = swapped(first_sent, *ACROSS_Y)
    second_grad, top, tail, second_taps_grad, most, *sums = backward_call(
        spans,
        first_pairs,
        PAIRS - first_pairs,
        16,
        shared(mixer_grad),
        (dots, mixed, params, sums),
    )
    if small_slice:
        top, tail, most, second_grad, sums, out_got, gate_got, first_got = (
            lax.optimization_barrier(
                (top, tail, most, second_grad, sums, out_got, gate_got, first_got)
            )
        )
    second_grad, tail = with_edge(second_grad, top, tail, first_pairs * LANES)
    if small_slice:
        out_kept, out_sent = along_z(joined_with(out_kept, out_got))
        first_kept, first_sent = along_z(joined_with(first_kept, first_got))
        out_got = [swapped(s, *way) for s, way in zip(out_sent, ACROSS_Z)]
        first_got = [swapped(s, *way) for s, way in zip(first_sent, ACROSS_Z)]
        most = jnp.maximum(most, jnp.max(sums[5][3]))
        second_most = largest_anywhere(most, tail, 3)
        second_part = summed_on_chip(normed, second_grad, product_bound * second_most)
        second_kept, second_sent = to_send(by_owner(second_part), y, 1)
        second_sent, out_got, first_got, gate_got, gate_grad, mixer_low = (
            lax.optimization_barrier(
                (second_sent, out_got, first_got, gate_got, gate_grad, mixer_low)
            )
        )
        second_got = swapped(second_sent, *ACROSS_Y)
    else:
        first_rows = owned_rows(row_products(normed, first_grad))
        second_rows = owned_rows(row_products(normed, second_grad))
    split_at = first_pairs * LANES
    second_width = CONVD + NH - split_at
    back_through = lambda grad, whole: jnp.einsum(
        "tk,dk->td", grad, whole, preferred_element_type=f32
    )
    block_out = (inputs + mm(mixer_low, whole_out)).astype(bf16)
    normed_grad = back_through(gate_grad, whole_gate)
    if small_slice:
        second_got, block_out, normed_grad, first_grad, second_grad = lax.optimization_barrier(
            (second_got, block_out, normed_grad, first_grad, second_grad)
        )
        second_kept, second_sent = along_z(joined_with(second_kept, second_got))
        second_got = [swapped(s, *way) for s, way in zip(second_sent, ACROSS_Z)]
        gate_rows = across_x(of_owner(gate_kept, gate_got))
        out_half = both_halves(of_owner(out_kept, out_got).value, ACROSS_X, x)
        out_rows = both_halves(out_half, CORE, core)
        first_rows = across_x(of_owner(first_kept, first_got))
    normed_grad = (
        normed_grad
        + back_through(first_grad, whole_conv[:, :split_at])
        + back_through(second_grad[:, :second_width], whole_conv[:, split_at:])
    )
    if small_slice:
        second_got, normed_grad = lax.optimization_barrier((second_got, normed_grad))
        second_rows = across_x(of_owner(second_kept, second_got))
    in_grad = jnp.concatenate([gate_rows, first_rows, second_rows[:, :second_width]], axis=1)

    unit = inputs * scale
    norm_gain_grad = jnp.sum(normed_grad * unit, axis=0)
    unit_grad = normed_grad * norm_gain[None, :]
    input_grad = cotangent.astype(f32) + scale * (
        unit_grad - unit * jnp.mean(unit_grad * unit, axis=-1, keepdims=True)
    )
    taps_grad = jnp.concatenate([first_taps_grad, second_taps_grad], axis=1)
    other_grads = sum_everywhere(
        jnp.concatenate(
            [
                gate_gain_grad[0],
                taps_grad[:CONV].T.reshape(-1),
                taps_grad[4],
                sums[5][0, :NH],
                sums[5][1, :NH],
                sums[5][2, :NH],
            ]
        ),
        ("fsdp", "ctx"),
    )
    small_grad = jnp.concatenate([sum_everywhere(norm_gain_grad, ("ctx", "fsdp")), other_grads])
    small_param = jnp.concatenate(
        [
            norm_gain,
            gate_gain,
            conv_weight.reshape(-1),
            conv_bias,
            delta_bias,
            decay_log,
            skip_scale,
        ]
    )
    small_new, small_first_new, small_second_new = adamw_update(
        small_param, small_grad, small_first, small_second, 0.0
    )
    in_new, in_first_new, in_second_new = adamw_update(
        in_proj, in_grad, in_first, in_second, weight_decay
    )
    out_new, out_first_new, out_second_new = adamw_update(
        out_proj, out_rows, out_first, out_second, weight_decay
    )
    return (
        block_out,
        input_grad,
        in_new,
        in_first_new,
        in_second_new,
        out_new,
        out_first_new,
        out_second_new,
        small_new,
        small_first_new,
        small_second_new,
    )


def solution(mesh):
    placed = (
        P(("fsdp", "ctx"), None),
        P(("fsdp", "ctx"), None),
        P("fsdp", None),
        P("fsdp", None),
        P("fsdp", None),
        P(),
        P(),
        P(),
        P(),
        P(),
        P(),
        P(),
        P("fsdp", None),
        P("fsdp", None),
        P("fsdp", None),
        P("fsdp", None),
        P(),
        P(),
    )
    return jax.shard_map(
        on_device,
        mesh=mesh,
        in_specs=placed,
        out_specs=(
            P(("fsdp", "ctx"), None),
            P(("fsdp", "ctx"), None),
            P("fsdp", None),
            P("fsdp", None),
            P("fsdp", None),
            P("fsdp", None),
            P("fsdp", None),
            P("fsdp", None),
            P(),
            P(),
            P(),
        ),
        check_vma=False,
    )
```

```python
import functools

import jax
import jax.numpy as jnp
from jax import lax
from jax.experimental import pallas as pl
from jax.experimental.pallas import tpu as pltpu
from jax.sharding import PartitionSpec as P

D = 1536
DI = 3072
NH = 48
HD = 64
DS = 128
CONV = 4
SPAN = 256
STEP = 5
CONVD = 3328
LANES = 128
PAIRS = DI // LANES
HALF = SPAN // 2
NORM_ROWS = 128
NORM_COLS = 512
MASKED = -1e30

highest = lax.Precision.HIGHEST
norm_eps = 1e-05
beta_one = 0.9
beta_two = 0.95
adam_eps = 1e-08
learn_rate = 0.05
weight_decay = 0.1
f32 = jnp.float32
bf16 = jnp.bfloat16
VMEM_LIMIT = 56 * 1024 * 1024


def split(value):
    high = value.astype(bf16)
    return high, (value - high.astype(f32)).astype(bf16)


def mm(a, b):
    return jnp.dot(a, b, preferred_element_type=f32)


def mm_nt(a, b):
    return lax.dot_general(a, b, (((1,), (1,)), ((), ())), preferred_element_type=f32)


def sigmoid(v):
    return 1.0 / (1.0 + jnp.exp(-v))


def conv_shifts(block, edge, inside, outside):
    shifted = []
    for j in range(1, CONV):
        body = inside[j - 1] * pltpu.roll(block, j, 0)
        head = body[:8] + outside[j - 1] * pltpu.roll(edge, j, 0)
        shifted.append(jnp.concatenate([head, body[8:]], axis=0))
    return shifted


def conv_pre(block, shifted, taps):
    total = taps[4:5] + taps[3:4] * block
    for j in range(1, CONV):
        total = total + taps[3 - j : 4 - j] * shifted[j - 1]
    return total


def pair_columns(packed, pair):
    turned = pltpu.roll(packed, lax.rem(LANES - 2 * pair, LANES), 1)
    lane = lax.broadcasted_iota(jnp.int32, packed.shape, 1)
    first = jnp.where(lane < HD, turned[:, 0:1], turned[:, 1:2])
    second = jnp.where(lane < HD, turned[:, 64:65], turned[:, 65:66])
    return turned, first, second


def pair_rows(rows, pair):
    turned = pltpu.roll(rows, lax.rem(LANES - 2 * pair, LANES), 1)
    lane = lax.broadcasted_iota(jnp.int32, rows.shape, 1)
    return jnp.where(lane < HD, turned[:, 0:1], turned[:, 1:2])


def head_row(block, head):
    sublane = lax.broadcasted_iota(jnp.int32, block.shape, 0)
    return jnp.sum(jnp.where(sublane == lax.rem(head, 8), block, 0.0), axis=0, keepdims=True)


def split_three(value):
    high, low = split(value)
    return high, low, (value - high.astype(f32) - low.astype(f32)).astype(bf16)


def prepare_kernel(
    spans,
    place_ref,
    raw_ref,
    params_ref,
    steps_out,
    decay_out,
    reach_out,
    turned_out,
    factor_out,
    start_out,
    inside_out,
    outside_out,
    mask_out,
    mask_turned_out,
):
    count = spans * SPAN
    begin = place_ref[0]
    ends = []
    for d in range(place_ref.shape[0] - 1):
        ends.append(place_ref[d + 1] + (ends[-1] if ends else 0))

    def segment(position):
        total = (position >= ends[0]).astype(jnp.int32)
        for end in ends[1:]:
            total = total + (position >= end).astype(jnp.int32)
        return total

    row = lax.broadcasted_iota(jnp.int32, (count, LANES), 0)
    here = segment(row + begin)
    for j in range(1, CONV):
        same = here == segment(row + (begin - j))
        inside_out[j - 1] = jnp.where(jnp.logical_and(same, row >= j), 1.0, 0.0)
        outside_out[j - 1] = jnp.where(jnp.logical_and(same, row < j), 1.0, 0.0)[:8]
    lane = lax.broadcasted_iota(jnp.int32, (count, LANES), 1)
    raw = jnp.where(lane < NH, raw_ref[...], 0.0) + params_ref[0:1]
    steps = jnp.where(lane < NH, jnp.maximum(raw, 0.0) + jnp.log1p(jnp.exp(-jnp.abs(raw))), 0.0)
    log_decay = params_ref[1:2] * steps
    tall = lax.broadcasted_iota(jnp.int32, (SPAN, SPAN), 0)
    wide = lax.broadcasted_iota(jnp.int32, (SPAN, SPAN), 1)
    lower = (tall >= wide).astype(bf16)
    span_lane = lax.broadcasted_iota(jnp.int32, (SPAN, LANES), 1)
    before = jnp.zeros((1, LANES), f32)
    start = jnp.ones((1, LANES), f32)
    starts, factors = [start], []
    reached = here == segment(begin - 1)
    for k in range(spans):
        at = k * SPAN
        rows = pl.ds(at, SPAN)
        parts = split_three(log_decay[at : at + SPAN])
        sums = mm(lower, jnp.concatenate(parts, axis=1))
        cumul = sums[:, :LANES] + sums[:, LANES : 2 * LANES] + sums[:, 2 * LANES :]
        last = cumul[SPAN - 1 : SPAN]
        span_here = here[at : at + SPAN]
        first = begin + at
        enters = jnp.logical_and(span_here == segment(first - 1), span_here >= 0)
        enter = jnp.where(jnp.logical_and(enters, first > 0), jnp.exp(cumul), 0.0)
        leave = jnp.where(
            span_here == segment(first + SPAN - 1), jnp.exp(last - cumul), 0.0
        )
        reach = jnp.where(
            jnp.logical_and(reached[at : at + SPAN], begin > 0), jnp.exp(cumul + before), 0.0
        )
        known = span_lane < NH
        steps_out[rows, :] = jnp.where(known, cumul, 0.0) + pltpu.roll(
            steps[at : at + SPAN], LANES // 2, 1
        )
        decay_out[rows, :] = jnp.where(known, enter, 0.0) + pltpu.roll(
            jnp.where(known, leave, 0.0), LANES // 2, 1
        )
        reach_out[rows, :] = jnp.where(known, reach, 0.0)
        turned_out[:, rows] = cumul.T[:NH]
        factors.append(enter[SPAN - 1 : SPAN])
        start = start * factors[-1]
        starts.append(start)
        before = before + last
        together = segment(tall + first) == segment(wide + first)
        mask_out[k] = jnp.where(jnp.logical_and(together, tall >= wide), 0.0, MASKED)
        mask_turned_out[k] = jnp.where(jnp.logical_and(together, tall <= wide), 0.0, MASKED)
    rest = lambda rows: jnp.concatenate(
        rows + [jnp.zeros((8 - len(rows), LANES), f32)], axis=0
    )
    factor_out[...] = rest(factors)
    start_out[...] = rest(starts)


def prepare_call(spans, place, mixed, params):
    count = spans * SPAN
    whole = lambda *s: pl.BlockSpec(s, lambda i: (0,) * len(s))
    shapes = [
        (count, LANES),
        (count, LANES),
        (count, LANES),
        (NH, count),
        (8, LANES),
        (8, LANES),
        (CONV - 1, count, LANES),
        (CONV - 1, 8, LANES),
        (spans, SPAN, SPAN),
        (spans, SPAN, SPAN),
    ]
    return pl.pallas_call(
        functools.partial(prepare_kernel, spans),
        grid=(1,),
        in_specs=[
            pl.BlockSpec(memory_space=pltpu.SMEM),
            pl.BlockSpec((count, LANES), lambda i: (0, CONVD // LANES)),
            whole(8, LANES),
        ],
        out_specs=[whole(*s) for s in shapes],
        out_shape=[jax.ShapeDtypeStruct(s, f32) for s in shapes],
        compiler_params=pltpu.CompilerParams(vmem_limit_bytes=VMEM_LIMIT),
        name="steps_and_masks",
    )(place, mixed, params)


MESH = pl.DeviceIdType.MESH
Z = 4
Y = 2


class Gathering:
    def __init__(self, blocks, wholes, sems):
        self.arrays = list(zip(blocks, wholes))
        self.own, self.up_sem, self.down_sem, self.z_sem, *sems = sems
        self.y_sent, self.y_sem, self.x_sent, self.x_sem, self.core_sent, self.core_sem = sems
        self.f, self.ctx = lax.axis_index("fsdp"), lax.axis_index("ctx")
        self.z, self.y = self.f // Y, lax.rem(self.f, Y)
        self.x, self.c = self.ctx // 2, lax.rem(self.ctx, 2)
        self.at_y = (self.z * Y + 1 - self.y, self.ctx)
        self.at_x = (self.f, (1 - self.x) * 2 + self.c)
        self.at_core = (self.f, self.x * 2 + 1 - self.c)

    def at_z(self, other):
        return other * Y + self.y, self.ctx

    def rows_of(self, n):
        return self.arrays[n][0].shape[0]

    def third(self, n):
        return self.rows_of(n) // 6

    def gathered(self, n):
        return self.c * (self.rows_of(n) // 2) + self.x * self.third(n), 2 * self.third(n)

    def move(self, n, block, row, size, sent, landed, partner, own=False):
        here = self.arrays[n][1].at[pl.ds(block * self.rows_of(n) + row, size)]
        source = self.arrays[n][0].at[pl.ds(row, size)] if own else here
        return pltpu.make_async_remote_copy(
            src_ref=source,
            dst_ref=here,
            send_sem=sent,
            recv_sem=landed,
            device_id=partner,
            device_id_type=MESH,
        )

    def up(self, n, zb, own=False):
        sems = self.up_sem.at[n, zb], self.z_sem.at[n, zb]
        block = zb * Y + self.y
        return self.move(n, block, *self.gathered(n), *sems, self.at_z(self.z + 1), own)

    def down(self, n, zb, own=False):
        sems = self.down_sem.at[n, zb], self.z_sem.at[n, zb]
        block = zb * Y + self.y
        return self.move(n, block, *self.gathered(n), *sems, self.at_z(self.z - 1), own)

    def along_y(self, n, zb, yb, own=False):
        sems = self.y_sent.at[n, zb], self.y_sem.at[n, zb]
        return self.move(n, zb * Y + yb, *self.gathered(n), *sems, self.at_y, own)

    def along_x(self, n, block, sender_x):
        row = self.c * (self.rows_of(n) // 2) + 2 * self.third(n) * sender_x
        sems = self.x_sent.at[n, block], self.x_sem.at[n, block]
        return self.move(n, block, row, self.third(n), *sems, self.at_x)

    def core_first(self, n, block, core):
        row = core * (self.rows_of(n) // 2) + self.x * self.third(n)
        sems = self.core_sent.at[n, block, 0], self.core_sem.at[n, block, 0]
        return self.move(n, block, row, 2 * self.third(n), *sems, self.at_core)

    def core_second(self, n, block, core):
        row = core * (self.rows_of(n) // 2) + 2 * self.third(n) * (1 - self.x)
        sems = self.core_sent.at[n, block, 1], self.core_sem.at[n, block, 1]
        return self.move(n, block, row, self.third(n), *sems, self.at_core)

    def own_copy(self, n):
        rows = self.rows_of(n)
        block, whole = self.arrays[n]
        return pltpu.make_async_copy(block, whole.at[pl.ds(self.f * rows, rows)], self.own.at[n])

    def begin(self):
        barrier = pltpu.get_barrier_semaphore()
        signal = functools.partial(
            pl.semaphore_signal, barrier, inc=1, device_id_type=MESH
        )
        for partner in (self.at_y, self.at_x, self.at_core):
            signal(device_id=partner)

        @pl.when(self.z > 0)
        def _():
            signal(device_id=self.at_z(self.z - 1))

        @pl.when(self.z < Z - 1)
        def _():
            signal(device_id=self.at_z(self.z + 1))

        middle = jnp.logical_and(self.z > 0, self.z < Z - 1).astype(jnp.int32)
        pl.semaphore_wait(barrier, 4 + middle)
        for n in range(len(self.arrays)):
            self.own_copy(n).start()

            @pl.when(self.z < Z - 1)
            def _():
                self.up(n, self.z, True).start()

            @pl.when(self.z > 0)
            def _():
                self.down(n, self.z, True).start()

            self.along_y(n, self.z, self.y, True).start()

    def spread(self, n, block):
        self.along_x(n, block, self.x).start()
        self.core_first(n, block, self.c).start()

    def from_z(self, n, distance):
        for way in (1, -1):
            zb = self.z - way * distance

            @pl.when(jnp.logical_and(zb >= 0, zb < Z))
            def _():
                self.up(n, zb).wait_recv()
                if way == 1:

                    @pl.when(self.z < Z - 1)
                    def _():
                        self.up(n, zb).start()
                else:

                    @pl.when(self.z > 0)
                    def _():
                        self.down(n, zb).start()

                self.along_y(n, zb, self.y).start()
                self.spread(n, zb * Y + self.y)

    def from_y(self, n, distance):
        for way in (1, -1) if distance else (1,):
            zb = self.z - way * distance

            @pl.when(jnp.logical_and(zb >= 0, zb < Z))
            def _():
                self.along_y(n, zb, 1 - self.y).wait_recv()
                self.spread(n, zb * Y + 1 - self.y)

    def each_block(self, do):
        def at(zb, yb):
            @pl.when(jnp.logical_and(zb >= 0, zb < Z))
            def _():
                for n in range(len(self.arrays)):
                    do(n, zb * Y + yb)

        for distance in range(Z):
            for way in (1, -1) if distance else (1,):
                if distance:
                    at(self.z - way * distance, self.y)
                at(self.z - way * distance, 1 - self.y)

    def end(self):
        def come_along_x(n, block):
            self.along_x(n, block, 1 - self.x).wait_recv()
            self.core_second(n, block, self.c).start()

        def finish(n, block):
            self.core_first(n, block, 1 - self.c).wait_recv()
            self.core_second(n, block, 1 - self.c).wait_recv()
            self.along_x(n, block, self.x).wait_send()
            self.core_first(n, block, self.c).wait_send()
            self.core_second(n, block, self.c).wait_send()

        self.each_block(come_along_x)
        self.each_block(finish)
        for n in range(len(self.arrays)):
            self.own_copy(n).wait()
            for zb in range(Z):
                self.along_y(n, zb, self.y).wait_send()

                @pl.when(jnp.logical_and(self.z < Z - 1, zb <= self.z))
                def _():
                    self.up(n, zb).wait_send()

                @pl.when(jnp.logical_and(self.z > 0, zb >= self.z))
                def _():
                    self.down(n, zb).wait_send()


def gathering_semaphores(count):
    dma = lambda *s: pltpu.SemaphoreType.DMA((count,) + s)
    size = Z * Y
    return [dma()] + [dma(Z)] * 5 + [dma(size)] * 2 + [dma(size, 2)] * 2


def whole_shapes(blocks):
    return [jax.ShapeDtypeStruct((b.shape[0] * Z * Y, b.shape[1]), b.dtype) for b in blocks]


def gather_kernel(count, *refs):
    gathering = Gathering(refs[:count], refs[count : 2 * count], refs[2 * count :])
    gathering.begin()
    for distance in range(Z):
        for n in range(count):
            if distance:
                gathering.from_z(n, distance)
                gathering.from_y(n, distance - 1)
    for n in range(count):
        gathering.from_y(n, Z - 1)
    gathering.end()


def gather_call(*blocks):
    count = len(blocks)
    return pl.pallas_call(
        functools.partial(gather_kernel, count),
        in_specs=[pl.BlockSpec(memory_space=pl.ANY)] * count,
        out_specs=[pl.BlockSpec(memory_space=pl.ANY)] * count,
        out_shape=whole_shapes(blocks),
        scratch_shapes=gathering_semaphores(count),
        compiler_params=pltpu.CompilerParams(collective_id=0, has_side_effects=True),
        name="gather_rows",
    )(*blocks)


Z_STEPS = {4: (0, 1), 7: (1, 1), 11: (0, 2), 14: (1, 2), 18: (0, 3), 21: (1, 3)}
Y_STEPS = {5: (0, 0), 8: (1, 0), 12: (0, 1), 15: (1, 1), 19: (0, 2), 22: (1, 2)}


def forward_kernel(
    spans,
    blocks,
    block_ref,
    key_ref,
    query_ref,
    edge_ref,
    key_edge_ref,
    query_edge_ref,
    taps_ref,
    key_taps_ref,
    query_taps_ref,
    inside_ref,
    outside_ref,
    steps_ref,
    decay_ref,
    rows_ref,
    factor_ref,
    mask_ref,
    *refs,
):
    block_refs, refs = refs[:blocks], refs[blocks:]
    inner_out, local_out, state_out, key_out, query_out, *refs = refs
    whole_refs, refs = refs[:blocks], refs[blocks:]
    scores, key_turned, query_both, *sems = refs
    pair = pl.program_id(0)
    if blocks:
        gathering = Gathering(block_refs, whole_refs, sems)
        pl.when(pair == 0)(gathering.begin)
        for at, what in Z_STEPS.items():
            pl.when(pair == at)(functools.partial(gathering.from_z, *what))
        for at, what in Y_STEPS.items():
            pl.when(pair == at)(functools.partial(gathering.from_y, *what))

    @pl.when(pair == 0)
    def _():
        for src, edge, taps, out in (
            (key_ref, key_edge_ref, key_taps_ref, key_out),
            (query_ref, query_edge_ref, query_taps_ref, query_out),
        ):
            pre = conv_pre(
                src[...], conv_shifts(src[...], edge[...], inside_ref, outside_ref), taps[...]
            )
            out[...] = pre * sigmoid(pre)
        for k in range(spans):
            rows = pl.ds(k * SPAN, SPAN)
            keys, queries = key_out[rows, :], query_out[rows, :]
            kh, kl = split(keys)
            qh, ql = split(queries)
            query_both[rows, :] = jnp.concatenate([qh, ql], axis=1)
            scores[k] = mm_nt(
                jnp.concatenate([qh, ql], axis=1), jnp.concatenate([kh, kh], axis=1)
            ) + mm_nt(qh, kl)
            th, tl = split(keys.T)
            key_turned[k, 0] = th
            key_turned[k, 1] = tl

    block = block_ref[...]
    pre = conv_pre(
        block, conv_shifts(block, edge_ref[...], inside_ref, outside_ref), taps_ref[...]
    )
    inner = pre * sigmoid(pre)
    inner_out[...] = inner
    turned, unused, steps = pair_columns(steps_ref[...], pair)
    unused, enter, leave = pair_columns(decay_ref[...], pair)
    scaled = steps * inner
    leaving = leave * scaled
    lane = lax.broadcasted_iota(jnp.int32, (HALF, LANES), 1)
    head_rows = [head_row(rows_ref[...], 2 * pair + a) for a in range(2)]
    factor = pair_rows(factor_ref[...], pair)
    state = None
    for k in range(spans):
        at = k * SPAN
        sh, sl = split(scaled[at : at + SPAN])
        both = jnp.concatenate([sh, sl], axis=1)
        parts = []
        for half in range(2):
            width = HALF * (half + 1)
            here, there = pl.ds(half * HALF, HALF), pl.ds(0, width)
            both_heads = []
            for a in range(2):
                row = head_rows[a][:, at : at + width]
                column = turned[at + half * HALF : at + (half + 1) * HALF, a : a + 1]
                decay = jnp.exp(jnp.minimum(column - row, mask_ref[k, here, there]))
                both_heads.append(decay * scores[k, here, there])
            wh, wl = split(jnp.concatenate(both_heads, axis=0))
            wide = mm(wh, both[:width])
            wide = wide[:, :LANES] + wide[:, LANES:] + mm(wl, sh[:width])
            parts.append(jnp.where(lane < HD, wide[:HALF], wide[HALF:]))
        local = jnp.concatenate(parts, axis=0)
        ph, pw = split(leaving[at : at + SPAN])
        fresh = mm(key_turned[k, 0], jnp.concatenate([ph, pw], axis=1))
        fresh = fresh[:, :LANES] + fresh[:, LANES:] + mm(key_turned[k, 1], ph)
        if state is None:
            state = fresh
        else:
            th, tl = split(state)
            q2 = query_both[pl.ds(at, SPAN), :]
            carried = mm(q2, jnp.concatenate([th, th], axis=0)) + mm(q2[:, :DS], tl)
            local = local + enter[at : at + SPAN] * carried
            state = factor[k : k + 1] * state + fresh
        state_out[k] = state
        local_out[pl.ds(at, SPAN), :] = local
    if blocks:

        @pl.when(pair == PAIRS - 1)
        def _():
            for n in range(blocks):
                gathering.from_y(n, Z - 1)
            gathering.end()


def forward_call(
    spans, mixed, edge, taps, inside, outside, steps, decay, rows, factor, mask, blocks
):
    count = spans * SPAN
    at_pair = lambda n: pl.BlockSpec((n, LANES), lambda i: (0, i))
    at_key = lambda n: pl.BlockSpec((n, LANES), lambda i: (0, PAIRS))
    at_query = lambda n: pl.BlockSpec((n, LANES), lambda i: (0, PAIRS + 1))
    whole = lambda *s: pl.BlockSpec(s, lambda i: (0,) * len(s))
    remote = dict(collective_id=5, has_side_effects=True) if blocks else {}
    return pl.pallas_call(
        functools.partial(forward_kernel, spans, len(blocks)),
        grid=(PAIRS,),
        in_specs=[
            at_pair(count),
            at_key(count),
            at_query(count),
            at_pair(8),
            at_key(8),
            at_query(8),
            at_pair(8),
            at_key(8),
            at_query(8),
            whole(3, count, LANES),
            whole(3, 8, LANES),
            whole(count, LANES),
            whole(count, LANES),
            pl.BlockSpec((8, count), lambda i: (i // 4, 0)),
            whole(8, LANES),
            whole(spans, SPAN, SPAN),
        ]
        + [pl.BlockSpec(memory_space=pl.ANY)] * len(blocks),
        out_specs=[
            at_pair(count),
            at_pair(count),
            pl.BlockSpec((spans, DS, LANES), lambda i: (0, 0, i)),
            whole(count, LANES),
            whole(count, LANES),
        ]
        + [pl.BlockSpec(memory_space=pl.ANY)] * len(blocks),
        out_shape=[
            jax.ShapeDtypeStruct((count, DI), f32),
            jax.ShapeDtypeStruct((count, DI), f32),
            jax.ShapeDtypeStruct((spans, DS, DI), f32),
            jax.ShapeDtypeStruct((count, DS), f32),
            jax.ShapeDtypeStruct((count, DS), f32),
        ]
        + whole_shapes(blocks),
        scratch_shapes=[
            pltpu.VMEM((spans, SPAN, SPAN), f32),
            pltpu.VMEM((spans, 2, DS, SPAN), bf16),
            pltpu.VMEM((count, 2 * DS), bf16),
        ]
        + (gathering_semaphores(len(blocks)) if blocks else []),
        compiler_params=pltpu.CompilerParams(vmem_limit_bytes=VMEM_LIMIT, **remote),
        cost_estimate=pl.CostEstimate(flops=1, bytes_accessed=1, transcendentals=0),
        name="recurrence_forward",
    )(
        mixed,
        mixed,
        mixed,
        edge,
        edge,
        edge,
        taps,
        taps,
        taps,
        inside,
        outside,
        steps,
        decay,
        rows,
        factor,
        mask,
        *blocks,
    )


def norm_kernel(
    local_ref,
    inner_ref,
    gate_ref,
    back_ref,
    query_ref,
    state_ref,
    reach_ref,
    spread_ref,
    skip_ref,
    gain_ref,
    out_ref,
    mixer_grad_ref,
    gate_grad_ref,
    gain_grad_ref,
    dots_ref,
    summary_ref,
    most_ref,
    mixed_y,
    state_both,
    reach_wide,
):
    step = pl.program_id(0)
    chunks = [pl.ds(c * NORM_COLS, NORM_COLS) for c in range(DI // NORM_COLS)]

    @pl.when(step == 0)
    def _():
        sh, sl = split(state_ref[...])
        state_both[0] = sh
        state_both[1] = sl
        gain_grad_ref[...] = jnp.zeros_like(gain_grad_ref)
        summary_ref[...] = jnp.zeros_like(summary_ref)
        most_ref[...] = jnp.zeros_like(most_ref)

    qh, ql = split(query_ref[...])
    query_both = jnp.concatenate([qh, ql], axis=1)
    rh, rl = split(reach_ref[...])
    reach_both = jnp.concatenate([rh, rl], axis=1)
    squares = jnp.zeros((NORM_ROWS, 1), f32)
    mixes = jnp.zeros((NORM_ROWS, 1), f32)
    for cols in chunks:
        sh, sl = state_both[0, :, cols], state_both[1, :, cols]
        spread = spread_ref[:, cols]
        reach = mm(reach_both, jnp.concatenate([spread, spread], axis=0))
        reach_wide[:, cols] = reach
        carried = mm(query_both, jnp.concatenate([sh, sh], axis=0)) + mm(qh, sl)
        y = local_ref[:, cols] + reach * carried
        mixed_y[:, cols] = y
        mixer = y + skip_ref[0:1, cols] * inner_ref[:, cols]
        gate = gate_ref[:, cols]
        gated = mixer * (gate * sigmoid(gate))
        squares = squares + jnp.sum(gated * gated, axis=1, keepdims=True)
        mixes = mixes + jnp.sum(
            gated * (back_ref[:, cols] * gain_ref[0:1, cols]), axis=1, keepdims=True
        )
    scale = lax.rsqrt(squares * (1.0 / DI) + norm_eps)
    pull = scale * mixes * (1.0 / DI)
    query_turned = query_ref[...].T
    th, tl = split(query_turned)
    dots = jnp.zeros((NORM_ROWS, LANES), f32)
    for cols in chunks:
        y = mixed_y[:, cols]
        mixer = y + skip_ref[0:1, cols] * inner_ref[:, cols]
        gate = gate_ref[:, cols]
        opened = sigmoid(gate)
        silu = gate * opened
        unit = mixer * silu * scale
        gain = gain_ref[0:1, cols]
        back = back_ref[:, cols]
        out_ref[:, cols] = (unit * gain).astype(bf16)
        gain_grad_ref[0:1, cols] += jnp.sum(back * unit, axis=0, keepdims=True)
        gated_grad = scale * (back * gain - unit * pull)
        mixer_grad = gated_grad * silu
        mixer_grad_ref[:, cols] = mixer_grad
        gate_grad = gated_grad * mixer * (opened * (1.0 + gate * (1.0 - opened)))
        gate_grad_ref[:, cols] = gate_grad.astype(bf16)
        most = jnp.max(jnp.abs(gate_grad).reshape(NORM_ROWS // 8, 8, NORM_COLS), axis=0)
        for c in range(NORM_COLS // LANES):
            most_ref[...] = jnp.maximum(most_ref[...], most[:, c * LANES : (c + 1) * LANES])
        dh, dl = split(mixer_grad * y)
        spread = spread_ref[:, cols]
        dots = dots + mm_nt(dh, spread) + mm_nt(dl, spread)
        mh, ml = split(reach_wide[:, cols] * mixer_grad)
        summary_ref[:, cols] += (
            mm(jnp.concatenate([th, tl], axis=1), jnp.concatenate([mh, mh], axis=0)) + mm(th, ml)
        )
    dots_ref[...] = dots


def norm_call(local, inner, gate, back, queries, state_in, reach, spread, skip, gain):
    count = local.shape[0]
    rows = lambda n: pl.BlockSpec((NORM_ROWS, n), lambda i: (i, 0))
    whole = lambda *s: pl.BlockSpec(s, lambda i: (0,) * len(s))
    return pl.pallas_call(
        norm_kernel,
        grid=(count // NORM_ROWS,),
        in_specs=[
            rows(DI),
            rows(DI),
            rows(DI),
            rows(DI),
            rows(DS),
            whole(DS, DI),
            rows(LANES),
            whole(LANES, DI),
            whole(8, DI),
            whole(8, DI),
        ],
        out_specs=[
            rows(DI),
            rows(DI),
            rows(DI),
            whole(8, DI),
            rows(LANES),
            whole(DS, DI),
            whole(8, LANES),
        ],
        out_shape=[
            jax.ShapeDtypeStruct((count, DI), bf16),
            jax.ShapeDtypeStruct((count, DI), f32),
            jax.ShapeDtypeStruct((count, DI), bf16),
            jax.ShapeDtypeStruct((8, DI), f32),
            jax.ShapeDtypeStruct((count, LANES), f32),
            jax.ShapeDtypeStruct((DS, DI), f32),
            jax.ShapeDtypeStruct((8, LANES), f32),
        ],
        scratch_shapes=[
            pltpu.VMEM((NORM_ROWS, DI), f32),
            pltpu.VMEM((2, DS, DI), bf16),
            pltpu.VMEM((NORM_ROWS, DI), f32),
        ],
        compiler_params=pltpu.CompilerParams(vmem_limit_bytes=VMEM_LIMIT),
        cost_estimate=pl.CostEstimate(flops=1, bytes_accessed=1, transcendentals=0),
        name="gated_norm",
    )(local, inner, gate, back, queries, state_in, reach, spread, skip, gain)


def backward_kernel(spans, first, pairs, last, *refs):
    (
        block_ref,
        edge_ref,
        taps_ref,
        inside_ref,
        outside_ref,
        keys_ref,
        queries_ref,
        back_ref,
        steps_ref,
        decay_ref,
        rows_ref,
        factor_ref,
        start_ref,
        mask_ref,
        states_ref,
        state_in_ref,
        state_back_ref,
        skip_ref,
        *refs,
    ) = refs
    if last:
        dots_ref, raw_ref, params_ref, *refs = refs
        old_scores_grad, old_key_grad, old_query_grad, old_steps, old_heads, *refs = refs
    grad_out, top_out, tail_out, taps_out, most_out, *refs = refs
    scores_grad, key_grad, query_grad, steps_out, heads_out, *refs = refs
    if last:
        sums_out, *refs = refs
    scores, key_both, query_both, query_turned = refs
    step = pl.program_id(0)
    pair = step + first
    lane = lax.broadcasted_iota(jnp.int32, (SPAN, LANES), 1)

    @pl.when(step == 0)
    def _():
        if last:
            key_grad[...] = old_key_grad[...]
            query_grad[...] = old_query_grad[...]
            scores_grad[...] = old_scores_grad[...]
            steps_out[...] = old_steps[...]
            heads_out[...] = old_heads[...]
        else:
            key_grad[...] = jnp.zeros_like(key_grad)
            query_grad[...] = jnp.zeros_like(query_grad)
            scores_grad[...] = jnp.zeros_like(scores_grad)
            steps_out[...] = jnp.zeros_like(steps_out)
            heads_out[...] = jnp.zeros_like(heads_out)
        for k in range(spans):
            rows = pl.ds(k * SPAN, SPAN)
            keys, queries = keys_ref[rows, :], queries_ref[rows, :]
            kh, kl = split(keys)
            qh, ql = split(queries)
            key_both[rows, :] = jnp.concatenate([kh, kl], axis=1)
            query_both[rows, :] = jnp.concatenate([qh, ql], axis=1)
            scores[k] = mm_nt(
                jnp.concatenate([kh, kl], axis=1), jnp.concatenate([qh, qh], axis=1)
            ) + mm_nt(kh, ql)
            th, tl = split(queries.T)
            query_turned[k, 0] = th
            query_turned[k, 1] = tl

    def conv_back(conved_grad, block, shifted, pre):
        opened = sigmoid(pre)
        pre_grad = conved_grad * (opened * (1.0 + pre * (1.0 - opened)))
        count = block.shape[0]
        taps = taps_ref[...]
        total = taps[3:4] * pre_grad
        sums = [None] * 8
        sums[3] = jnp.sum(pre_grad * block, axis=0, keepdims=True)
        sums[4] = jnp.sum(pre_grad, axis=0, keepdims=True)
        for j in range(1, CONV):
            total = total + taps[3 - j : 4 - j] * pltpu.roll(
                inside_ref[j - 1] * pre_grad, count - j, 0
            )
            sums[3 - j] = jnp.sum(pre_grad * shifted[j - 1], axis=0, keepdims=True)
        grad_out[...] = total.astype(bf16)
        tail_out[...] = total[count - 8 :]
        most_out[...] = jnp.max(jnp.abs(total).reshape(count // 8, 8, LANES), axis=0)
        top_out[...] = pre_grad[:8]
        return sums

    zero_row = jnp.zeros((1, LANES), f32)

    def of_conv():
        block = block_ref[...]
        shifted = conv_shifts(block, edge_ref[...], inside_ref, outside_ref)
        return block, shifted, conv_pre(block, shifted, taps_ref[...])

    @pl.when(step < pairs)
    def _():
        block, shifted, pre = of_conv()
        head_rows = [head_row(rows_ref[...], 2 * pair + a) for a in range(2)]
        factor = pair_rows(factor_ref[...], pair)
        start = pair_rows(start_ref[...], pair)
        skip = pair_rows(skip_ref[...], pair)
        inner = pre * sigmoid(pre)
        back = back_ref[...]
        turned, unused, steps = pair_columns(steps_ref[...], pair)
        unused, enter, leave = pair_columns(decay_ref[...], pair)
        scaled = steps * inner
        leaving = leave * scaled
        entering = enter * back
        state_in = state_in_ref[...]
        state_back = state_back_ref[...]
        scaled_grads = [None] * spans
        ends = [zero_row] * 8
        for k in reversed(range(spans)):
            at = k * SPAN
            rows = pl.ds(at, SPAN)
            bh, bl = split(back[at : at + SPAN])
            both = jnp.concatenate([bh, bl], axis=1)
            sh, sl = split(scaled[at : at + SPAN])
            zero = jnp.zeros((SPAN, LANES), bf16)
            sl_turned = pltpu.roll(sl.astype(f32), HD, 1).astype(bf16)
            bh_turned = pltpu.roll(bh.astype(f32), HD, 1).astype(bf16)
            lefts, rights = [], []
            for a in range(2):
                mine = (lane < HD) if a == 0 else (lane >= HD)
                of_mine = lambda one, other: jnp.where(mine, one, other)
                lefts.append(
                    jnp.concatenate([of_mine(sh, sl_turned), of_mine(sh, zero)], axis=1)
                )
                rights.append(
                    jnp.concatenate([of_mine(bh, bh_turned), of_mine(bl, zero)], axis=1)
                )
            parts = []
            for half in range(2):
                low = half * HALF
                width = SPAN - low
                here = pl.ds(low, HALF)
                there = pl.ds(low, width)
                both_heads = []
                grads = None
                for a in range(2):
                    row = head_rows[a][:, at + low : at + low + width]
                    column = turned[at + low : at + low + HALF, a : a + 1]
                    decay = jnp.exp(jnp.minimum(row - column, mask_ref[k, here, there]))
                    both_heads.append(decay * scores[k, here, there])
                    grad = decay * mm_nt(lefts[a][low : low + HALF], rights[a][low:])
                    grads = grad if grads is None else grads + grad
                scores_grad[k, here, there] += grads
                wh, wl = split(jnp.concatenate(both_heads, axis=0))
                wide = mm(wh, both[low:])
                wide = wide[:, :LANES] + wide[:, LANES:] + mm(wl, bh[low:])
                parts.append(jnp.where(lane[:HALF] < HD, wide[:HALF], wide[HALF:]))
            scaled_grad = jnp.concatenate(parts, axis=0)
            gh, gl = split(state_back)
            k2 = key_both[rows, :]
            scaled_grad = scaled_grad + leave[at : at + SPAN] * (
                mm(k2, jnp.concatenate([gh, gh], axis=0)) + mm(k2[:, :DS], gl)
            )
            scaled_grads[k] = scaled_grad
            lh, ll = split(leaving[at : at + SPAN])
            key_grad[rows, :] += mm_nt(
                jnp.concatenate([lh, ll], axis=1), jnp.concatenate([gh, gh], axis=1)
            ) + mm_nt(lh, gl)
            after = states_ref[k] + start[k + 1 : k + 2] * state_in
            ends[k] = jnp.sum(state_back * after, axis=0, keepdims=True)
            before = start[k : k + 1] * state_in
            if k > 0:
                before = before + states_ref[k - 1]
            th, tl = split(before)
            eh, el = split(entering[at : at + SPAN])
            query_grad[rows, :] += mm_nt(
                jnp.concatenate([eh, el], axis=1), jnp.concatenate([th, th], axis=1)
            ) + mm_nt(eh, tl)
            if k > 0:
                more = mm(query_turned[k, 0], jnp.concatenate([eh, el], axis=1))
                state_back = (
                    factor[k : k + 1] * state_back
                    + more[:, :LANES]
                    + more[:, LANES:]
                    + mm(query_turned[k, 1], eh)
                )
        scaled_grad = jnp.concatenate(scaled_grads, axis=0)
        target = lax.broadcasted_iota(jnp.int32, (LANES, LANES), 1)
        source = lax.broadcasted_iota(jnp.int32, (LANES, LANES), 0)
        place = (target == 2 * pair + source // HD).astype(bf16)
        dh, dl = split(inner * scaled_grad)
        steps_out[...] += mm(dh, place) + mm(dl, place)
        sums = conv_back(steps * scaled_grad + skip[0:1] * back, block, shifted, pre)
        ends[4] = jnp.sum(back * inner, axis=0, keepdims=True)
        taps_out[...] = jnp.concatenate([zero_row if s is None else s for s in sums], axis=0)
        eh, el, ew = split_three(jnp.concatenate(ends, axis=0))
        heads_out[...] += mm(eh, place) + mm(el, place) + mm(ew, place)

    if not last:
        return

    def of_scores(grad_ref, ones_ref, transposed):
        for k in range(spans):
            rows = pl.ds(k * SPAN, SPAN)
            grad = scores_grad[k]
            gh, gl = split(grad.T if transposed else grad)
            ones = ones_ref[rows, :]
            wide = mm(gh, ones)
            grad_ref[rows, :] += wide[:, :DS] + wide[:, DS:] + mm(gl, ones[:, :DS])

    @pl.when(jnp.logical_and(step >= pairs, step < pairs + 2))
    def _():
        @pl.when(step == pairs)
        def _():
            of_scores(key_grad, query_both, False)

        @pl.when(step == pairs + 1)
        def _():
            of_scores(query_grad, key_both, True)

        block, shifted, pre = of_conv()
        grad = jnp.where(step == pairs, key_grad[...], query_grad[...])
        sums = conv_back(grad, block, shifted, pre)
        taps_out[...] = jnp.concatenate([zero_row if s is None else s for s in sums], axis=0)

    @pl.when(step == pairs + 2)
    def _():
        tall = lax.broadcasted_iota(jnp.int32, (SPAN, SPAN), 0)
        wide = lax.broadcasted_iota(jnp.int32, (SPAN, SPAN), 1)
        upper = (tall <= wide).astype(bf16)
        known = lane < NH
        rate = params_ref[1:2]
        delta, decay, most = zero_row, zero_row, zero_row
        for k in range(spans):
            rows = pl.ds(k * SPAN, SPAN)
            steps = jnp.where(known, pltpu.roll(steps_ref[rows, :], LANES // 2, 1), 0.0)
            step_dots = steps_out[rows, :]
            cumul_grad = dots_ref[rows, :] - steps * step_dots
            parts = mm(upper, jnp.concatenate(split_three(cumul_grad), axis=1))
            decay_grad = parts[:, :LANES] + parts[:, LANES : 2 * LANES] + parts[:, 2 * LANES :]
            decay_grad = decay_grad + heads_out[k : k + 1]
            raw = jnp.where(known, raw_ref[rows, :], 0.0) + params_ref[0:1]
            raw_grad = (step_dots + rate * decay_grad) * sigmoid(raw)
            raw_grad = jnp.where(known, raw_grad, 0.0)
            grad_out[rows, :] = raw_grad.astype(bf16)
            most = jnp.maximum(most, jnp.max(jnp.abs(raw_grad), axis=0, keepdims=True))
            delta = delta + jnp.sum(raw_grad, axis=0, keepdims=True)
            decay = decay + jnp.sum(rate * steps * decay_grad, axis=0, keepdims=True)
        sums_out[...] = jnp.concatenate(
            [delta, decay, heads_out[4:5], most, jnp.zeros((4, LANES), f32)], axis=0
        )

    @pl.when(step > pairs + 2)
    def _():
        grad_out[...] = jnp.zeros_like(grad_out)


def backward_call(spans, first, pairs, columns, shared, finish=None):
    count = spans * SPAN
    last = finish is not None
    clip_block = lambda i: jnp.minimum(i + first, CONVD // LANES - 1)
    clip = lambda i: jnp.minimum(i, pairs - 1) + first
    at_block = lambda n: pl.BlockSpec((n, LANES), lambda i: (0, clip_block(i)))
    at_pair = lambda n: pl.BlockSpec((n, LANES), lambda i: (0, clip(i)))
    out_block = lambda n: pl.BlockSpec((n, LANES), lambda i: (0, i))
    whole = lambda *s: pl.BlockSpec(s, lambda i: (0,) * len(s))
    accumulators = [
        (spans, SPAN, SPAN),
        (count, DS),
        (count, DS),
        (count, LANES),
        (8, LANES),
    ]
    wide = columns * LANES
    side = (pairs + 2 if last else pairs) * LANES
    side_block = lambda: pl.BlockSpec(
        (8, LANES), lambda i: (0, jnp.minimum(i, side // LANES - 1))
    )
    in_specs = [
        at_block(count),
        at_block(8),
        at_block(8),
        whole(CONV - 1, count, LANES),
        whole(CONV - 1, 8, LANES),
        whole(count, DS),
        whole(count, DS),
        at_pair(count),
        whole(count, LANES),
        whole(count, LANES),
        pl.BlockSpec((8, count), lambda i: (clip(i) // 4, 0)),
        whole(8, LANES),
        whole(8, LANES),
        whole(spans, SPAN, SPAN),
        pl.BlockSpec((spans, DS, LANES), lambda i: (0, 0, clip(i))),
        at_pair(DS),
        at_pair(DS),
        whole(8, LANES),
    ]
    out_specs = [out_block(count)] + [side_block()] * 4 + [whole(*s) for s in accumulators]
    out_shape = [jax.ShapeDtypeStruct((count, wide), bf16)]
    out_shape += [jax.ShapeDtypeStruct((8, side), f32)] * 4
    out_shape += [jax.ShapeDtypeStruct(s, f32) for s in accumulators]
    operands = list(shared)
    if last:
        dots, mixed, params, earlier = finish
        in_specs += [
            whole(count, LANES),
            pl.BlockSpec((count, LANES), lambda i: (0, CONVD // LANES)),
            whole(8, LANES),
        ]
        in_specs += [whole(*s) for s in accumulators]
        operands += [dots, mixed, params, *earlier]
        out_specs += [whole(8, LANES)]
        out_shape += [jax.ShapeDtypeStruct((8, LANES), f32)]
    return pl.pallas_call(
        functools.partial(backward_kernel, spans, first, pairs, last),
        grid=(columns,),
        in_specs=in_specs,
        out_specs=out_specs,
        out_shape=out_shape,
        scratch_shapes=[
            pltpu.VMEM((spans, SPAN, SPAN), f32),
            pltpu.VMEM((count, 2 * DS), bf16),
            pltpu.VMEM((count, 2 * DS), bf16),
            pltpu.VMEM((spans, 2, DS, SPAN), bf16),
        ],
        compiler_params=pltpu.CompilerParams(vmem_limit_bytes=VMEM_LIMIT),
        cost_estimate=pl.CostEstimate(flops=1, bytes_accessed=1, transcendentals=0),
        name="recurrence_backward",
    )(*operands)


def agree_kernel(first_ref, second_ref, out_ref, own, shared, near, far, sent, landed):
    f, ctx = lax.axis_index("fsdp"), lax.axis_index("ctx")
    fsdp_size, ctx_size = lax.axis_size("fsdp"), lax.axis_size("ctx")
    partners = [(f, lax.rem(ctx + d, ctx_size)) for d in range(1, ctx_size)]
    partners += [(lax.rem(f + d, fsdp_size), ctx) for d in range(1, fsdp_size)]
    barrier = pltpu.get_barrier_semaphore()
    for partner in partners:
        pl.semaphore_signal(barrier, inc=1, device_id=partner, device_id_type=MESH)
    most = jnp.maximum(jnp.max(jnp.abs(first_ref[...])), jnp.max(jnp.abs(second_ref[...])))
    own[...] = jnp.full(own.shape, most, f32)
    pl.semaphore_wait(barrier, len(partners))

    def exchange(source, slots, first, count):
        copies = []
        for n in range(count):
            copies.append(
                pltpu.make_async_remote_copy(
                    src_ref=source,
                    dst_ref=slots.at[n],
                    send_sem=sent.at[first + n],
                    recv_sem=landed.at[first + n],
                    device_id=partners[first + n],
                    device_id_type=MESH,
                )
            )
            copies[-1].start()
        for copy in copies:
            copy.wait()

    exchange(own, near, 0, ctx_size - 1)
    shared[...] = jnp.maximum(own[...], jnp.max(near[...], axis=0))
    exchange(shared, far, ctx_size - 1, fsdp_size - 1)
    out_ref[0, 0] = jnp.max(jnp.maximum(shared[...], jnp.max(far[...], axis=0)))


def largest_anywhere(first, second, collective_id):
    partners = lax.axis_size("ctx") + lax.axis_size("fsdp") - 2
    out = pl.pallas_call(
        agree_kernel,
        in_specs=[pl.BlockSpec(memory_space=pltpu.VMEM)] * 2,
        out_specs=pl.BlockSpec(memory_space=pltpu.SMEM),
        out_shape=jax.ShapeDtypeStruct((1, 1), f32),
        scratch_shapes=[
            pltpu.VMEM((8, LANES), f32),
            pltpu.VMEM((8, LANES), f32),
            pltpu.VMEM((lax.axis_size("ctx") - 1, 8, LANES), f32),
            pltpu.VMEM((lax.axis_size("fsdp") - 1, 8, LANES), f32),
            pltpu.SemaphoreType.DMA((partners,)),
            pltpu.SemaphoreType.DMA((partners,)),
        ],
        compiler_params=pltpu.CompilerParams(collective_id=collective_id, has_side_effects=True),
        name="largest_anywhere",
    )(first, second)
    return out.reshape(()) * 1.01 + 1e-30


def sum_kernel(in_ref, out_ref, near, far, whole, sent, landed):
    f, ctx = lax.axis_index("fsdp"), lax.axis_index("ctx")
    fsdp_size, ctx_size = lax.axis_size("fsdp"), lax.axis_size("ctx")
    part = in_ref.shape[0] // fsdp_size
    in_ctx = [(f, lax.rem(ctx + d, ctx_size)) for d in range(1, ctx_size)]
    in_fsdp = [(lax.rem(f + d, fsdp_size), ctx) for d in range(1, fsdp_size)]
    barrier = pltpu.get_barrier_semaphore()
    for partner in in_ctx + in_fsdp:
        pl.semaphore_signal(barrier, inc=1, device_id=partner, device_id_type=MESH)
    pl.semaphore_wait(barrier, len(in_ctx) + len(in_fsdp))

    def exchange(phase, partners, source, target):
        copies = []
        for n, partner in enumerate(partners):
            copies.append(
                pltpu.make_async_remote_copy(
                    src_ref=source(partner),
                    dst_ref=target,
                    send_sem=sent.at[phase, n],
                    recv_sem=landed.at[phase, n],
                    device_id=partner,
                    device_id_type=MESH,
                )
            )
            copies[-1].start()
        return copies

    copies = exchange(0, in_ctx, lambda partner: in_ref, near.at[ctx])
    near[pl.ds(ctx, 1)] = in_ref[...][None]
    for copy in copies:
        copy.wait()
    whole[...] = jnp.sum(near[...], axis=0)
    mine = pl.ds(pl.multiple_of(f * part, 8), part)
    copies = exchange(
        1, in_fsdp, lambda partner: whole.at[pl.ds(pl.multiple_of(partner[0] * part, 8), part)], far.at[f]
    )
    far[pl.ds(f, 1)] = whole[mine, :][None]
    for copy in copies:
        copy.wait()
    out_ref[mine, :] = jnp.sum(far[...], axis=0)
    for copy in exchange(2, in_fsdp, lambda partner: out_ref.at[mine], out_ref.at[mine]):
        copy.wait()


def sum_everywhere(value):
    if not on_small_slice():
        return lax.psum(value, ("fsdp", "ctx"))
    fsdp_size, ctx_size = lax.axis_size("fsdp"), lax.axis_size("ctx")
    block = 8 * LANES * fsdp_size
    rows = -(-value.shape[0] // block) * block // LANES
    shape = (rows, LANES)
    padded_value = jnp.pad(value, (0, rows * LANES - value.shape[0])).reshape(shape)
    peers = max(fsdp_size, ctx_size) - 1
    out = pl.pallas_call(
        sum_kernel,
        in_specs=[pl.BlockSpec(memory_space=pltpu.VMEM)],
        out_specs=pl.BlockSpec(memory_space=pltpu.VMEM),
        out_shape=jax.ShapeDtypeStruct(shape, f32),
        scratch_shapes=[
            pltpu.VMEM((ctx_size,) + shape, f32),
            pltpu.VMEM((fsdp_size, rows // fsdp_size, LANES), f32),
            pltpu.VMEM(shape, f32),
            pltpu.SemaphoreType.DMA((3, peers)),
            pltpu.SemaphoreType.DMA((3, peers)),
        ],
        compiler_params=pltpu.CompilerParams(collective_id=4, has_side_effects=True),
        cost_estimate=pl.CostEstimate(flops=1, bytes_accessed=1, transcendentals=0),
        name="sum_everywhere",
    )(padded_value)
    return out.reshape(-1)[: value.shape[0]]


def block_out_kernel(mixer_ref, whole_ref, tokens_ref, out_ref):
    projected = mm(mixer_ref[...], whole_ref[...])
    out_ref[...] = (tokens_ref[...].astype(f32) + projected).astype(bf16)


def block_out_call(mixer_low, whole_out, tokens):
    count, width = tokens.shape
    rows = lambda n: pl.BlockSpec((SPAN, n), lambda i: (i, 0))
    return pl.pallas_call(
        block_out_kernel,
        grid=(count // SPAN,),
        in_specs=[
            rows(DI),
            pl.BlockSpec(whole_out.shape, lambda i: (0, 0), pipeline_mode=pl.Buffered(1)),
            rows(width),
        ],
        out_specs=rows(width),
        out_shape=jax.ShapeDtypeStruct(tokens.shape, bf16),
        compiler_params=pltpu.CompilerParams(vmem_limit_bytes=VMEM_LIMIT),
        cost_estimate=pl.CostEstimate(flops=1, bytes_accessed=1, transcendentals=0),
        name="block_out",
    )(mixer_low, whole_out, tokens)


def input_grad_kernel(
    split_at,
    second_width,
    gate_ref,
    first_ref,
    second_ref,
    whole_gate_ref,
    whole_conv_ref,
    tokens_ref,
    cotangent_ref,
    gain_ref,
    out_ref,
    gain_grad_ref,
):
    grad = mm_nt(gate_ref[...], whole_gate_ref[...])
    grad = grad + mm_nt(first_ref[...], whole_conv_ref[:, :split_at])
    grad = grad + mm_nt(
        second_ref[:, :second_width], whole_conv_ref[:, split_at : split_at + second_width]
    )
    inputs = tokens_ref[...].astype(f32)
    scale = lax.rsqrt(jnp.mean(inputs * inputs, axis=-1, keepdims=True) + norm_eps)
    unit = inputs * scale

    @pl.when(pl.program_id(0) == 0)
    def _():
        gain_grad_ref[...] = jnp.zeros_like(gain_grad_ref)

    gain_grad_ref[0:1] += jnp.sum(grad * unit, axis=0, keepdims=True)
    unit_grad = grad * gain_ref[0:1]
    mean = jnp.mean(unit_grad * unit, axis=-1, keepdims=True)
    out_ref[...] = cotangent_ref[...].astype(f32) + scale * (unit_grad - unit * mean)


def input_grad_call(
    split_at, gate_grad, first_grad, second_grad, whole_gate, whole_conv, tokens, cotangent, gain
):
    count, width = tokens.shape
    rows = lambda n: pl.BlockSpec((SPAN, n), lambda i: (i, 0))
    whole = lambda *s: pl.BlockSpec(s, lambda i: (0,) * len(s), pipeline_mode=pl.Buffered(1))
    return pl.pallas_call(
        functools.partial(input_grad_kernel, split_at, whole_conv.shape[1] - split_at),
        grid=(count // SPAN,),
        in_specs=[
            rows(gate_grad.shape[1]),
            rows(first_grad.shape[1]),
            rows(second_grad.shape[1]),
            whole(*whole_gate.shape),
            whole(*whole_conv.shape),
            rows(width),
            rows(width),
            whole(8, width),
        ],
        out_specs=[rows(width), pl.BlockSpec((8, width), lambda i: (0, 0))],
        out_shape=[
            jax.ShapeDtypeStruct((count, width), f32),
            jax.ShapeDtypeStruct((8, width), f32),
        ],
        compiler_params=pltpu.CompilerParams(vmem_limit_bytes=VMEM_LIMIT),
        cost_estimate=pl.CostEstimate(flops=1, bytes_accessed=1, transcendentals=0),
        name="input_grad",
    )(gate_grad, first_grad, second_grad, whole_gate, whole_conv, tokens, cotangent, gain)


ADAM_COLS = 256


def adam_kernel(blocks, core_ref, *refs):
    grads, refs = refs[: 2 * len(blocks)], refs[2 * len(blocks) :]
    param_ref, first_ref, second_ref = refs[:3]
    outs = refs[-3:]
    step = pl.program_id(0)
    begin = 0
    for n, half in enumerate(blocks):
        own_ref, other_ref = grads[2 * n], grads[2 * n + 1]

        @pl.when(jnp.logical_and(step >= begin, step < begin + 2 * half))
        def _():
            own = (step >= begin + half).astype(jnp.int32) == core_ref[0]
            grad = jnp.where(own, own_ref[...], other_ref[...])
            new = adamw_update(
                param_ref[...], grad, first_ref[...], second_ref[...], weight_decay
            )
            for out, value in zip(outs, new):
                out[...] = value

        begin += 2 * half


def adam_call(core, grads, first_block, param, first, second, earlier=None):
    rows = param.shape[0]
    halves = [own.shape[1] // ADAM_COLS for own, other in grads]
    steps = min(2 * sum(halves), -(-param.shape[1] // ADAM_COLS) - first_block)
    place = pl.BlockSpec((rows, ADAM_COLS), lambda j: (0, j + first_block))
    in_specs, operands, begin = [pl.BlockSpec(memory_space=pltpu.SMEM)], [core], 0
    for (own, other), half in zip(grads, halves):

        def column(j, begin=begin, half=half):
            at = jnp.minimum(jnp.maximum(j - begin, 0), 2 * half - 1)
            return 0, jnp.where(at < half, at, at - half)

        in_specs += [pl.BlockSpec((rows, ADAM_COLS), column)] * 2
        operands += [own, other]
        begin += 2 * half
    in_specs += [place] * 3
    operands += [param, first, second]
    aliases = {}
    if earlier is not None:
        aliases = {len(operands) + n: n for n in range(3)}
        operands += list(earlier)
        in_specs += [pl.BlockSpec(memory_space=pl.ANY)] * 3
    return pl.pallas_call(
        functools.partial(adam_kernel, tuple(halves)),
        grid=(steps,),
        in_specs=in_specs,
        out_specs=[place] * 3,
        out_shape=[jax.ShapeDtypeStruct(param.shape, f32)] * 3,
        input_output_aliases=aliases,
        compiler_params=pltpu.CompilerParams(vmem_limit_bytes=VMEM_LIMIT),
        cost_estimate=pl.CostEstimate(flops=1, bytes_accessed=1, transcendentals=0),
        name="adam_columns",
    )(*operands)


def adamw_update(param, grad, first, second, decay):
    first_new = beta_one * first + (1.0 - beta_one) * grad
    second_new = beta_two * second + (1.0 - beta_two) * grad * grad
    first_hat = first_new / (1.0 - beta_one**STEP)
    second_hat = second_new / (1.0 - beta_two**STEP)
    param_new = param - learn_rate * (first_hat / (jnp.sqrt(second_hat) + adam_eps) + decay * param)
    return (param_new, first_new, second_new)


def segment_of(lengths, positions):
    ends = jnp.cumsum(lengths)
    return jnp.sum((positions[..., None] >= ends).astype(jnp.int32), axis=-1)


def padded(*rows):
    out = jnp.stack([jnp.pad(r, (0, LANES - r.shape[0])) for r in rows])
    return jnp.pad(out, ((0, 8 - len(rows)), (0, 0)))


def spread_matrix():
    head = lax.broadcasted_iota(jnp.int32, (LANES, DI), 0)
    lane = lax.broadcasted_iota(jnp.int32, (LANES, DI), 1)
    return (head == lane // HD).astype(bf16)


def pass_on(own, factor, axis, backwards, kind):
    size, here = lax.axis_size(axis), lax.axis_index(axis)
    given = jnp.zeros_like(own)
    for turn in range(size - 1):
        source = size - 1 - turn if backwards else turn
        target = source - 1 if backwards else source + 1
        out = (factor * given + own).astype(kind)
        arrived = lax.ppermute(out, axis, [(source, target)]).astype(f32)
        given = jnp.where(here == target, arrived, given)
    return given


def on_small_slice():
    return lax.axis_size("fsdp") == Z * Y and lax.axis_size("ctx") == 4


def all_rows(block):
    return lax.all_gather(block, "fsdp", axis=0, tiled=True)


def swapped(value, axis, step):
    size = lax.axis_size(axis)
    return lax.ppermute(value, axis, [(i, i ^ step) for i in range(size)])


def after(value, *others):
    return lax.optimization_barrier((value,) + others)[0]


def coordinates():
    f, ctx = lax.axis_index("fsdp"), lax.axis_index("ctx")
    return ctx // 2, f % Y, f // Y, ctx % 2


CORE = ("ctx", 1)
ACROSS_X = ("ctx", 2)
ACROSS_Y = ("fsdp", 1)
ACROSS_Z = tuple(("fsdp", Y * m) for m in range(1, Z))


def row_products(columns, grads):
    return jnp.einsum("tk,tz->kz", columns, grads, preferred_element_type=f32)


def half_of(value, bit, axis):
    size = value.shape[axis] // 2
    return lax.dynamic_slice_in_dim(value, bit * size, size, axis)


class Part:
    def __init__(self, value, bound):
        self.value, self.bound = value, bound


def lowered(value, bound):
    return (value * (32768.0 / bound)).astype(jnp.float16)


def raised(value, bound):
    return value.astype(f32) * (bound * (1.0 / 32768.0))


def summed_on_chip(columns, grads, bound):
    core = coordinates()[3]
    theirs = row_products(columns, half_of(grads, 1 - core, 1))
    arrived = swapped(lowered(theirs, bound), *CORE)
    mine = row_products(columns, half_of(grads, core, 1))
    return Part(mine + raised(arrived, bound), 2.0 * bound)


def to_send(part, bit, axis):
    sent = lowered(half_of(part.value, 1 - bit, axis), part.bound)
    return Part(half_of(part.value, bit, axis), part.bound), sent


def joined_with(kept, arrived):
    return Part(kept.value + raised(arrived, kept.bound), 2.0 * kept.bound)


def by_owner(part):
    return Part(part.value.reshape(Z, Y, -1, part.value.shape[1]), part.bound)


def along_z(part):
    z = coordinates()[2]
    take = lambda at: lax.dynamic_index_in_dim(part.value[:, 0], at, 0, keepdims=False)
    sent = [lowered(take(z ^ m), part.bound) for m in range(1, Z)]
    return Part(take(z), part.bound), sent


def of_owner(kept, arrived):
    total = kept.value
    for one in arrived:
        total = total + raised(one, kept.bound)
    return Part(total, Z * kept.bound)


def both_columns(value, way, bit):
    other = swapped(value, *way)
    return jnp.where(
        bit == 0,
        jnp.concatenate([value, other], axis=1),
        jnp.concatenate([other, value], axis=1),
    )


def sum_of_two(low, arrived, bound):
    return raised(low, bound) + raised(arrived, bound)


def owned_rows(partial):
    return lax.psum(lax.psum_scatter(partial, "fsdp", scatter_dimension=0, tiled=True), "ctx")


def largest(value):
    return jnp.max(jnp.abs(value)).astype(f32) + 1e-30


def on_device(
    tokens_in,
    cotangent,
    doc_lengths,
    in_proj,
    out_proj,
    norm_gain,
    gate_gain,
    conv_weight,
    conv_bias,
    delta_bias,
    decay_log,
    skip_scale,
    in_first,
    in_second,
    out_first,
    out_second,
    small_first,
    small_second,
):
    count = tokens_in.shape[0]
    spans = count // SPAN
    ctx = lax.axis_size("ctx")
    begin = lax.axis_index("ctx") * count
    lengths = doc_lengths[0]
    small_slice = on_small_slice()

    conv_block, gate_block = in_proj[:, DI:].astype(bf16), in_proj[:, :DI].astype(bf16)
    out_block = out_proj.astype(bf16)
    if small_slice:
        (whole_conv,) = gather_call(conv_block)
    else:
        whole_conv, whole_gate, whole_out = map(all_rows, (conv_block, gate_block, out_block))
    inputs = tokens_in.astype(f32)
    scale = lax.rsqrt(jnp.mean(inputs * inputs, axis=-1, keepdims=True) + norm_eps)
    normed = (inputs * scale * norm_gain[None, :]).astype(bf16)

    mixed = mm(normed, whole_conv)
    edge = lax.ppermute(mixed[count - 8 :, :CONVD], "ctx", [(i, i + 1) for i in range(ctx - 1)])
    edge = jnp.where(jnp.arange(8)[:, None] >= 8 - (CONV - 1), edge, 0.0)

    place = jnp.concatenate([begin[None].astype(jnp.int32), lengths.astype(jnp.int32)])
    params = padded(delta_bias, -jnp.exp(decay_log))
    (
        steps,
        decay,
        reach,
        rows,
        factor,
        start,
        inside,
        outside,
        mask,
        mask_turned,
    ) = prepare_call(spans, place, mixed, params)
    taps = jnp.concatenate([conv_weight.T, conv_bias[None], jnp.zeros((3, CONVD), f32)], axis=0)

    inner, local, states, keys, queries, *wholes = forward_call(
        spans,
        mixed,
        edge,
        taps,
        inside,
        outside,
        steps,
        decay,
        rows,
        factor,
        mask,
        (gate_block, out_block) if small_slice else (),
    )
    if small_slice:
        whole_gate, whole_out = wholes
    total_lanes = jnp.repeat(start[spans, :NH], HD)[None]
    state_in = pass_on(states[spans - 1], total_lanes, "ctx", False, f32)
    gate = mm(normed, whole_gate)
    mixer_back = jnp.einsum("td,kd->tk", cotangent, whole_out, preferred_element_type=f32)
    mixer_low, mixer_grad, gate_grad, gate_gain_grad, dots, summary, gate_most_rows = norm_call(
        local,
        inner,
        gate,
        mixer_back,
        queries,
        state_in,
        reach,
        spread_matrix(),
        jnp.repeat(skip_scale, HD)[None] + jnp.zeros((8, 1), f32),
        gate_gain[None] + jnp.zeros((8, 1), f32),
    )
    state_back = pass_on(summary, total_lanes, "ctx", True, bf16)

    out_bound = count * 6.0 * (DI**0.5 * 1.01) * largest(gate_gain)
    product_bound = count * (D**0.5 * 1.01) * largest(norm_gain)
    x, y, z, core = coordinates()
    if small_slice:
        out_part = summed_on_chip(mixer_low, cotangent, out_bound)
        out_kept, out_sent = to_send(out_part, x, 1)
        gate_most = largest_anywhere(gate_most_rows, gate_most_rows, 1)
        gate_part = summed_on_chip(normed, gate_grad, product_bound * gate_most)
        gate_kept, gate_sent = to_send(by_owner(gate_part), y, 1)
        mixer_grad, out_sent, gate_sent = lax.optimization_barrier(
            (mixer_grad, out_sent, gate_sent)
        )
        out_got = swapped(out_sent, *ACROSS_X)
        gate_got = swapped(gate_sent, *ACROSS_Y)
    else:
        out_rows = owned_rows(row_products(mixer_low, cotangent))

    first_pairs = PAIRS // 2
    skip = padded(skip_scale)
    shared = lambda back: (
        mixed,
        edge,
        taps,
        inside,
        outside,
        keys,
        queries,
        back,
        steps,
        decay,
        rows,
        factor,
        start,
        mask_turned,
        states,
        state_in,
        state_back,
        skip,
    )
    following = segment_of(lengths, begin + count + jnp.arange(CONV, dtype=jnp.int32))
    own_last = segment_of(lengths, begin + count - CONV + jnp.arange(CONV, dtype=jnp.int32))

    def with_edge(grad, top, tail, at):
        next_top = lax.ppermute(top, "ctx", [(i + 1, i) for i in range(ctx - 1)])
        width = tail.shape[1]
        for j in range(1, CONV):
            joined = (following[:j] == own_last[CONV - j :]).astype(f32)
            more = joined[:, None] * next_top[:j] * taps[3 - j : 4 - j, at : at + width]
            tail = tail + jnp.pad(more, ((8 - j, 0), (0, 0)))
        return lax.dynamic_update_slice(grad, tail.astype(bf16), (count - 8, 0)), tail

    first_grad, top, tail, first_taps_grad, most, *sums = backward_call(
        spans, 0, first_pairs, first_pairs, shared(mixer_grad)
    )
    if small_slice:
        top, tail, most, first_grad, out_got, gate_got = lax.optimization_barrier(
            (top, tail, most, first_grad, out_got, gate_got)
        )
    first_grad, tail = with_edge(first_grad, top, tail, 0)
    if small_slice:
        out_kept, out_sent = to_send(by_owner(joined_with(out_kept, out_got)), y, 1)
        gate_kept, gate_sent = along_z(joined_with(gate_kept, gate_got))
        first_most = largest_anywhere(most, tail, 2)
        first_part = summed_on_chip(normed, first_grad, product_bound * first_most)
        first_kept, first_sent = to_send(by_owner(first_part), y, 1)
        mixer_grad, out_sent, gate_sent, first_sent = lax.optimization_barrier(
            (mixer_grad, out_sent, gate_sent, first_sent)
        )
        out_got = swapped(out_sent, *ACROSS_Y)
        gate_got = [swapped(s, *way) for s, way in zip(gate_sent, ACROSS_Z)]
        first_got = swapped(first_sent, *ACROSS_Y)
    second_grad, top, tail, second_taps_grad, most, *sums = backward_call(
        spans,
        first_pairs,
        PAIRS - first_pairs,
        16,
        shared(mixer_grad),
        (dots, mixed, params, sums),
    )
    split_at = first_pairs * LANES
    fence = lax.optimization_barrier
    if small_slice:
        top, tail, most, second_grad, sums, out_got, gate_got, first_got = fence(
            (top, tail, most, second_grad, sums, out_got, gate_got, first_got)
        )
        out_kept, out_sent = along_z(joined_with(out_kept, out_got))
        first_kept, first_sent = along_z(joined_with(first_kept, first_got))
        out_high = out_sent[0].shape[0] // 2
        both_sent = [
            jnp.concatenate([one, other[:out_high], other[out_high:]], axis=1)
            for one, other in zip(first_sent, out_sent)
        ]
        gate_part = of_owner(gate_kept, gate_got)
        gate_low = lowered(gate_part.value, gate_part.bound)
        both_sent, gate_low, tail, most = fence((both_sent, gate_low, tail, most))
        both_got = [swapped(s, *way) for s, way in zip(both_sent, ACROSS_Z)]
        gate_got = swapped(gate_low, *ACROSS_X)
    second_grad, tail = with_edge(second_grad, top, tail, split_at)
    if small_slice:
        most = jnp.maximum(most, jnp.max(sums[5][3]))
        second_most = largest_anywhere(most, tail, 3)
        second_part = summed_on_chip(normed, second_grad, product_bound * second_most)
        second_kept, second_sent = to_send(by_owner(second_part), y, 1)
        second_sent, gate_grad, mixer_low, sums, gate_gain_grad = fence(
            (second_sent, gate_grad, mixer_low, sums, gate_gain_grad)
        )
        second_got = swapped(second_sent, *ACROSS_Y)
    input_grad, norm_gain_grad = input_grad_call(
        split_at,
        gate_grad,
        first_grad,
        second_grad,
        whole_gate,
        whole_conv,
        tokens_in,
        cotangent,
        norm_gain[None] + jnp.zeros((8, 1), f32),
    )
    if small_slice:
        second_got, both_got, gate_got, input_grad, norm_gain_grad = fence(
            (second_got, both_got, gate_got, input_grad, norm_gain_grad)
        )
        second_kept, second_sent = along_z(joined_with(second_kept, second_got))
        first_wide = first_part.value.shape[1]
        out_wide = (both_got[0].shape[1] - first_wide) // 2
        out_got = [
            jnp.concatenate(
                [s[:, first_wide : first_wide + out_wide], s[:, first_wide + out_wide :]], axis=0
            )
            for s in both_got
        ]
        first_part = of_owner(first_kept, [s[:, :first_wide] for s in both_got])
        first_low = lowered(first_part.value, first_part.bound)
        out_total = of_owner(out_kept, out_got).value
        gate_rows = sum_of_two(gate_low, gate_got, gate_part.bound)
        second_sent, first_low, out_total, gate_rows, mixer_low = fence(
            (second_sent, first_low, out_total, gate_rows, mixer_low)
        )
        second_got = [swapped(s, *way) for s, way in zip(second_sent, ACROSS_Z)]
        first_got = swapped(first_low, *ACROSS_X)
        out_got = swapped(out_total, *ACROSS_X)
        gate_pair = gate_rows, swapped(gate_rows, *CORE)
    block_out = block_out_call(mixer_low, whole_out, tokens_in)
    if small_slice:
        block_out, first_got, out_got, gate_pair = fence(
            (block_out, first_got, out_got, gate_pair)
        )
        first_rows = sum_of_two(first_low, first_got, first_part.bound)
        out_rows = jnp.where(
            x == 0,
            jnp.concatenate([out_total, out_got], axis=1),
            jnp.concatenate([out_got, out_total], axis=1),
        )
        first_pair = first_rows, swapped(first_rows, *CORE)
        out_pair = out_rows, swapped(out_rows, *CORE)
        core_index = core[None].astype(jnp.int32)
    else:
        halves = lambda v: (v[:, : v.shape[1] // 2], v[:, v.shape[1] // 2 :])
        out_pair = halves(out_rows)
        gate_pair = halves(owned_rows(row_products(normed, gate_grad)))
        first_pair = halves(owned_rows(row_products(normed, first_grad)))
        second_pair = halves(owned_rows(row_products(normed, second_grad)))
        core_index = jnp.zeros((1,), jnp.int32)
    early = adam_call(core_index, (gate_pair, first_pair), 0, in_proj, in_first, in_second)
    out_new, out_first_new, out_second_new = adam_call(
        core_index, (out_pair,), 0, out_proj, out_first, out_second
    )
    if small_slice:
        second_got, early, out_new, norm_gain_grad = fence(
            (second_got, early, out_new, norm_gain_grad)
        )
        second_part = of_owner(second_kept, second_got)
        second_low = lowered(second_part.value, second_part.bound)
        second_low, norm_gain_grad = fence((second_low, norm_gain_grad))
        second_got = swapped(second_low, *ACROSS_X)
    taps_grad = jnp.concatenate([first_taps_grad, second_taps_grad], axis=1)
    small_grad = sum_everywhere(
        jnp.concatenate(
            [
                norm_gain_grad[0],
                gate_gain_grad[0],
                taps_grad[:CONV].T.reshape(-1),
                taps_grad[4],
                sums[5][0, :NH],
                sums[5][1, :NH],
                sums[5][2, :NH],
            ]
        )
    )
    if small_slice:
        second_got, small_grad = fence((second_got, small_grad))
        second_rows = sum_of_two(second_low, second_got, second_part.bound)
        second_pair = second_rows, swapped(second_rows, *CORE)
    in_new, in_first_new, in_second_new = adam_call(
        core_index,
        (second_pair,),
        (DI + split_at) // ADAM_COLS,
        in_proj,
        in_first,
        in_second,
        early,
    )
    small_param = jnp.concatenate(
        [
            norm_gain,
            gate_gain,
            conv_weight.reshape(-1),
            conv_bias,
            delta_bias,
            decay_log,
            skip_scale,
        ]
    )
    small_new, small_first_new, small_second_new = adamw_update(
        small_param, small_grad, small_first, small_second, 0.0
    )
    return (
        block_out,
        input_grad,
        in_new,
        in_first_new,
        in_second_new,
        out_new,
        out_first_new,
        out_second_new,
        small_new,
        small_first_new,
        small_second_new,
    )


def solution(mesh):
    placed = (
        P(("fsdp", "ctx"), None),
        P(("fsdp", "ctx"), None),
        P("fsdp", None),
        P("fsdp", None),
        P("fsdp", None),
        P(),
        P(),
        P(),
        P(),
        P(),
        P(),
        P(),
        P("fsdp", None),
        P("fsdp", None),
        P("fsdp", None),
        P("fsdp", None),
        P(),
        P(),
    )
    return jax.shard_map(
        on_device,
        mesh=mesh,
        in_specs=placed,
        out_specs=(
            P(("fsdp", "ctx"), None),
            P(("fsdp", "ctx"), None),
            P("fsdp", None),
            P("fsdp", None),
            P("fsdp", None),
            P("fsdp", None),
            P("fsdp", None),
            P("fsdp", None),
            P(),
            P(),
            P(),
        ),
        check_vma=False,
    )
```

```python
import functools

import jax
import jax.numpy as jnp
from jax import lax
from jax.experimental import pallas as pl
from jax.experimental.pallas import tpu as pltpu
from jax.sharding import PartitionSpec as P

D = 1536
DI = 3072
NH = 48
HD = 64
DS = 128
CONV = 4
SPAN = 256
STEP = 5
CONVD = 3328
LANES = 128
PAIRS = DI // LANES
HALF = SPAN // 2
NORM_ROWS = 128
NORM_COLS = 512
MASKED = -1e30

highest = lax.Precision.HIGHEST
norm_eps = 1e-05
beta_one = 0.9
beta_two = 0.95
adam_eps = 1e-08
learn_rate = 0.05
weight_decay = 0.1
f32 = jnp.float32
bf16 = jnp.bfloat16
VMEM_LIMIT = 56 * 1024 * 1024


def split(value):
    high = value.astype(bf16)
    return high, (value - high.astype(f32)).astype(bf16)


def mm(a, b):
    return jnp.dot(a, b, preferred_element_type=f32)


def mm_nt(a, b):
    return lax.dot_general(a, b, (((1,), (1,)), ((), ())), preferred_element_type=f32)


def sigmoid(v):
    return 1.0 / (1.0 + jnp.exp(-v))


def conv_shifts(block, edge, inside, outside, room):
    count = block.shape[0]
    room[pl.ds(8, count), :] = block
    shifted = []
    for j in range(1, CONV):
        body = inside[j - 1] * room[pl.ds(8 - j, count), :]
        head = inside[j - 1, :8] * pltpu.roll(block[:8], j, 0)
        head = head + outside[j - 1] * pltpu.roll(edge, j, 0)
        shifted.append(jnp.concatenate([head, body[8:]], axis=0))
    return shifted


def conv_pre(block, shifted, taps):
    total = taps[4:5] + taps[3:4] * block
    for j in range(1, CONV):
        total = total + taps[3 - j : 4 - j] * shifted[j - 1]
    return total


def pair_columns(packed, pair):
    turned = pltpu.roll(packed, lax.rem(LANES - 2 * pair, LANES), 1)
    lane = lax.broadcasted_iota(jnp.int32, packed.shape, 1)
    first = jnp.where(lane < HD, turned[:, 0:1], turned[:, 1:2])
    second = jnp.where(lane < HD, turned[:, 64:65], turned[:, 65:66])
    return turned, first, second


def spread_pair(both, pair):
    source = lax.broadcasted_iota(jnp.int32, (2 * LANES, LANES), 0)
    lane = lax.broadcasted_iota(jnp.int32, (2 * LANES, LANES), 1)
    return mm(both, (lax.rem(source, LANES) == 2 * pair + lane // HD).astype(bf16))


def pair_rows(rows, pair):
    turned = pltpu.roll(rows, lax.rem(LANES - 2 * pair, LANES), 1)
    lane = lax.broadcasted_iota(jnp.int32, rows.shape, 1)
    return jnp.where(lane < HD, turned[:, 0:1], turned[:, 1:2])


def head_row(block, head):
    sublane = lax.broadcasted_iota(jnp.int32, block.shape, 0)
    return jnp.sum(jnp.where(sublane == lax.rem(head, 8), block, 0.0), axis=0, keepdims=True)


def split_three(value):
    high, low = split(value)
    return high, low, (value - high.astype(f32) - low.astype(f32)).astype(bf16)


def prepare_kernel(
    spans,
    place_ref,
    raw_ref,
    params_ref,
    steps_out,
    decay_out,
    reach_out,
    turned_out,
    factor_out,
    start_out,
    inside_out,
    inside_back_out,
    outside_out,
    mask_out,
    mask_turned_out,
):
    count = spans * SPAN
    begin = place_ref[0]
    ends = []
    for d in range(place_ref.shape[0] - 1):
        ends.append(place_ref[d + 1] + (ends[-1] if ends else 0))

    def segment(position):
        total = (position >= ends[0]).astype(jnp.int32)
        for end in ends[1:]:
            total = total + (position >= end).astype(jnp.int32)
        return total

    row = lax.broadcasted_iota(jnp.int32, (count, LANES), 0)
    here = segment(row + begin)
    for j in range(1, CONV):
        same = here == segment(row + (begin - j))
        inside_out[j - 1] = jnp.where(jnp.logical_and(same, row >= j), 1.0, 0.0)
        later = here == segment(row + (begin + j))
        inside_back_out[j - 1] = jnp.where(jnp.logical_and(later, row + j < count), 1.0, 0.0)
        outside_out[j - 1] = jnp.where(jnp.logical_and(same, row < j), 1.0, 0.0)[:8]
    lane = lax.broadcasted_iota(jnp.int32, (count, LANES), 1)
    raw = jnp.where(lane < NH, raw_ref[...], 0.0) + params_ref[0:1]
    steps = jnp.where(lane < NH, jnp.maximum(raw, 0.0) + jnp.log1p(jnp.exp(-jnp.abs(raw))), 0.0)
    log_decay = params_ref[1:2] * steps
    tall = lax.broadcasted_iota(jnp.int32, (SPAN, SPAN), 0)
    wide = lax.broadcasted_iota(jnp.int32, (SPAN, SPAN), 1)
    lower = (tall >= wide).astype(bf16)
    span_lane = lax.broadcasted_iota(jnp.int32, (SPAN, LANES), 1)
    before = jnp.zeros((1, LANES), f32)
    start = jnp.ones((1, LANES), f32)
    starts, factors = [start], []
    reached = here == segment(begin - 1)
    for k in range(spans):
        at = k * SPAN
        rows = pl.ds(at, SPAN)
        parts = split_three(log_decay[at : at + SPAN])
        sums = mm(lower, jnp.concatenate(parts, axis=1))
        cumul = sums[:, :LANES] + sums[:, LANES : 2 * LANES] + sums[:, 2 * LANES :]
        last = cumul[SPAN - 1 : SPAN]
        span_here = here[at : at + SPAN]
        first = begin + at
        enters = jnp.logical_and(span_here == segment(first - 1), span_here >= 0)
        enter = jnp.where(jnp.logical_and(enters, first > 0), jnp.exp(cumul), 0.0)
        leave = jnp.where(
            span_here == segment(first + SPAN - 1), jnp.exp(last - cumul), 0.0
        )
        reach = jnp.where(
            jnp.logical_and(reached[at : at + SPAN], begin > 0), jnp.exp(cumul + before), 0.0
        )
        known = span_lane < NH
        steps_out[rows, :] = jnp.where(known, cumul, 0.0) + pltpu.roll(
            steps[at : at + SPAN], LANES // 2, 1
        )
        decay_out[rows, :] = jnp.where(known, enter, 0.0) + pltpu.roll(
            jnp.where(known, leave, 0.0), LANES // 2, 1
        )
        reach_out[rows, :] = jnp.where(known, reach, 0.0)
        turned_out[:, rows] = cumul.T[:NH]
        factors.append(enter[SPAN - 1 : SPAN])
        start = start * factors[-1]
        starts.append(start)
        before = before + last
        together = segment(tall + first) == segment(wide + first)
        mask_out[k] = jnp.where(jnp.logical_and(together, tall >= wide), 0.0, MASKED)
        mask_turned_out[k] = jnp.where(jnp.logical_and(together, tall <= wide), 0.0, MASKED)
    rest = lambda rows: jnp.concatenate(
        rows + [jnp.zeros((8 - len(rows), LANES), f32)], axis=0
    )
    factor_out[...] = rest(factors)
    start_out[...] = rest(starts)


def prepare_call(spans, place, mixed, params):
    count = spans * SPAN
    whole = lambda *s: pl.BlockSpec(s, lambda i: (0,) * len(s))
    shapes = [
        (count, LANES),
        (count, LANES),
        (count, LANES),
        (NH, count),
        (8, LANES),
        (8, LANES),
        (CONV - 1, count, LANES),
        (CONV - 1, count, LANES),
        (CONV - 1, 8, LANES),
        (spans, SPAN, SPAN),
        (spans, SPAN, SPAN),
    ]
    return pl.pallas_call(
        functools.partial(prepare_kernel, spans),
        grid=(1,),
        in_specs=[
            pl.BlockSpec(memory_space=pltpu.SMEM),
            pl.BlockSpec((count, LANES), lambda i: (0, CONVD // LANES)),
            whole(8, LANES),
        ],
        out_specs=[whole(*s) for s in shapes],
        out_shape=[jax.ShapeDtypeStruct(s, f32) for s in shapes],
        compiler_params=pltpu.CompilerParams(vmem_limit_bytes=VMEM_LIMIT),
        name="steps_and_masks",
    )(place, mixed, params)


MESH = pl.DeviceIdType.MESH
Z = 4
Y = 2


PARTS = 2


class Gathering:
    def __init__(self, blocks, wholes, sems):
        self.arrays = []
        for block, whole in zip(blocks, wholes):
            rows = block.shape[0] // PARTS
            self.arrays += [(block, whole, part * rows, rows) for part in range(PARTS)]
        self.own, self.up_sem, self.down_sem, self.z_sem, *sems = sems
        self.y_sent, self.y_sem, self.x_sent, self.x_sem, self.core_sent, self.core_sem = sems
        self.f, self.ctx = lax.axis_index("fsdp"), lax.axis_index("ctx")
        self.z, self.y = self.f // Y, lax.rem(self.f, Y)
        self.x, self.c = self.ctx // 2, lax.rem(self.ctx, 2)
        self.at_y = (self.z * Y + 1 - self.y, self.ctx)
        self.at_x = (self.f, (1 - self.x) * 2 + self.c)
        self.at_core = (self.f, self.x * 2 + 1 - self.c)

    def at_z(self, other):
        return other * Y + self.y, self.ctx

    def rows_of(self, n):
        return self.arrays[n][3]

    def place(self, n, block, row, size):
        own, whole, offset, rows = self.arrays[n]
        return whole.at[pl.ds(block * own.shape[0] + offset + row, size)]

    def third(self, n):
        return self.rows_of(n) // 6

    def gathered(self, n):
        return self.c * (self.rows_of(n) // 2) + self.x * self.third(n), 2 * self.third(n)

    def move(self, n, block, row, size, sent, landed, partner, own=False):
        here = self.place(n, block, row, size)
        source = self.arrays[n][0].at[pl.ds(self.arrays[n][2] + row, size)] if own else here
        return pltpu.make_async_remote_copy(
            src_ref=source,
            dst_ref=here,
            send_sem=sent,
            recv_sem=landed,
            device_id=partner,
            device_id_type=MESH,
        )

    def up(self, n, zb, own=False):
        sems = self.up_sem.at[n, zb], self.z_sem.at[n, zb]
        block = zb * Y + self.y
        return self.move(n, block, *self.gathered(n), *sems, self.at_z(self.z + 1), own)

    def down(self, n, zb, own=False):
        sems = self.down_sem.at[n, zb], self.z_sem.at[n, zb]
        block = zb * Y + self.y
        return self.move(n, block, *self.gathered(n), *sems, self.at_z(self.z - 1), own)

    def along_y(self, n, zb, yb, own=False):
        sems = self.y_sent.at[n, zb], self.y_sem.at[n, zb]
        return self.move(n, zb * Y + yb, *self.gathered(n), *sems, self.at_y, own)

    def along_x(self, n, block, sender_x):
        row = self.c * (self.rows_of(n) // 2) + 2 * self.third(n) * sender_x
        sems = self.x_sent.at[n, block], self.x_sem.at[n, block]
        return self.move(n, block, row, self.third(n), *sems, self.at_x)

    def core_first(self, n, block, core):
        row = core * (self.rows_of(n) // 2) + self.x * self.third(n)
        sems = self.core_sent.at[n, block, 0], self.core_sem.at[n, block, 0]
        return self.move(n, block, row, 2 * self.third(n), *sems, self.at_core)

    def core_second(self, n, block, core):
        row = core * (self.rows_of(n) // 2) + 2 * self.third(n) * (1 - self.x)
        sems = self.core_sent.at[n, block, 1], self.core_sem.at[n, block, 1]
        return self.move(n, block, row, self.third(n), *sems, self.at_core)

    def own_copy(self, n):
        block, whole, offset, rows = self.arrays[n]
        return pltpu.make_async_copy(
            block.at[pl.ds(offset, rows)], self.place(n, self.f, 0, rows), self.own.at[n]
        )

    def begin(self):
        barrier = pltpu.get_barrier_semaphore()
        signal = functools.partial(
            pl.semaphore_signal, barrier, inc=1, device_id_type=MESH
        )
        for partner in (self.at_y, self.at_x, self.at_core):
            signal(device_id=partner)

        @pl.when(self.z > 0)
        def _():
            signal(device_id=self.at_z(self.z - 1))

        @pl.when(self.z < Z - 1)
        def _():
            signal(device_id=self.at_z(self.z + 1))

        middle = jnp.logical_and(self.z > 0, self.z < Z - 1).astype(jnp.int32)
        pl.semaphore_wait(barrier, 4 + middle)
        for n in range(len(self.arrays)):
            self.own_copy(n).start()

            @pl.when(self.z < Z - 1)
            def _():
                self.up(n, self.z, True).start()

            @pl.when(self.z > 0)
            def _():
                self.down(n, self.z, True).start()

            self.along_y(n, self.z, self.y, True).start()

    def spread(self, n, block):
        self.along_x(n, block, self.x).start()
        self.core_first(n, block, self.c).start()

    def from_z(self, n, distance):
        for way in (1, -1):
            zb = self.z - way * distance

            @pl.when(jnp.logical_and(zb >= 0, zb < Z))
            def _():
                self.up(n, zb).wait_recv()
                if way == 1:

                    @pl.when(self.z < Z - 1)
                    def _():
                        self.up(n, zb).start()
                else:

                    @pl.when(self.z > 0)
                    def _():
                        self.down(n, zb).start()

                self.along_y(n, zb, self.y).start()
                self.spread(n, zb * Y + self.y)

    def from_y(self, n, distance):
        for way in (1, -1) if distance else (1,):
            zb = self.z - way * distance

            @pl.when(jnp.logical_and(zb >= 0, zb < Z))
            def _():
                self.along_y(n, zb, 1 - self.y).wait_recv()
                self.spread(n, zb * Y + 1 - self.y)

    def each_block(self, do):
        def at(zb, yb):
            @pl.when(jnp.logical_and(zb >= 0, zb < Z))
            def _():
                for n in range(len(self.arrays)):
                    do(n, zb * Y + yb)

        for distance in range(Z):
            for way in (1, -1) if distance else (1,):
                if distance:
                    at(self.z - way * distance, self.y)
                at(self.z - way * distance, 1 - self.y)

    def end(self):
        def come_along_x(n, block):
            self.along_x(n, block, 1 - self.x).wait_recv()
            self.core_second(n, block, self.c).start()

        def finish(n, block):
            self.core_first(n, block, 1 - self.c).wait_recv()
            self.core_second(n, block, 1 - self.c).wait_recv()
            self.along_x(n, block, self.x).wait_send()
            self.core_first(n, block, self.c).wait_send()
            self.core_second(n, block, self.c).wait_send()

        self.each_block(come_along_x)
        self.each_block(finish)
        for n in range(len(self.arrays)):
            self.own_copy(n).wait()
            for zb in range(Z):
                self.along_y(n, zb, self.y).wait_send()

                @pl.when(jnp.logical_and(self.z < Z - 1, zb <= self.z))
                def _():
                    self.up(n, zb).wait_send()

                @pl.when(jnp.logical_and(self.z > 0, zb >= self.z))
                def _():
                    self.down(n, zb).wait_send()


def gathering_semaphores(count):
    dma = lambda *s: pltpu.SemaphoreType.DMA((count * PARTS,) + s)
    size = Z * Y
    return [dma()] + [dma(Z)] * 5 + [dma(size)] * 2 + [dma(size, 2)] * 2


def whole_shapes(blocks):
    return [jax.ShapeDtypeStruct((b.shape[0] * Z * Y, b.shape[1]), b.dtype) for b in blocks]


def gather_kernel(count, *refs):
    gathering = Gathering(refs[:count], refs[count : 2 * count], refs[2 * count :])
    parts = range(len(gathering.arrays))
    gathering.begin()
    for distance in range(1, Z):
        for n in parts:
            gathering.from_z(n, distance)
            gathering.from_y(n, distance - 1)
    for n in parts:
        gathering.from_y(n, Z - 1)
    gathering.end()


def gather_call(*blocks):
    count = len(blocks)
    return pl.pallas_call(
        functools.partial(gather_kernel, count),
        in_specs=[pl.BlockSpec(memory_space=pl.ANY)] * count,
        out_specs=[pl.BlockSpec(memory_space=pl.ANY)] * count,
        out_shape=whole_shapes(blocks),
        scratch_shapes=gathering_semaphores(count),
        compiler_params=pltpu.CompilerParams(collective_id=0, has_side_effects=True),
        name="gather_rows",
    )(*blocks)


Z_STEPS = {at: (n % 4, 1 + n // 4) for n, at in enumerate((2, 4, 6, 7, 9, 11, 13, 14, 16, 18, 20, 21))}
Y_STEPS = {at: (n % 4, n // 4) for n, at in enumerate((3, 5, 7, 8, 10, 12, 14, 15, 17, 19, 21, 22))}


def forward_kernel(
    spans,
    blocks,
    block_ref,
    key_ref,
    query_ref,
    edge_ref,
    key_edge_ref,
    query_edge_ref,
    taps_ref,
    key_taps_ref,
    query_taps_ref,
    inside_ref,
    outside_ref,
    steps_ref,
    decay_ref,
    rows_ref,
    factor_ref,
    mask_ref,
    *refs,
):
    block_refs, refs = refs[:blocks], refs[blocks:]
    inner_out, local_out, state_out, key_out, query_out, *refs = refs
    whole_refs, refs = refs[:blocks], refs[blocks:]
    scores, key_turned, query_both, room, *sems = refs
    room[:8, :] = jnp.zeros((8, LANES), f32)
    pair = pl.program_id(0)
    if blocks:
        gathering = Gathering(block_refs, whole_refs, sems)
        pl.when(pair == 0)(gathering.begin)
        for at, what in Z_STEPS.items():
            pl.when(pair == at)(functools.partial(gathering.from_z, *what))
        for at, what in Y_STEPS.items():
            pl.when(pair == at)(functools.partial(gathering.from_y, *what))

    @pl.when(pair == 0)
    def _():
        for src, edge, taps, out in (
            (key_ref, key_edge_ref, key_taps_ref, key_out),
            (query_ref, query_edge_ref, query_taps_ref, query_out),
        ):
            pre = conv_pre(
                src[...], conv_shifts(src[...], edge[...], inside_ref, outside_ref, room), taps[...]
            )
            out[...] = pre * sigmoid(pre)
        for k in range(spans):
            rows = pl.ds(k * SPAN, SPAN)
            keys, queries = key_out[rows, :], query_out[rows, :]
            kh, kl = split(keys)
            qh, ql = split(queries)
            query_both[rows, :] = jnp.concatenate([qh, ql], axis=1)
            scores[k] = mm_nt(
                jnp.concatenate([qh, ql], axis=1), jnp.concatenate([kh, kh], axis=1)
            ) + mm_nt(qh, kl)
            th, tl = split(keys.T)
            key_turned[k, 0] = th
            key_turned[k, 1] = tl

    block = block_ref[...]
    pre = conv_pre(
        block, conv_shifts(block, edge_ref[...], inside_ref, outside_ref, room), taps_ref[...]
    )
    inner = pre * sigmoid(pre)
    inner_out[...] = inner
    turned, unused, steps = pair_columns(steps_ref[...], pair)
    unused, enter, leave = pair_columns(decay_ref[...], pair)
    scaled = steps * inner
    leaving = leave * scaled
    lane = lax.broadcasted_iota(jnp.int32, (HALF, LANES), 1)
    head_rows = [head_row(rows_ref[...], 2 * pair + a) for a in range(2)]
    factor = pair_rows(factor_ref[...], pair)
    state = None
    for k in range(spans):
        at = k * SPAN
        sh, sl = split(scaled[at : at + SPAN])
        both = jnp.concatenate([sh, sl], axis=1)
        parts = []
        for half in range(2):
            width = HALF * (half + 1)
            here, there = pl.ds(half * HALF, HALF), pl.ds(0, width)
            both_heads = []
            for a in range(2):
                row = head_rows[a][:, at : at + width]
                column = turned[at + half * HALF : at + (half + 1) * HALF, a : a + 1]
                decay = jnp.exp(jnp.minimum(column - row, mask_ref[k, here, there]))
                both_heads.append(decay * scores[k, here, there])
            wh, wl = split(jnp.concatenate(both_heads, axis=0))
            wide = mm(wh, both[:width])
            wide = wide[:, :LANES] + wide[:, LANES:] + mm(wl, sh[:width])
            parts.append(jnp.where(lane < HD, wide[:HALF], wide[HALF:]))
        local = jnp.concatenate(parts, axis=0)
        ph, pw = split(leaving[at : at + SPAN])
        fresh = mm(key_turned[k, 0], jnp.concatenate([ph, pw], axis=1))
        fresh = fresh[:, :LANES] + fresh[:, LANES:] + mm(key_turned[k, 1], ph)
        if state is None:
            state = fresh
        else:
            th, tl = split(state)
            q2 = query_both[pl.ds(at, SPAN), :]
            carried = mm(q2, jnp.concatenate([th, th], axis=0)) + mm(q2[:, :DS], tl)
            local = local + enter[at : at + SPAN] * carried
            state = factor[k : k + 1] * state + fresh
        state_out[k] = state
        local_out[pl.ds(at, SPAN), :] = local
    if blocks:

        @pl.when(pair == PAIRS - 1)
        def _():
            for n in range(blocks * PARTS):
                gathering.from_y(n, Z - 1)
            gathering.end()


def forward_call(
    spans, mixed, edge, taps, inside, outside, steps, decay, rows, factor, mask, blocks
):
    count = spans * SPAN
    at_pair = lambda n: pl.BlockSpec((n, LANES), lambda i: (0, i))
    at_key = lambda n: pl.BlockSpec((n, LANES), lambda i: (0, PAIRS))
    at_query = lambda n: pl.BlockSpec((n, LANES), lambda i: (0, PAIRS + 1))
    whole = lambda *s: pl.BlockSpec(s, lambda i: (0,) * len(s))
    remote = dict(collective_id=5, has_side_effects=True) if blocks else {}
    return pl.pallas_call(
        functools.partial(forward_kernel, spans, len(blocks)),
        grid=(PAIRS,),
        in_specs=[
            at_pair(count),
            at_key(count),
            at_query(count),
            at_pair(8),
            at_key(8),
            at_query(8),
            at_pair(8),
            at_key(8),
            at_query(8),
            whole(3, count, LANES),
            whole(3, 8, LANES),
            whole(count, LANES),
            whole(count, LANES),
            pl.BlockSpec((8, count), lambda i: (i // 4, 0)),
            whole(8, LANES),
            whole(spans, SPAN, SPAN),
        ]
        + [pl.BlockSpec(memory_space=pl.ANY)] * len(blocks),
        out_specs=[
            at_pair(count),
            at_pair(count),
            pl.BlockSpec((spans, DS, LANES), lambda i: (0, 0, i)),
            whole(count, LANES),
            whole(count, LANES),
        ]
        + [pl.BlockSpec(memory_space=pl.ANY)] * len(blocks),
        out_shape=[
            jax.ShapeDtypeStruct((count, DI), f32),
            jax.ShapeDtypeStruct((count, DI), f32),
            jax.ShapeDtypeStruct((spans, DS, DI), f32),
            jax.ShapeDtypeStruct((count, DS), f32),
            jax.ShapeDtypeStruct((count, DS), f32),
        ]
        + whole_shapes(blocks),
        scratch_shapes=[
            pltpu.VMEM((spans, SPAN, SPAN), f32),
            pltpu.VMEM((spans, 2, DS, SPAN), bf16),
            pltpu.VMEM((count, 2 * DS), bf16),
            pltpu.VMEM((count + 8, LANES), f32),
        ]
        + (gathering_semaphores(len(blocks)) if blocks else []),
        compiler_params=pltpu.CompilerParams(vmem_limit_bytes=VMEM_LIMIT, **remote),
        cost_estimate=pl.CostEstimate(flops=1, bytes_accessed=1, transcendentals=0),
        name="recurrence_forward",
    )(
        mixed,
        mixed,
        mixed,
        edge,
        edge,
        edge,
        taps,
        taps,
        taps,
        inside,
        outside,
        steps,
        decay,
        rows,
        factor,
        mask,
        *blocks,
    )


def norm_kernel(
    local_ref,
    inner_ref,
    gate_ref,
    back_ref,
    query_ref,
    state_ref,
    reach_ref,
    spread_ref,
    skip_ref,
    gain_ref,
    out_ref,
    mixer_grad_ref,
    gate_grad_ref,
    gain_grad_ref,
    dots_ref,
    summary_ref,
    most_ref,
    mixed_y,
    state_both,
    reach_wide,
):
    step = pl.program_id(0)
    chunks = [pl.ds(c * NORM_COLS, NORM_COLS) for c in range(DI // NORM_COLS)]

    @pl.when(step == 0)
    def _():
        sh, sl = split(state_ref[...])
        state_both[0] = sh
        state_both[1] = sl
        gain_grad_ref[...] = jnp.zeros_like(gain_grad_ref)
        summary_ref[...] = jnp.zeros_like(summary_ref)
        most_ref[...] = jnp.zeros_like(most_ref)

    qh, ql = split(query_ref[...])
    query_both = jnp.concatenate([qh, ql], axis=1)
    rh, rl = split(reach_ref[...])
    reach_both = jnp.concatenate([rh, rl], axis=1)
    squares = jnp.zeros((NORM_ROWS, 1), f32)
    mixes = jnp.zeros((NORM_ROWS, 1), f32)
    for cols in chunks:
        sh, sl = state_both[0, :, cols], state_both[1, :, cols]
        spread = spread_ref[:, cols]
        reach = mm(reach_both, jnp.concatenate([spread, spread], axis=0))
        reach_wide[:, cols] = reach
        carried = mm(query_both, jnp.concatenate([sh, sh], axis=0)) + mm(qh, sl)
        y = local_ref[:, cols] + reach * carried
        mixed_y[:, cols] = y
        mixer = y + skip_ref[0:1, cols] * inner_ref[:, cols]
        gate = gate_ref[:, cols]
        gated = mixer * (gate * sigmoid(gate))
        squares = squares + jnp.sum(gated * gated, axis=1, keepdims=True)
        mixes = mixes + jnp.sum(
            gated * (back_ref[:, cols] * gain_ref[0:1, cols]), axis=1, keepdims=True
        )
    scale = lax.rsqrt(squares * (1.0 / DI) + norm_eps)
    pull = scale * mixes * (1.0 / DI)
    query_turned = query_ref[...].T
    th, tl = split(query_turned)
    dots = jnp.zeros((NORM_ROWS, LANES), f32)
    for cols in chunks:
        y = mixed_y[:, cols]
        mixer = y + skip_ref[0:1, cols] * inner_ref[:, cols]
        gate = gate_ref[:, cols]
        opened = sigmoid(gate)
        silu = gate * opened
        unit = mixer * silu * scale
        gain = gain_ref[0:1, cols]
        back = back_ref[:, cols]
        out_ref[:, cols] = (unit * gain).astype(bf16)
        gain_grad_ref[0:1, cols] += jnp.sum(back * unit, axis=0, keepdims=True)
        gated_grad = scale * (back * gain - unit * pull)
        mixer_grad = gated_grad * silu
        mixer_grad_ref[:, cols] = mixer_grad
        gate_grad = gated_grad * mixer * (opened * (1.0 + gate * (1.0 - opened)))
        gate_grad_ref[:, cols] = gate_grad.astype(bf16)
        most = jnp.max(jnp.abs(gate_grad).reshape(NORM_ROWS // 8, 8, NORM_COLS), axis=0)
        for c in range(NORM_COLS // LANES):
            most_ref[...] = jnp.maximum(most_ref[...], most[:, c * LANES : (c + 1) * LANES])
        dh, dl = split(mixer_grad * y)
        spread = spread_ref[:, cols]
        dots = dots + mm_nt(dh, spread) + mm_nt(dl, spread)
        mh, ml = split(reach_wide[:, cols] * mixer_grad)
        summary_ref[:, cols] += (
            mm(jnp.concatenate([th, tl], axis=1), jnp.concatenate([mh, mh], axis=0)) + mm(th, ml)
        )
    dots_ref[...] = dots


def norm_call(local, inner, gate, back, queries, state_in, reach, spread, skip, gain):
    count = local.shape[0]
    rows = lambda n: pl.BlockSpec((NORM_ROWS, n), lambda i: (i, 0))
    whole = lambda *s: pl.BlockSpec(s, lambda i: (0,) * len(s))
    return pl.pallas_call(
        norm_kernel,
        grid=(count // NORM_ROWS,),
        in_specs=[
            rows(DI),
            rows(DI),
            rows(DI),
            rows(DI),
            rows(DS),
            whole(DS, DI),
            rows(LANES),
            whole(LANES, DI),
            whole(8, DI),
            whole(8, DI),
        ],
        out_specs=[
            rows(DI),
            rows(DI),
            rows(DI),
            whole(8, DI),
            rows(LANES),
            whole(DS, DI),
            whole(8, LANES),
        ],
        out_shape=[
            jax.ShapeDtypeStruct((count, DI), bf16),
            jax.ShapeDtypeStruct((count, DI), f32),
            jax.ShapeDtypeStruct((count, DI), bf16),
            jax.ShapeDtypeStruct((8, DI), f32),
            jax.ShapeDtypeStruct((count, LANES), f32),
            jax.ShapeDtypeStruct((DS, DI), f32),
            jax.ShapeDtypeStruct((8, LANES), f32),
        ],
        scratch_shapes=[
            pltpu.VMEM((NORM_ROWS, DI), f32),
            pltpu.VMEM((2, DS, DI), bf16),
            pltpu.VMEM((NORM_ROWS, DI), f32),
        ],
        compiler_params=pltpu.CompilerParams(vmem_limit_bytes=VMEM_LIMIT),
        cost_estimate=pl.CostEstimate(flops=1, bytes_accessed=1, transcendentals=0),
        name="gated_norm",
    )(local, inner, gate, back, queries, state_in, reach, spread, skip, gain)


class Agreement:
    def __init__(self, values_ref, out_ref, most, near, sent, landed):
        self.values_ref, self.out_ref = values_ref, out_ref
        self.most, self.near, self.sent, self.landed = most, near, sent, landed
        f, ctx = lax.axis_index("fsdp"), lax.axis_index("ctx")
        z, y, x, c = f // Y, lax.rem(f, Y), ctx // 2, lax.rem(ctx, 2)
        at = lambda z, y, x, c: (z * Y + y, x * 2 + c)
        self.phases = (
            [at(lax.rem(z + d, Z), y, x, c) for d in range(1, Z)],
            [at(z, y, x, 1 - c)],
            [at(z, y, 1 - x, c), at(z, 1 - y, x, c), at(z, 1 - y, 1 - x, c)],
        )

    def copies(self, phase):
        return [
            pltpu.make_async_remote_copy(
                src_ref=self.most.at[phase],
                dst_ref=self.near.at[phase, n],
                send_sem=self.sent.at[phase, n],
                recv_sem=self.landed.at[phase, n],
                device_id=partner,
                device_id_type=MESH,
            )
            for n, partner in enumerate(self.phases[phase])
        ]

    def begin(self):
        barrier = pltpu.get_barrier_semaphore()
        partners = [partner for phase in self.phases for partner in phase]
        for partner in partners:
            pl.semaphore_signal(barrier, inc=1, device_id=partner, device_id_type=MESH)
        self.most[0] = jnp.full((8, LANES), jnp.max(jnp.abs(self.values_ref[...])), f32)
        pl.semaphore_wait(barrier, len(partners))
        for copy in self.copies(0):
            copy.start()

    def arrived(self, phase):
        for copy in self.copies(phase):
            copy.wait()
        most = self.most[phase]
        for n in range(len(self.phases[phase])):
            most = jnp.maximum(most, self.near[phase, n])
        return most

    def go_on(self, phase):
        self.most[phase] = self.arrived(phase - 1)
        for copy in self.copies(phase):
            copy.start()

    def end(self):
        self.out_ref[0, 0] = jnp.max(self.arrived(2))


def agreement_scratch():
    return [
        pltpu.VMEM((3, 8, LANES), f32),
        pltpu.VMEM((3, 3, 8, LANES), f32),
        pltpu.SemaphoreType.DMA((3, 3)),
        pltpu.SemaphoreType.DMA((3, 3)),
    ]


def backward_kernel(spans, first, pairs, last, agree, *refs):
    (
        block_ref,
        edge_ref,
        taps_ref,
        inside_ref,
        inside_back_ref,
        outside_ref,
        keys_ref,
        queries_ref,
        back_ref,
        steps_ref,
        decay_ref,
        rows_ref,
        factor_ref,
        start_ref,
        mask_ref,
        states_ref,
        state_in_ref,
        state_back_ref,
        skip_ref,
        *refs,
    ) = refs
    if agree:
        most_ref, *refs = refs
    if last:
        dots_ref, raw_ref, params_ref, *refs = refs
        old_scores_grad, old_key_grad, old_query_grad, old_steps, old_heads, *refs = refs
    grad_out, top_out, tail_out, taps_out, most_out, *refs = refs
    scores_grad, key_grad, query_grad, steps_out, heads_out, *refs = refs
    if last:
        sums_out, *refs = refs
    if agree:
        agreed_out, *refs = refs
    scores, key_both, query_both, query_turned, room, columns, *refs = refs
    step = pl.program_id(0)
    if agree:
        agreement = Agreement(most_ref, agreed_out, *refs)
        pl.when(step == 0)(agreement.begin)
        pl.when(step == 3)(functools.partial(agreement.go_on, 1))
        pl.when(step == 6)(functools.partial(agreement.go_on, 2))
        pl.when(step == pairs - 1)(agreement.end)
    pair = step + first
    lane = lax.broadcasted_iota(jnp.int32, (SPAN, LANES), 1)

    @pl.when(step == 0)
    def _():
        if last:
            key_grad[...] = old_key_grad[...]
            query_grad[...] = old_query_grad[...]
            scores_grad[...] = old_scores_grad[...]
            steps_out[...] = old_steps[...]
            heads_out[...] = old_heads[...]
        else:
            key_grad[...] = jnp.zeros_like(key_grad)
            query_grad[...] = jnp.zeros_like(query_grad)
            scores_grad[...] = jnp.zeros_like(scores_grad)
            steps_out[...] = jnp.zeros_like(steps_out)
            heads_out[...] = jnp.zeros_like(heads_out)
        for n, (packed, shift) in enumerate(
            ((steps_ref, LANES // 2), (decay_ref, 0), (decay_ref, LANES // 2))
        ):
            values = pltpu.roll(packed[...], shift, 1) if shift else packed[...]
            columns[n] = jnp.concatenate(split(values), axis=1)
        for k in range(spans):
            rows = pl.ds(k * SPAN, SPAN)
            keys, queries = keys_ref[rows, :], queries_ref[rows, :]
            kh, kl = split(keys)
            qh, ql = split(queries)
            key_both[rows, :] = jnp.concatenate([kh, kl], axis=1)
            query_both[rows, :] = jnp.concatenate([qh, ql], axis=1)
            scores[k] = mm_nt(
                jnp.concatenate([kh, kl], axis=1), jnp.concatenate([qh, qh], axis=1)
            ) + mm_nt(kh, ql)
            th, tl = split(queries.T)
            query_turned[k, 0] = th
            query_turned[k, 1] = tl

    def conv_back(conved_grad, block, shifted, pre):
        opened = sigmoid(pre)
        pre_grad = conved_grad * (opened * (1.0 + pre * (1.0 - opened)))
        count = block.shape[0]
        taps = taps_ref[...]
        total = taps[3:4] * pre_grad
        sums = [None] * 8
        sums[3] = jnp.sum(pre_grad * block, axis=0, keepdims=True)
        sums[4] = jnp.sum(pre_grad, axis=0, keepdims=True)
        room[pl.ds(0, count), :] = pre_grad
        room[pl.ds(count, 8), :] = jnp.zeros((8, LANES), f32)
        for j in range(1, CONV):
            total = total + taps[3 - j : 4 - j] * (
                inside_back_ref[j - 1] * room[pl.ds(j, count), :]
            )
            sums[3 - j] = jnp.sum(pre_grad * shifted[j - 1], axis=0, keepdims=True)
        grad_out[...] = total.astype(bf16)
        tail_out[...] = total[count - 8 :]
        most_out[...] = jnp.max(jnp.abs(total).reshape(count // 8, 8, LANES), axis=0)
        top_out[...] = pre_grad[:8]
        return sums

    zero_row = jnp.zeros((1, LANES), f32)

    def of_conv():
        block = block_ref[...]
        room[:8, :] = jnp.zeros((8, LANES), f32)
        shifted = conv_shifts(block, edge_ref[...], inside_ref, outside_ref, room)
        return block, shifted, conv_pre(block, shifted, taps_ref[...])

    @pl.when(step < pairs)
    def _():
        block, shifted, pre = of_conv()
        head_rows = [head_row(rows_ref[...], 2 * pair + a) for a in range(2)]
        factor = pair_rows(factor_ref[...], pair)
        start = pair_rows(start_ref[...], pair)
        skip = pair_rows(skip_ref[...], pair)
        inner = pre * sigmoid(pre)
        back = back_ref[...]
        turned = pltpu.roll(steps_ref[...], lax.rem(LANES - 2 * pair, LANES), 1)
        steps, enter, leave = (spread_pair(columns[n], pair) for n in range(3))
        scaled = steps * inner
        leaving = leave * scaled
        entering = enter * back
        state_in = state_in_ref[...]
        state_back = state_back_ref[...]
        scaled_grads = [None] * spans
        ends = [zero_row] * 8
        for k in reversed(range(spans)):
            at = k * SPAN
            rows = pl.ds(at, SPAN)
            bh, bl = split(back[at : at + SPAN])
            both = jnp.concatenate([bh, bl], axis=1)
            sh, sl = split(scaled[at : at + SPAN])
            zero = jnp.zeros((SPAN, LANES), bf16)
            sl_turned = pltpu.roll(sl.astype(f32), HD, 1).astype(bf16)
            bh_turned = pltpu.roll(bh.astype(f32), HD, 1).astype(bf16)
            lefts, rights = [], []
            for a in range(2):
                mine = (lane < HD) if a == 0 else (lane >= HD)
                of_mine = lambda one, other: jnp.where(mine, one, other)
                lefts.append(
                    jnp.concatenate([of_mine(sh, sl_turned), of_mine(sh, zero)], axis=1)
                )
                rights.append(
                    jnp.concatenate([of_mine(bh, bh_turned), of_mine(bl, zero)], axis=1)
                )
            parts = []
            for half in range(2):
                low = half * HALF
                width = SPAN - low
                here = pl.ds(low, HALF)
                there = pl.ds(low, width)
                both_heads = []
                grads = None
                for a in range(2):
                    row = head_rows[a][:, at + low : at + low + width]
                    column = turned[at + low : at + low + HALF, a : a + 1]
                    decay = jnp.exp(jnp.minimum(row - column, mask_ref[k, here, there]))
                    both_heads.append(decay * scores[k, here, there])
                    grad = decay * mm_nt(lefts[a][low : low + HALF], rights[a][low:])
                    grads = grad if grads is None else grads + grad
                scores_grad[k, here, there] += grads
                wh, wl = split(jnp.concatenate(both_heads, axis=0))
                wide = mm(wh, both[low:])
                wide = wide[:, :LANES] + wide[:, LANES:] + mm(wl, bh[low:])
                parts.append(jnp.where(lane[:HALF] < HD, wide[:HALF], wide[HALF:]))
            scaled_grad = jnp.concatenate(parts, axis=0)
            gh, gl = split(state_back)
            k2 = key_both[rows, :]
            scaled_grad = scaled_grad + leave[at : at + SPAN] * (
                mm(k2, jnp.concatenate([gh, gh], axis=0)) + mm(k2[:, :DS], gl)
            )
            scaled_grads[k] = scaled_grad
            lh, ll = split(leaving[at : at + SPAN])
            key_grad[rows, :] += mm_nt(
                jnp.concatenate([lh, ll], axis=1), jnp.concatenate([gh, gh], axis=1)
            ) + mm_nt(lh, gl)
            after = states_ref[k] + start[k + 1 : k + 2] * state_in
            ends[k] = jnp.sum(state_back * after, axis=0, keepdims=True)
            before = start[k : k + 1] * state_in
            if k > 0:
                before = before + states_ref[k - 1]
            th, tl = split(before)
            eh, el = split(entering[at : at + SPAN])
            query_grad[rows, :] += mm_nt(
                jnp.concatenate([eh, el], axis=1), jnp.concatenate([th, th], axis=1)
            ) + mm_nt(eh, tl)
            if k > 0:
                more = mm(query_turned[k, 0], jnp.concatenate([eh, el], axis=1))
                state_back = (
                    factor[k : k + 1] * state_back
                    + more[:, :LANES]
                    + more[:, LANES:]
                    + mm(query_turned[k, 1], eh)
                )
        scaled_grad = jnp.concatenate(scaled_grads, axis=0)
        target = lax.broadcasted_iota(jnp.int32, (LANES, LANES), 1)
        source = lax.broadcasted_iota(jnp.int32, (LANES, LANES), 0)
        place = (target == 2 * pair + source // HD).astype(bf16)
        dh, dl = split(inner * scaled_grad)
        steps_out[...] += mm(dh, place) + mm(dl, place)
        sums = conv_back(steps * scaled_grad + skip[0:1] * back, block, shifted, pre)
        ends[4] = jnp.sum(back * inner, axis=0, keepdims=True)
        taps_out[...] = jnp.concatenate([zero_row if s is None else s for s in sums], axis=0)
        eh, el, ew = split_three(jnp.concatenate(ends, axis=0))
        heads_out[...] += mm(eh, place) + mm(el, place) + mm(ew, place)

    if not last:
        return

    def of_scores(grad_ref, ones_ref, transposed):
        for k in range(spans):
            rows = pl.ds(k * SPAN, SPAN)
            grad = scores_grad[k]
            gh, gl = split(grad.T if transposed else grad)
            ones = ones_ref[rows, :]
            wide = mm(gh, ones)
            grad_ref[rows, :] += wide[:, :DS] + wide[:, DS:] + mm(gl, ones[:, :DS])

    @pl.when(jnp.logical_and(step >= pairs, step < pairs + 2))
    def _():
        @pl.when(step == pairs)
        def _():
            of_scores(key_grad, query_both, False)

        @pl.when(step == pairs + 1)
        def _():
            of_scores(query_grad, key_both, True)

        block, shifted, pre = of_conv()
        grad = jnp.where(step == pairs, key_grad[...], query_grad[...])
        sums = conv_back(grad, block, shifted, pre)
        taps_out[...] = jnp.concatenate([zero_row if s is None else s for s in sums], axis=0)

    @pl.when(step == pairs + 2)
    def _():
        tall = lax.broadcasted_iota(jnp.int32, (SPAN, SPAN), 0)
        wide = lax.broadcasted_iota(jnp.int32, (SPAN, SPAN), 1)
        upper = (tall <= wide).astype(bf16)
        known = lane < NH
        rate = params_ref[1:2]
        delta, decay, most = zero_row, zero_row, zero_row
        for k in range(spans):
            rows = pl.ds(k * SPAN, SPAN)
            steps = jnp.where(known, pltpu.roll(steps_ref[rows, :], LANES // 2, 1), 0.0)
            step_dots = steps_out[rows, :]
            cumul_grad = dots_ref[rows, :] - steps * step_dots
            parts = mm(upper, jnp.concatenate(split_three(cumul_grad), axis=1))
            decay_grad = parts[:, :LANES] + parts[:, LANES : 2 * LANES] + parts[:, 2 * LANES :]
            decay_grad = decay_grad + heads_out[k : k + 1]
            raw = jnp.where(known, raw_ref[rows, :], 0.0) + params_ref[0:1]
            raw_grad = (step_dots + rate * decay_grad) * sigmoid(raw)
            raw_grad = jnp.where(known, raw_grad, 0.0)
            grad_out[rows, :] = raw_grad.astype(bf16)
            most = jnp.maximum(most, jnp.max(jnp.abs(raw_grad), axis=0, keepdims=True))
            delta = delta + jnp.sum(raw_grad, axis=0, keepdims=True)
            decay = decay + jnp.sum(rate * steps * decay_grad, axis=0, keepdims=True)
        sums_out[...] = jnp.concatenate(
            [delta, decay, heads_out[4:5], most, jnp.zeros((4, LANES), f32)], axis=0
        )

    @pl.when(step > pairs + 2)
    def _():
        grad_out[...] = jnp.zeros_like(grad_out)


def backward_call(spans, first, pairs, columns, shared, finish=None, most=None):
    count = spans * SPAN
    last = finish is not None
    clip_block = lambda i: jnp.minimum(i + first, CONVD // LANES - 1)
    clip = lambda i: jnp.minimum(i, pairs - 1) + first
    at_block = lambda n: pl.BlockSpec((n, LANES), lambda i: (0, clip_block(i)))
    at_pair = lambda n: pl.BlockSpec((n, LANES), lambda i: (0, clip(i)))
    out_block = lambda n: pl.BlockSpec((n, LANES), lambda i: (0, i))
    whole = lambda *s: pl.BlockSpec(s, lambda i: (0,) * len(s))
    accumulators = [
        (spans, SPAN, SPAN),
        (count, DS),
        (count, DS),
        (count, LANES),
        (8, LANES),
    ]
    wide = columns * LANES
    side = (pairs + 2 if last else pairs) * LANES
    side_block = lambda: pl.BlockSpec(
        (8, LANES), lambda i: (0, jnp.minimum(i, side // LANES - 1))
    )
    in_specs = [
        at_block(count),
        at_block(8),
        at_block(8),
        whole(CONV - 1, count, LANES),
        whole(CONV - 1, count, LANES),
        whole(CONV - 1, 8, LANES),
        whole(count, DS),
        whole(count, DS),
        at_pair(count),
        whole(count, LANES),
        whole(count, LANES),
        pl.BlockSpec((8, count), lambda i: (clip(i) // 4, 0)),
        whole(8, LANES),
        whole(8, LANES),
        whole(spans, SPAN, SPAN),
        pl.BlockSpec((spans, DS, LANES), lambda i: (0, 0, clip(i))),
        at_pair(DS),
        at_pair(DS),
        whole(8, LANES),
    ]
    out_specs = [out_block(count)] + [side_block()] * 4 + [whole(*s) for s in accumulators]
    out_shape = [jax.ShapeDtypeStruct((count, wide), bf16)]
    out_shape += [jax.ShapeDtypeStruct((8, side), f32)] * 4
    out_shape += [jax.ShapeDtypeStruct(s, f32) for s in accumulators]
    operands = list(shared)
    scratch, remote = [], {}
    if most is not None:
        in_specs += [whole(8, LANES)]
        operands += [most]
        scratch, remote = agreement_scratch(), dict(collective_id=6, has_side_effects=True)
    if last:
        dots, mixed, params, earlier = finish
        in_specs += [
            whole(count, LANES),
            pl.BlockSpec((count, LANES), lambda i: (0, CONVD // LANES)),
            whole(8, LANES),
        ]
        in_specs += [whole(*s) for s in accumulators]
        operands += [dots, mixed, params, *earlier]
        out_specs += [whole(8, LANES)]
        out_shape += [jax.ShapeDtypeStruct((8, LANES), f32)]
    if most is not None:
        out_specs += [pl.BlockSpec(memory_space=pltpu.SMEM)]
        out_shape += [jax.ShapeDtypeStruct((1, 1), f32)]
    return pl.pallas_call(
        functools.partial(backward_kernel, spans, first, pairs, last, most is not None),
        grid=(columns,),
        in_specs=in_specs,
        out_specs=out_specs,
        out_shape=out_shape,
        scratch_shapes=[
            pltpu.VMEM((spans, SPAN, SPAN), f32),
            pltpu.VMEM((count, 2 * DS), bf16),
            pltpu.VMEM((count, 2 * DS), bf16),
            pltpu.VMEM((spans, 2, DS, SPAN), bf16),
            pltpu.VMEM((count + 8, LANES), f32),
            pltpu.VMEM((3, count, 2 * LANES), bf16),
        ]
        + scratch,
        compiler_params=pltpu.CompilerParams(vmem_limit_bytes=VMEM_LIMIT, **remote),
        cost_estimate=pl.CostEstimate(flops=1, bytes_accessed=1, transcendentals=0),
        name="recurrence_backward",
    )(*operands)


def sum_kernel(in_ref, out_ref, near, far, whole, sent, landed):
    f, ctx = lax.axis_index("fsdp"), lax.axis_index("ctx")
    fsdp_size, ctx_size = lax.axis_size("fsdp"), lax.axis_size("ctx")
    part = in_ref.shape[0] // fsdp_size
    in_ctx = [(f, lax.rem(ctx + d, ctx_size)) for d in range(1, ctx_size)]
    in_fsdp = [(lax.rem(f + d, fsdp_size), ctx) for d in range(1, fsdp_size)]
    barrier = pltpu.get_barrier_semaphore()
    for partner in in_ctx + in_fsdp:
        pl.semaphore_signal(barrier, inc=1, device_id=partner, device_id_type=MESH)
    pl.semaphore_wait(barrier, len(in_ctx) + len(in_fsdp))

    def exchange(phase, partners, source, target):
        copies = []
        for n, partner in enumerate(partners):
            copies.append(
                pltpu.make_async_remote_copy(
                    src_ref=source(partner),
                    dst_ref=target,
                    send_sem=sent.at[phase, n],
                    recv_sem=landed.at[phase, n],
                    device_id=partner,
                    device_id_type=MESH,
                )
            )
            copies[-1].start()
        return copies

    copies = exchange(0, in_ctx, lambda partner: in_ref, near.at[ctx])
    near[pl.ds(ctx, 1)] = in_ref[...][None]
    for copy in copies:
        copy.wait()
    whole[...] = jnp.sum(near[...], axis=0)
    mine = pl.ds(pl.multiple_of(f * part, 8), part)
    copies = exchange(
        1, in_fsdp, lambda partner: whole.at[pl.ds(pl.multiple_of(partner[0] * part, 8), part)], far.at[f]
    )
    far[pl.ds(f, 1)] = whole[mine, :][None]
    for copy in copies:
        copy.wait()
    out_ref[mine, :] = jnp.sum(far[...], axis=0)
    for copy in exchange(2, in_fsdp, lambda partner: out_ref.at[mine], out_ref.at[mine]):
        copy.wait()


def sum_everywhere(value):
    if not on_small_slice():
        return lax.psum(value, ("fsdp", "ctx"))
    fsdp_size, ctx_size = lax.axis_size("fsdp"), lax.axis_size("ctx")
    block = 8 * LANES * fsdp_size
    rows = -(-value.shape[0] // block) * block // LANES
    shape = (rows, LANES)
    padded_value = jnp.pad(value, (0, rows * LANES - value.shape[0])).reshape(shape)
    peers = max(fsdp_size, ctx_size) - 1
    out = pl.pallas_call(
        sum_kernel,
        in_specs=[pl.BlockSpec(memory_space=pltpu.VMEM)],
        out_specs=pl.BlockSpec(memory_space=pltpu.VMEM),
        out_shape=jax.ShapeDtypeStruct(shape, f32),
        scratch_shapes=[
            pltpu.VMEM((ctx_size,) + shape, f32),
            pltpu.VMEM((fsdp_size, rows // fsdp_size, LANES), f32),
            pltpu.VMEM(shape, f32),
            pltpu.SemaphoreType.DMA((3, peers)),
            pltpu.SemaphoreType.DMA((3, peers)),
        ],
        compiler_params=pltpu.CompilerParams(collective_id=4, has_side_effects=True),
        cost_estimate=pl.CostEstimate(flops=1, bytes_accessed=1, transcendentals=0),
        name="sum_everywhere",
    )(padded_value)
    return out.reshape(-1)[: value.shape[0]]


FILL_COLS = 256


def block_out_kernel(mixer_ref, whole_ref, tokens_ref, out_ref):
    projected = mm(mixer_ref[...], whole_ref[...])
    out_ref[...] = (tokens_ref[...].astype(f32) + projected).astype(bf16)


def block_out_call(mixer_low, whole_out, tokens):
    count, width = tokens.shape
    columns = lambda n: pl.BlockSpec((n, FILL_COLS), lambda j: (0, j))
    return pl.pallas_call(
        block_out_kernel,
        grid=(width // FILL_COLS,),
        in_specs=[pl.BlockSpec((count, DI), lambda j: (0, 0)), columns(DI), columns(count)],
        out_specs=columns(count),
        out_shape=jax.ShapeDtypeStruct(tokens.shape, bf16),
        compiler_params=pltpu.CompilerParams(vmem_limit_bytes=VMEM_LIMIT),
        cost_estimate=pl.CostEstimate(flops=1, bytes_accessed=1, transcendentals=0),
        name="block_out",
    )(mixer_low, whole_out, tokens)


def input_grad_kernel(
    split_at,
    second_width,
    gate_ref,
    first_ref,
    second_ref,
    whole_gate_ref,
    whole_conv_ref,
    tokens_ref,
    cotangent_ref,
    gain_ref,
    out_ref,
    gain_grad_ref,
    unit_grads,
    scales,
    mixes,
):
    step, steps = pl.program_id(0), pl.num_programs(0)
    count = tokens_ref.shape[0]

    @pl.when(step == 0)
    def _():
        mixes[...] = jnp.zeros_like(mixes)
        for at in range(0, count, SPAN):
            rows = pl.ds(at, SPAN)
            inputs = tokens_ref[rows, :].astype(f32)
            mean = jnp.mean(inputs * inputs, axis=-1, keepdims=True)
            scales[rows, :] = jnp.broadcast_to(lax.rsqrt(mean + norm_eps), (SPAN, LANES))

    grad = mm_nt(gate_ref[...], whole_gate_ref[...])
    grad = grad + mm_nt(first_ref[...], whole_conv_ref[:, :split_at])
    grad = grad + mm_nt(
        second_ref[:, :second_width], whole_conv_ref[:, split_at : split_at + second_width]
    )
    here = pl.ds(pl.multiple_of(step * FILL_COLS, FILL_COLS), FILL_COLS)
    unit = tokens_ref[:, here].astype(f32) * scales[:, 0:1]
    gain_grad_ref[0:1, :] = jnp.sum(grad * unit, axis=0, keepdims=True)
    unit_grad = grad * gain_ref[0:1, :]
    unit_grads[step] = unit_grad
    mixes[...] += jnp.broadcast_to(
        jnp.sum(unit_grad * unit, axis=-1, keepdims=True), mixes.shape
    )

    @pl.when(step == steps - 1)
    def _():
        width = tokens_ref.shape[1]
        for at in range(0, count, SPAN):
            rows = pl.ds(at, SPAN)
            scale = scales[rows, 0:1]
            mean = mixes[rows, 0:1] * (1.0 / width)
            for n in range(width // FILL_COLS):
                cols = pl.ds(n * FILL_COLS, FILL_COLS)
                unit = tokens_ref[rows, cols].astype(f32) * scale
                out_ref[rows, cols] = cotangent_ref[rows, cols].astype(f32) + scale * (
                    unit_grads[n, rows, :] - unit * mean
                )


def input_grad_call(
    split_at,
    gate_grad,
    first_grad,
    second_grad,
    whole_gate,
    whole_conv,
    tokens,
    cotangent,
    gain,
):
    count, width = tokens.shape
    once = lambda *s: pl.BlockSpec(s, lambda j: (0,) * len(s), pipeline_mode=pl.Buffered(1))
    rows = lambda n: pl.BlockSpec((FILL_COLS, n), lambda j: (j, 0))
    columns = lambda n: pl.BlockSpec((n, FILL_COLS), lambda j: (0, j))
    steps = width // FILL_COLS
    return pl.pallas_call(
        functools.partial(input_grad_kernel, split_at, whole_conv.shape[1] - split_at),
        grid=(steps,),
        in_specs=[
            once(*gate_grad.shape),
            once(*first_grad.shape),
            once(*second_grad.shape),
            rows(whole_gate.shape[1]),
            rows(whole_conv.shape[1]),
            once(count, width),
            once(count, width),
            columns(8),
        ],
        out_specs=[pl.BlockSpec((count, width), lambda j: (0, 0)), columns(8)],
        out_shape=[
            jax.ShapeDtypeStruct((count, width), f32),
            jax.ShapeDtypeStruct((8, width), f32),
        ],
        scratch_shapes=[
            pltpu.VMEM((steps, count, FILL_COLS), f32),
            pltpu.VMEM((count, LANES), f32),
            pltpu.VMEM((count, LANES), f32),
        ],
        compiler_params=pltpu.CompilerParams(vmem_limit_bytes=VMEM_LIMIT),
        cost_estimate=pl.CostEstimate(flops=1, bytes_accessed=1, transcendentals=0),
        name="input_grad",
    )(gate_grad, first_grad, second_grad, whole_gate, whole_conv, tokens, cotangent, gain)


def adam_kernel(blocks, core_ref, *refs):
    grads, refs = refs[: 2 * blocks], refs[2 * blocks :]
    param_ref, first_ref, second_ref = refs[:3]
    outs = refs[-3:]
    width = param_ref.shape[1]
    own_first = core_ref[0] == 0
    begin = 0
    for n in range(blocks):
        own_ref, other_ref = grads[2 * n], grads[2 * n + 1]
        for left in (True, False):
            for at in range(0, own_ref.shape[1], LANES):
                size = min(LANES, width - begin)
                if size <= 0:
                    continue
                there, cols = pl.ds(at, size), pl.ds(begin, size)
                own, other = own_ref[:, there], other_ref[:, there]
                one, two = (own, other) if left else (other, own)
                new = adamw_update(
                    param_ref[:, cols],
                    jnp.where(own_first, one, two),
                    first_ref[:, cols],
                    second_ref[:, cols],
                    weight_decay,
                )
                for out, value in zip(outs, new):
                    out[:, cols] = value
                begin += size


def adam_call(core, grads, rows, param, first, second):
    total, width = param.shape
    rows = min(rows, total)
    place = lambda n: pl.BlockSpec((rows, n), lambda i: (i, 0))
    pieces = [piece for pair in grads for piece in pair]
    return pl.pallas_call(
        functools.partial(adam_kernel, len(grads)),
        grid=(total // rows,),
        in_specs=[pl.BlockSpec(memory_space=pltpu.SMEM)]
        + [place(piece.shape[1]) for piece in pieces]
        + [place(width)] * 3,
        out_specs=[place(width)] * 3,
        out_shape=[jax.ShapeDtypeStruct(param.shape, f32)] * 3,
        compiler_params=pltpu.CompilerParams(vmem_limit_bytes=VMEM_LIMIT),
        cost_estimate=pl.CostEstimate(flops=1, bytes_accessed=1, transcendentals=0),
        name="adam",
    )(core, *pieces, param, first, second)


def adamw_update(param, grad, first, second, decay):
    first_new = beta_one * first + (1.0 - beta_one) * grad
    second_new = beta_two * second + (1.0 - beta_two) * grad * grad
    first_hat = first_new / (1.0 - beta_one**STEP)
    second_hat = second_new / (1.0 - beta_two**STEP)
    param_new = param - learn_rate * (first_hat / (jnp.sqrt(second_hat) + adam_eps) + decay * param)
    return (param_new, first_new, second_new)


def segment_of(lengths, positions):
    ends = jnp.cumsum(lengths)
    return jnp.sum((positions[..., None] >= ends).astype(jnp.int32), axis=-1)


def padded(*rows):
    out = jnp.stack([jnp.pad(r, (0, LANES - r.shape[0])) for r in rows])
    return jnp.pad(out, ((0, 8 - len(rows)), (0, 0)))


def spread_matrix():
    head = lax.broadcasted_iota(jnp.int32, (LANES, DI), 0)
    lane = lax.broadcasted_iota(jnp.int32, (LANES, DI), 1)
    return (head == lane // HD).astype(bf16)


def pass_on(own, factor, axis, backwards, kind):
    size, here = lax.axis_size(axis), lax.axis_index(axis)
    given = jnp.zeros_like(own)
    for turn in range(size - 1):
        source = size - 1 - turn if backwards else turn
        target = source - 1 if backwards else source + 1
        out = (factor * given + own).astype(kind)
        arrived = lax.ppermute(out, axis, [(source, target)]).astype(f32)
        given = jnp.where(here == target, arrived, given)
    return given


def on_small_slice():
    return lax.axis_size("fsdp") == Z * Y and lax.axis_size("ctx") == 4


def all_rows(block):
    return lax.all_gather(block, "fsdp", axis=0, tiled=True)


def swapped(value, axis, step):
    size = lax.axis_size(axis)
    return lax.ppermute(value, axis, [(i, i ^ step) for i in range(size)])


def after(value, *others):
    return lax.optimization_barrier((value,) + others)[0]


def coordinates():
    f, ctx = lax.axis_index("fsdp"), lax.axis_index("ctx")
    return ctx // 2, f % Y, f // Y, ctx % 2


CORE = ("ctx", 1)
ACROSS_X = ("ctx", 2)
ACROSS_Y = ("fsdp", 1)
ACROSS_Z = tuple(("fsdp", Y * m) for m in range(1, Z))


def row_products(columns, grads):
    return jnp.einsum("tk,tz->kz", columns, grads, preferred_element_type=f32)


def half_of(value, bit, axis):
    size = value.shape[axis] // 2
    return lax.dynamic_slice_in_dim(value, bit * size, size, axis)


class Part:
    def __init__(self, value, bound):
        self.value, self.bound = value, bound

    def plus(self, arrived, other):
        return Part(self.value + raised(arrived, other), self.bound + other)


def lowered(value, bound):
    return (value * (32768.0 / bound)).astype(jnp.float16)


def raised(value, bound):
    return value.astype(f32) * (bound * (1.0 / 32768.0))


def summed_on_chip(columns, grads, bound, other=None):
    core = coordinates()[3]
    theirs = row_products(columns, half_of(grads, 1 - core, 1))
    arrived = swapped(lowered(theirs, bound), *CORE)
    mine = Part(row_products(columns, half_of(grads, core, 1)), bound)
    return mine.plus(arrived, bound if other is None else other)


def to_send(part, bit, axis):
    sent = lowered(half_of(part.value, 1 - bit, axis), part.bound)
    return Part(half_of(part.value, bit, axis), part.bound), sent


def joined_with(kept, arrived, other=None):
    return kept.plus(arrived, kept.bound if other is None else other)


def by_owner(part):
    return Part(part.value.reshape(Z, Y, -1, part.value.shape[1]), part.bound)


def along_z(part):
    z = coordinates()[2]
    take = lambda at: lax.dynamic_index_in_dim(part.value[:, 0], at, 0, keepdims=False)
    sent = [lowered(take(z ^ m), part.bound) for m in range(1, Z)]
    return Part(take(z), part.bound), sent


def of_owner(kept, arrived):
    total = kept
    for one in arrived:
        total = total.plus(one, kept.bound)
    return total


def both_columns(value, way, bit):
    other = swapped(value, *way)
    return jnp.where(
        bit == 0,
        jnp.concatenate([value, other], axis=1),
        jnp.concatenate([other, value], axis=1),
    )


def sum_of_two(low, arrived, bound):
    return raised(low, bound) + raised(arrived, bound)


ROOM = 64.0


def over_room(bound, product_bound, *values):
    most = functools.reduce(jnp.maximum, [largest(v) for v in values])
    return (~(1.01 * product_bound * most <= bound)).astype(f32)


def owned_rows(partial):
    return lax.psum(lax.psum_scatter(partial, "fsdp", scatter_dimension=0, tiled=True), "ctx")


def largest(value):
    return jnp.max(jnp.abs(value)).astype(f32) + 1e-30


def on_device(
    tokens_in,
    cotangent,
    doc_lengths,
    in_proj,
    out_proj,
    norm_gain,
    gate_gain,
    conv_weight,
    conv_bias,
    delta_bias,
    decay_log,
    skip_scale,
    in_first,
    in_second,
    out_first,
    out_second,
    small_first,
    small_second,
):
    count = tokens_in.shape[0]
    spans = count // SPAN
    ctx = lax.axis_size("ctx")
    begin = lax.axis_index("ctx") * count
    lengths = doc_lengths[0]
    small_slice = on_small_slice()

    conv_block, gate_block = in_proj[:, DI:].astype(bf16), in_proj[:, :DI].astype(bf16)
    out_block = out_proj.astype(bf16)
    if small_slice:
        (whole_conv,) = gather_call(conv_block)
    else:
        whole_conv, whole_gate, whole_out = map(all_rows, (conv_block, gate_block, out_block))
    inputs = tokens_in.astype(f32)
    scale = lax.rsqrt(jnp.mean(inputs * inputs, axis=-1, keepdims=True) + norm_eps)
    normed = (inputs * scale * norm_gain[None, :]).astype(bf16)

    mixed = mm(normed, whole_conv)
    edge = lax.ppermute(mixed[count - 8 :, :CONVD], "ctx", [(i, i + 1) for i in range(ctx - 1)])
    edge = jnp.where(jnp.arange(8)[:, None] >= 8 - (CONV - 1), edge, 0.0)

    place = jnp.concatenate([begin[None].astype(jnp.int32), lengths.astype(jnp.int32)])
    params = padded(delta_bias, -jnp.exp(decay_log))
    (
        steps,
        decay,
        reach,
        rows,
        factor,
        start,
        inside,
        inside_back,
        outside,
        mask,
        mask_turned,
    ) = prepare_call(spans, place, mixed, params)
    taps = jnp.concatenate([conv_weight.T, conv_bias[None], jnp.zeros((3, CONVD), f32)], axis=0)

    inner, local, states, keys, queries, *wholes = forward_call(
        spans,
        mixed,
        edge,
        taps,
        inside,
        outside,
        steps,
        decay,
        rows,
        factor,
        mask,
        (gate_block, out_block) if small_slice else (),
    )
    if small_slice:
        whole_gate, whole_out = wholes
    total_lanes = jnp.repeat(start[spans, :NH], HD)[None]
    state_in = pass_on(states[spans - 1], total_lanes, "ctx", False, f32)
    gate = mm(normed, whole_gate)
    mixer_back = jnp.einsum("td,kd->tk", cotangent, whole_out, preferred_element_type=f32)
    mixer_low, mixer_grad, gate_grad, gate_gain_grad, dots, summary, gate_most_rows = norm_call(
        local,
        inner,
        gate,
        mixer_back,
        queries,
        state_in,
        reach,
        spread_matrix(),
        jnp.repeat(skip_scale, HD)[None] + jnp.zeros((8, 1), f32),
        gate_gain[None] + jnp.zeros((8, 1), f32),
    )
    state_back = pass_on(summary, total_lanes, "ctx", True, bf16)

    out_bound = count * 6.0 * (DI**0.5 * 1.01) * largest(gate_gain)
    product_bound = count * (D**0.5 * 1.01) * largest(norm_gain)
    x, y, z, core = coordinates()
    if small_slice:
        out_part = summed_on_chip(mixer_low, cotangent, out_bound)
        out_kept, out_sent = to_send(out_part, x, 1)
        mosts, others = [1.01 * product_bound * largest(gate_most_rows)], []
        for way in (CORE, ACROSS_Y):
            others.append(swapped(mosts[-1].reshape(1, 1), *way).reshape(()))
            mosts.append(jnp.maximum(mosts[-1], others[-1]))
        gate_part = summed_on_chip(normed, gate_grad, mosts[0], others[0])
        gate_kept, gate_sent = to_send(by_owner(Part(gate_part.value, 2.0 * mosts[1])), y, 1)
        mixer_grad, out_sent, gate_sent = lax.optimization_barrier(
            (mixer_grad, out_sent, gate_sent)
        )
        out_got = swapped(out_sent, *ACROSS_X)
        gate_got = swapped(gate_sent, *ACROSS_Y)

    first_pairs = 14
    skip = padded(skip_scale)
    shared = lambda back: (
        mixed,
        edge,
        taps,
        inside,
        inside_back,
        outside,
        keys,
        queries,
        back,
        steps,
        decay,
        rows,
        factor,
        start,
        mask_turned,
        states,
        state_in,
        state_back,
        skip,
    )
    following = segment_of(lengths, begin + count + jnp.arange(CONV, dtype=jnp.int32))
    own_last = segment_of(lengths, begin + count - CONV + jnp.arange(CONV, dtype=jnp.int32))

    def with_edge(grad, top, tail, at):
        next_top = lax.ppermute(top, "ctx", [(i + 1, i) for i in range(ctx - 1)])
        width = tail.shape[1]
        for j in range(1, CONV):
            joined = (following[:j] == own_last[CONV - j :]).astype(f32)
            more = joined[:, None] * next_top[:j] * taps[3 - j : 4 - j, at : at + width]
            tail = tail + jnp.pad(more, ((8 - j, 0), (0, 0)))
        return lax.dynamic_update_slice(grad, tail.astype(bf16), (count - 8, 0)), tail

    first_grad, top, tail, first_taps_grad, most, *sums = backward_call(
        spans,
        0,
        first_pairs,
        first_pairs,
        shared(mixer_grad),
        most=gate_most_rows if small_slice else None,
    )
    if small_slice:
        top, tail, most, first_grad, out_got, gate_got = lax.optimization_barrier(
            (top, tail, most, first_grad, out_got, gate_got)
        )
    first_grad, tail = with_edge(first_grad, top, tail, 0)
    if small_slice:
        out_kept, out_sent = to_send(by_owner(joined_with(out_kept, out_got)), y, 1)
        *sums, agreed = sums
        gate_most = 1.01 * product_bound * agreed.reshape(()) + 1e-30
        gate_part = joined_with(gate_kept, gate_got, 2.0 * others[1])
        gate_kept, gate_sent = along_z(Part(gate_part.value, 4.0 * gate_most))
        conv_bound = ROOM * gate_most
        first_sizes = most, tail
        first_part = summed_on_chip(normed, first_grad, conv_bound)
        first_kept, first_sent = to_send(by_owner(first_part), y, 1)
        mixer_grad, out_sent, gate_sent, first_sent = lax.optimization_barrier(
            (mixer_grad, out_sent, gate_sent, first_sent)
        )
        out_got = swapped(out_sent, *ACROSS_Y)
        gate_got = [swapped(s, *way) for s, way in zip(gate_sent, ACROSS_Z)]
        first_got = swapped(first_sent, *ACROSS_Y)
    second_grad, top, tail, second_taps_grad, most, *sums = backward_call(
        spans,
        first_pairs,
        PAIRS - first_pairs,
        14,
        shared(mixer_grad),
        (dots, mixed, params, sums),
    )
    split_at = first_pairs * LANES
    fence = lax.optimization_barrier
    if small_slice:
        top, tail, most, second_grad, sums, out_got, gate_got, first_got = fence(
            (top, tail, most, second_grad, sums, out_got, gate_got, first_got)
        )
        out_kept, out_sent = along_z(joined_with(out_kept, out_got))
        first_kept, first_sent = along_z(joined_with(first_kept, first_got))
        out_high = out_sent[0].shape[0] // 2
        both_sent = [
            jnp.concatenate([one, other[:out_high], other[out_high:]], axis=1)
            for one, other in zip(first_sent, out_sent)
        ]
        gate_part = Part(of_owner(gate_kept, gate_got).value, 16.0 * gate_most)
        gate_low = lowered(gate_part.value, gate_part.bound)
        both_sent, gate_low, tail, most = fence((both_sent, gate_low, tail, most))
        both_got = [swapped(s, *way) for s, way in zip(both_sent, ACROSS_Z)]
        gate_got = swapped(gate_low, *ACROSS_X)
    second_grad, tail = with_edge(second_grad, top, tail, split_at)
    if small_slice:
        second_part = summed_on_chip(normed, second_grad, conv_bound)
        second_kept, second_sent = to_send(by_owner(second_part), y, 1)
        (
            second_sent,
            gate_grad,
            mixer_low,
            sums,
            gate_gain_grad,
            first_taps_grad,
            second_taps_grad,
            conv_weight,
            sizes,
        ) = fence(
            (
                second_sent,
                gate_grad,
                mixer_low,
                sums,
                gate_gain_grad,
                first_taps_grad,
                second_taps_grad,
                conv_weight,
                (*first_sizes, most, tail),
            )
        )
        second_got = swapped(second_sent, *ACROSS_Y)
    input_grad, norm_gain_grad = input_grad_call(
        split_at,
        gate_grad,
        first_grad,
        second_grad,
        whole_gate,
        whole_conv,
        tokens_in,
        cotangent,
        norm_gain[None] + jnp.zeros((8, 1), f32),
    )
    if small_slice:
        second_got, both_got, gate_got, input_grad, norm_gain_grad = fence(
            (second_got, both_got, gate_got, input_grad, norm_gain_grad)
        )
        second_kept, second_sent = along_z(joined_with(second_kept, second_got))
        first_wide = first_part.value.shape[1]
        out_wide = (both_got[0].shape[1] - first_wide) // 2
        out_got = [
            jnp.concatenate(
                [s[:, first_wide : first_wide + out_wide], s[:, first_wide + out_wide :]], axis=0
            )
            for s in both_got
        ]
        first_part = of_owner(first_kept, [s[:, :first_wide] for s in both_got])
        first_low = lowered(first_part.value, first_part.bound)
        out_total = of_owner(out_kept, out_got).value
        gate_rows = sum_of_two(gate_low, gate_got, gate_part.bound)
        second_sent, first_low, out_total, gate_rows, mixer_low = fence(
            (second_sent, first_low, out_total, gate_rows, mixer_low)
        )
        second_got = [swapped(s, *way) for s, way in zip(second_sent, ACROSS_Z)]
        first_got = swapped(first_low, *ACROSS_X)
        out_got = swapped(out_total, *ACROSS_X)
        gate_pair = gate_rows, swapped(gate_rows, *CORE)
    block_out = block_out_call(mixer_low, whole_out, tokens_in)
    if small_slice:
        block_out, first_got, out_got, gate_pair = fence(
            (block_out, first_got, out_got, gate_pair)
        )
        first_rows = sum_of_two(first_low, first_got, first_part.bound)
        out_rows = jnp.where(
            x == 0,
            jnp.concatenate([out_total, out_got], axis=1),
            jnp.concatenate([out_got, out_total], axis=1),
        )
        first_pair = first_rows, swapped(first_rows, *CORE)
        out_pair = out_rows, swapped(out_rows, *CORE)
        core_index = core[None].astype(jnp.int32)
    if small_slice:
        second_got, block_out = fence((second_got, block_out))
        second_part = of_owner(second_kept, second_got)
        second_low = lowered(second_part.value, second_part.bound)
        second_low, norm_gain_grad = fence((second_low, norm_gain_grad))
        second_got = swapped(second_low, *ACROSS_X)
        over = over_room(conv_bound, product_bound, *sizes, sums[5][3])
    else:
        over = jnp.zeros((), f32)
    taps_grad = jnp.concatenate([first_taps_grad, second_taps_grad], axis=1)
    small_grad = sum_everywhere(
        jnp.concatenate(
            [
                norm_gain_grad[0],
                gate_gain_grad[0],
                taps_grad[:CONV].T.reshape(-1),
                taps_grad[4],
                sums[5][0, :NH],
                sums[5][1, :NH],
                sums[5][2, :NH],
                over[None],
            ]
        )
    )
    over, small_grad = small_grad[-1] > 0.0, small_grad[:-1]

    def updated(core, out_pair, *in_pairs):
        ins = adam_call(core, in_pairs, 48, in_proj, in_first, in_second)
        return *ins, *adam_call(core, (out_pair,), 96, out_proj, out_first, out_second)

    def in_float32():
        halves = lambda v: (v[:, : v.shape[1] // 2], v[:, v.shape[1] // 2 :])
        pairs = [
            halves(owned_rows(row_products(columns, grads)))
            for columns, grads in (
                (mixer_low, cotangent),
                (normed, gate_grad),
                (normed, first_grad),
                (normed, second_grad),
            )
        ]
        return updated(jnp.zeros((1,), jnp.int32), *pairs)

    if small_slice:
        second_got, small_grad = fence((second_got, small_grad))
        second_rows = sum_of_two(second_low, second_got, second_part.bound)
        second_pair = second_rows, swapped(second_rows, *CORE)
        news = lax.cond(
            over,
            in_float32,
            lambda: updated(core_index, out_pair, gate_pair, first_pair, second_pair),
        )
    else:
        news = in_float32()
    in_new, in_first_new, in_second_new, out_new, out_first_new, out_second_new = news
    small_param = jnp.concatenate(
        [
            norm_gain,
            gate_gain,
            conv_weight.reshape(-1),
            conv_bias,
            delta_bias,
            decay_log,
            skip_scale,
        ]
    )
    small_new, small_first_new, small_second_new = adamw_update(
        small_param, small_grad, small_first, small_second, 0.0
    )
    return (
        block_out,
        input_grad,
        in_new,
        in_first_new,
        in_second_new,
        out_new,
        out_first_new,
        out_second_new,
        small_new,
        small_first_new,
        small_second_new,
    )


def solution(mesh):
    placed = (
        P(("fsdp", "ctx"), None),
        P(("fsdp", "ctx"), None),
        P("fsdp", None),
        P("fsdp", None),
        P("fsdp", None),
        P(),
        P(),
        P(),
        P(),
        P(),
        P(),
        P(),
        P("fsdp", None),
        P("fsdp", None),
        P("fsdp", None),
        P("fsdp", None),
        P(),
        P(),
    )
    return jax.shard_map(
        on_device,
        mesh=mesh,
        in_specs=placed,
        out_specs=(
            P(("fsdp", "ctx"), None),
            P(("fsdp", "ctx"), None),
            P("fsdp", None),
            P("fsdp", None),
            P("fsdp", None),
            P("fsdp", None),
            P("fsdp", None),
            P("fsdp", None),
            P(),
            P(),
            P(),
        ),
        check_vma=False,
    )
```

```python
import functools

import jax
import jax.numpy as jnp
from jax import lax
from jax.experimental import pallas as pl
from jax.experimental.pallas import tpu as pltpu
from jax.sharding import PartitionSpec as P

D = 1536
DI = 3072
NH = 48
HD = 64
DS = 128
CONV = 4
SPAN = 256
STEP = 5
CONVD = 3328
LANES = 128
PAIRS = DI // LANES
HALF = SPAN // 2
NORM_ROWS = 128
NORM_COLS = 512
MASKED = -1e30

highest = lax.Precision.HIGHEST
norm_eps = 1e-05
beta_one = 0.9
beta_two = 0.95
adam_eps = 1e-08
learn_rate = 0.05
weight_decay = 0.1
f32 = jnp.float32
bf16 = jnp.bfloat16
VMEM_LIMIT = 56 * 1024 * 1024


def split(value):
    high = value.astype(bf16)
    return high, (value - high.astype(f32)).astype(bf16)


def mm(a, b):
    return jnp.dot(a, b, preferred_element_type=f32)


def mm_nt(a, b):
    return lax.dot_general(a, b, (((1,), (1,)), ((), ())), preferred_element_type=f32)


def sigmoid(v):
    return 1.0 / (1.0 + jnp.exp(-v))


def conv_shifts(block, edge, inside, outside, room):
    count = block.shape[0]
    room[pl.ds(8, count), :] = block
    shifted = []
    for j in range(1, CONV):
        body = inside[j - 1] * room[pl.ds(8 - j, count), :]
        head = inside[j - 1, :8] * pltpu.roll(block[:8], j, 0)
        head = head + outside[j - 1] * pltpu.roll(edge, j, 0)
        shifted.append(jnp.concatenate([head, body[8:]], axis=0))
    return shifted


def conv_pre(block, shifted, taps):
    total = taps[4:5] + taps[3:4] * block
    for j in range(1, CONV):
        total = total + taps[3 - j : 4 - j] * shifted[j - 1]
    return total


def pair_columns(packed, pair):
    turned = pltpu.roll(packed, lax.rem(LANES - 2 * pair, LANES), 1)
    lane = lax.broadcasted_iota(jnp.int32, packed.shape, 1)
    first = jnp.where(lane < HD, turned[:, 0:1], turned[:, 1:2])
    second = jnp.where(lane < HD, turned[:, 64:65], turned[:, 65:66])
    return turned, first, second


def spread_pair(both, pair):
    source = lax.broadcasted_iota(jnp.int32, (2 * LANES, LANES), 0)
    lane = lax.broadcasted_iota(jnp.int32, (2 * LANES, LANES), 1)
    return mm(both, (lax.rem(source, LANES) == 2 * pair + lane // HD).astype(bf16))


def pair_rows(rows, pair):
    turned = pltpu.roll(rows, lax.rem(LANES - 2 * pair, LANES), 1)
    lane = lax.broadcasted_iota(jnp.int32, rows.shape, 1)
    return jnp.where(lane < HD, turned[:, 0:1], turned[:, 1:2])


def head_row(block, head):
    sublane = lax.broadcasted_iota(jnp.int32, block.shape, 0)
    return jnp.sum(jnp.where(sublane == lax.rem(head, 8), block, 0.0), axis=0, keepdims=True)


def split_three(value):
    high, low = split(value)
    return high, low, (value - high.astype(f32) - low.astype(f32)).astype(bf16)


def cast_kernel(in_ref, out_ref, gate_low, conv_low, out_low):
    gate_low[...] = in_ref[:, :DI].astype(bf16)
    conv_low[...] = in_ref[:, DI:].astype(bf16)
    out_low[...] = out_ref[...].astype(bf16)


def cast_call(in_proj, out_proj):
    steps = 4
    widths = DI, in_proj.shape[1] - DI
    rows = lambda array, width: pl.BlockSpec((array.shape[0] // steps, width), lambda i: (i, 0))
    return pl.pallas_call(
        cast_kernel,
        grid=(steps,),
        in_specs=[rows(in_proj, in_proj.shape[1]), rows(out_proj, out_proj.shape[1])],
        out_specs=[rows(in_proj, w) for w in widths] + [rows(out_proj, out_proj.shape[1])],
        out_shape=[jax.ShapeDtypeStruct((in_proj.shape[0], w), bf16) for w in widths]
        + [jax.ShapeDtypeStruct(out_proj.shape, bf16)],
        compiler_params=pltpu.CompilerParams(vmem_limit_bytes=VMEM_LIMIT),
        name="cast_rows",
    )(in_proj, out_proj)


def prepare_kernel(
    spans,
    place_ref,
    raw_ref,
    params_ref,
    steps_out,
    decay_out,
    reach_out,
    turned_out,
    factor_out,
    start_out,
    inside_out,
    inside_back_out,
    outside_out,
    mask_out,
    mask_turned_out,
):
    count = spans * SPAN
    begin = place_ref[0]
    ends = []
    for d in range(place_ref.shape[0] - 1):
        ends.append(place_ref[d + 1] + (ends[-1] if ends else 0))

    def segment(position):
        total = (position >= ends[0]).astype(jnp.int32)
        for end in ends[1:]:
            total = total + (position >= end).astype(jnp.int32)
        return total

    row = lax.broadcasted_iota(jnp.int32, (count, LANES), 0)
    here = segment(row + begin)
    for j in range(1, CONV):
        same = here == segment(row + (begin - j))
        inside_out[j - 1] = jnp.where(jnp.logical_and(same, row >= j), 1.0, 0.0)
        later = here == segment(row + (begin + j))
        inside_back_out[j - 1] = jnp.where(jnp.logical_and(later, row + j < count), 1.0, 0.0)
        outside_out[j - 1] = jnp.where(jnp.logical_and(same, row < j), 1.0, 0.0)[:8]
    lane = lax.broadcasted_iota(jnp.int32, (count, LANES), 1)
    raw = jnp.where(lane < NH, raw_ref[...], 0.0) + params_ref[0:1]
    steps = jnp.where(lane < NH, jnp.maximum(raw, 0.0) + jnp.log1p(jnp.exp(-jnp.abs(raw))), 0.0)
    log_decay = params_ref[1:2] * steps
    tall = lax.broadcasted_iota(jnp.int32, (SPAN, SPAN), 0)
    wide = lax.broadcasted_iota(jnp.int32, (SPAN, SPAN), 1)
    lower = (tall >= wide).astype(bf16)
    span_lane = lax.broadcasted_iota(jnp.int32, (SPAN, LANES), 1)
    before = jnp.zeros((1, LANES), f32)
    start = jnp.ones((1, LANES), f32)
    starts, factors = [start], []
    reached = here == segment(begin - 1)
    for k in range(spans):
        at = k * SPAN
        rows = pl.ds(at, SPAN)
        parts = split_three(log_decay[at : at + SPAN])
        sums = mm(lower, jnp.concatenate(parts, axis=1))
        cumul = sums[:, :LANES] + sums[:, LANES : 2 * LANES] + sums[:, 2 * LANES :]
        last = cumul[SPAN - 1 : SPAN]
        span_here = here[at : at + SPAN]
        first = begin + at
        enters = jnp.logical_and(span_here == segment(first - 1), span_here >= 0)
        enter = jnp.where(jnp.logical_and(enters, first > 0), jnp.exp(cumul), 0.0)
        leave = jnp.where(
            span_here == segment(first + SPAN - 1), jnp.exp(last - cumul), 0.0
        )
        reach = jnp.where(
            jnp.logical_and(reached[at : at + SPAN], begin > 0), jnp.exp(cumul + before), 0.0
        )
        known = span_lane < NH
        steps_out[rows, :] = jnp.where(known, cumul, 0.0) + pltpu.roll(
            steps[at : at + SPAN], LANES // 2, 1
        )
        decay_out[rows, :] = jnp.where(known, enter, 0.0) + pltpu.roll(
            jnp.where(known, leave, 0.0), LANES // 2, 1
        )
        reach_out[rows, :] = jnp.where(known, reach, 0.0)
        turned_out[:, rows] = cumul.T[:NH]
        factors.append(enter[SPAN - 1 : SPAN])
        start = start * factors[-1]
        starts.append(start)
        before = before + last
        together = segment(tall + first) == segment(wide + first)
        mask_out[k] = jnp.where(jnp.logical_and(together, tall >= wide), 0.0, MASKED)
        mask_turned_out[k] = jnp.where(jnp.logical_and(together, tall <= wide), 0.0, MASKED)
    rest = lambda rows: jnp.concatenate(
        rows + [jnp.zeros((8 - len(rows), LANES), f32)], axis=0
    )
    factor_out[...] = rest(factors)
    start_out[...] = rest(starts)


def prepare_call(spans, place, mixed, params):
    count = spans * SPAN
    whole = lambda *s: pl.BlockSpec(s, lambda i: (0,) * len(s))
    shapes = [
        (count, LANES),
        (count, LANES),
        (count, LANES),
        (NH, count),
        (8, LANES),
        (8, LANES),
        (CONV - 1, count, LANES),
        (CONV - 1, count, LANES),
        (CONV - 1, 8, LANES),
        (spans, SPAN, SPAN),
        (spans, SPAN, SPAN),
    ]
    return pl.pallas_call(
        functools.partial(prepare_kernel, spans),
        grid=(1,),
        in_specs=[
            pl.BlockSpec(memory_space=pltpu.SMEM),
            pl.BlockSpec((count, LANES), lambda i: (0, CONVD // LANES)),
            whole(8, LANES),
        ],
        out_specs=[whole(*s) for s in shapes],
        out_shape=[jax.ShapeDtypeStruct(s, f32) for s in shapes],
        compiler_params=pltpu.CompilerParams(vmem_limit_bytes=VMEM_LIMIT),
        name="steps_and_masks",
    )(place, mixed, params)


MESH = pl.DeviceIdType.MESH
Z = 4
Y = 2


PARTS = 2


class Gathering:
    def __init__(self, blocks, wholes, sems):
        self.arrays = []
        for block, whole in zip(blocks, wholes):
            rows = block.shape[0] // PARTS
            self.arrays += [(block, whole, part * rows, rows) for part in range(PARTS)]
        self.own, self.up_sem, self.down_sem, self.z_sem, *sems = sems
        self.y_sent, self.y_sem, self.x_sent, self.x_sem, self.core_sent, self.core_sem = sems
        self.f, self.ctx = lax.axis_index("fsdp"), lax.axis_index("ctx")
        self.z, self.y = self.f // Y, lax.rem(self.f, Y)
        self.x, self.c = self.ctx // 2, lax.rem(self.ctx, 2)
        self.at_y = (self.z * Y + 1 - self.y, self.ctx)
        self.at_x = (self.f, (1 - self.x) * 2 + self.c)
        self.at_core = (self.f, self.x * 2 + 1 - self.c)

    def at_z(self, other):
        return other * Y + self.y, self.ctx

    def rows_of(self, n):
        return self.arrays[n][3]

    def place(self, n, block, row, size):
        own, whole, offset, rows = self.arrays[n]
        return whole.at[pl.ds(block * own.shape[0] + offset + row, size)]

    def third(self, n):
        return self.rows_of(n) // 6

    def gathered(self, n):
        return self.c * (self.rows_of(n) // 2) + self.x * self.third(n), 2 * self.third(n)

    def move(self, n, block, row, size, sent, landed, partner, own=False):
        here = self.place(n, block, row, size)
        source = self.arrays[n][0].at[pl.ds(self.arrays[n][2] + row, size)] if own else here
        return pltpu.make_async_remote_copy(
            src_ref=source,
            dst_ref=here,
            send_sem=sent,
            recv_sem=landed,
            device_id=partner,
            device_id_type=MESH,
        )

    def up(self, n, zb, own=False):
        sems = self.up_sem.at[n, zb], self.z_sem.at[n, zb]
        block = zb * Y + self.y
        return self.move(n, block, *self.gathered(n), *sems, self.at_z(self.z + 1), own)

    def down(self, n, zb, own=False):
        sems = self.down_sem.at[n, zb], self.z_sem.at[n, zb]
        block = zb * Y + self.y
        return self.move(n, block, *self.gathered(n), *sems, self.at_z(self.z - 1), own)

    def along_y(self, n, zb, yb, own=False):
        sems = self.y_sent.at[n, zb], self.y_sem.at[n, zb]
        return self.move(n, zb * Y + yb, *self.gathered(n), *sems, self.at_y, own)

    def along_x(self, n, block, sender_x):
        row = self.c * (self.rows_of(n) // 2) + 2 * self.third(n) * sender_x
        sems = self.x_sent.at[n, block], self.x_sem.at[n, block]
        return self.move(n, block, row, self.third(n), *sems, self.at_x)

    def core_first(self, n, block, core):
        row = core * (self.rows_of(n) // 2) + self.x * self.third(n)
        sems = self.core_sent.at[n, block, 0], self.core_sem.at[n, block, 0]
        return self.move(n, block, row, 2 * self.third(n), *sems, self.at_core)

    def core_second(self, n, block, core):
        row = core * (self.rows_of(n) // 2) + 2 * self.third(n) * (1 - self.x)
        sems = self.core_sent.at[n, block, 1], self.core_sem.at[n, block, 1]
        return self.move(n, block, row, self.third(n), *sems, self.at_core)

    def own_copy(self, n):
        block, whole, offset, rows = self.arrays[n]
        return pltpu.make_async_copy(
            block.at[pl.ds(offset, rows)], self.place(n, self.f, 0, rows), self.own.at[n]
        )

    def begin(self):
        barrier = pltpu.get_barrier_semaphore()
        signal = functools.partial(
            pl.semaphore_signal, barrier, inc=1, device_id_type=MESH
        )
        for partner in (self.at_y, self.at_x, self.at_core):
            signal(device_id=partner)

        @pl.when(self.z > 0)
        def _():
            signal(device_id=self.at_z(self.z - 1))

        @pl.when(self.z < Z - 1)
        def _():
            signal(device_id=self.at_z(self.z + 1))

        middle = jnp.logical_and(self.z > 0, self.z < Z - 1).astype(jnp.int32)
        pl.semaphore_wait(barrier, 4 + middle)
        for n in range(len(self.arrays)):
            self.own_copy(n).start()

            @pl.when(self.z < Z - 1)
            def _():
                self.up(n, self.z, True).start()

            @pl.when(self.z > 0)
            def _():
                self.down(n, self.z, True).start()

            self.along_y(n, self.z, self.y, True).start()

    def spread(self, n, block):
        self.along_x(n, block, self.x).start()
        self.core_first(n, block, self.c).start()

    def from_z(self, n, distance):
        for way in (1, -1):
            zb = self.z - way * distance

            @pl.when(jnp.logical_and(zb >= 0, zb < Z))
            def _():
                self.up(n, zb).wait_recv()
                if way == 1:

                    @pl.when(self.z < Z - 1)
                    def _():
                        self.up(n, zb).start()
                else:

                    @pl.when(self.z > 0)
                    def _():
                        self.down(n, zb).start()

                self.along_y(n, zb, self.y).start()
                self.spread(n, zb * Y + self.y)

    def from_y(self, n, distance):
        for way in (1, -1) if distance else (1,):
            zb = self.z - way * distance

            @pl.when(jnp.logical_and(zb >= 0, zb < Z))
            def _():
                self.along_y(n, zb, 1 - self.y).wait_recv()
                self.spread(n, zb * Y + 1 - self.y)

    def each_block(self, do):
        def at(zb, yb):
            @pl.when(jnp.logical_and(zb >= 0, zb < Z))
            def _():
                for n in range(len(self.arrays)):
                    do(n, zb * Y + yb)

        for distance in range(Z):
            for way in (1, -1) if distance else (1,):
                if distance:
                    at(self.z - way * distance, self.y)
                at(self.z - way * distance, 1 - self.y)

    def end(self):
        def come_along_x(n, block):
            self.along_x(n, block, 1 - self.x).wait_recv()
            self.core_second(n, block, self.c).start()

        def finish(n, block):
            self.core_first(n, block, 1 - self.c).wait_recv()
            self.core_second(n, block, 1 - self.c).wait_recv()
            self.along_x(n, block, self.x).wait_send()
            self.core_first(n, block, self.c).wait_send()
            self.core_second(n, block, self.c).wait_send()

        self.each_block(come_along_x)
        self.each_block(finish)
        for n in range(len(self.arrays)):
            self.own_copy(n).wait()
            for zb in range(Z):
                self.along_y(n, zb, self.y).wait_send()

                @pl.when(jnp.logical_and(self.z < Z - 1, zb <= self.z))
                def _():
                    self.up(n, zb).wait_send()

                @pl.when(jnp.logical_and(self.z > 0, zb >= self.z))
                def _():
                    self.down(n, zb).wait_send()


def gathering_semaphores(count):
    dma = lambda *s: pltpu.SemaphoreType.DMA((count * PARTS,) + s)
    size = Z * Y
    return [dma()] + [dma(Z)] * 5 + [dma(size)] * 2 + [dma(size, 2)] * 2


def whole_shapes(blocks):
    return [jax.ShapeDtypeStruct((b.shape[0] * Z * Y, b.shape[1]), b.dtype) for b in blocks]


def gather_kernel(count, *refs):
    gathering = Gathering(refs[:count], refs[count : 2 * count], refs[2 * count :])
    parts = range(len(gathering.arrays))
    gathering.begin()
    for distance in range(1, Z):
        for n in parts:
            gathering.from_z(n, distance)
            gathering.from_y(n, distance - 1)
    for n in parts:
        gathering.from_y(n, Z - 1)
    gathering.end()


def gather_call(*blocks):
    count = len(blocks)
    return pl.pallas_call(
        functools.partial(gather_kernel, count),
        in_specs=[pl.BlockSpec(memory_space=pl.ANY)] * count,
        out_specs=[pl.BlockSpec(memory_space=pl.ANY)] * count,
        out_shape=whole_shapes(blocks),
        scratch_shapes=gathering_semaphores(count),
        compiler_params=pltpu.CompilerParams(collective_id=0, has_side_effects=True),
        name="gather_rows",
    )(*blocks)


Z_STEPS = {at: (n % 4, 1 + n // 4) for n, at in enumerate((2, 4, 6, 7, 9, 11, 13, 14, 16, 18, 20, 21))}
Y_STEPS = {at: (n % 4, n // 4) for n, at in enumerate((3, 5, 7, 8, 10, 12, 14, 15, 17, 19, 21, 22))}


def forward_kernel(
    spans,
    blocks,
    block_ref,
    key_ref,
    query_ref,
    edge_ref,
    key_edge_ref,
    query_edge_ref,
    taps_ref,
    key_taps_ref,
    query_taps_ref,
    inside_ref,
    outside_ref,
    steps_ref,
    decay_ref,
    rows_ref,
    factor_ref,
    mask_ref,
    *refs,
):
    block_refs, refs = refs[:blocks], refs[blocks:]
    inner_out, local_out, state_out, key_out, query_out, *refs = refs
    whole_refs, refs = refs[:blocks], refs[blocks:]
    scores, key_turned, query_both, room, *sems = refs
    room[:8, :] = jnp.zeros((8, LANES), f32)
    pair = pl.program_id(0)
    if blocks:
        gathering = Gathering(block_refs, whole_refs, sems)
        pl.when(pair == 0)(gathering.begin)
        for at, what in Z_STEPS.items():
            pl.when(pair == at)(functools.partial(gathering.from_z, *what))
        for at, what in Y_STEPS.items():
            pl.when(pair == at)(functools.partial(gathering.from_y, *what))

    @pl.when(pair == 0)
    def _():
        for src, edge, taps, out in (
            (key_ref, key_edge_ref, key_taps_ref, key_out),
            (query_ref, query_edge_ref, query_taps_ref, query_out),
        ):
            pre = conv_pre(
                src[...], conv_shifts(src[...], edge[...], inside_ref, outside_ref, room), taps[...]
            )
            out[...] = pre * sigmoid(pre)
        for k in range(spans):
            rows = pl.ds(k * SPAN, SPAN)
            keys, queries = key_out[rows, :], query_out[rows, :]
            kh, kl = split(keys)
            qh, ql = split(queries)
            query_both[rows, :] = jnp.concatenate([qh, ql], axis=1)
            scores[k] = mm_nt(
                jnp.concatenate([qh, ql], axis=1), jnp.concatenate([kh, kh], axis=1)
            ) + mm_nt(qh, kl)
            th, tl = split(keys.T)
            key_turned[k, 0] = th
            key_turned[k, 1] = tl

    block = block_ref[...]
    pre = conv_pre(
        block, conv_shifts(block, edge_ref[...], inside_ref, outside_ref, room), taps_ref[...]
    )
    inner = pre * sigmoid(pre)
    inner_out[...] = inner
    turned, unused, steps = pair_columns(steps_ref[...], pair)
    unused, enter, leave = pair_columns(decay_ref[...], pair)
    scaled = steps * inner
    leaving = leave * scaled
    lane = lax.broadcasted_iota(jnp.int32, (HALF, LANES), 1)
    head_rows = [head_row(rows_ref[...], 2 * pair + a) for a in range(2)]
    factor = pair_rows(factor_ref[...], pair)
    state = None
    for k in range(spans):
        at = k * SPAN
        sh, sl = split(scaled[at : at + SPAN])
        both = jnp.concatenate([sh, sl], axis=1)
        parts = []
        for half in range(2):
            width = HALF * (half + 1)
            here, there = pl.ds(half * HALF, HALF), pl.ds(0, width)
            both_heads = []
            for a in range(2):
                row = head_rows[a][:, at : at + width]
                column = turned[at + half * HALF : at + (half + 1) * HALF, a : a + 1]
                decay = jnp.exp(jnp.minimum(column - row, mask_ref[k, here, there]))
                both_heads.append(decay * scores[k, here, there])
            wh, wl = split(jnp.concatenate(both_heads, axis=0))
            wide = mm(wh, both[:width])
            wide = wide[:, :LANES] + wide[:, LANES:] + mm(wl, sh[:width])
            parts.append(jnp.where(lane < HD, wide[:HALF], wide[HALF:]))
        local = jnp.concatenate(parts, axis=0)
        ph, pw = split(leaving[at : at + SPAN])
        fresh = mm(key_turned[k, 0], jnp.concatenate([ph, pw], axis=1))
        fresh = fresh[:, :LANES] + fresh[:, LANES:] + mm(key_turned[k, 1], ph)
        if state is None:
            state = fresh
        else:
            th, tl = split(state)
            q2 = query_both[pl.ds(at, SPAN), :]
            carried = mm(q2, jnp.concatenate([th, th], axis=0)) + mm(q2[:, :DS], tl)
            local = local + enter[at : at + SPAN] * carried
            state = factor[k : k + 1] * state + fresh
        state_out[k] = state
        local_out[pl.ds(at, SPAN), :] = local
    if blocks:

        @pl.when(pair == PAIRS - 1)
        def _():
            for n in range(blocks * PARTS):
                gathering.from_y(n, Z - 1)
            gathering.end()


def forward_call(
    spans, mixed, edge, taps, inside, outside, steps, decay, rows, factor, mask, blocks
):
    count = spans * SPAN
    at_pair = lambda n: pl.BlockSpec((n, LANES), lambda i: (0, i))
    at_key = lambda n: pl.BlockSpec((n, LANES), lambda i: (0, PAIRS))
    at_query = lambda n: pl.BlockSpec((n, LANES), lambda i: (0, PAIRS + 1))
    whole = lambda *s: pl.BlockSpec(s, lambda i: (0,) * len(s))
    remote = dict(collective_id=5, has_side_effects=True) if blocks else {}
    return pl.pallas_call(
        functools.partial(forward_kernel, spans, len(blocks)),
        grid=(PAIRS,),
        in_specs=[
            at_pair(count),
            at_key(count),
            at_query(count),
            at_pair(8),
            at_key(8),
            at_query(8),
            at_pair(8),
            at_key(8),
            at_query(8),
            whole(3, count, LANES),
            whole(3, 8, LANES),
            whole(count, LANES),
            whole(count, LANES),
            pl.BlockSpec((8, count), lambda i: (i // 4, 0)),
            whole(8, LANES),
            whole(spans, SPAN, SPAN),
        ]
        + [pl.BlockSpec(memory_space=pl.ANY)] * len(blocks),
        out_specs=[
            at_pair(count),
            at_pair(count),
            pl.BlockSpec((spans, DS, LANES), lambda i: (0, 0, i)),
            whole(count, LANES),
            whole(count, LANES),
        ]
        + [pl.BlockSpec(memory_space=pl.ANY)] * len(blocks),
        out_shape=[
            jax.ShapeDtypeStruct((count, DI), f32),
            jax.ShapeDtypeStruct((count, DI), f32),
            jax.ShapeDtypeStruct((spans, DS, DI), f32),
            jax.ShapeDtypeStruct((count, DS), f32),
            jax.ShapeDtypeStruct((count, DS), f32),
        ]
        + whole_shapes(blocks),
        scratch_shapes=[
            pltpu.VMEM((spans, SPAN, SPAN), f32),
            pltpu.VMEM((spans, 2, DS, SPAN), bf16),
            pltpu.VMEM((count, 2 * DS), bf16),
            pltpu.VMEM((count + 8, LANES), f32),
        ]
        + (gathering_semaphores(len(blocks)) if blocks else []),
        compiler_params=pltpu.CompilerParams(vmem_limit_bytes=VMEM_LIMIT, **remote),
        cost_estimate=pl.CostEstimate(flops=1, bytes_accessed=1, transcendentals=0),
        name="recurrence_forward",
    )(
        mixed,
        mixed,
        mixed,
        edge,
        edge,
        edge,
        taps,
        taps,
        taps,
        inside,
        outside,
        steps,
        decay,
        rows,
        factor,
        mask,
        *blocks,
    )


def norm_kernel(
    local_ref,
    inner_ref,
    gate_ref,
    back_ref,
    query_ref,
    state_ref,
    reach_ref,
    spread_ref,
    skip_ref,
    gain_ref,
    out_ref,
    mixer_grad_ref,
    gate_grad_ref,
    gain_grad_ref,
    dots_ref,
    summary_ref,
    most_ref,
    mixed_y,
    state_both,
    reach_wide,
):
    step = pl.program_id(0)
    chunks = [pl.ds(c * NORM_COLS, NORM_COLS) for c in range(DI // NORM_COLS)]

    @pl.when(step == 0)
    def _():
        sh, sl = split(state_ref[...])
        state_both[0] = sh
        state_both[1] = sl
        gain_grad_ref[...] = jnp.zeros_like(gain_grad_ref)
        summary_ref[...] = jnp.zeros_like(summary_ref)
        most_ref[...] = jnp.zeros_like(most_ref)

    qh, ql = split(query_ref[...])
    query_both = jnp.concatenate([qh, ql], axis=1)
    rh, rl = split(reach_ref[...])
    reach_both = jnp.concatenate([rh, rl], axis=1)
    squares = jnp.zeros((NORM_ROWS, 1), f32)
    mixes = jnp.zeros((NORM_ROWS, 1), f32)
    for cols in chunks:
        sh, sl = state_both[0, :, cols], state_both[1, :, cols]
        spread = spread_ref[:, cols]
        reach = mm(reach_both, jnp.concatenate([spread, spread], axis=0))
        reach_wide[:, cols] = reach
        carried = mm(query_both, jnp.concatenate([sh, sh], axis=0)) + mm(qh, sl)
        y = local_ref[:, cols] + reach * carried
        mixed_y[:, cols] = y
        mixer = y + skip_ref[0:1, cols] * inner_ref[:, cols]
        gate = gate_ref[:, cols]
        gated = mixer * (gate * sigmoid(gate))
        squares = squares + jnp.sum(gated * gated, axis=1, keepdims=True)
        mixes = mixes + jnp.sum(
            gated * (back_ref[:, cols] * gain_ref[0:1, cols]), axis=1, keepdims=True
        )
    scale = lax.rsqrt(squares * (1.0 / DI) + norm_eps)
    pull = scale * mixes * (1.0 / DI)
    query_turned = query_ref[...].T
    th, tl = split(query_turned)
    dots = jnp.zeros((NORM_ROWS, LANES), f32)
    for cols in chunks:
        y = mixed_y[:, cols]
        mixer = y + skip_ref[0:1, cols] * inner_ref[:, cols]
        gate = gate_ref[:, cols]
        opened = sigmoid(gate)
        silu = gate * opened
        unit = mixer * silu * scale
        gain = gain_ref[0:1, cols]
        back = back_ref[:, cols]
        out_ref[:, cols] = (unit * gain).astype(bf16)
        gain_grad_ref[0:1, cols] += jnp.sum(back * unit, axis=0, keepdims=True)
        gated_grad = scale * (back * gain - unit * pull)
        mixer_grad = gated_grad * silu
        mixer_grad_ref[:, cols] = mixer_grad
        gate_grad = gated_grad * mixer * (opened * (1.0 + gate * (1.0 - opened)))
        gate_grad_ref[:, cols] = gate_grad.astype(bf16)
        most = jnp.max(jnp.abs(gate_grad).reshape(NORM_ROWS // 8, 8, NORM_COLS), axis=0)
        for c in range(NORM_COLS // LANES):
            most_ref[...] = jnp.maximum(most_ref[...], most[:, c * LANES : (c + 1) * LANES])
        dh, dl = split(mixer_grad * y)
        spread = spread_ref[:, cols]
        dots = dots + mm_nt(dh, spread) + mm_nt(dl, spread)
        mh, ml = split(reach_wide[:, cols] * mixer_grad)
        summary_ref[:, cols] += (
            mm(jnp.concatenate([th, tl], axis=1), jnp.concatenate([mh, mh], axis=0)) + mm(th, ml)
        )
    dots_ref[...] = dots


def norm_call(local, inner, gate, back, queries, state_in, reach, spread, skip, gain):
    count = local.shape[0]
    rows = lambda n: pl.BlockSpec((NORM_ROWS, n), lambda i: (i, 0))
    whole = lambda *s: pl.BlockSpec(s, lambda i: (0,) * len(s))
    return pl.pallas_call(
        norm_kernel,
        grid=(count // NORM_ROWS,),
        in_specs=[
            rows(DI),
            rows(DI),
            rows(DI),
            rows(DI),
            rows(DS),
            whole(DS, DI),
            rows(LANES),
            whole(LANES, DI),
            whole(8, DI),
            whole(8, DI),
        ],
        out_specs=[
            rows(DI),
            rows(DI),
            rows(DI),
            whole(8, DI),
            rows(LANES),
            whole(DS, DI),
            whole(8, LANES),
        ],
        out_shape=[
            jax.ShapeDtypeStruct((count, DI), bf16),
            jax.ShapeDtypeStruct((count, DI), f32),
            jax.ShapeDtypeStruct((count, DI), bf16),
            jax.ShapeDtypeStruct((8, DI), f32),
            jax.ShapeDtypeStruct((count, LANES), f32),
            jax.ShapeDtypeStruct((DS, DI), f32),
            jax.ShapeDtypeStruct((8, LANES), f32),
        ],
        scratch_shapes=[
            pltpu.VMEM((NORM_ROWS, DI), f32),
            pltpu.VMEM((2, DS, DI), bf16),
            pltpu.VMEM((NORM_ROWS, DI), f32),
        ],
        compiler_params=pltpu.CompilerParams(vmem_limit_bytes=VMEM_LIMIT),
        cost_estimate=pl.CostEstimate(flops=1, bytes_accessed=1, transcendentals=0),
        name="gated_norm",
    )(local, inner, gate, back, queries, state_in, reach, spread, skip, gain)


class Agreement:
    def __init__(self, values_ref, out_ref, most, near, sent, landed):
        self.values_ref, self.out_ref = values_ref, out_ref
        self.most, self.near, self.sent, self.landed = most, near, sent, landed
        f, ctx = lax.axis_index("fsdp"), lax.axis_index("ctx")
        z, y, x, c = f // Y, lax.rem(f, Y), ctx // 2, lax.rem(ctx, 2)
        at = lambda z, y, x, c: (z * Y + y, x * 2 + c)
        self.phases = (
            [at(lax.rem(z + d, Z), y, x, c) for d in range(1, Z)],
            [at(z, y, x, 1 - c)],
            [at(z, y, 1 - x, c), at(z, 1 - y, x, c), at(z, 1 - y, 1 - x, c)],
        )

    def copies(self, phase):
        return [
            pltpu.make_async_remote_copy(
                src_ref=self.most.at[phase],
                dst_ref=self.near.at[phase, n],
                send_sem=self.sent.at[phase, n],
                recv_sem=self.landed.at[phase, n],
                device_id=partner,
                device_id_type=MESH,
            )
            for n, partner in enumerate(self.phases[phase])
        ]

    def begin(self):
        barrier = pltpu.get_barrier_semaphore()
        partners = [partner for phase in self.phases for partner in phase]
        for partner in partners:
            pl.semaphore_signal(barrier, inc=1, device_id=partner, device_id_type=MESH)
        self.most[0] = jnp.full((8, LANES), jnp.max(jnp.abs(self.values_ref[...])), f32)
        pl.semaphore_wait(barrier, len(partners))
        for copy in self.copies(0):
            copy.start()

    def arrived(self, phase):
        for copy in self.copies(phase):
            copy.wait()
        most = self.most[phase]
        for n in range(len(self.phases[phase])):
            most = jnp.maximum(most, self.near[phase, n])
        return most

    def go_on(self, phase):
        self.most[phase] = self.arrived(phase - 1)
        for copy in self.copies(phase):
            copy.start()

    def end(self):
        self.out_ref[0, 0] = jnp.max(self.arrived(2))


def agreement_scratch():
    return [
        pltpu.VMEM((3, 8, LANES), f32),
        pltpu.VMEM((3, 3, 8, LANES), f32),
        pltpu.SemaphoreType.DMA((3, 3)),
        pltpu.SemaphoreType.DMA((3, 3)),
    ]


def backward_kernel(spans, first, pairs, last, agree, *refs):
    (
        block_ref,
        edge_ref,
        taps_ref,
        inside_ref,
        inside_back_ref,
        outside_ref,
        keys_ref,
        queries_ref,
        back_ref,
        steps_ref,
        decay_ref,
        rows_ref,
        factor_ref,
        start_ref,
        mask_ref,
        states_ref,
        state_in_ref,
        state_back_ref,
        skip_ref,
        *refs,
    ) = refs
    if agree:
        most_ref, *refs = refs
    if last:
        dots_ref, raw_ref, params_ref, *refs = refs
        old_scores_grad, old_key_grad, old_query_grad, old_steps, old_heads, *refs = refs
    grad_out, top_out, tail_out, taps_out, most_out, *refs = refs
    scores_grad, key_grad, query_grad, steps_out, heads_out, *refs = refs
    if last:
        sums_out, *refs = refs
    if agree:
        agreed_out, *refs = refs
    scores, key_both, query_both, query_turned, room, columns, *refs = refs
    step = pl.program_id(0)
    if agree:
        agreement = Agreement(most_ref, agreed_out, *refs)
        pl.when(step == 0)(agreement.begin)
        pl.when(step == 3)(functools.partial(agreement.go_on, 1))
        pl.when(step == 6)(functools.partial(agreement.go_on, 2))
        pl.when(step == pairs - 1)(agreement.end)
    pair = step + first
    lane = lax.broadcasted_iota(jnp.int32, (SPAN, LANES), 1)

    @pl.when(step == 0)
    def _():
        if last:
            key_grad[...] = old_key_grad[...]
            query_grad[...] = old_query_grad[...]
            scores_grad[...] = old_scores_grad[...]
            steps_out[...] = old_steps[...]
            heads_out[...] = old_heads[...]
        else:
            key_grad[...] = jnp.zeros_like(key_grad)
            query_grad[...] = jnp.zeros_like(query_grad)
            scores_grad[...] = jnp.zeros_like(scores_grad)
            steps_out[...] = jnp.zeros_like(steps_out)
            heads_out[...] = jnp.zeros_like(heads_out)
        for n, (packed, shift) in enumerate(
            ((steps_ref, LANES // 2), (decay_ref, 0), (decay_ref, LANES // 2))
        ):
            values = pltpu.roll(packed[...], shift, 1) if shift else packed[...]
            columns[n] = jnp.concatenate(split(values), axis=1)
        for k in range(spans):
            rows = pl.ds(k * SPAN, SPAN)
            keys, queries = keys_ref[rows, :], queries_ref[rows, :]
            kh, kl = split(keys)
            qh, ql = split(queries)
            key_both[rows, :] = jnp.concatenate([kh, kl], axis=1)
            query_both[rows, :] = jnp.concatenate([qh, ql], axis=1)
            scores[k] = mm_nt(
                jnp.concatenate([kh, kl], axis=1), jnp.concatenate([qh, qh], axis=1)
            ) + mm_nt(kh, ql)
            th, tl = split(queries.T)
            query_turned[k, 0] = th
            query_turned[k, 1] = tl

    def conv_back(conved_grad, block, shifted, pre):
        opened = sigmoid(pre)
        pre_grad = conved_grad * (opened * (1.0 + pre * (1.0 - opened)))
        count = block.shape[0]
        taps = taps_ref[...]
        total = taps[3:4] * pre_grad
        sums = [None] * 8
        sums[3] = jnp.sum(pre_grad * block, axis=0, keepdims=True)
        sums[4] = jnp.sum(pre_grad, axis=0, keepdims=True)
        room[pl.ds(0, count), :] = pre_grad
        room[pl.ds(count, 8), :] = jnp.zeros((8, LANES), f32)
        for j in range(1, CONV):
            total = total + taps[3 - j : 4 - j] * (
                inside_back_ref[j - 1] * room[pl.ds(j, count), :]
            )
            sums[3 - j] = jnp.sum(pre_grad * shifted[j - 1], axis=0, keepdims=True)
        grad_out[...] = total.astype(bf16)
        tail_out[...] = total[count - 8 :]
        most_out[...] = jnp.max(jnp.abs(total).reshape(count // 8, 8, LANES), axis=0)
        top_out[...] = pre_grad[:8]
        return sums

    zero_row = jnp.zeros((1, LANES), f32)

    def of_conv():
        block = block_ref[...]
        room[:8, :] = jnp.zeros((8, LANES), f32)
        shifted = conv_shifts(block, edge_ref[...], inside_ref, outside_ref, room)
        return block, shifted, conv_pre(block, shifted, taps_ref[...])

    @pl.when(step < pairs)
    def _():
        block, shifted, pre = of_conv()
        head_rows = [head_row(rows_ref[...], 2 * pair + a) for a in range(2)]
        factor = pair_rows(factor_ref[...], pair)
        start = pair_rows(start_ref[...], pair)
        skip = pair_rows(skip_ref[...], pair)
        inner = pre * sigmoid(pre)
        back = back_ref[...]
        turned = pltpu.roll(steps_ref[...], lax.rem(LANES - 2 * pair, LANES), 1)
        steps, enter, leave = (spread_pair(columns[n], pair) for n in range(3))
        scaled = steps * inner
        leaving = leave * scaled
        entering = enter * back
        state_in = state_in_ref[...]
        state_back = state_back_ref[...]
        scaled_grads = [None] * spans
        ends = [zero_row] * 8
        for k in reversed(range(spans)):
            at = k * SPAN
            rows = pl.ds(at, SPAN)
            bh, bl = split(back[at : at + SPAN])
            both = jnp.concatenate([bh, bl], axis=1)
            sh, sl = split(scaled[at : at + SPAN])
            zero = jnp.zeros((SPAN, LANES), bf16)
            sl_turned = pltpu.roll(sl.astype(f32), HD, 1).astype(bf16)
            bh_turned = pltpu.roll(bh.astype(f32), HD, 1).astype(bf16)
            lefts, rights = [], []
            for a in range(2):
                mine = (lane < HD) if a == 0 else (lane >= HD)
                of_mine = lambda one, other: jnp.where(mine, one, other)
                lefts.append(
                    jnp.concatenate([of_mine(sh, sl_turned), of_mine(sh, zero)], axis=1)
                )
                rights.append(
                    jnp.concatenate([of_mine(bh, bh_turned), of_mine(bl, zero)], axis=1)
                )
            parts = []
            for half in range(2):
                low = half * HALF
                width = SPAN - low
                here = pl.ds(low, HALF)
                there = pl.ds(low, width)
                both_heads = []
                grads = None
                for a in range(2):
                    row = head_rows[a][:, at + low : at + low + width]
                    column = turned[at + low : at + low + HALF, a : a + 1]
                    decay = jnp.exp(jnp.minimum(row - column, mask_ref[k, here, there]))
                    both_heads.append(decay * scores[k, here, there])
                    grad = decay * mm_nt(lefts[a][low : low + HALF], rights[a][low:])
                    grads = grad if grads is None else grads + grad
                scores_grad[k, here, there] += grads
                wh, wl = split(jnp.concatenate(both_heads, axis=0))
                wide = mm(wh, both[low:])
                wide = wide[:, :LANES] + wide[:, LANES:] + mm(wl, bh[low:])
                parts.append(jnp.where(lane[:HALF] < HD, wide[:HALF], wide[HALF:]))
            scaled_grad = jnp.concatenate(parts, axis=0)
            gh, gl = split(state_back)
            k2 = key_both[rows, :]
            scaled_grad = scaled_grad + leave[at : at + SPAN] * (
                mm(k2, jnp.concatenate([gh, gh], axis=0)) + mm(k2[:, :DS], gl)
            )
            scaled_grads[k] = scaled_grad
            lh, ll = split(leaving[at : at + SPAN])
            key_grad[rows, :] += mm_nt(
                jnp.concatenate([lh, ll], axis=1), jnp.concatenate([gh, gh], axis=1)
            ) + mm_nt(lh, gl)
            after = states_ref[k] + start[k + 1 : k + 2] * state_in
            ends[k] = jnp.sum(state_back * after, axis=0, keepdims=True)
            before = start[k : k + 1] * state_in
            if k > 0:
                before = before + states_ref[k - 1]
            th, tl = split(before)
            eh, el = split(entering[at : at + SPAN])
            query_grad[rows, :] += mm_nt(
                jnp.concatenate([eh, el], axis=1), jnp.concatenate([th, th], axis=1)
            ) + mm_nt(eh, tl)
            if k > 0:
                more = mm(query_turned[k, 0], jnp.concatenate([eh, el], axis=1))
                state_back = (
                    factor[k : k + 1] * state_back
                    + more[:, :LANES]
                    + more[:, LANES:]
                    + mm(query_turned[k, 1], eh)
                )
        scaled_grad = jnp.concatenate(scaled_grads, axis=0)
        target = lax.broadcasted_iota(jnp.int32, (LANES, LANES), 1)
        source = lax.broadcasted_iota(jnp.int32, (LANES, LANES), 0)
        place = (target == 2 * pair + source // HD).astype(bf16)
        dh, dl = split(inner * scaled_grad)
        steps_out[...] += mm(dh, place) + mm(dl, place)
        sums = conv_back(steps * scaled_grad + skip[0:1] * back, block, shifted, pre)
        ends[4] = jnp.sum(back * inner, axis=0, keepdims=True)
        taps_out[...] = jnp.concatenate([zero_row if s is None else s for s in sums], axis=0)
        eh, el, ew = split_three(jnp.concatenate(ends, axis=0))
        heads_out[...] += mm(eh, place) + mm(el, place) + mm(ew, place)

    if not last:
        return

    def of_scores(grad_ref, ones_ref, transposed):
        for k in range(spans):
            rows = pl.ds(k * SPAN, SPAN)
            grad = scores_grad[k]
            gh, gl = split(grad.T if transposed else grad)
            ones = ones_ref[rows, :]
            wide = mm(gh, ones)
            grad_ref[rows, :] += wide[:, :DS] + wide[:, DS:] + mm(gl, ones[:, :DS])

    @pl.when(jnp.logical_and(step >= pairs, step < pairs + 2))
    def _():
        @pl.when(step == pairs)
        def _():
            of_scores(key_grad, query_both, False)

        @pl.when(step == pairs + 1)
        def _():
            of_scores(query_grad, key_both, True)

        block, shifted, pre = of_conv()
        grad = jnp.where(step == pairs, key_grad[...], query_grad[...])
        sums = conv_back(grad, block, shifted, pre)
        taps_out[...] = jnp.concatenate([zero_row if s is None else s for s in sums], axis=0)

    @pl.when(step == pairs + 2)
    def _():
        tall = lax.broadcasted_iota(jnp.int32, (SPAN, SPAN), 0)
        wide = lax.broadcasted_iota(jnp.int32, (SPAN, SPAN), 1)
        upper = (tall <= wide).astype(bf16)
        known = lane < NH
        rate = params_ref[1:2]
        delta, decay, most = zero_row, zero_row, zero_row
        for k in range(spans):
            rows = pl.ds(k * SPAN, SPAN)
            steps = jnp.where(known, pltpu.roll(steps_ref[rows, :], LANES // 2, 1), 0.0)
            step_dots = steps_out[rows, :]
            cumul_grad = dots_ref[rows, :] - steps * step_dots
            parts = mm(upper, jnp.concatenate(split_three(cumul_grad), axis=1))
            decay_grad = parts[:, :LANES] + parts[:, LANES : 2 * LANES] + parts[:, 2 * LANES :]
            decay_grad = decay_grad + heads_out[k : k + 1]
            raw = jnp.where(known, raw_ref[rows, :], 0.0) + params_ref[0:1]
            raw_grad = (step_dots + rate * decay_grad) * sigmoid(raw)
            raw_grad = jnp.where(known, raw_grad, 0.0)
            grad_out[rows, :] = raw_grad.astype(bf16)
            most = jnp.maximum(most, jnp.max(jnp.abs(raw_grad), axis=0, keepdims=True))
            delta = delta + jnp.sum(raw_grad, axis=0, keepdims=True)
            decay = decay + jnp.sum(rate * steps * decay_grad, axis=0, keepdims=True)
        sums_out[...] = jnp.concatenate(
            [delta, decay, heads_out[4:5], most, jnp.zeros((4, LANES), f32)], axis=0
        )

    @pl.when(step > pairs + 2)
    def _():
        grad_out[...] = jnp.zeros_like(grad_out)


def backward_call(spans, first, pairs, columns, shared, finish=None, most=None):
    count = spans * SPAN
    last = finish is not None
    clip_block = lambda i: jnp.minimum(i + first, CONVD // LANES - 1)
    clip = lambda i: jnp.minimum(i, pairs - 1) + first
    at_block = lambda n: pl.BlockSpec((n, LANES), lambda i: (0, clip_block(i)))
    at_pair = lambda n: pl.BlockSpec((n, LANES), lambda i: (0, clip(i)))
    out_block = lambda n: pl.BlockSpec((n, LANES), lambda i: (0, i))
    whole = lambda *s: pl.BlockSpec(s, lambda i: (0,) * len(s))
    accumulators = [
        (spans, SPAN, SPAN),
        (count, DS),
        (count, DS),
        (count, LANES),
        (8, LANES),
    ]
    wide = columns * LANES
    side = (pairs + 2 if last else pairs) * LANES
    side_block = lambda: pl.BlockSpec(
        (8, LANES), lambda i: (0, jnp.minimum(i, side // LANES - 1))
    )
    in_specs = [
        at_block(count),
        at_block(8),
        at_block(8),
        whole(CONV - 1, count, LANES),
        whole(CONV - 1, count, LANES),
        whole(CONV - 1, 8, LANES),
        whole(count, DS),
        whole(count, DS),
        at_pair(count),
        whole(count, LANES),
        whole(count, LANES),
        pl.BlockSpec((8, count), lambda i: (clip(i) // 4, 0)),
        whole(8, LANES),
        whole(8, LANES),
        whole(spans, SPAN, SPAN),
        pl.BlockSpec((spans, DS, LANES), lambda i: (0, 0, clip(i))),
        at_pair(DS),
        at_pair(DS),
        whole(8, LANES),
    ]
    out_specs = [out_block(count)] + [side_block()] * 4 + [whole(*s) for s in accumulators]
    out_shape = [jax.ShapeDtypeStruct((count, wide), bf16)]
    out_shape += [jax.ShapeDtypeStruct((8, side), f32)] * 4
    out_shape += [jax.ShapeDtypeStruct(s, f32) for s in accumulators]
    operands = list(shared)
    scratch, remote = [], {}
    if most is not None:
        in_specs += [whole(8, LANES)]
        operands += [most]
        scratch, remote = agreement_scratch(), dict(collective_id=6, has_side_effects=True)
    if last:
        dots, mixed, params, earlier = finish
        in_specs += [
            whole(count, LANES),
            pl.BlockSpec((count, LANES), lambda i: (0, CONVD // LANES)),
            whole(8, LANES),
        ]
        in_specs += [whole(*s) for s in accumulators]
        operands += [dots, mixed, params, *earlier]
        out_specs += [whole(8, LANES)]
        out_shape += [jax.ShapeDtypeStruct((8, LANES), f32)]
    if most is not None:
        out_specs += [pl.BlockSpec(memory_space=pltpu.SMEM)]
        out_shape += [jax.ShapeDtypeStruct((1, 1), f32)]
    return pl.pallas_call(
        functools.partial(backward_kernel, spans, first, pairs, last, most is not None),
        grid=(columns,),
        in_specs=in_specs,
        out_specs=out_specs,
        out_shape=out_shape,
        scratch_shapes=[
            pltpu.VMEM((spans, SPAN, SPAN), f32),
            pltpu.VMEM((count, 2 * DS), bf16),
            pltpu.VMEM((count, 2 * DS), bf16),
            pltpu.VMEM((spans, 2, DS, SPAN), bf16),
            pltpu.VMEM((count + 8, LANES), f32),
            pltpu.VMEM((3, count, 2 * LANES), bf16),
        ]
        + scratch,
        compiler_params=pltpu.CompilerParams(vmem_limit_bytes=VMEM_LIMIT, **remote),
        cost_estimate=pl.CostEstimate(flops=1, bytes_accessed=1, transcendentals=0),
        name="recurrence_backward",
    )(*operands)


def sum_kernel(in_ref, limit_ref, *refs):
    *sizes, out_ref, own, near, far, whole, sent, landed = refs
    f, ctx = lax.axis_index("fsdp"), lax.axis_index("ctx")
    fsdp_size, ctx_size = lax.axis_size("fsdp"), lax.axis_size("ctx")
    most = functools.reduce(jnp.maximum, [jnp.max(jnp.abs(size[...])) for size in sizes])
    row = lax.broadcasted_iota(jnp.int32, in_ref.shape, 0)
    lane = lax.broadcasted_iota(jnp.int32, in_ref.shape, 1)
    last = jnp.logical_and(row == in_ref.shape[0] - 1, lane == LANES - 1)
    over = jnp.where(most <= limit_ref[0, 0], 0.0, 1.0)
    own[...] = in_ref[...] + jnp.where(last, over, 0.0)
    part = in_ref.shape[0] // fsdp_size
    in_ctx = [(f, lax.rem(ctx + d, ctx_size)) for d in range(1, ctx_size)]
    in_fsdp = [(lax.rem(f + d, fsdp_size), ctx) for d in range(1, fsdp_size)]
    barrier = pltpu.get_barrier_semaphore()
    for partner in in_ctx + in_fsdp:
        pl.semaphore_signal(barrier, inc=1, device_id=partner, device_id_type=MESH)
    pl.semaphore_wait(barrier, len(in_ctx) + len(in_fsdp))

    def exchange(phase, partners, source, target):
        copies = []
        for n, partner in enumerate(partners):
            copies.append(
                pltpu.make_async_remote_copy(
                    src_ref=source(partner),
                    dst_ref=target,
                    send_sem=sent.at[phase, n],
                    recv_sem=landed.at[phase, n],
                    device_id=partner,
                    device_id_type=MESH,
                )
            )
            copies[-1].start()
        return copies

    copies = exchange(0, in_ctx, lambda partner: own, near.at[ctx])
    near[pl.ds(ctx, 1)] = own[...][None]
    for copy in copies:
        copy.wait()
    whole[...] = jnp.sum(near[...], axis=0)
    mine = pl.ds(pl.multiple_of(f * part, 8), part)
    copies = exchange(
        1, in_fsdp, lambda partner: whole.at[pl.ds(pl.multiple_of(partner[0] * part, 8), part)], far.at[f]
    )
    far[pl.ds(f, 1)] = whole[mine, :][None]
    for copy in copies:
        copy.wait()
    out_ref[mine, :] = jnp.sum(far[...], axis=0)
    for copy in exchange(2, in_fsdp, lambda partner: out_ref.at[mine], out_ref.at[mine]):
        copy.wait()


def sum_everywhere(value, limit, sizes):
    if not on_small_slice():
        return lax.psum(value, ("fsdp", "ctx")), None
    fsdp_size, ctx_size = lax.axis_size("fsdp"), lax.axis_size("ctx")
    block = 8 * LANES * fsdp_size
    rows = -(-(value.shape[0] + 1) // block) * block // LANES
    shape = (rows, LANES)
    padded_value = jnp.pad(value, (0, rows * LANES - value.shape[0])).reshape(shape)
    peers = max(fsdp_size, ctx_size) - 1
    out = pl.pallas_call(
        sum_kernel,
        in_specs=[
            pl.BlockSpec(memory_space=pltpu.VMEM),
            pl.BlockSpec(memory_space=pltpu.SMEM),
        ]
        + [pl.BlockSpec(memory_space=pltpu.VMEM)] * len(sizes),
        out_specs=pl.BlockSpec(memory_space=pltpu.VMEM),
        out_shape=jax.ShapeDtypeStruct(shape, f32),
        scratch_shapes=[
            pltpu.VMEM(shape, f32),
            pltpu.VMEM((ctx_size,) + shape, f32),
            pltpu.VMEM((fsdp_size, rows // fsdp_size, LANES), f32),
            pltpu.VMEM(shape, f32),
            pltpu.SemaphoreType.DMA((3, peers)),
            pltpu.SemaphoreType.DMA((3, peers)),
        ],
        compiler_params=pltpu.CompilerParams(collective_id=4, has_side_effects=True),
        cost_estimate=pl.CostEstimate(flops=1, bytes_accessed=1, transcendentals=0),
        name="sum_everywhere",
    )(padded_value, limit.reshape(1, 1), *sizes)
    return out.reshape(-1)[: value.shape[0]], out[rows - 1, LANES - 1] > 0.0


FILL_COLS = 256


def block_out_kernel(mixer_ref, whole_ref, tokens_ref, out_ref):
    projected = mm(mixer_ref[...], whole_ref[...])
    out_ref[...] = (tokens_ref[...].astype(f32) + projected).astype(bf16)


def block_out_call(mixer_low, whole_out, tokens):
    count, width = tokens.shape
    columns = lambda n: pl.BlockSpec((n, FILL_COLS), lambda j: (0, j))
    return pl.pallas_call(
        block_out_kernel,
        grid=(width // FILL_COLS,),
        in_specs=[pl.BlockSpec((count, DI), lambda j: (0, 0)), columns(DI), columns(count)],
        out_specs=columns(count),
        out_shape=jax.ShapeDtypeStruct(tokens.shape, bf16),
        compiler_params=pltpu.CompilerParams(vmem_limit_bytes=VMEM_LIMIT),
        cost_estimate=pl.CostEstimate(flops=1, bytes_accessed=1, transcendentals=0),
        name="block_out",
    )(mixer_low, whole_out, tokens)


def input_grad_kernel(
    split_at,
    second_width,
    gate_ref,
    first_ref,
    second_ref,
    whole_gate_ref,
    whole_conv_ref,
    tokens_ref,
    cotangent_ref,
    gain_ref,
    out_ref,
    gain_grad_ref,
    unit_grads,
    scales,
    mixes,
):
    step, steps = pl.program_id(0), pl.num_programs(0)
    count = tokens_ref.shape[0]

    @pl.when(step == 0)
    def _():
        mixes[...] = jnp.zeros_like(mixes)
        for at in range(0, count, SPAN):
            rows = pl.ds(at, SPAN)
            inputs = tokens_ref[rows, :].astype(f32)
            mean = jnp.mean(inputs * inputs, axis=-1, keepdims=True)
            scales[rows, :] = jnp.broadcast_to(lax.rsqrt(mean + norm_eps), (SPAN, LANES))

    grad = mm_nt(gate_ref[...], whole_gate_ref[...])
    grad = grad + mm_nt(first_ref[...], whole_conv_ref[:, :split_at])
    grad = grad + mm_nt(
        second_ref[:, :second_width], whole_conv_ref[:, split_at : split_at + second_width]
    )
    here = pl.ds(pl.multiple_of(step * FILL_COLS, FILL_COLS), FILL_COLS)
    unit = tokens_ref[:, here].astype(f32) * scales[:, 0:1]
    gain_grad_ref[0:1, :] = jnp.sum(grad * unit, axis=0, keepdims=True)
    unit_grad = grad * gain_ref[0:1, :]
    unit_grads[step] = unit_grad
    mixes[...] += jnp.broadcast_to(
        jnp.sum(unit_grad * unit, axis=-1, keepdims=True), mixes.shape
    )

    @pl.when(step == steps - 1)
    def _():
        width = tokens_ref.shape[1]
        for at in range(0, count, SPAN):
            rows = pl.ds(at, SPAN)
            scale = scales[rows, 0:1]
            mean = mixes[rows, 0:1] * (1.0 / width)
            for n in range(width // FILL_COLS):
                cols = pl.ds(n * FILL_COLS, FILL_COLS)
                unit = tokens_ref[rows, cols].astype(f32) * scale
                out_ref[rows, cols] = cotangent_ref[rows, cols].astype(f32) + scale * (
                    unit_grads[n, rows, :] - unit * mean
                )


def input_grad_call(
    split_at,
    gate_grad,
    first_grad,
    second_grad,
    whole_gate,
    whole_conv,
    tokens,
    cotangent,
    gain,
):
    count, width = tokens.shape
    once = lambda *s: pl.BlockSpec(s, lambda j: (0,) * len(s), pipeline_mode=pl.Buffered(1))
    rows = lambda n: pl.BlockSpec((FILL_COLS, n), lambda j: (j, 0))
    columns = lambda n: pl.BlockSpec((n, FILL_COLS), lambda j: (0, j))
    steps = width // FILL_COLS
    return pl.pallas_call(
        functools.partial(input_grad_kernel, split_at, whole_conv.shape[1] - split_at),
        grid=(steps,),
        in_specs=[
            once(*gate_grad.shape),
            once(*first_grad.shape),
            once(*second_grad.shape),
            rows(whole_gate.shape[1]),
            rows(whole_conv.shape[1]),
            once(count, width),
            once(count, width),
            columns(8),
        ],
        out_specs=[pl.BlockSpec((count, width), lambda j: (0, 0)), columns(8)],
        out_shape=[
            jax.ShapeDtypeStruct((count, width), f32),
            jax.ShapeDtypeStruct((8, width), f32),
        ],
        scratch_shapes=[
            pltpu.VMEM((steps, count, FILL_COLS), f32),
            pltpu.VMEM((count, LANES), f32),
            pltpu.VMEM((count, LANES), f32),
        ],
        compiler_params=pltpu.CompilerParams(vmem_limit_bytes=VMEM_LIMIT),
        cost_estimate=pl.CostEstimate(flops=1, bytes_accessed=1, transcendentals=0),
        name="input_grad",
    )(gate_grad, first_grad, second_grad, whole_gate, whole_conv, tokens, cotangent, gain)


def adam_kernel(blocks, core_ref, *refs):
    grads, refs = refs[: 2 * blocks], refs[2 * blocks :]
    param_ref, first_ref, second_ref = refs[:3]
    outs = refs[-3:]
    width = param_ref.shape[1]
    own_first = core_ref[0] == 0
    begin = 0
    for n in range(blocks):
        own_ref, other_ref = grads[2 * n], grads[2 * n + 1]
        for left in (True, False):
            for at in range(0, own_ref.shape[1], LANES):
                size = min(LANES, width - begin)
                if size <= 0:
                    continue
                there, cols = pl.ds(at, size), pl.ds(begin, size)
                own, other = own_ref[:, there], other_ref[:, there]
                one, two = (own, other) if left else (other, own)
                new = adamw_update(
                    param_ref[:, cols],
                    jnp.where(own_first, one, two),
                    first_ref[:, cols],
                    second_ref[:, cols],
                    weight_decay,
                )
                for out, value in zip(outs, new):
                    out[:, cols] = value
                begin += size


def adam_call(core, grads, rows, param, first, second):
    total, width = param.shape
    rows = min(rows, total)
    place = lambda n: pl.BlockSpec((rows, n), lambda i: (i, 0))
    pieces = [piece for pair in grads for piece in pair]
    return pl.pallas_call(
        functools.partial(adam_kernel, len(grads)),
        grid=(total // rows,),
        in_specs=[pl.BlockSpec(memory_space=pltpu.SMEM)]
        + [place(piece.shape[1]) for piece in pieces]
        + [place(width)] * 3,
        out_specs=[place(width)] * 3,
        out_shape=[jax.ShapeDtypeStruct(param.shape, f32)] * 3,
        compiler_params=pltpu.CompilerParams(vmem_limit_bytes=VMEM_LIMIT),
        cost_estimate=pl.CostEstimate(flops=1, bytes_accessed=1, transcendentals=0),
        name="adam",
    )(core, *pieces, param, first, second)


def adamw_update(param, grad, first, second, decay):
    first_new = beta_one * first + (1.0 - beta_one) * grad
    second_new = beta_two * second + (1.0 - beta_two) * grad * grad
    first_hat = first_new / (1.0 - beta_one**STEP)
    second_hat = second_new / (1.0 - beta_two**STEP)
    param_new = param - learn_rate * (first_hat / (jnp.sqrt(second_hat) + adam_eps) + decay * param)
    return (param_new, first_new, second_new)


def segment_of(lengths, positions):
    ends = jnp.cumsum(lengths)
    return jnp.sum((positions[..., None] >= ends).astype(jnp.int32), axis=-1)


def padded(*rows):
    out = jnp.stack([jnp.pad(r, (0, LANES - r.shape[0])) for r in rows])
    return jnp.pad(out, ((0, 8 - len(rows)), (0, 0)))


def spread_matrix():
    head = lax.broadcasted_iota(jnp.int32, (LANES, DI), 0)
    lane = lax.broadcasted_iota(jnp.int32, (LANES, DI), 1)
    return (head == lane // HD).astype(bf16)


def pass_on(own, factor, axis, backwards, kind):
    size, here = lax.axis_size(axis), lax.axis_index(axis)
    given = jnp.zeros_like(own)
    for turn in range(size - 1):
        source = size - 1 - turn if backwards else turn
        target = source - 1 if backwards else source + 1
        out = (factor * given + own).astype(kind)
        arrived = lax.ppermute(out, axis, [(source, target)]).astype(f32)
        given = jnp.where(here == target, arrived, given)
    return given


def on_small_slice():
    return lax.axis_size("fsdp") == Z * Y and lax.axis_size("ctx") == 4


def all_rows(block):
    return lax.all_gather(block, "fsdp", axis=0, tiled=True)


def swapped(value, axis, step):
    size = lax.axis_size(axis)
    return lax.ppermute(value, axis, [(i, i ^ step) for i in range(size)])


def after(value, *others):
    return lax.optimization_barrier((value,) + others)[0]


def coordinates():
    f, ctx = lax.axis_index("fsdp"), lax.axis_index("ctx")
    return ctx // 2, f % Y, f // Y, ctx % 2


CORE = ("ctx", 1)
ACROSS_X = ("ctx", 2)
ACROSS_Y = ("fsdp", 1)
ACROSS_Z = tuple(("fsdp", Y * m) for m in range(1, Z))


def row_products(columns, grads):
    return jnp.einsum("tk,tz->kz", columns, grads, preferred_element_type=f32)


def half_of(value, bit, axis):
    size = value.shape[axis] // 2
    return lax.dynamic_slice_in_dim(value, bit * size, size, axis)


class Part:
    def __init__(self, value, bound):
        self.value, self.bound = value, bound

    def plus(self, arrived, other):
        return Part(self.value + raised(arrived, other), self.bound + other)


def lowered(value, bound):
    return (value * (32768.0 / bound)).astype(jnp.float16)


def raised(value, bound):
    return value.astype(f32) * (bound * (1.0 / 32768.0))


def summed_on_chip(columns, grads, bound, other=None):
    core = coordinates()[3]
    theirs = row_products(columns, half_of(grads, 1 - core, 1))
    arrived = swapped(lowered(theirs, bound), *CORE)
    mine = Part(row_products(columns, half_of(grads, core, 1)), bound)
    return mine.plus(arrived, bound if other is None else other)


def to_send(part, bit, axis):
    sent = lowered(half_of(part.value, 1 - bit, axis), part.bound)
    return Part(half_of(part.value, bit, axis), part.bound), sent


def joined_with(kept, arrived, other=None):
    return kept.plus(arrived, kept.bound if other is None else other)


def by_owner(part):
    return Part(part.value.reshape(Z, Y, -1, part.value.shape[1]), part.bound)


def along_z(part):
    z = coordinates()[2]
    take = lambda at: lax.dynamic_index_in_dim(part.value[:, 0], at, 0, keepdims=False)
    sent = [lowered(take(z ^ m), part.bound) for m in range(1, Z)]
    return Part(take(z), part.bound), sent


def of_owner(kept, arrived):
    total = kept
    for one in arrived:
        total = total.plus(one, kept.bound)
    return total


def both_columns(value, way, bit):
    other = swapped(value, *way)
    return jnp.where(
        bit == 0,
        jnp.concatenate([value, other], axis=1),
        jnp.concatenate([other, value], axis=1),
    )


def sum_of_two(low, arrived, bound):
    return raised(low, bound) + raised(arrived, bound)


ROOM = 64.0


def owned_rows(partial):
    return lax.psum(lax.psum_scatter(partial, "fsdp", scatter_dimension=0, tiled=True), "ctx")


def largest(value):
    return jnp.max(jnp.abs(value)).astype(f32) + 1e-30


def on_device(
    tokens_in,
    cotangent,
    doc_lengths,
    in_proj,
    out_proj,
    norm_gain,
    gate_gain,
    conv_weight,
    conv_bias,
    delta_bias,
    decay_log,
    skip_scale,
    in_first,
    in_second,
    out_first,
    out_second,
    small_first,
    small_second,
):
    count = tokens_in.shape[0]
    spans = count // SPAN
    ctx = lax.axis_size("ctx")
    begin = lax.axis_index("ctx") * count
    lengths = doc_lengths[0]
    small_slice = on_small_slice()

    if small_slice:
        gate_block, conv_block, out_block = cast_call(in_proj, out_proj)
        (whole_conv,) = gather_call(conv_block)
    else:
        blocks = in_proj[:, DI:], in_proj[:, :DI], out_proj
        whole_conv, whole_gate, whole_out = (all_rows(b.astype(bf16)) for b in blocks)
    inputs = tokens_in.astype(f32)
    scale = lax.rsqrt(jnp.mean(inputs * inputs, axis=-1, keepdims=True) + norm_eps)
    normed = (inputs * scale * norm_gain[None, :]).astype(bf16)

    mixed = mm(normed, whole_conv)
    edge = lax.ppermute(mixed[count - 8 :, :CONVD], "ctx", [(i, i + 1) for i in range(ctx - 1)])
    edge = jnp.where(jnp.arange(8)[:, None] >= 8 - (CONV - 1), edge, 0.0)

    place = jnp.concatenate([begin[None].astype(jnp.int32), lengths.astype(jnp.int32)])
    params = padded(delta_bias, -jnp.exp(decay_log))
    (
        steps,
        decay,
        reach,
        rows,
        factor,
        start,
        inside,
        inside_back,
        outside,
        mask,
        mask_turned,
    ) = prepare_call(spans, place, mixed, params)
    taps = jnp.concatenate([conv_weight.T, conv_bias[None], jnp.zeros((3, CONVD), f32)], axis=0)

    inner, local, states, keys, queries, *wholes = forward_call(
        spans,
        mixed,
        edge,
        taps,
        inside,
        outside,
        steps,
        decay,
        rows,
        factor,
        mask,
        (gate_block, out_block) if small_slice else (),
    )
    if small_slice:
        whole_gate, whole_out = wholes
    total_lanes = jnp.repeat(start[spans, :NH], HD)[None]
    state_in = pass_on(states[spans - 1], total_lanes, "ctx", False, f32)
    gate = mm(normed, whole_gate)
    mixer_back = jnp.einsum("td,kd->tk", cotangent, whole_out, preferred_element_type=f32)
    mixer_low, mixer_grad, gate_grad, gate_gain_grad, dots, summary, gate_most_rows = norm_call(
        local,
        inner,
        gate,
        mixer_back,
        queries,
        state_in,
        reach,
        spread_matrix(),
        jnp.repeat(skip_scale, HD)[None] + jnp.zeros((8, 1), f32),
        gate_gain[None] + jnp.zeros((8, 1), f32),
    )
    state_back = pass_on(summary, total_lanes, "ctx", True, bf16)

    out_bound = count * 6.0 * (DI**0.5 * 1.01) * largest(gate_gain)
    product_bound = count * (D**0.5 * 1.01) * largest(norm_gain)
    x, y, z, core = coordinates()
    if small_slice:
        out_part = summed_on_chip(mixer_low, cotangent, out_bound)
        out_kept, out_sent = to_send(out_part, x, 1)
        mosts, others = [1.01 * product_bound * largest(gate_most_rows)], []
        for way in (CORE, ACROSS_Y):
            others.append(swapped(mosts[-1].reshape(1, 1), *way).reshape(()))
            mosts.append(jnp.maximum(mosts[-1], others[-1]))
        gate_part = summed_on_chip(normed, gate_grad, mosts[0], others[0])
        gate_kept, gate_sent = to_send(by_owner(Part(gate_part.value, 2.0 * mosts[1])), y, 1)
        mixer_grad, out_sent, gate_sent = lax.optimization_barrier(
            (mixer_grad, out_sent, gate_sent)
        )
        out_got = swapped(out_sent, *ACROSS_X)
        gate_got = swapped(gate_sent, *ACROSS_Y)

    first_pairs = 14
    skip = padded(skip_scale)
    shared = lambda back: (
        mixed,
        edge,
        taps,
        inside,
        inside_back,
        outside,
        keys,
        queries,
        back,
        steps,
        decay,
        rows,
        factor,
        start,
        mask_turned,
        states,
        state_in,
        state_back,
        skip,
    )
    following = segment_of(lengths, begin + count + jnp.arange(CONV, dtype=jnp.int32))
    own_last = segment_of(lengths, begin + count - CONV + jnp.arange(CONV, dtype=jnp.int32))

    def with_edge(grad, top, tail, at):
        next_top = lax.ppermute(top, "ctx", [(i + 1, i) for i in range(ctx - 1)])
        width = tail.shape[1]
        for j in range(1, CONV):
            joined = (following[:j] == own_last[CONV - j :]).astype(f32)
            more = joined[:, None] * next_top[:j] * taps[3 - j : 4 - j, at : at + width]
            tail = tail + jnp.pad(more, ((8 - j, 0), (0, 0)))
        return lax.dynamic_update_slice(grad, tail.astype(bf16), (count - 8, 0)), tail

    first_grad, top, tail, first_taps_grad, most, *sums = backward_call(
        spans,
        0,
        first_pairs,
        first_pairs,
        shared(mixer_grad),
        most=gate_most_rows if small_slice else None,
    )
    if small_slice:
        top, tail, most, first_grad, out_got, gate_got = lax.optimization_barrier(
            (top, tail, most, first_grad, out_got, gate_got)
        )
    first_grad, tail = with_edge(first_grad, top, tail, 0)
    if small_slice:
        out_kept, out_sent = to_send(by_owner(joined_with(out_kept, out_got)), y, 1)
        *sums, agreed = sums
        gate_most = 1.01 * product_bound * agreed.reshape(()) + 1e-30
        gate_part = joined_with(gate_kept, gate_got, 2.0 * others[1])
        gate_kept, gate_sent = along_z(Part(gate_part.value, 4.0 * gate_most))
        conv_bound = ROOM * gate_most
        first_sizes = most, tail
        first_part = summed_on_chip(normed, first_grad, conv_bound)
        first_kept, first_sent = to_send(by_owner(first_part), y, 1)
        mixer_grad, out_sent, gate_sent, first_sent = lax.optimization_barrier(
            (mixer_grad, out_sent, gate_sent, first_sent)
        )
        out_got = swapped(out_sent, *ACROSS_Y)
        gate_got = [swapped(s, *way) for s, way in zip(gate_sent, ACROSS_Z)]
        first_got = swapped(first_sent, *ACROSS_Y)
    second_grad, top, tail, second_taps_grad, most, *sums = backward_call(
        spans,
        first_pairs,
        PAIRS - first_pairs,
        14,
        shared(mixer_grad),
        (dots, mixed, params, sums),
    )
    split_at = first_pairs * LANES
    fence = lax.optimization_barrier
    if small_slice:
        top, tail, most, second_grad, sums, out_got, gate_got, first_got = fence(
            (top, tail, most, second_grad, sums, out_got, gate_got, first_got)
        )
        out_kept, out_sent = along_z(joined_with(out_kept, out_got))
        first_kept, first_sent = along_z(joined_with(first_kept, first_got))
        out_high = out_sent[0].shape[0] // 2
        both_sent = [
            jnp.concatenate([one, other[:out_high], other[out_high:]], axis=1)
            for one, other in zip(first_sent, out_sent)
        ]
        gate_part = Part(of_owner(gate_kept, gate_got).value, 16.0 * gate_most)
        gate_low = lowered(gate_part.value, gate_part.bound)
        both_sent, gate_low, tail, most = fence((both_sent, gate_low, tail, most))
        both_got = [swapped(s, *way) for s, way in zip(both_sent, ACROSS_Z)]
        gate_got = swapped(gate_low, *ACROSS_X)
    second_grad, tail = with_edge(second_grad, top, tail, split_at)
    if small_slice:
        second_part = summed_on_chip(normed, second_grad, conv_bound)
        second_kept, second_sent = to_send(by_owner(second_part), y, 1)
        (
            second_sent,
            gate_grad,
            mixer_low,
            sums,
            gate_gain_grad,
            first_taps_grad,
            second_taps_grad,
            conv_weight,
            sizes,
        ) = fence(
            (
                second_sent,
                gate_grad,
                mixer_low,
                sums,
                gate_gain_grad,
                first_taps_grad,
                second_taps_grad,
                conv_weight,
                (*first_sizes, most, tail),
            )
        )
        second_got = swapped(second_sent, *ACROSS_Y)
    input_grad, norm_gain_grad = input_grad_call(
        split_at,
        gate_grad,
        first_grad,
        second_grad,
        whole_gate,
        whole_conv,
        tokens_in,
        cotangent,
        norm_gain[None] + jnp.zeros((8, 1), f32),
    )
    block_out = block_out_call(mixer_low, whole_out, tokens_in)
    limit = None
    if not small_slice:
        sizes = ()
    if small_slice:
        second_got, both_got, gate_got, input_grad, norm_gain_grad, block_out = fence(
            (second_got, both_got, gate_got, input_grad, norm_gain_grad, block_out)
        )
        second_kept, second_sent = along_z(joined_with(second_kept, second_got))
        first_wide = first_part.value.shape[1]
        out_wide = (both_got[0].shape[1] - first_wide) // 2
        out_got = [
            jnp.concatenate(
                [s[:, first_wide : first_wide + out_wide], s[:, first_wide + out_wide :]], axis=0
            )
            for s in both_got
        ]
        first_part = of_owner(first_kept, [s[:, :first_wide] for s in both_got])
        first_low = lowered(first_part.value, first_part.bound)
        out_total = of_owner(out_kept, out_got).value
        gate_rows = sum_of_two(gate_low, gate_got, gate_part.bound)
        second_sent, first_low, out_total, gate_rows, norm_gain_grad = fence(
            (second_sent, first_low, out_total, gate_rows, norm_gain_grad)
        )
        second_got = [swapped(s, *way) for s, way in zip(second_sent, ACROSS_Z)]
        first_got = swapped(first_low, *ACROSS_X)
        out_got = swapped(out_total, *ACROSS_X)
        limit = conv_bound * (1.0 / (1.01 * product_bound))
        sizes = *sizes, sums[5][3:4]
    taps_grad = jnp.concatenate([first_taps_grad, second_taps_grad], axis=1)
    small_grad, over = sum_everywhere(
        jnp.concatenate(
            [
                norm_gain_grad[0],
                gate_gain_grad[0],
                taps_grad[:CONV].T.reshape(-1),
                taps_grad[4],
                sums[5][0, :NH],
                sums[5][1, :NH],
                sums[5][2, :NH],
            ]
        ),
        limit,
        sizes,
    )

    def in_updated(core, *pairs):
        return tuple(adam_call(core, pairs, 48, in_proj, in_first, in_second))

    def out_updated(core, pair):
        return tuple(adam_call(core, (pair,), 96, out_proj, out_first, out_second))

    def halves_in_float32(columns, grads):
        rows = owned_rows(row_products(columns, grads))
        return rows[:, : rows.shape[1] // 2], rows[:, rows.shape[1] // 2 :]

    def in_float32():
        grads = gate_grad, first_grad, second_grad
        pairs = [halves_in_float32(normed, one) for one in grads]
        return in_updated(jnp.zeros((1,), jnp.int32), *pairs)

    def out_in_float32():
        return out_updated(jnp.zeros((1,), jnp.int32), halves_in_float32(mixer_low, cotangent))

    if small_slice:
        small_grad, over, first_got, out_got, gate_rows, second_got = fence(
            (small_grad, over, first_got, out_got, gate_rows, second_got)
        )
        second_part = of_owner(second_kept, second_got)
        second_low = lowered(second_part.value, second_part.bound)
        second_low, first_got, out_got = fence((second_low, first_got, out_got))
        second_got = swapped(second_low, *ACROSS_X)
        first_rows = sum_of_two(first_low, first_got, first_part.bound)
        out_rows = jnp.where(
            x == 0,
            jnp.concatenate([out_total, out_got], axis=1),
            jnp.concatenate([out_got, out_total], axis=1),
        )
        gate_pair = gate_rows, swapped(gate_rows, *CORE)
        first_pair = first_rows, swapped(first_rows, *CORE)
        out_pair = out_rows, swapped(out_rows, *CORE)
        core_index = core[None].astype(jnp.int32)
        out_news = lax.cond(over, out_in_float32, lambda: out_updated(core_index, out_pair))
        second_got, out_news = fence((second_got, out_news))
        second_rows = sum_of_two(second_low, second_got, second_part.bound)
        second_pair = second_rows, swapped(second_rows, *CORE)
        in_news = lax.cond(
            over,
            in_float32,
            lambda: in_updated(core_index, gate_pair, first_pair, second_pair),
        )
    else:
        in_news, out_news = in_float32(), out_in_float32()
    in_new, in_first_new, in_second_new = in_news
    out_new, out_first_new, out_second_new = out_news
    small_param = jnp.concatenate(
        [
            norm_gain,
            gate_gain,
            conv_weight.reshape(-1),
            conv_bias,
            delta_bias,
            decay_log,
            skip_scale,
        ]
    )
    small_new, small_first_new, small_second_new = adamw_update(
        small_param, small_grad, small_first, small_second, 0.0
    )
    return (
        block_out,
        input_grad,
        in_new,
        in_first_new,
        in_second_new,
        out_new,
        out_first_new,
        out_second_new,
        small_new,
        small_first_new,
        small_second_new,
    )


def solution(mesh):
    placed = (
        P(("fsdp", "ctx"), None),
        P(("fsdp", "ctx"), None),
        P("fsdp", None),
        P("fsdp", None),
        P("fsdp", None),
        P(),
        P(),
        P(),
        P(),
        P(),
        P(),
        P(),
        P("fsdp", None),
        P("fsdp", None),
        P("fsdp", None),
        P("fsdp", None),
        P(),
        P(),
    )
    return jax.shard_map(
        on_device,
        mesh=mesh,
        in_specs=placed,
        out_specs=(
            P(("fsdp", "ctx"), None),
            P(("fsdp", "ctx"), None),
            P("fsdp", None),
            P("fsdp", None),
            P("fsdp", None),
            P("fsdp", None),
            P("fsdp", None),
            P("fsdp", None),
            P(),
            P(),
            P(),
        ),
        check_vma=False,
    )
```

```python
import functools

import jax
import jax.numpy as jnp
from jax import lax
from jax.experimental import pallas as pl
from jax.experimental.pallas import tpu as pltpu
from jax.sharding import PartitionSpec as P

D = 1536
DI = 3072
NH = 48
HD = 64
DS = 128
CONV = 4
SPAN = 256
STEP = 5
CONVD = 3328
LANES = 128
PAIRS = DI // LANES
HALF = SPAN // 2
NORM_ROWS = 128
NORM_COLS = 512
MASKED = -1e30

highest = lax.Precision.HIGHEST
norm_eps = 1e-05
beta_one = 0.9
beta_two = 0.95
adam_eps = 1e-08
learn_rate = 0.05
weight_decay = 0.1
f32 = jnp.float32
bf16 = jnp.bfloat16
VMEM_LIMIT = 56 * 1024 * 1024


def split(value):
    high = value.astype(bf16)
    return high, (value - high.astype(f32)).astype(bf16)


def mm(a, b):
    return jnp.dot(a, b, preferred_element_type=f32)


def mm_nt(a, b):
    return lax.dot_general(a, b, (((1,), (1,)), ((), ())), preferred_element_type=f32)


def sigmoid(v):
    return 1.0 / (1.0 + jnp.exp(-v))


def conv_shifts(block, edge, inside, outside, room):
    count = block.shape[0]
    room[pl.ds(8, count), :] = block
    shifted = []
    for j in range(1, CONV):
        body = inside[j - 1] * room[pl.ds(8 - j, count), :]
        head = inside[j - 1, :8] * pltpu.roll(block[:8], j, 0)
        head = head + outside[j - 1] * pltpu.roll(edge, j, 0)
        shifted.append(jnp.concatenate([head, body[8:]], axis=0))
    return shifted


def conv_pre(block, shifted, taps):
    total = taps[4:5] + taps[3:4] * block
    for j in range(1, CONV):
        total = total + taps[3 - j : 4 - j] * shifted[j - 1]
    return total


def pair_columns(packed, pair):
    turned = pltpu.roll(packed, lax.rem(LANES - 2 * pair, LANES), 1)
    lane = lax.broadcasted_iota(jnp.int32, packed.shape, 1)
    first = jnp.where(lane < HD, turned[:, 0:1], turned[:, 1:2])
    second = jnp.where(lane < HD, turned[:, 64:65], turned[:, 65:66])
    return turned, first, second


def spread_pair(both, pair):
    source = lax.broadcasted_iota(jnp.int32, (2 * LANES, LANES), 0)
    lane = lax.broadcasted_iota(jnp.int32, (2 * LANES, LANES), 1)
    return mm(both, (lax.rem(source, LANES) == 2 * pair + lane // HD).astype(bf16))


def pair_rows(rows, pair):
    turned = pltpu.roll(rows, lax.rem(LANES - 2 * pair, LANES), 1)
    lane = lax.broadcasted_iota(jnp.int32, rows.shape, 1)
    return jnp.where(lane < HD, turned[:, 0:1], turned[:, 1:2])


def head_row(block, head):
    sublane = lax.broadcasted_iota(jnp.int32, block.shape, 0)
    return jnp.sum(jnp.where(sublane == lax.rem(head, 8), block, 0.0), axis=0, keepdims=True)


def split_three(value):
    high, low = split(value)
    return high, low, (value - high.astype(f32) - low.astype(f32)).astype(bf16)


def cast_kernel(in_ref, out_ref, gate_low, conv_low, out_low):
    gate_low[...] = in_ref[:, :DI].astype(bf16)
    conv_low[...] = in_ref[:, DI:].astype(bf16)
    out_low[...] = out_ref[...].astype(bf16)


def cast_call(in_proj, out_proj):
    steps = 4
    widths = DI, in_proj.shape[1] - DI
    rows = lambda array, width: pl.BlockSpec((array.shape[0] // steps, width), lambda i: (i, 0))
    return pl.pallas_call(
        cast_kernel,
        grid=(steps,),
        in_specs=[rows(in_proj, in_proj.shape[1]), rows(out_proj, out_proj.shape[1])],
        out_specs=[rows(in_proj, w) for w in widths] + [rows(out_proj, out_proj.shape[1])],
        out_shape=[jax.ShapeDtypeStruct((in_proj.shape[0], w), bf16) for w in widths]
        + [jax.ShapeDtypeStruct(out_proj.shape, bf16)],
        compiler_params=pltpu.CompilerParams(vmem_limit_bytes=VMEM_LIMIT),
        name="cast_rows",
    )(in_proj, out_proj)


def prepare_kernel(
    spans,
    place_ref,
    raw_ref,
    params_ref,
    steps_out,
    decay_out,
    reach_out,
    turned_out,
    factor_out,
    start_out,
    inside_out,
    inside_back_out,
    outside_out,
    mask_out,
    mask_turned_out,
):
    count = spans * SPAN
    begin = place_ref[0]
    ends = []
    for d in range(place_ref.shape[0] - 1):
        ends.append(place_ref[d + 1] + (ends[-1] if ends else 0))

    def segment(position):
        total = (position >= ends[0]).astype(jnp.int32)
        for end in ends[1:]:
            total = total + (position >= end).astype(jnp.int32)
        return total

    row = lax.broadcasted_iota(jnp.int32, (count, LANES), 0)
    here = segment(row + begin)
    for j in range(1, CONV):
        same = here == segment(row + (begin - j))
        inside_out[j - 1] = jnp.where(jnp.logical_and(same, row >= j), 1.0, 0.0)
        later = here == segment(row + (begin + j))
        inside_back_out[j - 1] = jnp.where(jnp.logical_and(later, row + j < count), 1.0, 0.0)
        outside_out[j - 1] = jnp.where(jnp.logical_and(same, row < j), 1.0, 0.0)[:8]
    lane = lax.broadcasted_iota(jnp.int32, (count, LANES), 1)
    raw = jnp.where(lane < NH, raw_ref[...], 0.0) + params_ref[0:1]
    steps = jnp.where(lane < NH, jnp.maximum(raw, 0.0) + jnp.log1p(jnp.exp(-jnp.abs(raw))), 0.0)
    log_decay = params_ref[1:2] * steps
    tall = lax.broadcasted_iota(jnp.int32, (SPAN, SPAN), 0)
    wide = lax.broadcasted_iota(jnp.int32, (SPAN, SPAN), 1)
    lower = (tall >= wide).astype(bf16)
    span_lane = lax.broadcasted_iota(jnp.int32, (SPAN, LANES), 1)
    before = jnp.zeros((1, LANES), f32)
    start = jnp.ones((1, LANES), f32)
    starts, factors = [start], []
    reached = here == segment(begin - 1)
    for k in range(spans):
        at = k * SPAN
        rows = pl.ds(at, SPAN)
        parts = split_three(log_decay[at : at + SPAN])
        sums = mm(lower, jnp.concatenate(parts, axis=1))
        cumul = sums[:, :LANES] + sums[:, LANES : 2 * LANES] + sums[:, 2 * LANES :]
        last = cumul[SPAN - 1 : SPAN]
        span_here = here[at : at + SPAN]
        first = begin + at
        enters = jnp.logical_and(span_here == segment(first - 1), span_here >= 0)
        enter = jnp.where(jnp.logical_and(enters, first > 0), jnp.exp(cumul), 0.0)
        leave = jnp.where(
            span_here == segment(first + SPAN - 1), jnp.exp(last - cumul), 0.0
        )
        reach = jnp.where(
            jnp.logical_and(reached[at : at + SPAN], begin > 0), jnp.exp(cumul + before), 0.0
        )
        known = span_lane < NH
        steps_out[rows, :] = jnp.where(known, cumul, 0.0) + pltpu.roll(
            steps[at : at + SPAN], LANES // 2, 1
        )
        decay_out[rows, :] = jnp.where(known, enter, 0.0) + pltpu.roll(
            jnp.where(known, leave, 0.0), LANES // 2, 1
        )
        reach_out[rows, :] = jnp.where(known, reach, 0.0)
        turned_out[:, rows] = cumul.T[:NH]
        factors.append(enter[SPAN - 1 : SPAN])
        start = start * factors[-1]
        starts.append(start)
        before = before + last
        together = segment(tall + first) == segment(wide + first)
        mask_out[k] = jnp.where(jnp.logical_and(together, tall >= wide), 0.0, MASKED)
        mask_turned_out[k] = jnp.where(jnp.logical_and(together, tall <= wide), 0.0, MASKED)
    rest = lambda rows: jnp.concatenate(
        rows + [jnp.zeros((8 - len(rows), LANES), f32)], axis=0
    )
    factor_out[...] = rest(factors)
    start_out[...] = rest(starts)


def prepare_call(spans, place, mixed, params):
    count = spans * SPAN
    whole = lambda *s: pl.BlockSpec(s, lambda i: (0,) * len(s))
    shapes = [
        (count, LANES),
        (count, LANES),
        (count, LANES),
        (NH, count),
        (8, LANES),
        (8, LANES),
        (CONV - 1, count, LANES),
        (CONV - 1, count, LANES),
        (CONV - 1, 8, LANES),
        (spans, SPAN, SPAN),
        (spans, SPAN, SPAN),
    ]
    return pl.pallas_call(
        functools.partial(prepare_kernel, spans),
        grid=(1,),
        in_specs=[
            pl.BlockSpec(memory_space=pltpu.SMEM),
            pl.BlockSpec((count, LANES), lambda i: (0, CONVD // LANES)),
            whole(8, LANES),
        ],
        out_specs=[whole(*s) for s in shapes],
        out_shape=[jax.ShapeDtypeStruct(s, f32) for s in shapes],
        compiler_params=pltpu.CompilerParams(vmem_limit_bytes=VMEM_LIMIT),
        name="steps_and_masks",
    )(place, mixed, params)


MESH = pl.DeviceIdType.MESH
Z = 4
Y = 2


PARTS = 2


class Gathering:
    def __init__(self, blocks, wholes, sems):
        self.arrays = []
        for block, whole in zip(blocks, wholes):
            rows = block.shape[0] // PARTS
            self.arrays += [(block, whole, part * rows, rows) for part in range(PARTS)]
        self.own, self.up_sem, self.down_sem, self.z_sem, *sems = sems
        self.y_sent, self.y_sem, self.x_sent, self.x_sem, self.core_sent, self.core_sem = sems
        self.f, self.ctx = lax.axis_index("fsdp"), lax.axis_index("ctx")
        self.z, self.y = self.f // Y, lax.rem(self.f, Y)
        self.x, self.c = self.ctx // 2, lax.rem(self.ctx, 2)
        self.at_y = (self.z * Y + 1 - self.y, self.ctx)
        self.at_x = (self.f, (1 - self.x) * 2 + self.c)
        self.at_core = (self.f, self.x * 2 + 1 - self.c)

    def at_z(self, other):
        return other * Y + self.y, self.ctx

    def rows_of(self, n):
        return self.arrays[n][3]

    def place(self, n, block, row, size):
        own, whole, offset, rows = self.arrays[n]
        return whole.at[pl.ds(block * own.shape[0] + offset + row, size)]

    def third(self, n):
        return self.rows_of(n) // 6

    def gathered(self, n):
        return self.c * (self.rows_of(n) // 2) + self.x * self.third(n), 2 * self.third(n)

    def move(self, n, block, row, size, sent, landed, partner, own=False):
        here = self.place(n, block, row, size)
        source = self.arrays[n][0].at[pl.ds(self.arrays[n][2] + row, size)] if own else here
        return pltpu.make_async_remote_copy(
            src_ref=source,
            dst_ref=here,
            send_sem=sent,
            recv_sem=landed,
            device_id=partner,
            device_id_type=MESH,
        )

    def up(self, n, zb, own=False):
        sems = self.up_sem.at[n, zb], self.z_sem.at[n, zb]
        block = zb * Y + self.y
        return self.move(n, block, *self.gathered(n), *sems, self.at_z(self.z + 1), own)

    def down(self, n, zb, own=False):
        sems = self.down_sem.at[n, zb], self.z_sem.at[n, zb]
        block = zb * Y + self.y
        return self.move(n, block, *self.gathered(n), *sems, self.at_z(self.z - 1), own)

    def along_y(self, n, zb, yb, own=False):
        sems = self.y_sent.at[n, zb], self.y_sem.at[n, zb]
        return self.move(n, zb * Y + yb, *self.gathered(n), *sems, self.at_y, own)

    def along_x(self, n, block, sender_x):
        row = self.c * (self.rows_of(n) // 2) + 2 * self.third(n) * sender_x
        sems = self.x_sent.at[n, block], self.x_sem.at[n, block]
        return self.move(n, block, row, self.third(n), *sems, self.at_x)

    def core_first(self, n, block, core):
        row = core * (self.rows_of(n) // 2) + self.x * self.third(n)
        sems = self.core_sent.at[n, block, 0], self.core_sem.at[n, block, 0]
        return self.move(n, block, row, 2 * self.third(n), *sems, self.at_core)

    def core_second(self, n, block, core):
        row = core * (self.rows_of(n) // 2) + 2 * self.third(n) * (1 - self.x)
        sems = self.core_sent.at[n, block, 1], self.core_sem.at[n, block, 1]
        return self.move(n, block, row, self.third(n), *sems, self.at_core)

    def own_copy(self, n):
        block, whole, offset, rows = self.arrays[n]
        return pltpu.make_async_copy(
            block.at[pl.ds(offset, rows)], self.place(n, self.f, 0, rows), self.own.at[n]
        )

    def begin(self):
        barrier = pltpu.get_barrier_semaphore()
        signal = functools.partial(
            pl.semaphore_signal, barrier, inc=1, device_id_type=MESH
        )
        for partner in (self.at_y, self.at_x, self.at_core):
            signal(device_id=partner)

        @pl.when(self.z > 0)
        def _():
            signal(device_id=self.at_z(self.z - 1))

        @pl.when(self.z < Z - 1)
        def _():
            signal(device_id=self.at_z(self.z + 1))

        middle = jnp.logical_and(self.z > 0, self.z < Z - 1).astype(jnp.int32)
        pl.semaphore_wait(barrier, 4 + middle)
        for n in range(len(self.arrays)):
            self.own_copy(n).start()

            @pl.when(self.z < Z - 1)
            def _():
                self.up(n, self.z, True).start()

            @pl.when(self.z > 0)
            def _():
                self.down(n, self.z, True).start()

            self.along_y(n, self.z, self.y, True).start()

    def spread(self, n, block):
        self.along_x(n, block, self.x).start()
        self.core_first(n, block, self.c).start()

    def from_z(self, n, distance):
        for way in (1, -1):
            zb = self.z - way * distance

            @pl.when(jnp.logical_and(zb >= 0, zb < Z))
            def _():
                self.up(n, zb).wait_recv()
                if way == 1:

                    @pl.when(self.z < Z - 1)
                    def _():
                        self.up(n, zb).start()
                else:

                    @pl.when(self.z > 0)
                    def _():
                        self.down(n, zb).start()

                self.along_y(n, zb, self.y).start()
                self.spread(n, zb * Y + self.y)

    def from_y(self, n, distance):
        for way in (1, -1) if distance else (1,):
            zb = self.z - way * distance

            @pl.when(jnp.logical_and(zb >= 0, zb < Z))
            def _():
                self.along_y(n, zb, 1 - self.y).wait_recv()
                self.spread(n, zb * Y + 1 - self.y)

    def each_block(self, do):
        def at(zb, yb):
            @pl.when(jnp.logical_and(zb >= 0, zb < Z))
            def _():
                for n in range(len(self.arrays)):
                    do(n, zb * Y + yb)

        for distance in range(Z):
            for way in (1, -1) if distance else (1,):
                if distance:
                    at(self.z - way * distance, self.y)
                at(self.z - way * distance, 1 - self.y)

    def end(self):
        def come_along_x(n, block):
            self.along_x(n, block, 1 - self.x).wait_recv()
            self.core_second(n, block, self.c).start()

        def finish(n, block):
            self.core_first(n, block, 1 - self.c).wait_recv()
            self.core_second(n, block, 1 - self.c).wait_recv()
            self.along_x(n, block, self.x).wait_send()
            self.core_first(n, block, self.c).wait_send()
            self.core_second(n, block, self.c).wait_send()

        self.each_block(come_along_x)
        self.each_block(finish)
        for n in range(len(self.arrays)):
            self.own_copy(n).wait()
            for zb in range(Z):
                self.along_y(n, zb, self.y).wait_send()

                @pl.when(jnp.logical_and(self.z < Z - 1, zb <= self.z))
                def _():
                    self.up(n, zb).wait_send()

                @pl.when(jnp.logical_and(self.z > 0, zb >= self.z))
                def _():
                    self.down(n, zb).wait_send()


def gathering_semaphores(count):
    dma = lambda *s: pltpu.SemaphoreType.DMA((count * PARTS,) + s)
    size = Z * Y
    return [dma()] + [dma(Z)] * 5 + [dma(size)] * 2 + [dma(size, 2)] * 2


def whole_shapes(blocks):
    return [jax.ShapeDtypeStruct((b.shape[0] * Z * Y, b.shape[1]), b.dtype) for b in blocks]


def gather_kernel(count, *refs):
    gathering = Gathering(refs[:count], refs[count : 2 * count], refs[2 * count :])
    parts = range(len(gathering.arrays))
    gathering.begin()
    for distance in range(1, Z):
        for n in parts:
            gathering.from_z(n, distance)
            gathering.from_y(n, distance - 1)
    for n in parts:
        gathering.from_y(n, Z - 1)
    gathering.end()


def gather_call(*blocks):
    count = len(blocks)
    return pl.pallas_call(
        functools.partial(gather_kernel, count),
        in_specs=[pl.BlockSpec(memory_space=pl.ANY)] * count,
        out_specs=[pl.BlockSpec(memory_space=pl.ANY)] * count,
        out_shape=whole_shapes(blocks),
        scratch_shapes=gathering_semaphores(count),
        compiler_params=pltpu.CompilerParams(collective_id=0, has_side_effects=True),
        name="gather_rows",
    )(*blocks)


Z_STEPS = {at: (n % 4, 1 + n // 4) for n, at in enumerate((2, 4, 6, 7, 9, 11, 13, 14, 16, 18, 20, 21))}
Y_STEPS = {at: (n % 4, n // 4) for n, at in enumerate((3, 5, 7, 8, 10, 12, 14, 15, 17, 19, 21, 22))}


def forward_kernel(
    spans,
    blocks,
    block_ref,
    key_ref,
    query_ref,
    edge_ref,
    key_edge_ref,
    query_edge_ref,
    taps_ref,
    key_taps_ref,
    query_taps_ref,
    inside_ref,
    outside_ref,
    steps_ref,
    decay_ref,
    rows_ref,
    factor_ref,
    mask_ref,
    *refs,
):
    block_refs, refs = refs[:blocks], refs[blocks:]
    inner_out, local_out, state_out, key_out, query_out, *refs = refs
    whole_refs, refs = refs[:blocks], refs[blocks:]
    scores, key_turned, query_both, room, *sems = refs
    room[:8, :] = jnp.zeros((8, LANES), f32)
    pair = pl.program_id(0)
    if blocks:
        gathering = Gathering(block_refs, whole_refs, sems)
        pl.when(pair == 0)(gathering.begin)
        for at, what in Z_STEPS.items():
            pl.when(pair == at)(functools.partial(gathering.from_z, *what))
        for at, what in Y_STEPS.items():
            pl.when(pair == at)(functools.partial(gathering.from_y, *what))

    @pl.when(pair == 0)
    def _():
        for src, edge, taps, out in (
            (key_ref, key_edge_ref, key_taps_ref, key_out),
            (query_ref, query_edge_ref, query_taps_ref, query_out),
        ):
            pre = conv_pre(
                src[...], conv_shifts(src[...], edge[...], inside_ref, outside_ref, room), taps[...]
            )
            out[...] = pre * sigmoid(pre)
        for k in range(spans):
            rows = pl.ds(k * SPAN, SPAN)
            keys, queries = key_out[rows, :], query_out[rows, :]
            kh, kl = split(keys)
            qh, ql = split(queries)
            query_both[rows, :] = jnp.concatenate([qh, ql], axis=1)
            scores[k] = mm_nt(
                jnp.concatenate([qh, ql], axis=1), jnp.concatenate([kh, kh], axis=1)
            ) + mm_nt(qh, kl)
            th, tl = split(keys.T)
            key_turned[k, 0] = th
            key_turned[k, 1] = tl

    block = block_ref[...]
    pre = conv_pre(
        block, conv_shifts(block, edge_ref[...], inside_ref, outside_ref, room), taps_ref[...]
    )
    inner = pre * sigmoid(pre)
    inner_out[...] = inner
    turned, unused, steps = pair_columns(steps_ref[...], pair)
    unused, enter, leave = pair_columns(decay_ref[...], pair)
    scaled = steps * inner
    leaving = leave * scaled
    lane = lax.broadcasted_iota(jnp.int32, (HALF, LANES), 1)
    head_rows = [head_row(rows_ref[...], 2 * pair + a) for a in range(2)]
    factor = pair_rows(factor_ref[...], pair)
    state = None
    for k in range(spans):
        at = k * SPAN
        sh, sl = split(scaled[at : at + SPAN])
        both = jnp.concatenate([sh, sl], axis=1)
        parts = []
        for half in range(2):
            width = HALF * (half + 1)
            here, there = pl.ds(half * HALF, HALF), pl.ds(0, width)
            both_heads = []
            for a in range(2):
                row = head_rows[a][:, at : at + width]
                column = turned[at + half * HALF : at + (half + 1) * HALF, a : a + 1]
                decay = jnp.exp(jnp.minimum(column - row, mask_ref[k, here, there]))
                both_heads.append(decay * scores[k, here, there])
            wh, wl = split(jnp.concatenate(both_heads, axis=0))
            wide = mm(wh, both[:width])
            wide = wide[:, :LANES] + wide[:, LANES:] + mm(wl, sh[:width])
            parts.append(jnp.where(lane < HD, wide[:HALF], wide[HALF:]))
        local = jnp.concatenate(parts, axis=0)
        ph, pw = split(leaving[at : at + SPAN])
        fresh = mm(key_turned[k, 0], jnp.concatenate([ph, pw], axis=1))
        fresh = fresh[:, :LANES] + fresh[:, LANES:] + mm(key_turned[k, 1], ph)
        if state is None:
            state = fresh
        else:
            th, tl = split(state)
            q2 = query_both[pl.ds(at, SPAN), :]
            carried = mm(q2, jnp.concatenate([th, th], axis=0)) + mm(q2[:, :DS], tl)
            local = local + enter[at : at + SPAN] * carried
            state = factor[k : k + 1] * state + fresh
        state_out[k] = state
        local_out[pl.ds(at, SPAN), :] = local
    if blocks:

        @pl.when(pair == PAIRS - 1)
        def _():
            for n in range(blocks * PARTS):
                gathering.from_y(n, Z - 1)
            gathering.end()


def forward_call(
    spans, mixed, edge, taps, inside, outside, steps, decay, rows, factor, mask, blocks
):
    count = spans * SPAN
    at_pair = lambda n: pl.BlockSpec((n, LANES), lambda i: (0, i))
    at_key = lambda n: pl.BlockSpec((n, LANES), lambda i: (0, PAIRS))
    at_query = lambda n: pl.BlockSpec((n, LANES), lambda i: (0, PAIRS + 1))
    whole = lambda *s: pl.BlockSpec(s, lambda i: (0,) * len(s))
    remote = dict(collective_id=5, has_side_effects=True) if blocks else {}
    return pl.pallas_call(
        functools.partial(forward_kernel, spans, len(blocks)),
        grid=(PAIRS,),
        in_specs=[
            at_pair(count),
            at_key(count),
            at_query(count),
            at_pair(8),
            at_key(8),
            at_query(8),
            at_pair(8),
            at_key(8),
            at_query(8),
            whole(3, count, LANES),
            whole(3, 8, LANES),
            whole(count, LANES),
            whole(count, LANES),
            pl.BlockSpec((8, count), lambda i: (i // 4, 0)),
            whole(8, LANES),
            whole(spans, SPAN, SPAN),
        ]
        + [pl.BlockSpec(memory_space=pl.ANY)] * len(blocks),
        out_specs=[
            at_pair(count),
            at_pair(count),
            pl.BlockSpec((spans, DS, LANES), lambda i: (0, 0, i)),
            whole(count, LANES),
            whole(count, LANES),
        ]
        + [pl.BlockSpec(memory_space=pl.ANY)] * len(blocks),
        out_shape=[
            jax.ShapeDtypeStruct((count, DI), f32),
            jax.ShapeDtypeStruct((count, DI), f32),
            jax.ShapeDtypeStruct((spans, DS, DI), f32),
            jax.ShapeDtypeStruct((count, DS), f32),
            jax.ShapeDtypeStruct((count, DS), f32),
        ]
        + whole_shapes(blocks),
        scratch_shapes=[
            pltpu.VMEM((spans, SPAN, SPAN), f32),
            pltpu.VMEM((spans, 2, DS, SPAN), bf16),
            pltpu.VMEM((count, 2 * DS), bf16),
            pltpu.VMEM((count + 8, LANES), f32),
        ]
        + (gathering_semaphores(len(blocks)) if blocks else []),
        compiler_params=pltpu.CompilerParams(vmem_limit_bytes=VMEM_LIMIT, **remote),
        cost_estimate=pl.CostEstimate(flops=1, bytes_accessed=1, transcendentals=0),
        name="recurrence_forward",
    )(
        mixed,
        mixed,
        mixed,
        edge,
        edge,
        edge,
        taps,
        taps,
        taps,
        inside,
        outside,
        steps,
        decay,
        rows,
        factor,
        mask,
        *blocks,
    )


def norm_kernel(
    local_ref,
    inner_ref,
    gate_ref,
    back_ref,
    query_ref,
    state_ref,
    reach_ref,
    spread_ref,
    skip_ref,
    gain_ref,
    out_ref,
    mixer_grad_ref,
    gate_grad_ref,
    gain_grad_ref,
    dots_ref,
    summary_ref,
    most_ref,
    mixed_y,
    state_both,
    reach_wide,
):
    step = pl.program_id(0)
    chunks = [pl.ds(c * NORM_COLS, NORM_COLS) for c in range(DI // NORM_COLS)]

    @pl.when(step == 0)
    def _():
        sh, sl = split(state_ref[...])
        state_both[0] = sh
        state_both[1] = sl
        gain_grad_ref[...] = jnp.zeros_like(gain_grad_ref)
        summary_ref[...] = jnp.zeros_like(summary_ref)
        most_ref[...] = jnp.zeros_like(most_ref)

    qh, ql = split(query_ref[...])
    query_both = jnp.concatenate([qh, ql], axis=1)
    rh, rl = split(reach_ref[...])
    reach_both = jnp.concatenate([rh, rl], axis=1)
    squares = jnp.zeros((NORM_ROWS, 1), f32)
    mixes = jnp.zeros((NORM_ROWS, 1), f32)
    for cols in chunks:
        sh, sl = state_both[0, :, cols], state_both[1, :, cols]
        spread = spread_ref[:, cols]
        reach = mm(reach_both, jnp.concatenate([spread, spread], axis=0))
        reach_wide[:, cols] = reach
        carried = mm(query_both, jnp.concatenate([sh, sh], axis=0)) + mm(qh, sl)
        y = local_ref[:, cols] + reach * carried
        mixed_y[:, cols] = y
        mixer = y + skip_ref[0:1, cols] * inner_ref[:, cols]
        gate = gate_ref[:, cols]
        gated = mixer * (gate * sigmoid(gate))
        squares = squares + jnp.sum(gated * gated, axis=1, keepdims=True)
        mixes = mixes + jnp.sum(
            gated * (back_ref[:, cols] * gain_ref[0:1, cols]), axis=1, keepdims=True
        )
    scale = lax.rsqrt(squares * (1.0 / DI) + norm_eps)
    pull = scale * mixes * (1.0 / DI)
    query_turned = query_ref[...].T
    th, tl = split(query_turned)
    dots = jnp.zeros((NORM_ROWS, LANES), f32)
    for cols in chunks:
        y = mixed_y[:, cols]
        mixer = y + skip_ref[0:1, cols] * inner_ref[:, cols]
        gate = gate_ref[:, cols]
        opened = sigmoid(gate)
        silu = gate * opened
        unit = mixer * silu * scale
        gain = gain_ref[0:1, cols]
        back = back_ref[:, cols]
        out_ref[:, cols] = (unit * gain).astype(bf16)
        gain_grad_ref[0:1, cols] += jnp.sum(back * unit, axis=0, keepdims=True)
        gated_grad = scale * (back * gain - unit * pull)
        mixer_grad = gated_grad * silu
        mixer_grad_ref[:, cols] = mixer_grad
        gate_grad = gated_grad * mixer * (opened * (1.0 + gate * (1.0 - opened)))
        gate_grad_ref[:, cols] = gate_grad.astype(bf16)
        most = jnp.max(jnp.abs(gate_grad).reshape(NORM_ROWS // 8, 8, NORM_COLS), axis=0)
        for c in range(NORM_COLS // LANES):
            most_ref[...] = jnp.maximum(most_ref[...], most[:, c * LANES : (c + 1) * LANES])
        dh, dl = split(mixer_grad * y)
        spread = spread_ref[:, cols]
        dots = dots + mm_nt(dh, spread) + mm_nt(dl, spread)
        mh, ml = split(reach_wide[:, cols] * mixer_grad)
        summary_ref[:, cols] += (
            mm(jnp.concatenate([th, tl], axis=1), jnp.concatenate([mh, mh], axis=0)) + mm(th, ml)
        )
    dots_ref[...] = dots


def norm_call(local, inner, gate, back, queries, state_in, reach, spread, skip, gain):
    count = local.shape[0]
    rows = lambda n: pl.BlockSpec((NORM_ROWS, n), lambda i: (i, 0))
    whole = lambda *s: pl.BlockSpec(s, lambda i: (0,) * len(s))
    return pl.pallas_call(
        norm_kernel,
        grid=(count // NORM_ROWS,),
        in_specs=[
            rows(DI),
            rows(DI),
            rows(DI),
            rows(DI),
            rows(DS),
            whole(DS, DI),
            rows(LANES),
            whole(LANES, DI),
            whole(8, DI),
            whole(8, DI),
        ],
        out_specs=[
            rows(DI),
            rows(DI),
            rows(DI),
            whole(8, DI),
            rows(LANES),
            whole(DS, DI),
            whole(8, LANES),
        ],
        out_shape=[
            jax.ShapeDtypeStruct((count, DI), bf16),
            jax.ShapeDtypeStruct((count, DI), f32),
            jax.ShapeDtypeStruct((count, DI), bf16),
            jax.ShapeDtypeStruct((8, DI), f32),
            jax.ShapeDtypeStruct((count, LANES), f32),
            jax.ShapeDtypeStruct((DS, DI), f32),
            jax.ShapeDtypeStruct((8, LANES), f32),
        ],
        scratch_shapes=[
            pltpu.VMEM((NORM_ROWS, DI), f32),
            pltpu.VMEM((2, DS, DI), bf16),
            pltpu.VMEM((NORM_ROWS, DI), f32),
        ],
        compiler_params=pltpu.CompilerParams(vmem_limit_bytes=VMEM_LIMIT),
        cost_estimate=pl.CostEstimate(flops=1, bytes_accessed=1, transcendentals=0),
        name="gated_norm",
    )(local, inner, gate, back, queries, state_in, reach, spread, skip, gain)


class Agreement:
    def __init__(self, values_ref, out_ref, most, near, sent, landed):
        self.values_ref, self.out_ref = values_ref, out_ref
        self.most, self.near, self.sent, self.landed = most, near, sent, landed
        f, ctx = lax.axis_index("fsdp"), lax.axis_index("ctx")
        z, y, x, c = f // Y, lax.rem(f, Y), ctx // 2, lax.rem(ctx, 2)
        at = lambda z, y, x, c: (z * Y + y, x * 2 + c)
        self.phases = (
            [at(lax.rem(z + d, Z), y, x, c) for d in range(1, Z)],
            [at(z, y, x, 1 - c)],
            [at(z, y, 1 - x, c), at(z, 1 - y, x, c), at(z, 1 - y, 1 - x, c)],
        )

    def copies(self, phase):
        return [
            pltpu.make_async_remote_copy(
                src_ref=self.most.at[phase],
                dst_ref=self.near.at[phase, n],
                send_sem=self.sent.at[phase, n],
                recv_sem=self.landed.at[phase, n],
                device_id=partner,
                device_id_type=MESH,
            )
            for n, partner in enumerate(self.phases[phase])
        ]

    def begin(self):
        barrier = pltpu.get_barrier_semaphore()
        partners = [partner for phase in self.phases for partner in phase]
        for partner in partners:
            pl.semaphore_signal(barrier, inc=1, device_id=partner, device_id_type=MESH)
        self.most[0] = jnp.full((8, LANES), jnp.max(jnp.abs(self.values_ref[...])), f32)
        pl.semaphore_wait(barrier, len(partners))
        for copy in self.copies(0):
            copy.start()

    def arrived(self, phase):
        for copy in self.copies(phase):
            copy.wait()
        most = self.most[phase]
        for n in range(len(self.phases[phase])):
            most = jnp.maximum(most, self.near[phase, n])
        return most

    def go_on(self, phase):
        self.most[phase] = self.arrived(phase - 1)
        for copy in self.copies(phase):
            copy.start()

    def end(self):
        self.out_ref[0, 0] = jnp.max(self.arrived(2))


def agreement_scratch():
    return [
        pltpu.VMEM((3, 8, LANES), f32),
        pltpu.VMEM((3, 3, 8, LANES), f32),
        pltpu.SemaphoreType.DMA((3, 3)),
        pltpu.SemaphoreType.DMA((3, 3)),
    ]


def backward_kernel(spans, first, pairs, last, agree, *refs):
    (
        block_ref,
        edge_ref,
        taps_ref,
        inside_ref,
        inside_back_ref,
        outside_ref,
        keys_ref,
        queries_ref,
        back_ref,
        steps_ref,
        decay_ref,
        rows_ref,
        factor_ref,
        start_ref,
        mask_ref,
        states_ref,
        state_in_ref,
        state_back_ref,
        skip_ref,
        *refs,
    ) = refs
    if agree:
        most_ref, *refs = refs
    if last:
        dots_ref, raw_ref, params_ref, *refs = refs
        old_scores_grad, old_key_grad, old_query_grad, old_steps, old_heads, *refs = refs
    grad_out, top_out, tail_out, taps_out, most_out, *refs = refs
    scores_grad, key_grad, query_grad, steps_out, heads_out, *refs = refs
    if last:
        sums_out, *refs = refs
    if agree:
        agreed_out, *refs = refs
    scores, key_both, query_both, query_turned, room, columns, *refs = refs
    step = pl.program_id(0)
    if agree:
        agreement = Agreement(most_ref, agreed_out, *refs)
        pl.when(step == 0)(agreement.begin)
        pl.when(step == 3)(functools.partial(agreement.go_on, 1))
        pl.when(step == 6)(functools.partial(agreement.go_on, 2))
        pl.when(step == pairs - 1)(agreement.end)
    pair = step + first
    lane = lax.broadcasted_iota(jnp.int32, (SPAN, LANES), 1)

    @pl.when(step == 0)
    def _():
        if last:
            key_grad[...] = old_key_grad[...]
            query_grad[...] = old_query_grad[...]
            scores_grad[...] = old_scores_grad[...]
            steps_out[...] = old_steps[...]
            heads_out[...] = old_heads[...]
        else:
            key_grad[...] = jnp.zeros_like(key_grad)
            query_grad[...] = jnp.zeros_like(query_grad)
            scores_grad[...] = jnp.zeros_like(scores_grad)
            steps_out[...] = jnp.zeros_like(steps_out)
            heads_out[...] = jnp.zeros_like(heads_out)
        for n, (packed, shift) in enumerate(
            ((steps_ref, LANES // 2), (decay_ref, 0), (decay_ref, LANES // 2))
        ):
            values = pltpu.roll(packed[...], shift, 1) if shift else packed[...]
            columns[n] = jnp.concatenate(split(values), axis=1)
        for k in range(spans):
            rows = pl.ds(k * SPAN, SPAN)
            keys, queries = keys_ref[rows, :], queries_ref[rows, :]
            kh, kl = split(keys)
            qh, ql = split(queries)
            key_both[rows, :] = jnp.concatenate([kh, kl], axis=1)
            query_both[rows, :] = jnp.concatenate([qh, ql], axis=1)
            scores[k] = mm_nt(
                jnp.concatenate([kh, kl], axis=1), jnp.concatenate([qh, qh], axis=1)
            ) + mm_nt(kh, ql)
            th, tl = split(queries.T)
            query_turned[k, 0] = th
            query_turned[k, 1] = tl

    def conv_back(conved_grad, block, shifted, pre):
        opened = sigmoid(pre)
        pre_grad = conved_grad * (opened * (1.0 + pre * (1.0 - opened)))
        count = block.shape[0]
        taps = taps_ref[...]
        total = taps[3:4] * pre_grad
        sums = [None] * 8
        sums[3] = jnp.sum(pre_grad * block, axis=0, keepdims=True)
        sums[4] = jnp.sum(pre_grad, axis=0, keepdims=True)
        room[pl.ds(0, count), :] = pre_grad
        room[pl.ds(count, 8), :] = jnp.zeros((8, LANES), f32)
        for j in range(1, CONV):
            total = total + taps[3 - j : 4 - j] * (
                inside_back_ref[j - 1] * room[pl.ds(j, count), :]
            )
            sums[3 - j] = jnp.sum(pre_grad * shifted[j - 1], axis=0, keepdims=True)
        grad_out[...] = total.astype(bf16)
        tail_out[...] = total[count - 8 :]
        most_out[...] = jnp.max(jnp.abs(total).reshape(count // 8, 8, LANES), axis=0)
        top_out[...] = pre_grad[:8]
        return sums

    zero_row = jnp.zeros((1, LANES), f32)

    def of_conv():
        block = block_ref[...]
        room[:8, :] = jnp.zeros((8, LANES), f32)
        shifted = conv_shifts(block, edge_ref[...], inside_ref, outside_ref, room)
        return block, shifted, conv_pre(block, shifted, taps_ref[...])

    @pl.when(step < pairs)
    def _():
        block, shifted, pre = of_conv()
        head_rows = [head_row(rows_ref[...], 2 * pair + a) for a in range(2)]
        factor = pair_rows(factor_ref[...], pair)
        start = pair_rows(start_ref[...], pair)
        skip = pair_rows(skip_ref[...], pair)
        inner = pre * sigmoid(pre)
        back = back_ref[...]
        turned = pltpu.roll(steps_ref[...], lax.rem(LANES - 2 * pair, LANES), 1)
        steps, enter, leave = (spread_pair(columns[n], pair) for n in range(3))
        scaled = steps * inner
        leaving = leave * scaled
        entering = enter * back
        state_in = state_in_ref[...]
        state_back = state_back_ref[...]
        scaled_grads = [None] * spans
        ends = [zero_row] * 8
        for k in reversed(range(spans)):
            at = k * SPAN
            rows = pl.ds(at, SPAN)
            bh, bl = split(back[at : at + SPAN])
            both = jnp.concatenate([bh, bl], axis=1)
            sh, sl = split(scaled[at : at + SPAN])
            zero = jnp.zeros((SPAN, LANES), bf16)
            sl_turned = pltpu.roll(sl.astype(f32), HD, 1).astype(bf16)
            bh_turned = pltpu.roll(bh.astype(f32), HD, 1).astype(bf16)
            lefts, rights = [], []
            for a in range(2):
                mine = (lane < HD) if a == 0 else (lane >= HD)
                of_mine = lambda one, other: jnp.where(mine, one, other)
                lefts.append(
                    jnp.concatenate([of_mine(sh, sl_turned), of_mine(sh, zero)], axis=1)
                )
                rights.append(
                    jnp.concatenate([of_mine(bh, bh_turned), of_mine(bl, zero)], axis=1)
                )
            parts = []
            for half in range(2):
                low = half * HALF
                width = SPAN - low
                here = pl.ds(low, HALF)
                there = pl.ds(low, width)
                both_heads = []
                grads = None
                for a in range(2):
                    row = head_rows[a][:, at + low : at + low + width]
                    column = turned[at + low : at + low + HALF, a : a + 1]
                    decay = jnp.exp(jnp.minimum(row - column, mask_ref[k, here, there]))
                    both_heads.append(decay * scores[k, here, there])
                    grad = decay * mm_nt(lefts[a][low : low + HALF], rights[a][low:])
                    grads = grad if grads is None else grads + grad
                scores_grad[k, here, there] += grads
                wh, wl = split(jnp.concatenate(both_heads, axis=0))
                wide = mm(wh, both[low:])
                wide = wide[:, :LANES] + wide[:, LANES:] + mm(wl, bh[low:])
                parts.append(jnp.where(lane[:HALF] < HD, wide[:HALF], wide[HALF:]))
            scaled_grad = jnp.concatenate(parts, axis=0)
            gh, gl = split(state_back)
            k2 = key_both[rows, :]
            scaled_grad = scaled_grad + leave[at : at + SPAN] * (
                mm(k2, jnp.concatenate([gh, gh], axis=0)) + mm(k2[:, :DS], gl)
            )
            scaled_grads[k] = scaled_grad
            lh, ll = split(leaving[at : at + SPAN])
            key_grad[rows, :] += mm_nt(
                jnp.concatenate([lh, ll], axis=1), jnp.concatenate([gh, gh], axis=1)
            ) + mm_nt(lh, gl)
            after = states_ref[k] + start[k + 1 : k + 2] * state_in
            ends[k] = jnp.sum(state_back * after, axis=0, keepdims=True)
            before = start[k : k + 1] * state_in
            if k > 0:
                before = before + states_ref[k - 1]
            th, tl = split(before)
            eh, el = split(entering[at : at + SPAN])
            query_grad[rows, :] += mm_nt(
                jnp.concatenate([eh, el], axis=1), jnp.concatenate([th, th], axis=1)
            ) + mm_nt(eh, tl)
            if k > 0:
                more = mm(query_turned[k, 0], jnp.concatenate([eh, el], axis=1))
                state_back = (
                    factor[k : k + 1] * state_back
                    + more[:, :LANES]
                    + more[:, LANES:]
                    + mm(query_turned[k, 1], eh)
                )
        scaled_grad = jnp.concatenate(scaled_grads, axis=0)
        target = lax.broadcasted_iota(jnp.int32, (LANES, LANES), 1)
        source = lax.broadcasted_iota(jnp.int32, (LANES, LANES), 0)
        place = (target == 2 * pair + source // HD).astype(bf16)
        dh, dl = split(inner * scaled_grad)
        steps_out[...] += mm(dh, place) + mm(dl, place)
        sums = conv_back(steps * scaled_grad + skip[0:1] * back, block, shifted, pre)
        ends[4] = jnp.sum(back * inner, axis=0, keepdims=True)
        taps_out[...] = jnp.concatenate([zero_row if s is None else s for s in sums], axis=0)
        eh, el, ew = split_three(jnp.concatenate(ends, axis=0))
        heads_out[...] += mm(eh, place) + mm(el, place) + mm(ew, place)

    if not last:
        return

    def of_scores(grad_ref, ones_ref, transposed):
        for k in range(spans):
            rows = pl.ds(k * SPAN, SPAN)
            grad = scores_grad[k]
            gh, gl = split(grad.T if transposed else grad)
            ones = ones_ref[rows, :]
            wide = mm(gh, ones)
            grad_ref[rows, :] += wide[:, :DS] + wide[:, DS:] + mm(gl, ones[:, :DS])

    @pl.when(jnp.logical_and(step >= pairs, step < pairs + 2))
    def _():
        @pl.when(step == pairs)
        def _():
            of_scores(key_grad, query_both, False)

        @pl.when(step == pairs + 1)
        def _():
            of_scores(query_grad, key_both, True)

        block, shifted, pre = of_conv()
        grad = jnp.where(step == pairs, key_grad[...], query_grad[...])
        sums = conv_back(grad, block, shifted, pre)
        taps_out[...] = jnp.concatenate([zero_row if s is None else s for s in sums], axis=0)

    @pl.when(step == pairs + 2)
    def _():
        tall = lax.broadcasted_iota(jnp.int32, (SPAN, SPAN), 0)
        wide = lax.broadcasted_iota(jnp.int32, (SPAN, SPAN), 1)
        upper = (tall <= wide).astype(bf16)
        known = lane < NH
        rate = params_ref[1:2]
        delta, decay, most = zero_row, zero_row, zero_row
        for k in range(spans):
            rows = pl.ds(k * SPAN, SPAN)
            steps = jnp.where(known, pltpu.roll(steps_ref[rows, :], LANES // 2, 1), 0.0)
            step_dots = steps_out[rows, :]
            cumul_grad = dots_ref[rows, :] - steps * step_dots
            parts = mm(upper, jnp.concatenate(split_three(cumul_grad), axis=1))
            decay_grad = parts[:, :LANES] + parts[:, LANES : 2 * LANES] + parts[:, 2 * LANES :]
            decay_grad = decay_grad + heads_out[k : k + 1]
            raw = jnp.where(known, raw_ref[rows, :], 0.0) + params_ref[0:1]
            raw_grad = (step_dots + rate * decay_grad) * sigmoid(raw)
            raw_grad = jnp.where(known, raw_grad, 0.0)
            grad_out[rows, :] = raw_grad.astype(bf16)
            most = jnp.maximum(most, jnp.max(jnp.abs(raw_grad), axis=0, keepdims=True))
            delta = delta + jnp.sum(raw_grad, axis=0, keepdims=True)
            decay = decay + jnp.sum(rate * steps * decay_grad, axis=0, keepdims=True)
        sums_out[...] = jnp.concatenate(
            [delta, decay, heads_out[4:5], most, jnp.zeros((4, LANES), f32)], axis=0
        )

    @pl.when(step > pairs + 2)
    def _():
        grad_out[...] = jnp.zeros_like(grad_out)


def backward_call(spans, first, pairs, columns, shared, finish=None, most=None):
    count = spans * SPAN
    last = finish is not None
    clip_block = lambda i: jnp.minimum(i + first, CONVD // LANES - 1)
    clip = lambda i: jnp.minimum(i, pairs - 1) + first
    at_block = lambda n: pl.BlockSpec((n, LANES), lambda i: (0, clip_block(i)))
    at_pair = lambda n: pl.BlockSpec((n, LANES), lambda i: (0, clip(i)))
    out_block = lambda n: pl.BlockSpec((n, LANES), lambda i: (0, i))
    whole = lambda *s: pl.BlockSpec(s, lambda i: (0,) * len(s))
    accumulators = [
        (spans, SPAN, SPAN),
        (count, DS),
        (count, DS),
        (count, LANES),
        (8, LANES),
    ]
    wide = columns * LANES
    side = (pairs + 2 if last else pairs) * LANES
    side_block = lambda: pl.BlockSpec(
        (8, LANES), lambda i: (0, jnp.minimum(i, side // LANES - 1))
    )
    in_specs = [
        at_block(count),
        at_block(8),
        at_block(8),
        whole(CONV - 1, count, LANES),
        whole(CONV - 1, count, LANES),
        whole(CONV - 1, 8, LANES),
        whole(count, DS),
        whole(count, DS),
        at_pair(count),
        whole(count, LANES),
        whole(count, LANES),
        pl.BlockSpec((8, count), lambda i: (clip(i) // 4, 0)),
        whole(8, LANES),
        whole(8, LANES),
        whole(spans, SPAN, SPAN),
        pl.BlockSpec((spans, DS, LANES), lambda i: (0, 0, clip(i))),
        at_pair(DS),
        at_pair(DS),
        whole(8, LANES),
    ]
    out_specs = [out_block(count)] + [side_block()] * 4 + [whole(*s) for s in accumulators]
    out_shape = [jax.ShapeDtypeStruct((count, wide), bf16)]
    out_shape += [jax.ShapeDtypeStruct((8, side), f32)] * 4
    out_shape += [jax.ShapeDtypeStruct(s, f32) for s in accumulators]
    operands = list(shared)
    scratch, remote = [], {}
    if most is not None:
        in_specs += [whole(8, LANES)]
        operands += [most]
        scratch, remote = agreement_scratch(), dict(collective_id=6, has_side_effects=True)
    if last:
        dots, mixed, params, earlier = finish
        in_specs += [
            whole(count, LANES),
            pl.BlockSpec((count, LANES), lambda i: (0, CONVD // LANES)),
            whole(8, LANES),
        ]
        in_specs += [whole(*s) for s in accumulators]
        operands += [dots, mixed, params, *earlier]
        out_specs += [whole(8, LANES)]
        out_shape += [jax.ShapeDtypeStruct((8, LANES), f32)]
    if most is not None:
        out_specs += [pl.BlockSpec(memory_space=pltpu.SMEM)]
        out_shape += [jax.ShapeDtypeStruct((1, 1), f32)]
    return pl.pallas_call(
        functools.partial(backward_kernel, spans, first, pairs, last, most is not None),
        grid=(columns,),
        in_specs=in_specs,
        out_specs=out_specs,
        out_shape=out_shape,
        scratch_shapes=[
            pltpu.VMEM((spans, SPAN, SPAN), f32),
            pltpu.VMEM((count, 2 * DS), bf16),
            pltpu.VMEM((count, 2 * DS), bf16),
            pltpu.VMEM((spans, 2, DS, SPAN), bf16),
            pltpu.VMEM((count + 8, LANES), f32),
            pltpu.VMEM((3, count, 2 * LANES), bf16),
        ]
        + scratch,
        compiler_params=pltpu.CompilerParams(vmem_limit_bytes=VMEM_LIMIT, **remote),
        cost_estimate=pl.CostEstimate(flops=1, bytes_accessed=1, transcendentals=0),
        name="recurrence_backward",
    )(*operands)


def sum_kernel(in_ref, limit_ref, *refs):
    *sizes, out_ref, own, near, far, whole, sent, landed = refs
    f, ctx = lax.axis_index("fsdp"), lax.axis_index("ctx")
    fsdp_size, ctx_size = lax.axis_size("fsdp"), lax.axis_size("ctx")
    most = functools.reduce(jnp.maximum, [jnp.max(jnp.abs(size[...])) for size in sizes])
    row = lax.broadcasted_iota(jnp.int32, in_ref.shape, 0)
    lane = lax.broadcasted_iota(jnp.int32, in_ref.shape, 1)
    last = jnp.logical_and(row == in_ref.shape[0] - 1, lane == LANES - 1)
    over = jnp.where(most <= limit_ref[0, 0], 0.0, 1.0)
    own[...] = in_ref[...] + jnp.where(last, over, 0.0)
    part = in_ref.shape[0] // fsdp_size
    in_ctx = [(f, lax.rem(ctx + d, ctx_size)) for d in range(1, ctx_size)]
    in_fsdp = [(lax.rem(f + d, fsdp_size), ctx) for d in range(1, fsdp_size)]
    barrier = pltpu.get_barrier_semaphore()
    for partner in in_ctx + in_fsdp:
        pl.semaphore_signal(barrier, inc=1, device_id=partner, device_id_type=MESH)
    pl.semaphore_wait(barrier, len(in_ctx) + len(in_fsdp))

    def exchange(phase, partners, source, target):
        copies = []
        for n, partner in enumerate(partners):
            copies.append(
                pltpu.make_async_remote_copy(
                    src_ref=source(partner),
                    dst_ref=target,
                    send_sem=sent.at[phase, n],
                    recv_sem=landed.at[phase, n],
                    device_id=partner,
                    device_id_type=MESH,
                )
            )
            copies[-1].start()
        return copies

    copies = exchange(0, in_ctx, lambda partner: own, near.at[ctx])
    near[pl.ds(ctx, 1)] = own[...][None]
    for copy in copies:
        copy.wait()
    whole[...] = jnp.sum(near[...], axis=0)
    mine = pl.ds(pl.multiple_of(f * part, 8), part)
    copies = exchange(
        1, in_fsdp, lambda partner: whole.at[pl.ds(pl.multiple_of(partner[0] * part, 8), part)], far.at[f]
    )
    far[pl.ds(f, 1)] = whole[mine, :][None]
    for copy in copies:
        copy.wait()
    out_ref[mine, :] = jnp.sum(far[...], axis=0)
    for copy in exchange(2, in_fsdp, lambda partner: out_ref.at[mine], out_ref.at[mine]):
        copy.wait()


def sum_everywhere(value, limit, sizes):
    if not on_small_slice():
        return lax.psum(value, ("fsdp", "ctx")), None
    fsdp_size, ctx_size = lax.axis_size("fsdp"), lax.axis_size("ctx")
    block = 8 * LANES * fsdp_size
    rows = -(-(value.shape[0] + 1) // block) * block // LANES
    shape = (rows, LANES)
    padded_value = jnp.pad(value, (0, rows * LANES - value.shape[0])).reshape(shape)
    peers = max(fsdp_size, ctx_size) - 1
    out = pl.pallas_call(
        sum_kernel,
        in_specs=[
            pl.BlockSpec(memory_space=pltpu.VMEM),
            pl.BlockSpec(memory_space=pltpu.SMEM),
        ]
        + [pl.BlockSpec(memory_space=pltpu.VMEM)] * len(sizes),
        out_specs=pl.BlockSpec(memory_space=pltpu.VMEM),
        out_shape=jax.ShapeDtypeStruct(shape, f32),
        scratch_shapes=[
            pltpu.VMEM(shape, f32),
            pltpu.VMEM((ctx_size,) + shape, f32),
            pltpu.VMEM((fsdp_size, rows // fsdp_size, LANES), f32),
            pltpu.VMEM(shape, f32),
            pltpu.SemaphoreType.DMA((3, peers)),
            pltpu.SemaphoreType.DMA((3, peers)),
        ],
        compiler_params=pltpu.CompilerParams(collective_id=4, has_side_effects=True),
        cost_estimate=pl.CostEstimate(flops=1, bytes_accessed=1, transcendentals=0),
        name="sum_everywhere",
    )(padded_value, limit.reshape(1, 1), *sizes)
    return out.reshape(-1)[: value.shape[0]], out[rows - 1, LANES - 1] > 0.0


FILL_COLS = 256


def block_out_kernel(mixer_ref, whole_ref, tokens_ref, out_ref):
    projected = mm(mixer_ref[...], whole_ref[...])
    out_ref[...] = (tokens_ref[...].astype(f32) + projected).astype(bf16)


def block_out_call(mixer_low, whole_out, tokens):
    count, width = tokens.shape
    columns = lambda n: pl.BlockSpec((n, FILL_COLS), lambda j: (0, j))
    return pl.pallas_call(
        block_out_kernel,
        grid=(width // FILL_COLS,),
        in_specs=[pl.BlockSpec((count, DI), lambda j: (0, 0)), columns(DI), columns(count)],
        out_specs=columns(count),
        out_shape=jax.ShapeDtypeStruct(tokens.shape, bf16),
        compiler_params=pltpu.CompilerParams(vmem_limit_bytes=VMEM_LIMIT),
        cost_estimate=pl.CostEstimate(flops=1, bytes_accessed=1, transcendentals=0),
        name="block_out",
    )(mixer_low, whole_out, tokens)


def input_grad_kernel(
    split_at,
    second_width,
    gate_ref,
    first_ref,
    second_ref,
    whole_gate_ref,
    whole_conv_ref,
    tokens_ref,
    cotangent_ref,
    gain_ref,
    out_ref,
    gain_grad_ref,
    unit_grads,
    scales,
    mixes,
):
    step, steps = pl.program_id(0), pl.num_programs(0)
    count = tokens_ref.shape[0]

    @pl.when(step == 0)
    def _():
        mixes[...] = jnp.zeros_like(mixes)
        for at in range(0, count, SPAN):
            rows = pl.ds(at, SPAN)
            inputs = tokens_ref[rows, :].astype(f32)
            mean = jnp.mean(inputs * inputs, axis=-1, keepdims=True)
            scales[rows, :] = jnp.broadcast_to(lax.rsqrt(mean + norm_eps), (SPAN, LANES))

    grad = mm_nt(gate_ref[...], whole_gate_ref[...])
    grad = grad + mm_nt(first_ref[...], whole_conv_ref[:, :split_at])
    grad = grad + mm_nt(
        second_ref[:, :second_width], whole_conv_ref[:, split_at : split_at + second_width]
    )
    here = pl.ds(pl.multiple_of(step * FILL_COLS, FILL_COLS), FILL_COLS)
    unit = tokens_ref[:, here].astype(f32) * scales[:, 0:1]
    gain_grad_ref[0:1, :] = jnp.sum(grad * unit, axis=0, keepdims=True)
    unit_grad = grad * gain_ref[0:1, :]
    unit_grads[step] = unit_grad
    mixes[...] += jnp.broadcast_to(
        jnp.sum(unit_grad * unit, axis=-1, keepdims=True), mixes.shape
    )

    @pl.when(step == steps - 1)
    def _():
        width = tokens_ref.shape[1]
        for at in range(0, count, SPAN):
            rows = pl.ds(at, SPAN)
            scale = scales[rows, 0:1]
            mean = mixes[rows, 0:1] * (1.0 / width)
            for n in range(width // FILL_COLS):
                cols = pl.ds(n * FILL_COLS, FILL_COLS)
                unit = tokens_ref[rows, cols].astype(f32) * scale
                out_ref[rows, cols] = cotangent_ref[rows, cols].astype(f32) + scale * (
                    unit_grads[n, rows, :] - unit * mean
                )


def input_grad_call(
    split_at,
    gate_grad,
    first_grad,
    second_grad,
    whole_gate,
    whole_conv,
    tokens,
    cotangent,
    gain,
):
    count, width = tokens.shape
    once = lambda *s: pl.BlockSpec(s, lambda j: (0,) * len(s), pipeline_mode=pl.Buffered(1))
    rows = lambda n: pl.BlockSpec((FILL_COLS, n), lambda j: (j, 0))
    columns = lambda n: pl.BlockSpec((n, FILL_COLS), lambda j: (0, j))
    steps = width // FILL_COLS
    return pl.pallas_call(
        functools.partial(input_grad_kernel, split_at, whole_conv.shape[1] - split_at),
        grid=(steps,),
        in_specs=[
            once(*gate_grad.shape),
            once(*first_grad.shape),
            once(*second_grad.shape),
            rows(whole_gate.shape[1]),
            rows(whole_conv.shape[1]),
            once(count, width),
            once(count, width),
            columns(8),
        ],
        out_specs=[pl.BlockSpec((count, width), lambda j: (0, 0)), columns(8)],
        out_shape=[
            jax.ShapeDtypeStruct((count, width), f32),
            jax.ShapeDtypeStruct((8, width), f32),
        ],
        scratch_shapes=[
            pltpu.VMEM((steps, count, FILL_COLS), f32),
            pltpu.VMEM((count, LANES), f32),
            pltpu.VMEM((count, LANES), f32),
        ],
        compiler_params=pltpu.CompilerParams(vmem_limit_bytes=VMEM_LIMIT),
        cost_estimate=pl.CostEstimate(flops=1, bytes_accessed=1, transcendentals=0),
        name="input_grad",
    )(gate_grad, first_grad, second_grad, whole_gate, whole_conv, tokens, cotangent, gain)


def adam_kernel(blocks, core_ref, *refs):
    grads, refs = refs[: 2 * blocks], refs[2 * blocks :]
    param_ref, first_ref, second_ref = refs[:3]
    outs = refs[-3:]
    width = param_ref.shape[1]
    own_first = core_ref[0] == 0
    begin = 0
    for n in range(blocks):
        own_ref, other_ref = grads[2 * n], grads[2 * n + 1]
        for left in (True, False):
            for at in range(0, own_ref.shape[1], LANES):
                size = min(LANES, width - begin)
                if size <= 0:
                    continue
                there, cols = pl.ds(at, size), pl.ds(begin, size)
                own, other = own_ref[:, there], other_ref[:, there]
                one, two = (own, other) if left else (other, own)
                new = adamw_update(
                    param_ref[:, cols],
                    jnp.where(own_first, one, two),
                    first_ref[:, cols],
                    second_ref[:, cols],
                    weight_decay,
                )
                for out, value in zip(outs, new):
                    out[:, cols] = value
                begin += size


def adam_call(core, grads, rows, param, first, second):
    total, width = param.shape
    rows = min(rows, total)
    place = lambda n: pl.BlockSpec((rows, n), lambda i: (i, 0))
    pieces = [piece for pair in grads for piece in pair]
    return pl.pallas_call(
        functools.partial(adam_kernel, len(grads)),
        grid=(total // rows,),
        in_specs=[pl.BlockSpec(memory_space=pltpu.SMEM)]
        + [place(piece.shape[1]) for piece in pieces]
        + [place(width)] * 3,
        out_specs=[place(width)] * 3,
        out_shape=[jax.ShapeDtypeStruct(param.shape, f32)] * 3,
        compiler_params=pltpu.CompilerParams(vmem_limit_bytes=VMEM_LIMIT),
        cost_estimate=pl.CostEstimate(flops=1, bytes_accessed=1, transcendentals=0),
        name="adam",
    )(core, *pieces, param, first, second)


def adamw_update(param, grad, first, second, decay):
    first_new = beta_one * first + (1.0 - beta_one) * grad
    second_new = beta_two * second + (1.0 - beta_two) * grad * grad
    first_hat = first_new / (1.0 - beta_one**STEP)
    second_hat = second_new / (1.0 - beta_two**STEP)
    param_new = param - learn_rate * (first_hat / (jnp.sqrt(second_hat) + adam_eps) + decay * param)
    return (param_new, first_new, second_new)


def segment_of(lengths, positions):
    ends = jnp.cumsum(lengths)
    return jnp.sum((positions[..., None] >= ends).astype(jnp.int32), axis=-1)


def padded(*rows):
    out = jnp.stack([jnp.pad(r, (0, LANES - r.shape[0])) for r in rows])
    return jnp.pad(out, ((0, 8 - len(rows)), (0, 0)))


def spread_matrix():
    head = lax.broadcasted_iota(jnp.int32, (LANES, DI), 0)
    lane = lax.broadcasted_iota(jnp.int32, (LANES, DI), 1)
    return (head == lane // HD).astype(bf16)


def pass_on(own, factor, axis, backwards, kind):
    size, here = lax.axis_size(axis), lax.axis_index(axis)
    given = jnp.zeros_like(own)
    for turn in range(size - 1):
        source = size - 1 - turn if backwards else turn
        target = source - 1 if backwards else source + 1
        out = (factor * given + own).astype(kind)
        arrived = lax.ppermute(out, axis, [(source, target)]).astype(f32)
        given = jnp.where(here == target, arrived, given)
    return given


def on_small_slice():
    return lax.axis_size("fsdp") == Z * Y and lax.axis_size("ctx") == 4


def all_rows(block):
    return lax.all_gather(block, "fsdp", axis=0, tiled=True)


def swapped(value, axis, step):
    size = lax.axis_size(axis)
    return lax.ppermute(value, axis, [(i, i ^ step) for i in range(size)])


def after(value, *others):
    return lax.optimization_barrier((value,) + others)[0]


def coordinates():
    f, ctx = lax.axis_index("fsdp"), lax.axis_index("ctx")
    return ctx // 2, f % Y, f // Y, ctx % 2


CORE = ("ctx", 1)
ACROSS_X = ("ctx", 2)
ACROSS_Y = ("fsdp", 1)
ACROSS_Z = tuple(("fsdp", Y * m) for m in range(1, Z))


def row_products(columns, grads):
    return jnp.einsum("tk,tz->kz", columns, grads, preferred_element_type=f32)


def half_of(value, bit, axis):
    size = value.shape[axis] // 2
    return lax.dynamic_slice_in_dim(value, bit * size, size, axis)


class Part:
    def __init__(self, value, bound):
        self.value, self.bound = value, bound

    def plus(self, arrived, other):
        return Part(self.value + raised(arrived, other), self.bound + other)


def lowered(value, bound):
    return (value * (32768.0 / bound)).astype(jnp.float16)


def raised(value, bound):
    return value.astype(f32) * (bound * (1.0 / 32768.0))


def summed_on_chip(columns, grads, bound, other=None):
    core = coordinates()[3]
    theirs = row_products(columns, half_of(grads, 1 - core, 1))
    arrived = swapped(lowered(theirs, bound), *CORE)
    mine = Part(row_products(columns, half_of(grads, core, 1)), bound)
    return mine.plus(arrived, bound if other is None else other)


def to_send(part, bit, axis):
    sent = lowered(half_of(part.value, 1 - bit, axis), part.bound)
    return Part(half_of(part.value, bit, axis), part.bound), sent


def joined_with(kept, arrived, other=None):
    return kept.plus(arrived, kept.bound if other is None else other)


def by_owner(part):
    return Part(part.value.reshape(Z, Y, -1, part.value.shape[1]), part.bound)


def along_z(part):
    z = coordinates()[2]
    take = lambda at: lax.dynamic_index_in_dim(part.value[:, 0], at, 0, keepdims=False)
    sent = [lowered(take(z ^ m), part.bound) for m in range(1, Z)]
    return Part(take(z), part.bound), sent


def of_owner(kept, arrived):
    total = kept
    for one in arrived:
        total = total.plus(one, kept.bound)
    return total


def both_columns(value, way, bit):
    other = swapped(value, *way)
    return jnp.where(
        bit == 0,
        jnp.concatenate([value, other], axis=1),
        jnp.concatenate([other, value], axis=1),
    )


def sum_of_two(low, arrived, bound):
    return raised(low, bound) + raised(arrived, bound)


ROOM = 64.0


def owned_rows(partial):
    return lax.psum(lax.psum_scatter(partial, "fsdp", scatter_dimension=0, tiled=True), "ctx")


def largest(value):
    return jnp.max(jnp.abs(value)).astype(f32) + 1e-30


def on_device(
    tokens_in,
    cotangent,
    doc_lengths,
    in_proj,
    out_proj,
    norm_gain,
    gate_gain,
    conv_weight,
    conv_bias,
    delta_bias,
    decay_log,
    skip_scale,
    in_first,
    in_second,
    out_first,
    out_second,
    small_first,
    small_second,
):
    count = tokens_in.shape[0]
    spans = count // SPAN
    ctx = lax.axis_size("ctx")
    begin = lax.axis_index("ctx") * count
    lengths = doc_lengths[0]
    small_slice = on_small_slice()

    if small_slice:
        gate_block, conv_block, out_block = cast_call(in_proj, out_proj)
        (whole_conv,) = gather_call(conv_block)
    else:
        blocks = in_proj[:, DI:], in_proj[:, :DI], out_proj
        whole_conv, whole_gate, whole_out = (all_rows(b.astype(bf16)) for b in blocks)
    inputs = tokens_in.astype(f32)
    scale = lax.rsqrt(jnp.mean(inputs * inputs, axis=-1, keepdims=True) + norm_eps)
    normed = (inputs * scale * norm_gain[None, :]).astype(bf16)

    mixed = mm(normed, whole_conv)
    edge = lax.ppermute(mixed[count - 8 :, :CONVD], "ctx", [(i, i + 1) for i in range(ctx - 1)])
    edge = jnp.where(jnp.arange(8)[:, None] >= 8 - (CONV - 1), edge, 0.0)

    place = jnp.concatenate([begin[None].astype(jnp.int32), lengths.astype(jnp.int32)])
    params = padded(delta_bias, -jnp.exp(decay_log))
    (
        steps,
        decay,
        reach,
        rows,
        factor,
        start,
        inside,
        inside_back,
        outside,
        mask,
        mask_turned,
    ) = prepare_call(spans, place, mixed, params)
    taps = jnp.concatenate([conv_weight.T, conv_bias[None], jnp.zeros((3, CONVD), f32)], axis=0)

    inner, local, states, keys, queries, *wholes = forward_call(
        spans,
        mixed,
        edge,
        taps,
        inside,
        outside,
        steps,
        decay,
        rows,
        factor,
        mask,
        (gate_block, out_block) if small_slice else (),
    )
    if small_slice:
        whole_gate, whole_out = wholes
    total_lanes = jnp.repeat(start[spans, :NH], HD)[None]
    state_in = pass_on(states[spans - 1], total_lanes, "ctx", False, f32)
    gate = mm(normed, whole_gate)
    mixer_back = jnp.einsum("td,kd->tk", cotangent, whole_out, preferred_element_type=f32)
    mixer_low, mixer_grad, gate_grad, gate_gain_grad, dots, summary, gate_most_rows = norm_call(
        local,
        inner,
        gate,
        mixer_back,
        queries,
        state_in,
        reach,
        spread_matrix(),
        jnp.repeat(skip_scale, HD)[None] + jnp.zeros((8, 1), f32),
        gate_gain[None] + jnp.zeros((8, 1), f32),
    )
    state_back = pass_on(summary, total_lanes, "ctx", True, bf16)

    out_bound = count * 6.0 * (DI**0.5 * 1.01) * largest(gate_gain)
    product_bound = count * (D**0.5 * 1.01) * largest(norm_gain)
    x, y, z, core = coordinates()
    if small_slice:
        out_part = summed_on_chip(mixer_low, cotangent, out_bound)
        out_kept, out_sent = to_send(out_part, x, 1)
        mosts, others = [1.01 * product_bound * largest(gate_most_rows)], []
        for way in (CORE, ACROSS_Y):
            others.append(swapped(mosts[-1].reshape(1, 1), *way).reshape(()))
            mosts.append(jnp.maximum(mosts[-1], others[-1]))
        gate_part = summed_on_chip(normed, gate_grad, mosts[0], others[0])
        gate_kept, gate_sent = to_send(by_owner(Part(gate_part.value, 2.0 * mosts[1])), y, 1)
        mixer_grad, out_sent, gate_sent = lax.optimization_barrier(
            (mixer_grad, out_sent, gate_sent)
        )
        out_got = swapped(out_sent, *ACROSS_X)
        gate_got = swapped(gate_sent, *ACROSS_Y)

    first_pairs = 14
    skip = padded(skip_scale)
    shared = lambda back: (
        mixed,
        edge,
        taps,
        inside,
        inside_back,
        outside,
        keys,
        queries,
        back,
        steps,
        decay,
        rows,
        factor,
        start,
        mask_turned,
        states,
        state_in,
        state_back,
        skip,
    )
    following = segment_of(lengths, begin + count + jnp.arange(CONV, dtype=jnp.int32))
    own_last = segment_of(lengths, begin + count - CONV + jnp.arange(CONV, dtype=jnp.int32))

    def with_edge(grad, top, tail, at):
        next_top = lax.ppermute(top, "ctx", [(i + 1, i) for i in range(ctx - 1)])
        width = tail.shape[1]
        for j in range(1, CONV):
            joined = (following[:j] == own_last[CONV - j :]).astype(f32)
            more = joined[:, None] * next_top[:j] * taps[3 - j : 4 - j, at : at + width]
            tail = tail + jnp.pad(more, ((8 - j, 0), (0, 0)))
        return lax.dynamic_update_slice(grad, tail.astype(bf16), (count - 8, 0)), tail

    first_grad, top, tail, first_taps_grad, most, *sums = backward_call(
        spans,
        0,
        first_pairs,
        first_pairs,
        shared(mixer_grad),
        most=gate_most_rows if small_slice else None,
    )
    if small_slice:
        top, tail, most, first_grad, out_got, gate_got = lax.optimization_barrier(
            (top, tail, most, first_grad, out_got, gate_got)
        )
    first_grad, tail = with_edge(first_grad, top, tail, 0)
    if small_slice:
        out_kept, out_sent = to_send(by_owner(joined_with(out_kept, out_got)), y, 1)
        *sums, agreed = sums
        gate_most = 1.01 * product_bound * agreed.reshape(()) + 1e-30
        gate_part = joined_with(gate_kept, gate_got, 2.0 * others[1])
        gate_kept, gate_sent = along_z(Part(gate_part.value, 4.0 * gate_most))
        conv_bound = ROOM * gate_most
        first_sizes = most, tail
        first_part = summed_on_chip(normed, first_grad, conv_bound)
        first_kept, first_sent = to_send(by_owner(first_part), y, 1)
        mixer_grad, out_sent, gate_sent, first_sent = lax.optimization_barrier(
            (mixer_grad, out_sent, gate_sent, first_sent)
        )
        out_got = swapped(out_sent, *ACROSS_Y)
        gate_got = [swapped(s, *way) for s, way in zip(gate_sent, ACROSS_Z)]
        first_got = swapped(first_sent, *ACROSS_Y)
    second_grad, top, tail, second_taps_grad, most, *sums = backward_call(
        spans,
        first_pairs,
        PAIRS - first_pairs,
        14,
        shared(mixer_grad),
        (dots, mixed, params, sums),
    )
    split_at = first_pairs * LANES
    fence = lax.optimization_barrier
    if small_slice:
        top, tail, most, second_grad, sums, out_got, gate_got, first_got = fence(
            (top, tail, most, second_grad, sums, out_got, gate_got, first_got)
        )
        out_kept, out_sent = along_z(joined_with(out_kept, out_got))
        first_kept, first_sent = along_z(joined_with(first_kept, first_got))
        out_high = out_sent[0].shape[0] // 2
        both_sent = [
            jnp.concatenate([one, other[:out_high], other[out_high:]], axis=1)
            for one, other in zip(first_sent, out_sent)
        ]
        gate_part = Part(of_owner(gate_kept, gate_got).value, 16.0 * gate_most)
        gate_low = lowered(gate_part.value, gate_part.bound)
        both_sent, gate_low, tail, most = fence((both_sent, gate_low, tail, most))
        both_got = [swapped(s, *way) for s, way in zip(both_sent, ACROSS_Z)]
        gate_got = swapped(gate_low, *ACROSS_X)
    second_grad, tail = with_edge(second_grad, top, tail, split_at)
    if small_slice:
        second_part = summed_on_chip(normed, second_grad, conv_bound)
        second_kept, second_sent = to_send(by_owner(second_part), y, 1)
        (
            second_sent,
            gate_grad,
            mixer_low,
            sums,
            gate_gain_grad,
            first_taps_grad,
            second_taps_grad,
            conv_weight,
            sizes,
        ) = fence(
            (
                second_sent,
                gate_grad,
                mixer_low,
                sums,
                gate_gain_grad,
                first_taps_grad,
                second_taps_grad,
                conv_weight,
                (*first_sizes, most, tail),
            )
        )
        second_got = swapped(second_sent, *ACROSS_Y)
    input_grad, norm_gain_grad = input_grad_call(
        split_at,
        gate_grad,
        first_grad,
        second_grad,
        whole_gate,
        whole_conv,
        tokens_in,
        cotangent,
        norm_gain[None] + jnp.zeros((8, 1), f32),
    )
    block_out = block_out_call(mixer_low, whole_out, tokens_in)
    limit = None
    if not small_slice:
        sizes = ()
    if small_slice:
        second_got, both_got, gate_got, input_grad, norm_gain_grad, block_out = fence(
            (second_got, both_got, gate_got, input_grad, norm_gain_grad, block_out)
        )
        second_kept, second_sent = along_z(joined_with(second_kept, second_got))
        first_wide = first_part.value.shape[1]
        out_wide = (both_got[0].shape[1] - first_wide) // 2
        out_got = [
            jnp.concatenate(
                [s[:, first_wide : first_wide + out_wide], s[:, first_wide + out_wide :]], axis=0
            )
            for s in both_got
        ]
        first_part = of_owner(first_kept, [s[:, :first_wide] for s in both_got])
        first_low = lowered(first_part.value, first_part.bound)
        out_total = of_owner(out_kept, out_got).value
        gate_rows = sum_of_two(gate_low, gate_got, gate_part.bound)
        second_sent, first_low, out_total, gate_rows, norm_gain_grad = fence(
            (second_sent, first_low, out_total, gate_rows, norm_gain_grad)
        )
        second_got = [swapped(s, *way) for s, way in zip(second_sent, ACROSS_Z)]
        first_got = swapped(first_low, *ACROSS_X)
        out_got = swapped(out_total, *ACROSS_X)
        limit = conv_bound * (1.0 / (1.01 * product_bound))
        sizes = *sizes, sums[5][3:4]
    flat_weight, norm_gain_grad = fence((conv_weight.reshape(-1), norm_gain_grad))
    taps_grad = jnp.concatenate([first_taps_grad, second_taps_grad], axis=1)
    small_grad, over = sum_everywhere(
        jnp.concatenate(
            [
                norm_gain_grad[0],
                gate_gain_grad[0],
                taps_grad[:CONV].T.reshape(-1),
                taps_grad[4],
                sums[5][0, :NH],
                sums[5][1, :NH],
                sums[5][2, :NH],
            ]
        ),
        limit,
        sizes,
    )

    def in_updated(core, *pairs):
        return tuple(adam_call(core, pairs, 24, in_proj, in_first, in_second))

    def out_updated(core, pair):
        return tuple(adam_call(core, (pair,), 48, out_proj, out_first, out_second))

    def halves_in_float32(columns, grads):
        rows = owned_rows(row_products(columns, grads))
        return rows[:, : rows.shape[1] // 2], rows[:, rows.shape[1] // 2 :]

    def in_float32():
        grads = gate_grad, first_grad, second_grad
        pairs = [halves_in_float32(normed, one) for one in grads]
        return in_updated(jnp.zeros((1,), jnp.int32), *pairs)

    def out_in_float32():
        return out_updated(jnp.zeros((1,), jnp.int32), halves_in_float32(mixer_low, cotangent))

    if small_slice:
        small_grad, over, first_got, out_got, gate_rows, second_got = fence(
            (small_grad, over, first_got, out_got, gate_rows, second_got)
        )
        second_part = of_owner(second_kept, second_got)
        second_low = lowered(second_part.value, second_part.bound)
        second_low, first_got, out_got = fence((second_low, first_got, out_got))
        second_got = swapped(second_low, *ACROSS_X)
        first_rows = sum_of_two(first_low, first_got, first_part.bound)
        out_rows = jnp.where(
            x == 0,
            jnp.concatenate([out_total, out_got], axis=1),
            jnp.concatenate([out_got, out_total], axis=1),
        )
        gate_pair = gate_rows, swapped(gate_rows, *CORE)
        first_pair = first_rows, swapped(first_rows, *CORE)
        out_pair = out_rows, swapped(out_rows, *CORE)
        core_index = core[None].astype(jnp.int32)
        out_news = lax.cond(over, out_in_float32, lambda: out_updated(core_index, out_pair))
        second_got, out_news = fence((second_got, out_news))
        second_rows = sum_of_two(second_low, second_got, second_part.bound)
        second_pair = second_rows, swapped(second_rows, *CORE)
        in_news = lax.cond(
            over,
            in_float32,
            lambda: in_updated(core_index, gate_pair, first_pair, second_pair),
        )
    else:
        in_news, out_news = in_float32(), out_in_float32()
    in_new, in_first_new, in_second_new = in_news
    out_new, out_first_new, out_second_new = out_news
    small_param = jnp.concatenate(
        [
            norm_gain,
            gate_gain,
            flat_weight,
            conv_bias,
            delta_bias,
            decay_log,
            skip_scale,
        ]
    )
    small_new, small_first_new, small_second_new = adamw_update(
        small_param, small_grad, small_first, small_second, 0.0
    )
    return (
        block_out,
        input_grad,
        in_new,
        in_first_new,
        in_second_new,
        out_new,
        out_first_new,
        out_second_new,
        small_new,
        small_first_new,
        small_second_new,
    )


def solution(mesh):
    placed = (
        P(("fsdp", "ctx"), None),
        P(("fsdp", "ctx"), None),
        P("fsdp", None),
        P("fsdp", None),
        P("fsdp", None),
        P(),
        P(),
        P(),
        P(),
        P(),
        P(),
        P(),
        P("fsdp", None),
        P("fsdp", None),
        P("fsdp", None),
        P("fsdp", None),
        P(),
        P(),
    )
    return jax.shard_map(
        on_device,
        mesh=mesh,
        in_specs=placed,
        out_specs=(
            P(("fsdp", "ctx"), None),
            P(("fsdp", "ctx"), None),
            P("fsdp", None),
            P("fsdp", None),
            P("fsdp", None),
            P("fsdp", None),
            P("fsdp", None),
            P("fsdp", None),
            P(),
            P(),
            P(),
        ),
        check_vma=False,
    )
```
